32 devices in a mesh: ctx: 8 (over z, core), fsdp: 4 (over y, x).
Axes of the slice: x: 2, y: 2, z: 4, core: 2. Of those that a mesh axis runs over, the one named last changes fastest.
Arguments:
- tokens: bfloat16 [4, 3072, 1536], P('fsdp', 'ctx'), may hold values from -6 to 6
- grad_out: bfloat16 [4, 3072, 1536], P('fsdp', 'ctx'), may hold values from -6 to 6
- order: int32 [4, 3072], P('fsdp'), may hold values from 0 to 3071, each once within a row
- lengths: int32 [4, 3], P('fsdp'), may hold values from 1 to 1536, 3072 in all within a row
- routes: int32 [4, 3072, 4], P('fsdp', 'ctx'), may hold values from 0 to 15, all different within a row
- gain_one: bfloat16 [1536], P('fsdp'), may hold values from 0.5 to 1.5
- gain_two: bfloat16 [1536], P('fsdp'), may hold values from 0.5 to 1.5
- w_query: bfloat16 [1536, 1536], P('fsdp'), may hold values from -0.21875 to 0.21875
- w_key: bfloat16 [1536, 256], P('fsdp'), may hold values from -0.21875 to 0.21875
- w_value: bfloat16 [1536, 256], P('fsdp'), may hold values from -0.15625 to 0.15625
- w_out: bfloat16 [1536, 1536], P('fsdp'), may hold values from -3.5 to 3.5
- w_router: bfloat16 [1536, 16], P('fsdp'), may hold values from -0.078125 to 0.078125
- w_gate: bfloat16 [16, 1536, 768], P('ctx', 'fsdp'), may hold values from -0.15625 to 0.15625
- w_up: bfloat16 [16, 1536, 768], P('ctx', 'fsdp'), may hold values from -0.15625 to 0.15625
- w_down: bfloat16 [16, 768, 1536], P('ctx', None, 'fsdp'), may hold values from -0.4375 to 0.4375
Outputs:
- output: bfloat16 [4, 3072, 1536], P('fsdp', 'ctx')
- input_grad: bfloat16 [4, 3072, 1536], P('fsdp', 'ctx')
- grad_gain_one: float32 [1536], P('fsdp')
- grad_gain_two: float32 [1536], P('fsdp')
- grad_query: float32 [1536, 1536], P('fsdp')
- grad_key: float32 [1536, 256], P('fsdp')
- grad_value: float32 [1536, 256], P('fsdp')
- grad_out_proj: float32 [1536, 1536], P('fsdp')
- grad_router: float32 [1536, 16], P('fsdp')
- grad_gate: float32 [16, 1536, 768], P('ctx', 'fsdp')
- grad_up: float32 [16, 1536, 768], P('ctx', 'fsdp')
- grad_down: float32 [16, 768, 1536], P('ctx', None, 'fsdp')
The draws below stay inside these ranges and needn't reach their ends.
Inputs may be any that keep to these rules, and one draw needn't show every extreme that they name: `order`: each row is a permutation of the numbers below 3072. `lengths`: each row sums to 3072, and its largest entry is 1536. `routes`: each row names 4 different experts.
All inputs are finite; a program needn't handle non-finite values.
Results may differ from the reference program's by a relative error of at most 0.024.
Values may be sent and summed in bfloat16 or wider, within the bound.
A program may use at most 192 MiB of HBM per device.

```python
import math
import jax
import jax.numpy as jnp
import numpy as np
from jax import lax

D = 1536
QUERY_HEADS = 12
KVH = 2
HEAD_SIZE = 128
FF = 768
TOP = 4
TOK_DEV = 384
NSEQ = 3
EXPERTS = 16
GROUP = 3072
GROUPS = 4
MAXLEN = 1536
CAP = 120
KEY_BLOCK_ROWS = 512
N_CTX = 8


def levels(stream_key, extent, pieces, smallest, high):
    level = 1.0
    for dim, blocks in pieces:
        heights = jax.random.uniform(jax.random.fold_in(jax.random.fold_in(stream_key, 6), dim), (blocks,), jnp.float32, smallest / len(pieces), high / len(pieces))
        level = level * jnp.repeat(jnp.exp(heights), extent[dim] // blocks).reshape((-1,) + (1,) * (len(extent) - 1 - dim))
    return level


def distinct(key, rows, count, top, lift):
    ranking = jax.random.permutation(jax.random.fold_in(key, 1), count)
    boost = ranking
    for power in range(3):
        boost = boost * boost // count
    boost = boost * lift // count
    chance = jax.random.randint(jax.random.fold_in(key, 2), (rows, count), 0, 4096) + boost
    fixed_rows = jax.random.permutation(jax.random.fold_in(key, 3), rows)[jnp.arange(count) % rows]
    chance = jnp.where(jnp.arange(rows)[:, None] == fixed_rows[None, :], 1 << 14, chance)
    merit = chance * count + jnp.arange(count)
    return lax.top_k(merit.astype(jnp.int32), top)[1].astype(jnp.int32)


def split_up(count, total, reach, skew):
    portions = [(1 << 20) // math.isqrt(grade ** skew) + 1 for grade in range(2, count + 1)]
    surplus, given = total - reach - (count - 1), [1] * (count - 1)
    while surplus > 0:
        candidates = [i for i in range(count - 1) if given[i] < reach]
        pool, left = sum([portions[i] for i in candidates]), surplus
        for i in candidates:
            addition = min(reach - given[i], max(1, left * portions[i] // pool), surplus)
            given[i] = given[i] + addition
            surplus = surplus - addition
    return np.array([reach] + given)


def ragged(own_key, amount, total, most, lean):
    if amount == 2:
        one = jax.random.randint(own_key, (), max(1, total - most), min(most, total - 1) + 1)
        return jnp.stack([one, total - one])
    tallies = jnp.asarray(split_up(amount, total, most, lean), jnp.int32)
    pairs = (amount - 1) // 2
    donor, receiver = tallies[1:1 + 2 * pairs:2], tallies[2:2 + 2 * pairs:2]
    margin = jnp.minimum(donor - 1, most - receiver)
    passed = jax.random.randint(jax.random.fold_in(own_key, 1), (pairs,), 0, 1 << 20) % (margin + 1)
    tallies = tallies.at[1:1 + 2 * pairs:2].set(donor - passed).at[2:2 + 2 * pairs:2].set(receiver + passed)
    return tallies[jax.random.permutation(jax.random.fold_in(own_key, 2), amount)]


def centred(key, dims, deviation, bound, split=(), kind=jnp.bfloat16):
    values = deviation * jax.random.normal(key, dims, jnp.float32)
    if split:
        values = values * levels(key, dims, split, -0.22, 0.18)
    return jnp.clip(values, -bound, bound).astype(kind)


def setup_inputs(seed: int = 0) -> dict:
    keys = jax.random.split(jax.random.key(seed), 16)
    tokens = centred(keys[0], (GROUPS, GROUP, D), 1.0, 6.0, ((0, 4), (1, 8)))
    grad_out = centred(keys[1], (GROUPS, GROUP, D), 1.0, 6.0, ((0, 4), (1, 8)))
    order = jax.vmap(lambda own: jax.random.permutation(own, GROUP))(jax.random.split(keys[2], GROUPS)).reshape((GROUPS, GROUP)).astype(jnp.int32)
    lengths = jax.vmap(lambda own: ragged(own, NSEQ, GROUP, MAXLEN, 1))(jax.random.split(keys[3], GROUPS)).reshape((GROUPS, NSEQ)).astype(jnp.int32)
    routes = distinct(keys[4], GROUPS * GROUP, EXPERTS, TOP, 2048).reshape((GROUPS, GROUP, TOP))
    gain_one = jnp.clip(1.0 + 0.1 * jax.random.normal(keys[5], (D,), jnp.float32), 0.5, 1.5).astype(jnp.bfloat16)
    gain_two = jnp.clip(1.0 + 0.1 * jax.random.normal(keys[6], (D,), jnp.float32), 0.5, 1.5).astype(jnp.bfloat16)
    w_query = centred(keys[7], (D, QUERY_HEADS * HEAD_SIZE), (D // 2) ** -0.5, 0.21875, ((0, 4),))
    w_key = centred(keys[8], (D, KVH * HEAD_SIZE), (D // 2) ** -0.5, 0.21875, ((0, 4),))
    w_value = centred(keys[9], (D, KVH * HEAD_SIZE), D ** -0.5, 0.15625, ((0, 4),))
    w_out = centred(keys[10], (QUERY_HEADS * HEAD_SIZE, D), (max(1, QUERY_HEADS * HEAD_SIZE * 2 * NSEQ // GROUP)) ** -0.5, 3.5, ((0, 4),))
    w_router = centred(keys[11], (D, EXPERTS), (4 * D) ** -0.5, 0.078125, ((0, 4),))
    w_gate = centred(keys[12], (EXPERTS, D, FF), D ** -0.5, 0.15625, ((0, 8), (1, 4)))
    w_up = centred(keys[13], (EXPERTS, D, FF), D ** -0.5, 0.15625, ((0, 8), (1, 4)))
    w_down = centred(keys[14], (EXPERTS, FF, D), (FF // 4) ** -0.5, 0.4375, ((0, 8), (2, 4)))
    return dict(tokens=tokens, grad_out=grad_out, order=order, lengths=lengths, routes=routes, gain_one=gain_one, gain_two=gain_two, w_query=w_query, w_key=w_key, w_value=w_value, w_out=w_out, w_router=w_router, w_gate=w_gate, w_up=w_up, w_down=w_down)


@jax.custom_vjp
def low(v):
    return lax.optimization_barrier(v.astype(jnp.bfloat16)).astype(jnp.float32)

@jax.custom_vjp
def lower_backward(v):
    return v

def low_keep(v):
    return (low(v), None)

def low_pass(kept, grad):
    return (grad,)

def back_keep(v):
    return (v, None)

def back_low(kept, grad):
    return (low(grad),)
low.defvjp(low_keep, low_pass)
lower_backward.defvjp(back_keep, back_low)
EPSILON = 1e-06
ROPE_BASE = 10000.0
MASKED = -1e+30
HIGH_PRECISION = lax.Precision.HIGHEST

def highest(left, right):
    return jnp.dot(left, right, precision=HIGH_PRECISION, preferred_element_type=jnp.float32)

def rms_scale(value_rows, gain):
    return value_rows * lax.rsqrt(lax.optimization_barrier(jnp.mean(value_rows * value_rows, axis=-1, keepdims=True)) + EPSILON) * gain

def rotate(value_rows, position):
    half_dim = value_rows.shape[-1] // 2
    freqs = ROPE_BASE ** (-2.0 * jnp.arange(half_dim).astype(jnp.float32) / value_rows.shape[-1])
    angles = position.astype(jnp.float32)[:, None] * freqs[None, :]
    cosine = jnp.cos(angles)[:, None, :]
    sine = jnp.sin(angles)[:, None, :]
    first = value_rows[..., :half_dim]
    second = value_rows[..., half_dim:]
    return jnp.concatenate([first * cosine - second * sine, second * cosine + first * sine], axis=-1)

def token_tables(order_row, length_row):
    ends = jnp.cumsum(length_row).astype(jnp.int32)
    starts = ends - length_row
    doc_ids = lax.optimization_barrier(jnp.sum((order_row[:, None] >= ends[None, :]).astype(jnp.int32), axis=1))
    seq_ids = jnp.arange(length_row.shape[0]).astype(jnp.int32)
    doc_start = lax.optimization_barrier(jnp.sum(jnp.where(doc_ids[:, None] == seq_ids[None, :], starts[None, :], 0), axis=1))
    return (doc_ids.astype(jnp.int32), (order_row - doc_start).astype(jnp.int32))

def slot_ranks(orig_dev, routes_dev):
    earlier = (orig_dev[None, :] < orig_dev[:, None]).astype(jnp.float32)
    route_onehot = (routes_dev[:, :, None] == jnp.arange(EXPERTS).astype(jnp.int32)[None, None, :]).astype(jnp.float32)
    counts = jnp.dot(earlier, lax.optimization_barrier(jnp.sum(route_onehot, axis=1)), preferred_element_type=jnp.float32)
    return lax.optimization_barrier(jnp.sum(counts[:, None, :] * route_onehot, axis=2)).astype(jnp.int32)

def attention(queries, key_rows, value_rows, doc_ids, orig):
    per_group = QUERY_HEADS // KVH
    grouped = queries.reshape(GROUP // KEY_BLOCK_ROWS, KEY_BLOCK_ROWS, KVH, per_group, HEAD_SIZE)

    def block(partial_results):
        query_tile, doc_block, orig_block = partial_results
        attention_scores = lower_backward(jnp.einsum('mjie,aje->jima', query_tile, key_rows, precision=HIGH_PRECISION) * HEAD_SIZE ** (-0.5))
        allowed = (doc_block[:, None] == doc_ids[None, :]) & (orig[None, :] <= orig_block[:, None])
        attention_scores = jnp.where(allowed[None, None], attention_scores, MASKED)
        attention_probs = low(jax.nn.softmax(attention_scores, axis=-1))
        return jnp.einsum('enjk,keo->jeno', attention_probs, value_rows, precision=HIGH_PRECISION).reshape(KEY_BLOCK_ROWS, QUERY_HEADS * HEAD_SIZE)
    blocks = lax.map(jax.checkpoint(block), (grouped, doc_ids.reshape(-1, KEY_BLOCK_ROWS), orig.reshape(-1, KEY_BLOCK_ROWS)))
    return lower_backward(low(blocks.reshape(GROUP, QUERY_HEADS * HEAD_SIZE)))

def expert_apply(partial_results):
    expert_rows, gate_w, up_w, down_w = partial_results
    gate_pre = lower_backward(highest(expert_rows, gate_w))
    up_pre = lower_backward(highest(expert_rows, up_w))
    inner = low(jax.nn.silu(gate_pre) * up_pre)
    return lower_backward(low(highest(inner, down_w)))

def group_forward(weights, inputs, orig, length_row, route_rows):
    gain_a, gain_b, query_w, key_w, value_w, out_w, router_w, gate_w, up_w, down_w = weights
    doc_ids, positions = token_tables(orig, length_row)
    normed_one = low(rms_scale(inputs, gain_a))
    query_pre = lower_backward(highest(normed_one, query_w))
    key_pre = lower_backward(highest(normed_one, key_w))
    value_pre = lower_backward(highest(normed_one, value_w))
    queries = low(rotate(query_pre.reshape(GROUP, QUERY_HEADS, HEAD_SIZE), positions))
    key_rows = low(rotate(key_pre.reshape(GROUP, KVH, HEAD_SIZE), positions))
    value_rows = low(value_pre).reshape(GROUP, KVH, HEAD_SIZE)
    attended = attention(queries, key_rows, value_rows, doc_ids, orig)
    middle = inputs + lower_backward(highest(attended, out_w))
    normed_two = low(rms_scale(middle, gain_b))
    logits = lower_backward(highest(normed_two, router_w))
    route_onehot = (route_rows[:, :, None] == jnp.arange(EXPERTS).astype(jnp.int32)[None, None, :]).astype(jnp.float32)
    chosen = lax.optimization_barrier(jnp.sum(logits[:, None, :] * route_onehot, axis=2))
    gate_weights = jax.nn.softmax(chosen, axis=-1)
    ranks = jax.vmap(slot_ranks)(orig.reshape(N_CTX, TOK_DEV), route_rows.reshape(N_CTX, TOK_DEV, TOP)).reshape(GROUP, TOP)
    device = (jnp.arange(GROUP).astype(jnp.int32) // TOK_DEV).astype(jnp.int32)
    slot_count = EXPERTS * N_CTX * CAP
    flat = jnp.where(ranks < CAP, route_rows * (N_CTX * CAP) + device[:, None] * CAP + ranks, slot_count).astype(jnp.int32)
    token_ids = jnp.repeat(jnp.arange(GROUP).astype(jnp.int32), TOP)
    table = jnp.full((slot_count + 1,), GROUP, jnp.int32).at[flat.reshape(-1)].set(token_ids)
    padded = jnp.concatenate([normed_two, jnp.zeros((1, D), normed_two.dtype)], axis=0)
    buffers = lower_backward(padded[table[:slot_count]]).reshape(EXPERTS, N_CTX * CAP, D)
    returned = lax.map(expert_apply, (buffers, gate_w, up_w, down_w))
    back = jnp.concatenate([returned.reshape(slot_count, D), jnp.zeros((1, D), returned.dtype)], axis=0)
    picked = back[flat]
    return middle + lax.optimization_barrier(jnp.sum(gate_weights[:, :, None] * picked, axis=1))

def reference(tokens, grad_out, order, lengths, routes, gain_one, gain_two, w_query, w_key, w_value, w_out, w_router, w_gate, w_up, w_down):
    weights = tuple((w.astype(jnp.float32) for w in (gain_one, gain_two, w_query, w_key, w_value, w_out, w_router, w_gate, w_up, w_down)))
    inputs = tokens.astype(jnp.float32)

    def forward(all_inputs, all_weights):
        return jnp.stack([group_forward(all_weights, all_inputs[g], order[g], lengths[g], routes[g]) for g in range(GROUPS)])
    result, pullback = jax.vjp(forward, inputs, weights)
    input_grad, weight_grads = pullback(grad_out.astype(jnp.float32))
    return (result.astype(jnp.bfloat16), input_grad.astype(jnp.bfloat16)) + tuple(weight_grads)
```

```python
import functools

import jax
import jax.numpy as jnp
from jax import lax
from jax.experimental import pallas as pl
from jax.experimental.pallas import tpu as pltpu
from jax.sharding import PartitionSpec as P

QUERY_HEADS = 12
KVH = 2
HEAD_SIZE = 128

EPSILON = 1e-06
ROPE_BASE = 10000.0
MASKED = -1e30
LOG2E = 1.4426950408889634
LANES = 128
SLOT_STEP = 64
KEY_TILE = 512
VMEM_BYTES = 60 * 1024 * 1024
MESH = pl.DeviceIdType.MESH
F32 = jnp.float32
BF16 = jnp.bfloat16


def dot(left, right, contract):
    return lax.dot_general(left, right, (contract, ((), ())), preferred_element_type=F32)


NN = ((1,), (0,))
NT = ((1,), (1,))
TN = ((0,), (0,))


def rms_scale(value_rows, gain):
    return (
        value_rows
        * lax.rsqrt(jnp.mean(value_rows * value_rows, axis=-1, keepdims=True) + EPSILON)
        * gain
    )


def rotate(value_rows, cosine, sine):
    half_dim = value_rows.shape[-1] // 2
    first = value_rows[..., :half_dim]
    second = value_rows[..., half_dim:]
    return jnp.concatenate(
        [first * cosine - second * sine, second * cosine + first * sine], axis=-1
    )


def place():
    ctx = lax.axis_index("ctx")
    core = lax.rem(ctx, 2)
    return ctx, lax.axis_index("fsdp"), ctx // 2, core, ctx + 1 - 2 * core


def peers_of(me, fsdp):
    peers = []
    for shift in range(1, fsdp):
        peer = me
        for bit in range(fsdp.bit_length() - 1):
            if (shift >> bit) & 1:
                digit = lax.rem(me // (1 << bit), 2)
                peer = peer + (1 << bit) - (2 << bit) * digit
        peers.append(peer)
    return peers


def greet(chips, peers, line):
    ctx, me, chip, core, sibling = place()
    barrier = pltpu.get_barrier_semaphore()
    for peer in peers:
        pl.semaphore_signal(barrier, inc=1, device_id=(ctx, peer), device_id_type=MESH)
    pl.semaphore_signal(barrier, inc=1, device_id=(sibling, me), device_id_type=MESH)
    known = len(peers) + 1
    if not line:
        pl.semaphore_wait(barrier, known)
        return
    has_right = chip + 1 < chips
    has_left = chip >= 1

    @pl.when(has_right)
    def _():
        pl.semaphore_signal(barrier, inc=1, device_id=(ctx + 2, me), device_id_type=MESH)

    @pl.when(has_left)
    def _():
        pl.semaphore_signal(barrier, inc=1, device_id=(ctx - 2, me), device_id_type=MESH)

    @pl.when(has_right & has_left)
    def _():
        pl.semaphore_wait(barrier, known + 2)

    @pl.when(jnp.logical_not(has_right & has_left))
    def _():
        pl.semaphore_wait(barrier, known + 1)


def remote(src, dst, send_sem, recv_sem, device):
    return pltpu.make_async_remote_copy(
        src_ref=src,
        dst_ref=dst,
        send_sem=send_sem,
        recv_sem=recv_sem,
        device_id=device,
        device_id_type=MESH,
    )


class DenseGather:
    def __init__(self, ins, outs, sems, fsdp):
        local_sem, send_sem, recv_sem, pass_sem, took_sem = sems
        ctx, me, chip, core, sibling = place()
        self.sends, self.passes, self.locals = [], [], []
        for i in range(len(ins)):
            rows = ins[i].shape[0]
            half = rows // 2
            for j, peer in enumerate(peers_of(me, fsdp)):
                self.sends.append(
                    remote(
                        ins[i].at[pl.ds(core * half, half)],
                        outs[i].at[pl.ds(me * rows + core * half, half)],
                        send_sem.at[i, j],
                        recv_sem.at[i, j],
                        (ctx, peer),
                    )
                )
                got = outs[i].at[pl.ds(peer * rows + core * half, half)]
                self.passes.append(
                    remote(got, got, pass_sem.at[i, j], took_sem.at[i, j], (sibling, me))
                )
            self.locals.append(
                pltpu.make_async_copy(
                    ins[i], outs[i].at[pl.ds(me * rows, rows)], local_sem.at[i]
                )
            )

    def start(self):
        for copy in self.sends + self.locals:
            copy.start()

    def finish(self):
        for send, copy in zip(self.sends, self.passes):
            send.wait_recv()
            copy.start()
        for send in self.sends:
            send.wait_send()
        for copy in self.passes + self.locals:
            copy.wait()


def dense_sems(count, fsdp):
    return [pltpu.SemaphoreType.DMA((count,))] + [
        pltpu.SemaphoreType.DMA((count, fsdp - 1)) for unused in range(4)
    ]


class LineGather:
    def __init__(self, ins, outs, sems, chips):
        self.ins, self.outs, self.chips = ins, outs, chips
        self.sems = sems
        self.ctx, self.me, self.chip, core, self.sibling = place()
        self.count = len(ins)

    def to_right(self, i, step):
        outs, chips = self.outs, self.chips
        return remote(
            self.ins[i] if step == 0 else outs[i].at[0, chips - step],
            outs[i].at[0, chips - 1 - step],
            self.sems[1].at[i, step],
            self.sems[2].at[i, step],
            (self.ctx + 2, self.me),
        )

    def to_left(self, i, step):
        outs = self.outs
        return remote(
            self.ins[i] if step == 0 else outs[i].at[0, step],
            outs[i].at[0, step + 1],
            self.sems[3].at[i, step],
            self.sems[4].at[i, step],
            (self.ctx - 2, self.me),
        )

    def across(self, i, slot):
        return remote(
            self.ins[i] if slot == 0 else self.outs[i].at[0, slot],
            self.outs[i].at[1, slot],
            self.sems[5].at[i, slot],
            self.sems[6].at[i, slot],
            (self.sibling, self.me),
        )

    def local(self, i):
        return pltpu.make_async_copy(self.ins[i], self.outs[i].at[0, 0], self.sems[0].at[i])

    def run(self):
        chip, chips, count = self.chip, self.chips, self.count
        for step in range(chips - 1):

            @pl.when((chip + 1 < chips) & (chip >= step))
            def _():
                for i in range(count):
                    self.to_right(i, step).start()

            @pl.when((chip >= 1) & (chip + step < chips))
            def _():
                for i in range(count):
                    self.to_left(i, step).start()

            if step == 0:
                for i in range(count):
                    self.across(i, 0).start()
                    self.local(i).start()

            @pl.when(chip >= step + 1)
            def _():
                for i in range(count):
                    self.to_right(i, step).wait_recv()
                    self.across(i, chips - 1 - step).start()

            @pl.when(chip + step + 1 < chips)
            def _():
                for i in range(count):
                    self.to_left(i, step).wait_recv()
                    self.across(i, step + 1).start()

    def finish(self):
        chip, chips, count = self.chip, self.chips, self.count
        for step in range(chips - 1):

            @pl.when((chip + 1 < chips) & (chip >= step))
            def _():
                for i in range(count):
                    self.to_right(i, step).wait_send()

            @pl.when((chip >= 1) & (chip + step < chips))
            def _():
                for i in range(count):
                    self.to_left(i, step).wait_send()

        for slot in range(chips):
            for i in range(count):
                self.across(i, slot).wait()
        for i in range(count):
            self.local(i).wait()


def line_sems(count, chips):
    return (
        [pltpu.SemaphoreType.DMA((count,))]
        + [pltpu.SemaphoreType.DMA((count, chips - 1)) for unused in range(4)]
        + [pltpu.SemaphoreType.DMA((count, chips)) for unused in range(2)]
    )


def gather_kernel(dense, line, fsdp, chips, *refs):
    ins, outs, sems = refs[: dense + line], refs[dense + line : 2 * (dense + line)], None
    sems = refs[2 * (dense + line) :]
    ctx, me, chip, core, sibling = place()
    greet(chips, peers_of(me, fsdp) if dense else [], line > 0)
    if dense:
        first = DenseGather(ins[:dense], outs[:dense], sems[:5], fsdp)
        first.start()
    if line:
        second = LineGather(ins[dense:], outs[dense:], sems[-7:], chips)
        second.run()
    if dense:
        first.finish()
    if line:
        second.finish()


def gather(dense, line, fsdp, chips, collective_id):
    arrays = list(dense) + list(line)
    count = len(arrays)
    scratch = (dense_sems(len(dense), fsdp) if dense else []) + (
        line_sems(len(line), chips) if line else []
    )
    return pl.pallas_call(
        functools.partial(gather_kernel, len(dense), len(line), fsdp, chips),
        out_shape=[jax.ShapeDtypeStruct((fsdp * a.shape[0],) + a.shape[1:], a.dtype) for a in dense]
        + [jax.ShapeDtypeStruct((2, chips) + a.shape, a.dtype) for a in line],
        in_specs=[pl.BlockSpec(memory_space=pl.ANY)] * count,
        out_specs=[pl.BlockSpec(memory_space=pl.ANY)] * count,
        scratch_shapes=scratch,
        compiler_params=pltpu.CompilerParams(collective_id=collective_id, has_side_effects=True),
        name="gather",
    )(*arrays)


def add(*parts):
    total = parts[0].astype(F32)
    for part in parts[1:]:
        total = total + part.astype(F32)
    return total


def line_sum(chips, first, take, sends, gots, sems, done):
    ctx, me, chip, core, sibling = place()
    send_right, send_left = sends
    got_right, got_left = gots
    right_send, right_recv, left_send, left_recv = sems

    def right(step):
        return remote(
            send_right.at[step],
            got_right.at[step],
            right_send.at[step],
            right_recv.at[step],
            (ctx + 2, me),
        )

    def left(step):
        return remote(
            send_left.at[step],
            got_left.at[step],
            left_send.at[step],
            left_recv.at[step],
            (ctx - 2, me),
        )

    for step in range(chips - 1):
        far_right, far_left = chips - 1 - step, step + 1

        @pl.when(chip <= step)
        def _():
            take(far_right)
            if step == 0:
                send_right[step] = add(*first(far_right)).astype(BF16)
            else:

                @pl.when(chip == 0)
                def _():
                    send_right[step] = add(*first(far_right)).astype(BF16)

                @pl.when(chip >= 1)
                def _():
                    right(step - 1).wait_recv()
                    send_right[step] = add(*first(far_right), got_right[step - 1]).astype(BF16)

            right(step).start()

        @pl.when(chip >= chips - 1 - step)
        def _():
            take(far_left)
            if step == 0:
                send_left[step] = add(*first(far_left)).astype(BF16)
            else:

                @pl.when(chip == chips - 1)
                def _():
                    send_left[step] = add(*first(far_left)).astype(BF16)

                @pl.when(chip < chips - 1)
                def _():
                    left(step - 1).wait_recv()
                    send_left[step] = add(*first(far_left), got_left[step - 1]).astype(BF16)

            left(step).start()

    last = chips - 2
    take(0)

    @pl.when(chip == 0)
    def _():
        left(last).wait_recv()
        done(add(*first(0), got_left[last]))

    @pl.when(chip == chips - 1)
    def _():
        right(last).wait_recv()
        done(add(*first(0), got_right[last]))

    @pl.when((chip >= 1) & (chip < chips - 1))
    def _():
        left(last).wait_recv()
        right(last).wait_recv()
        done(add(*first(0), got_left[last], got_right[last]))

    def finish():
        for step in range(chips - 1):

            @pl.when(chip <= step)
            def _():
                right(step).wait_send()

            @pl.when(chip >= chips - 1 - step)
            def _():
                left(step).wait_send()

    return finish


def line_reduce_kernel(
    chips, mine_ref, other_ref, out_ref, pair, sr, sl, gr, gl, ps, pr, s0, s1, s2, s3
):
    ctx, me, chip, core, sibling = place()
    greet(chips, [], True)
    swaps = [
        remote(other_ref.at[r], pair.at[r], ps.at[r], pr.at[r], (sibling, me))
        for r in range(chips)
    ]
    order = []
    for step in range(chips - 1):
        for r in (chips - 1 - step, step + 1):
            if r not in order:
                order.append(r)
    for r in order + [0]:
        swaps[r].start()

    def done(total):
        out_ref[...] = total

    finish = line_sum(
        chips,
        lambda r: (mine_ref[r], pair[r]),
        lambda r: swaps[r].wait_recv(),
        (sr, sl),
        (gr, gl),
        (s0, s1, s2, s3),
        done,
    )
    finish()
    for swap in swaps:
        swap.wait_send()


def line_reduce_now(mine, other, chips, collective_id):
    unused, rows, width = mine.shape
    vmem = pl.BlockSpec(memory_space=pltpu.VMEM)
    return pl.pallas_call(
        functools.partial(line_reduce_kernel, chips),
        out_shape=jax.ShapeDtypeStruct((rows, width), F32),
        in_specs=[vmem, vmem],
        out_specs=vmem,
        scratch_shapes=[pltpu.VMEM((chips, rows, width), BF16)]
        + [pltpu.VMEM((chips - 1, rows, width), BF16) for unused in range(4)]
        + [pltpu.SemaphoreType.DMA((chips,)) for unused in range(2)]
        + [pltpu.SemaphoreType.DMA((chips - 1,)) for unused in range(4)],
        compiler_params=pltpu.CompilerParams(
            collective_id=collective_id, has_side_effects=True, vmem_limit_bytes=VMEM_BYTES
        ),
        name="line_reduce",
    )(mine, other)


def dense_reduce_kernel(
    fsdp,
    chips,
    local_ref,
    out_ref,
    pair,
    mine,
    cross,
    sums,
    sr,
    sl,
    gr,
    gl,
    spread,
    ps,
    pr,
    xs,
    xr,
    s0,
    s1,
    s2,
    s3,
    g0,
    g1,
    g2,
    g3,
    a0,
    a1,
):
    ctx, me, chip, core, sibling = place()
    peers = peers_of(me, fsdp)
    greet(chips, peers, True)
    cut = sums.shape[1] // chips
    owners = peers + [me]

    swaps = [
        remote(local_ref.at[owner, 1 - core], pair.at[j], ps.at[j], pr.at[j], (sibling, me))
        for j, owner in enumerate(owners)
    ]
    for swap in swaps:
        swap.start()

    crossings = []
    for j, owner in enumerate(owners):
        swaps[j].wait_recv()
        mine[j] = add(local_ref[owner, core], pair[j]).astype(BF16)
        if j < len(peers):
            copy = remote(mine.at[j], cross.at[j], xs.at[j], xr.at[j], (ctx, owner))
            copy.start()
            crossings.append(copy)
    for copy in crossings:
        copy.wait_recv()
    sums[...] = add(mine[len(peers)], *[cross[j] for j in range(len(peers))]).astype(BF16)

    def columns(r):
        owner = lax.rem(chip + r, chips)
        return pl.ds(pl.multiple_of(owner * cut, LANES), cut)

    def done(total):
        spread[0, 0] = total.astype(BF16)

    finish = line_sum(
        chips,
        lambda r: (sums[:, columns(r)],),
        lambda r: None,
        (sr, sl),
        (gr, gl),
        (s0, s1, s2, s3),
        done,
    )

    def to_right(step):
        return remote(
            spread.at[0, (chips - step) % chips],
            spread.at[0, chips - 1 - step],
            g0.at[step],
            g1.at[step],
            (ctx + 2, me),
        )

    def to_left(step):
        return remote(
            spread.at[0, step], spread.at[0, step + 1], g2.at[step], g3.at[step], (ctx - 2, me)
        )

    def across(slot):
        return remote(
            spread.at[0, slot], spread.at[1, slot], a0.at[slot], a1.at[slot], (sibling, me)
        )

    for step in range(chips - 1):

        @pl.when((chip + 1 < chips) & (chip >= step))
        def _():
            to_right(step).start()

        @pl.when((chip >= 1) & (chip + step < chips))
        def _():
            to_left(step).start()

        if step == 0:
            across(0).start()

        @pl.when(chip >= step + 1)
        def _():
            to_right(step).wait_recv()
            across(chips - 1 - step).start()

        @pl.when(chip + step + 1 < chips)
        def _():
            to_left(step).wait_recv()
            across(step + 1).start()

    for r in range(chips):
        out_ref[core, :, columns(r)] = spread[0, r]
    for r in range(chips):
        across(r).wait()
        out_ref[1 - core, :, columns(r)] = spread[1, r]
    for step in range(chips - 1):

        @pl.when((chip + 1 < chips) & (chip >= step))
        def _():
            to_right(step).wait_send()

        @pl.when((chip >= 1) & (chip + step < chips))
        def _():
            to_left(step).wait_send()

    finish()
    for copy in crossings + swaps:
        copy.wait_send()


def dense_reduce(local, fsdp, chips, collective_id):
    unused, unused_two, rows, width = local.shape
    cut = width // chips
    vmem = pl.BlockSpec(memory_space=pltpu.VMEM)
    return pl.pallas_call(
        functools.partial(dense_reduce_kernel, fsdp, chips),
        out_shape=jax.ShapeDtypeStruct((2, rows, width), BF16),
        in_specs=[vmem],
        out_specs=vmem,
        scratch_shapes=[
            pltpu.VMEM((fsdp, rows, width), BF16),
            pltpu.VMEM((fsdp, rows, width), BF16),
            pltpu.VMEM((fsdp - 1, rows, width), BF16),
            pltpu.VMEM((rows, width), BF16),
        ]
        + [pltpu.VMEM((chips - 1, rows, cut), BF16) for unused in range(4)]
        + [pltpu.VMEM((2, chips, rows, cut), BF16)]
        + [pltpu.SemaphoreType.DMA((fsdp,)) for unused in range(2)]
        + [pltpu.SemaphoreType.DMA((fsdp - 1,)) for unused in range(2)]
        + [pltpu.SemaphoreType.DMA((chips - 1,)) for unused in range(8)]
        + [pltpu.SemaphoreType.DMA((chips,)) for unused in range(2)],
        compiler_params=pltpu.CompilerParams(
            collective_id=collective_id, has_side_effects=True, vmem_limit_bytes=VMEM_BYTES
        ),
        name="dense_reduce",
    )(local)


def right_pairs(chips, least):
    return [(2 * z + k, 2 * z + 2 + k) for z in range(chips - 1) if least <= z for k in range(2)]


def left_pairs(chips, most):
    return [(2 * z + k, 2 * z - 2 + k) for z in range(1, chips) if z <= most for k in range(2)]


def swap_pairs(chips):
    return [(i, i ^ 1) for i in range(2 * chips)]


def after(value, *others):
    return lax.optimization_barrier((value,) + others)[0]


def line_gather_async(rows, chips, chip, ties):
    right, left = rows, rows
    got_right, got_left = [], []
    for step in range(chips - 1):
        if step >= 1:
            right = after(right, *ties[min(step, len(ties)) - 1])
            left = after(left, *ties[min(step, len(ties)) - 1])
        right = lax.ppermute(right, "ctx", right_pairs(chips, step))
        left = lax.ppermute(left, "ctx", left_pairs(chips, chips - 1 - step))
        got_right.append(right)
        got_left.append(left)
    slots = [rows]
    for r in range(1, chips):
        slots.append(jnp.where(chip + r < chips, got_left[r - 1], got_right[chips - 1 - r]))
    mine = jnp.stack(slots)
    return mine, lax.ppermute(mine, "ctx", swap_pairs(chips))


def line_reduce(mine, other, chips, ties):
    recv = lax.ppermute(other, "ctx", swap_pairs(chips))
    right = left = None
    for step in range(chips - 1):
        r_right, r_left = chips - 1 - step, step + 1
        parts_right, parts_left = [mine[r_right], recv[r_right]], [mine[r_left], recv[r_left]]
        if step > 0:
            parts_right.append(right)
            parts_left.append(left)
        send_right, send_left = add(*parts_right).astype(BF16), add(*parts_left).astype(BF16)
        tie = ties[min(step, len(ties) - 1)]
        if tie:
            send_right, send_left = after(send_right, *tie), after(send_left, *tie)
        right = lax.ppermute(
            send_right,
            "ctx",
            [(2 * z + k, 2 * z + 2 + k) for z in range(step + 1) for k in range(2)],
        )
        left = lax.ppermute(
            send_left,
            "ctx",
            [
                (2 * z + k, 2 * z - 2 + k)
                for z in range(chips - 1 - step, chips)
                for k in range(2)
            ],
        )
    return add(mine[0], recv[0], right, left)


def attention_kernel(
    scale, q_ref, k_ref, v_ref, oq_ref, pq_ref, ok_ref, out_ref, lse_ref, bias, scores
):
    keys = k_ref.shape[0]
    tiles = keys // KEY_TILE
    rows = q_ref.shape[0]

    @pl.when(pl.program_id(0) == 0)
    def _():
        def fill(t, carry):
            tile = pl.ds(pl.multiple_of(t * KEY_TILE, KEY_TILE), KEY_TILE)
            gap = oq_ref[...] - ok_ref[:, tile]
            bias[:, tile] = jnp.where((gap >= 0) & (gap <= pq_ref[...]), 0.0, MASKED)
            return carry

        lax.fori_loop(0, tiles, fill, 0)

    query = q_ref[...]

    def score(t, top):
        tile = pl.ds(pl.multiple_of(t * KEY_TILE, KEY_TILE), KEY_TILE)
        raw = dot(query, k_ref[tile, :], NT) * (scale * LOG2E) + bias[:, tile]
        scores[:, tile] = raw
        for part in range(KEY_TILE // LANES):
            top = jnp.maximum(top, raw[:, part * LANES : (part + 1) * LANES])
        return top

    top = lax.fori_loop(0, tiles, score, jnp.full((rows, LANES), MASKED, F32))
    top = jnp.max(top, axis=1, keepdims=True)

    def weigh(t, carry):
        total, acc = carry
        tile = pl.ds(pl.multiple_of(t * KEY_TILE, KEY_TILE), KEY_TILE)
        probs = jnp.exp2(scores[:, tile] - top)
        for part in range(KEY_TILE // LANES):
            total = total + probs[:, part * LANES : (part + 1) * LANES]
        acc = acc + dot(probs.astype(BF16), v_ref[tile, :], NN)
        return total, acc

    total, acc = lax.fori_loop(
        0, tiles, weigh, (jnp.zeros((rows, LANES), F32), jnp.zeros((rows, HEAD_SIZE), F32))
    )
    total = jnp.sum(total, axis=1, keepdims=True)
    out_ref[...] = (acc / total).astype(BF16)
    lse = jnp.broadcast_to(top + jnp.log2(total), (rows, LANES))
    lse_ref[0] = lse.T[:1, :]


def attention(queries, kv, order_mine, pos_mine, order_keys, group):
    rows = queries.shape[0]
    keys = kv.shape[0]
    per_group = QUERY_HEADS // KVH
    return pl.pallas_call(
        functools.partial(attention_kernel, HEAD_SIZE ** (-0.5)),
        grid=(per_group,),
        out_shape=[
            jax.ShapeDtypeStruct((rows, per_group * HEAD_SIZE), BF16),
            jax.ShapeDtypeStruct((per_group, 1, rows), F32),
        ],
        in_specs=[
            pl.BlockSpec((rows, HEAD_SIZE), lambda h: (0, group * per_group + h)),
            pl.BlockSpec((keys, HEAD_SIZE), lambda h: (0, group)),
            pl.BlockSpec((keys, HEAD_SIZE), lambda h: (0, KVH + group)),
            pl.BlockSpec((rows, 1), lambda h: (0, 0)),
            pl.BlockSpec((rows, 1), lambda h: (0, 0)),
            pl.BlockSpec((1, keys), lambda h: (0, 0)),
        ],
        out_specs=[
            pl.BlockSpec((rows, HEAD_SIZE), lambda h: (0, h)),
            pl.BlockSpec((1, 1, rows), lambda h: (h, 0, 0)),
        ],
        scratch_shapes=[pltpu.VMEM((rows, keys), F32), pltpu.VMEM((rows, keys), F32)],
        compiler_params=pltpu.CompilerParams(vmem_limit_bytes=VMEM_BYTES),
        cost_estimate=pl.CostEstimate(
            flops=4 * rows * keys * HEAD_SIZE * per_group,
            bytes_accessed=4 * rows * per_group * HEAD_SIZE + 4 * keys * HEAD_SIZE,
            transcendentals=rows * keys * per_group,
        ),
        name="attention",
    )(queries, kv, kv, order_mine[:, None], pos_mine[:, None], order_keys[None, :])


def attention_back_kernel(
    scale,
    per_group,
    q_ref,
    k_ref,
    v_ref,
    o_ref,
    do_ref,
    lse_ref,
    oq_ref,
    pq_ref,
    ok_ref,
    dq_ref,
    dk_ref,
    dv_ref,
    bias,
    dk_acc,
    dv_acc,
):
    keys = k_ref.shape[0]
    tiles = keys // KEY_TILE
    rows = q_ref.shape[0]
    head = pl.program_id(0)

    @pl.when(head == 0)
    def _():
        def fill(t, carry):
            tile = pl.ds(pl.multiple_of(t * KEY_TILE, KEY_TILE), KEY_TILE)
            gap = oq_ref[...] - ok_ref[tile, :]
            bias[tile, :] = jnp.where((gap >= 0) & (gap <= pq_ref[...]), 0.0, MASKED)
            return carry

        lax.fori_loop(0, tiles, fill, 0)

    @pl.when(lax.rem(head, per_group) == 0)
    def _():
        dk_acc[...] = jnp.zeros_like(dk_acc)
        dv_acc[...] = jnp.zeros_like(dv_acc)

    query = q_ref[...]
    grad = do_ref[...]
    lse = lse_ref[0]
    product = grad.astype(F32) * o_ref[...].astype(F32)
    delta = jnp.sum(product.T, axis=0, keepdims=True)

    def step(t, acc):
        tile = pl.ds(pl.multiple_of(t * KEY_TILE, KEY_TILE), KEY_TILE)
        key = k_ref[tile, :]
        raw = dot(key, query, NT) * (scale * LOG2E) + bias[tile, :]
        probs = jnp.exp2(raw - lse)
        prob_grad = dot(v_ref[tile, :], grad, NT)
        score_grad = (probs * (prob_grad - delta)).astype(BF16)
        dv_acc[tile, :] += dot(probs.astype(BF16), grad, NN)
        dk_acc[tile, :] += dot(score_grad, query, NN)
        return acc + dot(score_grad, key, TN)

    acc = lax.fori_loop(0, tiles, step, jnp.zeros((rows, HEAD_SIZE), F32))
    dq_ref[...] = acc * scale

    @pl.when(lax.rem(head, per_group) == per_group - 1)
    def _():
        dk_ref[...] = (dk_acc[...] * scale).astype(BF16)
        dv_ref[...] = dv_acc[...].astype(BF16)


def attention_back(
    queries, kv, attended, attended_grad, lse, order_mine, pos_mine, order_keys, group
):
    rows = queries.shape[0]
    keys = kv.shape[0]
    per_group = QUERY_HEADS // KVH
    head_rows = pl.BlockSpec((rows, HEAD_SIZE), lambda h: (0, group * per_group + h))
    group_rows = pl.BlockSpec((rows, HEAD_SIZE), lambda h: (0, h))
    return pl.pallas_call(
        functools.partial(attention_back_kernel, HEAD_SIZE ** (-0.5), per_group),
        grid=(per_group,),
        out_shape=[
            jax.ShapeDtypeStruct((rows, per_group * HEAD_SIZE), F32),
            jax.ShapeDtypeStruct((keys, HEAD_SIZE), BF16),
            jax.ShapeDtypeStruct((keys, HEAD_SIZE), BF16),
        ],
        in_specs=[
            head_rows,
            pl.BlockSpec((keys, HEAD_SIZE), lambda h: (0, group)),
            pl.BlockSpec((keys, HEAD_SIZE), lambda h: (0, KVH + group)),
            group_rows,
            head_rows,
            pl.BlockSpec((1, 1, rows), lambda h: (h, 0, 0)),
            pl.BlockSpec((1, rows), lambda h: (0, 0)),
            pl.BlockSpec((1, rows), lambda h: (0, 0)),
            pl.BlockSpec((keys, 1), lambda h: (0, 0)),
        ],
        out_specs=[
            group_rows,
            pl.BlockSpec((keys, HEAD_SIZE), lambda h: (0, 0)),
            pl.BlockSpec((keys, HEAD_SIZE), lambda h: (0, 0)),
        ],
        scratch_shapes=[
            pltpu.VMEM((keys, rows), F32),
            pltpu.VMEM((keys, HEAD_SIZE), F32),
            pltpu.VMEM((keys, HEAD_SIZE), F32),
        ],
        compiler_params=pltpu.CompilerParams(vmem_limit_bytes=VMEM_BYTES),
        cost_estimate=pl.CostEstimate(
            flops=10 * rows * keys * HEAD_SIZE * per_group,
            bytes_accessed=10 * rows * per_group * HEAD_SIZE + 8 * keys * HEAD_SIZE,
            transcendentals=rows * keys * per_group,
        ),
        name="attention_back",
    )(
        queries,
        kv,
        kv,
        attended,
        attended_grad,
        lse,
        order_mine[None, :],
        pos_mine[None, :],
        order_keys[:, None],
    )


def expert_kernel(
    capacity,
    local_experts,
    expert_count,
    first_ref,
    hidden_ref,
    grad_mine_ref,
    grad_other_ref,
    table_ref,
    weight_ref,
    gate_ref,
    up_ref,
    down_ref,
    out_mine,
    out_other,
    rows_mine,
    rows_other,
    save_x,
    save_pg,
    save_inner,
    save_da,
    save_db,
):
    tokens = hidden_ref.shape[2]
    slot_rows = save_x.shape[1] // 2
    first = first_ref[0]
    slot = lax.broadcasted_iota(jnp.int32, (slot_rows, tokens), 0).astype(F32) + 1.0
    slot = jnp.where(slot <= capacity, slot, -1.0)
    lane = lax.broadcasted_iota(jnp.int32, (2 * slot_rows, LANES), 1)
    picks = [[], []]
    outs = [[], []]
    backs = [[], []]
    for e in range(local_experts):
        rows_x, rows_g, rows_w = [], [], []
        for q in range(2):
            row = table_ref[q, 0, pl.ds(first + e, 1), :]
            hit = slot == row
            pick = jnp.where(hit, 1.0, 0.0).astype(BF16)
            weight = weight_ref[q, 0, pl.ds(first + e, 1), :]
            rows_w.append(jnp.sum(jnp.where(hit, weight, 0.0), axis=1, keepdims=True))
            rows_x.append(dot(pick, hidden_ref[q, 0], NN).astype(BF16))
            grad_rows = grad_mine_ref[0] if q == 0 else grad_other_ref[0]
            rows_g.append(dot(pick, grad_rows, NN))
            picks[q].append(pick)
        x = jnp.concatenate(rows_x, axis=0)
        g = jnp.concatenate(rows_g, axis=0)
        w = jnp.concatenate(rows_w, axis=0)
        pair_grad = (w * g).astype(BF16)
        gate_pre = dot(x, gate_ref[e], NN)
        up_pre = dot(x, up_ref[e], NN)
        sig = jax.nn.sigmoid(gate_pre)
        silu = gate_pre * sig
        inner = (silu * up_pre).astype(BF16)
        expert_out = dot(inner, down_ref[e], NN).astype(BF16).astype(F32)
        gate_grad = jnp.sum(expert_out * g, axis=1, keepdims=True)
        inner_grad = dot(pair_grad, down_ref[e], NT)
        da = (inner_grad * up_pre * sig * (1.0 + gate_pre * (1.0 - sig))).astype(BF16)
        db = (inner_grad * silu).astype(BF16)
        row_grad = (dot(da, gate_ref[e], NT) + dot(db, up_ref[e], NT)).astype(BF16)
        high = gate_grad.astype(BF16).astype(F32)
        extra = jnp.where(lane == first + e, high, 0.0) + jnp.where(
            lane == expert_count + first + e, gate_grad - high, 0.0
        )
        back = jnp.concatenate([row_grad, extra.astype(BF16)], axis=1)
        out_rows = (w * expert_out).astype(BF16)
        for q in range(2):
            part = slice(q * slot_rows, (q + 1) * slot_rows)
            outs[q].append(out_rows[part])
            backs[q].append(back[part])
        save_x[e] = x
        save_pg[e] = pair_grad
        save_inner[e] = inner
        save_da[e] = da
        save_db[e] = db
    for q in range(2):
        pick = jnp.concatenate(picks[q], axis=0)
        out_ref = out_mine if q == 0 else out_other
        rows_ref = rows_mine if q == 0 else rows_other
        out_ref[0] = dot(pick, jnp.concatenate(outs[q], axis=0), TN).astype(BF16)
        rows_ref[0] = dot(pick, jnp.concatenate(backs[q], axis=0), TN).astype(BF16)


def expert_rows_pass(
    first, hidden, grad_mine, grad_other, table, weights, gate, up, down, capacity, expert_count
):
    chips, tokens, width = grad_mine.shape
    local_experts, unused, hidden_units = gate.shape
    slots = 2 * SLOT_STEP * -(-capacity // SLOT_STEP)
    total = chips * slots
    once = pl.Buffered(1)

    def whole(shape):
        return pl.BlockSpec(shape, lambda r, s: (0,) * len(shape), pipeline_mode=once)

    def saved(columns):
        return pl.BlockSpec((local_experts, slots, columns), lambda r, s: (0, r, 0))

    chunk = pl.BlockSpec((1, tokens, width), lambda r, s: (r, 0, 0))
    wide = pl.BlockSpec((1, tokens, width + LANES), lambda r, s: (r, 0, 0))
    small = pl.BlockSpec((2, 1, expert_count, tokens), lambda r, s: (0, r, 0, 0))
    flops = 2 * total * width * hidden_units * local_experts * 6 + 8 * total * tokens * width
    return pl.pallas_call(
        functools.partial(expert_kernel, capacity, local_experts, expert_count),
        grid_spec=pltpu.PrefetchScalarGridSpec(
            num_scalar_prefetch=1,
            grid=(chips,),
            in_specs=[
                pl.BlockSpec((2, 1, tokens, width), lambda r, s: (0, r, 0, 0)),
                chunk,
                chunk,
                small,
                small,
                whole(gate.shape),
                whole(up.shape),
                whole(down.shape),
            ],
            out_specs=[
                chunk,
                chunk,
                wide,
                wide,
                saved(width),
                saved(width),
                saved(hidden_units),
                saved(hidden_units),
                saved(hidden_units),
            ],
        ),
        out_shape=[jax.ShapeDtypeStruct((chips, tokens, width), BF16)] * 2
        + [jax.ShapeDtypeStruct((chips, tokens, width + LANES), BF16)] * 2
        + [jax.ShapeDtypeStruct((local_experts, total, width), BF16)] * 2
        + [jax.ShapeDtypeStruct((local_experts, total, hidden_units), BF16)] * 3,
        compiler_params=pltpu.CompilerParams(vmem_limit_bytes=VMEM_BYTES),
        cost_estimate=pl.CostEstimate(
            flops=flops, bytes_accessed=80_000_000, transcendentals=total * hidden_units * 2
        ),
        name="expert_rows",
    )(first, hidden, grad_mine, grad_other, table, weights, gate, up, down)


def outer_kernel(per, split_left, left_ref, right_ref, out_ref):
    product = dot(left_ref[0], right_ref[0], TN).astype(BF16)
    axis = 0 if split_left else 1
    size = product.shape[axis] // per
    for i in range(per):
        out_ref[i, 0] = lax.slice_in_dim(product, i * size, (i + 1) * size, axis=axis)


def outer_products(left, right, fsdp, split_left):
    experts, total, m = left.shape
    n = right.shape[2]
    per = 1 if ((m if split_left else n) // fsdp) % LANES == 0 else 2
    if split_left:
        m = m // fsdp
    else:
        n = n // fsdp
    return pl.pallas_call(
        functools.partial(outer_kernel, per, split_left),
        grid=(experts, fsdp // per),
        out_shape=jax.ShapeDtypeStruct((fsdp, experts, m, n), BF16),
        in_specs=[
            pl.BlockSpec(
                (1, total, m * per if split_left else m),
                lambda e, f: (e, 0, f if split_left else 0),
            ),
            pl.BlockSpec(
                (1, total, n if split_left else n * per),
                lambda e, f: (e, 0, 0 if split_left else f),
            ),
        ],
        out_specs=pl.BlockSpec((per, 1, m, n), lambda e, f: (f, e, 0, 0)),
        compiler_params=pltpu.CompilerParams(vmem_limit_bytes=VMEM_BYTES),
        cost_estimate=pl.CostEstimate(
            flops=2 * total * m * n * experts * fsdp, bytes_accessed=14_000_000, transcendentals=0
        ),
        name="outer_products",
    )(left, right)


def body(
    tokens,
    grad_out,
    order,
    lengths,
    routes,
    gain_one,
    gain_two,
    w_query,
    w_key,
    w_value,
    w_out,
    w_router,
    w_gate,
    w_up,
    w_down,
):
    fsdp = lax.axis_size("fsdp")
    chips = lax.axis_size("ctx") // 2
    ctx_index = lax.axis_index("ctx")
    chip = ctx_index // 2
    core = lax.rem(ctx_index, 2)
    tok_rows = tokens.shape[1]
    width = tokens.shape[2]
    top_count = routes.shape[2]
    local_experts = w_gate.shape[0]
    expert_count = local_experts * chips * 2
    capacity = 5 * tok_rows * top_count // (4 * expert_count)
    kv_width = KVH * HEAD_SIZE
    shard = gain_one.shape[0]

    small = jnp.concatenate(
        [
            w_router,
            gain_one[:, None],
            gain_two[:, None],
            jnp.zeros((shard, LANES - expert_count - 2), BF16),
        ],
        axis=1,
    )
    qkv_shard = jnp.concatenate([w_query, w_key, w_value], axis=1)
    qkv_full, small_full = gather([qkv_shard, small], [], fsdp, chips, 0)

    qkv_full, w_gate, w_up, w_down = lax.optimization_barrier((qkv_full, w_gate, w_up, w_down))
    gate_full, up_full, down_full = (
        lax.all_gather(w_gate, "fsdp", axis=1, tiled=True),
        lax.all_gather(w_up, "fsdp", axis=1, tiled=True),
        lax.all_gather(w_down, "fsdp", axis=2, tiled=True),
    )
    router_full = small_full[:, :expert_count]
    gain_a = small_full[:, expert_count].astype(F32)
    gain_b = small_full[:, expert_count + 1].astype(F32)

    order_row = order[0]
    start_row = ctx_index * tok_rows
    order_mine = lax.dynamic_slice_in_dim(order_row, start_row, tok_rows)
    ends = jnp.cumsum(lengths[0])
    starts = ends - lengths[0]
    past = order_mine[:, None] >= ends[None, :]
    doc_start = jnp.max(jnp.where(past, ends[None, :], starts[:1]), axis=1)
    pos_mine = order_mine - doc_start
    by_chip = jnp.roll(order_row.reshape(chips, 2, tok_rows), -chip, axis=0)
    by_chip = jnp.where(core == 0, by_chip, by_chip[:, ::-1])
    order_keys = jnp.swapaxes(by_chip, 0, 1).reshape(-1)

    route_rows = routes[0]
    route_onehot = (route_rows[:, :, None] == jnp.arange(expert_count)[None, None, :]).astype(F32)
    routed = jnp.sum(route_onehot, axis=1)
    earlier = (order_mine[None, :] < order_mine[:, None]).astype(BF16)
    ranks = jnp.dot(earlier, routed.astype(BF16), preferred_element_type=F32)
    table = jnp.where(routed > 0, jnp.minimum(ranks, capacity) + 1.0, 0.0)

    half_dim = HEAD_SIZE // 2
    freqs = ROPE_BASE ** (-2.0 * jnp.arange(half_dim).astype(F32) / HEAD_SIZE)
    angles = pos_mine.astype(F32)[:, None] * freqs[None, :]
    cosine = jnp.cos(angles)[:, None, :]
    sine = jnp.sin(angles)[:, None, :]

    inputs = tokens[0].astype(F32)
    hidden_one = rms_scale(inputs, gain_a).astype(BF16)
    pre = jnp.dot(hidden_one, qkv_full, preferred_element_type=F32)
    turned = rotate(
        pre[:, : width + kv_width].reshape(tok_rows, QUERY_HEADS + KVH, HEAD_SIZE), cosine, sine
    )
    queries = turned[:, :QUERY_HEADS].astype(BF16).reshape(tok_rows, width)
    kv_mine = jnp.concatenate(
        [
            turned[:, QUERY_HEADS:].astype(BF16).reshape(tok_rows, kv_width),
            pre[:, width + kv_width :].astype(BF16),
        ],
        axis=1,
    )
    out_full, kv_all, table_all = gather([w_out], [kv_mine, table.T], fsdp, chips, 1)
    kv_all = kv_all.reshape(-1, 2 * kv_width)
    attended, lse = [], []
    for group in range(KVH):
        part, part_lse = attention(
            after(queries, *attended[-1:]), kv_all, order_mine, pos_mine, order_keys, group
        )
        attended.append(part)
        lse.append(part_lse)
    grad_mine, grad_other = line_gather_async(grad_out[0], chips, chip, [(kv_all,), attended[:1]])
    attended_parts, attended = attended, jnp.concatenate(attended, axis=1)
    middle = inputs + jnp.dot(attended, out_full, preferred_element_type=F32)
    hidden_two = rms_scale(middle, gain_b).astype(BF16)
    logits = jnp.dot(hidden_two, router_full, preferred_element_type=F32)
    chosen = jnp.where(routed > 0, logits, MASKED)
    gate_weights = jnp.where(routed > 0, jax.nn.softmax(chosen, axis=-1), 0.0)

    hidden_all, weights_all = gather([], [hidden_two, gate_weights.T], fsdp, chips, 2)
    first = (ctx_index * local_experts).astype(jnp.int32).reshape(1)
    (
        out_mine,
        out_other,
        rows_mine,
        rows_other,
        save_x,
        save_pg,
        save_inner,
        save_da,
        save_db,
    ) = expert_rows_pass(
        first,
        hidden_all,
        grad_mine,
        grad_other,
        table_all,
        weights_all,
        gate_full,
        up_full,
        down_full,
        capacity,
        expert_count,
    )
    gate_local = outer_products(save_x, save_da, fsdp, True)
    up_local = outer_products(save_x, save_db, fsdp, True)
    down_local = outer_products(save_inner, save_pg, fsdp, False)
    gate_grad_out, up_grad_out, down_grad_out = (
        lax.psum_scatter(part, "fsdp", scatter_dimension=0, tiled=True)[0].astype(F32)
        for part in (gate_local, up_local, down_local)
    )
    returned = line_reduce(
        rows_mine, rows_other, chips, [(gate_local,), (up_local,), (down_local,)]
    )

    out_grad = grad_out[0].astype(F32)
    extra = returned[:, width:]
    gate_grad = extra[:, :expert_count] + extra[:, expert_count : 2 * expert_count]
    logit_grad = (
        gate_weights * (gate_grad - jnp.sum(gate_weights * gate_grad, axis=-1, keepdims=True))
    ).astype(BF16)
    router_local = jnp.einsum("td,te->de", hidden_two, logit_grad, preferred_element_type=F32)
    hidden_two_grad = returned[:, :width] + jnp.einsum(
        "te,de->td", logit_grad, router_full, preferred_element_type=F32
    )
    unused_two, norm_two_back = jax.vjp(rms_scale, middle, gain_b)
    middle_part, gain_two_local = norm_two_back(hidden_two_grad)
    middle_grad = out_grad + middle_part
    branch_grad = middle_grad.astype(BF16)
    out_local = jnp.einsum("tc,td->cd", attended, branch_grad, preferred_element_type=F32)
    attended_grad = jnp.einsum(
        "td,cd->tc", branch_grad, out_full, preferred_element_type=F32
    ).astype(BF16)

    query_grad, kv_grads = [], [None] * (2 * KVH)
    for group in range(KVH):
        parts = attention_back(
            queries,
            kv_all,
            attended_parts[group],
            after(attended_grad, *query_grad[-1:]),
            lse[group],
            order_mine,
            pos_mine,
            order_keys,
            group,
        )
        query_grad.append(parts[0])
        kv_grads[group], kv_grads[KVH + group] = parts[1:]
    result = middle + line_reduce(
        after(out_mine, returned),
        after(out_other, returned),
        chips,
        [(branch_grad,), (attended_grad,), (query_grad[0],)],
    )
    kv_grads = jnp.concatenate(kv_grads, axis=1).reshape(2, chips, tok_rows, 2 * kv_width)
    kv_grad = line_reduce_now(kv_grads[0], kv_grads[1], chips, 3)
    turned_grad = rotate(
        jnp.concatenate(query_grad + [kv_grad[:, :kv_width]], axis=1).reshape(
            tok_rows, QUERY_HEADS + KVH, HEAD_SIZE
        ),
        cosine,
        -sine,
    ).reshape(tok_rows, width + kv_width)
    pre_grad = jnp.concatenate(
        [turned_grad.astype(BF16), kv_grad[:, kv_width:].astype(BF16)], axis=1
    )
    qkv_local = jnp.einsum("td,tc->dc", hidden_one, pre_grad, preferred_element_type=F32)
    hidden_one_grad = jnp.einsum("tc,dc->td", pre_grad, qkv_full, preferred_element_type=F32)
    unused_one, norm_one_back = jax.vjp(rms_scale, inputs, gain_a)
    input_part, gain_one_local = norm_one_back(hidden_one_grad)
    input_grad = (middle_grad + input_part).astype(BF16)

    first_local = jnp.concatenate([out_local, router_local, gain_two_local[:, None]], axis=1)
    first_grads = lax.psum(
        lax.psum_scatter(first_local.astype(BF16), "fsdp", scatter_dimension=0, tiled=True), "ctx"
    ).astype(F32)
    edge = width + 2 * kv_width
    extra_rows = jnp.pad(
        gain_one_local.reshape(fsdp, 1, 1, shard).astype(BF16),
        ((0, 0), (0, 1), (0, 15), (0, edge - shard)),
    )
    last_local = jnp.concatenate(
        [qkv_local.astype(BF16).reshape(fsdp, 2, shard // 2, edge), extra_rows], axis=2
    )
    last_grads = dense_reduce(last_local, fsdp, chips, 4)
    qkv_grads = last_grads[:, : shard // 2].reshape(shard, edge).astype(F32)
    return (
        result.astype(BF16)[None],
        input_grad[None],
        last_grads[0, shard // 2, :shard].astype(F32),
        first_grads[:, width + expert_count],
        qkv_grads[:, :width],
        qkv_grads[:, width : width + kv_width],
        qkv_grads[:, width + kv_width :],
        first_grads[:, :width],
        first_grads[:, width : width + expert_count],
        gate_grad_out,
        up_grad_out,
        down_grad_out,
    )


def solution(mesh):
    placed = (
        P("fsdp", "ctx", None),
        P("fsdp", "ctx", None),
        P("fsdp", None),
        P("fsdp", None),
        P("fsdp", "ctx", None),
        P("fsdp"),
        P("fsdp"),
        P("fsdp", None),
        P("fsdp", None),
        P("fsdp", None),
        P("fsdp", None),
        P("fsdp", None),
        P("ctx", "fsdp", None),
        P("ctx", "fsdp", None),
        P("ctx", None, "fsdp"),
    )
    return jax.shard_map(
        body,
        mesh=mesh,
        in_specs=placed,
        out_specs=(
            P("fsdp", "ctx", None),
            P("fsdp", "ctx", None),
            P("fsdp"),
            P("fsdp"),
            P("fsdp", None),
            P("fsdp", None),
            P("fsdp", None),
            P("fsdp", None),
            P("fsdp", None),
            P("ctx", "fsdp", None),
            P("ctx", "fsdp", None),
            P("ctx", None, "fsdp"),
        ),
        check_vma=False,
    )
```

```python
import functools

import jax
import jax.numpy as jnp
from jax import lax
from jax.experimental import pallas as pl
from jax.experimental.pallas import tpu as pltpu
from jax.sharding import PartitionSpec as P

QUERY_HEADS = 12
KVH = 2
HEAD_SIZE = 128

EPSILON = 1e-06
ROPE_BASE = 10000.0
MASKED = -1e30
LOG2E = 1.4426950408889634
LANES = 128
SLOT_STEP = 64
DENSE_PIECE = 1024
KEY_TILE = 512
VMEM_BYTES = 60 * 1024 * 1024
MESH = pl.DeviceIdType.MESH
F32 = jnp.float32
BF16 = jnp.bfloat16


def dot(left, right, contract):
    return lax.dot_general(left, right, (contract, ((), ())), preferred_element_type=F32)


NN = ((1,), (0,))
NT = ((1,), (1,))
TN = ((0,), (0,))


def rms_scale(value_rows, gain):
    return (
        value_rows
        * lax.rsqrt(jnp.mean(value_rows * value_rows, axis=-1, keepdims=True) + EPSILON)
        * gain
    )


def rotate(value_rows, cosine, sine):
    half_dim = value_rows.shape[-1] // 2
    first = value_rows[..., :half_dim]
    second = value_rows[..., half_dim:]
    return jnp.concatenate(
        [first * cosine - second * sine, second * cosine + first * sine], axis=-1
    )


def place():
    ctx = lax.axis_index("ctx")
    core = lax.rem(ctx, 2)
    return ctx, lax.axis_index("fsdp"), ctx // 2, core, ctx + 1 - 2 * core


def peers_of(me, fsdp):
    peers = []
    for shift in range(1, fsdp):
        peer = me
        for bit in range(fsdp.bit_length() - 1):
            if (shift >> bit) & 1:
                digit = lax.rem(me // (1 << bit), 2)
                peer = peer + (1 << bit) - (2 << bit) * digit
        peers.append(peer)
    return peers


def greet(chips, peers, line):
    ctx, me, chip, core, sibling = place()
    barrier = pltpu.get_barrier_semaphore()
    for peer in peers:
        pl.semaphore_signal(barrier, inc=1, device_id=(ctx, peer), device_id_type=MESH)
    pl.semaphore_signal(barrier, inc=1, device_id=(sibling, me), device_id_type=MESH)
    known = len(peers) + 1
    if not line:
        pl.semaphore_wait(barrier, known)
        return
    has_right = chip + 1 < chips
    has_left = chip >= 1

    @pl.when(has_right)
    def _():
        pl.semaphore_signal(barrier, inc=1, device_id=(ctx + 2, me), device_id_type=MESH)

    @pl.when(has_left)
    def _():
        pl.semaphore_signal(barrier, inc=1, device_id=(ctx - 2, me), device_id_type=MESH)

    @pl.when(has_right & has_left)
    def _():
        pl.semaphore_wait(barrier, known + 2)

    @pl.when(jnp.logical_not(has_right & has_left))
    def _():
        pl.semaphore_wait(barrier, known + 1)


class Bounce:
    def __init__(self, src, dst, buffer, sem):
        self.inward = pltpu.make_async_copy(src, buffer, sem)
        self.outward = pltpu.make_async_copy(buffer, dst, sem)

    def start(self):
        self.inward.start()

    def turn(self):
        self.inward.wait()
        self.outward.start()

    def wait(self):
        self.outward.wait()


def remote(src, dst, send_sem, recv_sem, device):
    return pltpu.make_async_remote_copy(
        src_ref=src,
        dst_ref=dst,
        send_sem=send_sem,
        recv_sem=recv_sem,
        device_id=device,
        device_id_type=MESH,
    )


class DenseGather:
    def __init__(self, ins, outs, sems, fsdp):
        buffers, local_sem, send_sem, recv_sem, pass_sem, took_sem = sems
        ctx, me, chip, core, sibling = place()
        self.sends, self.passes, self.locals = [], [], []
        for i in range(len(ins)):
            rows = ins[i].shape[0]
            half = rows // 2
            for j, peer in enumerate(peers_of(me, fsdp)):
                self.sends.append(
                    remote(
                        ins[i].at[pl.ds(core * half, half)],
                        outs[i].at[pl.ds(me * rows + core * half, half)],
                        send_sem.at[i, j],
                        recv_sem.at[i, j],
                        (ctx, peer),
                    )
                )
                got = outs[i].at[pl.ds(peer * rows + core * half, half)]
                self.passes.append(
                    remote(got, got, pass_sem.at[i, j], took_sem.at[i, j], (sibling, me))
                )
            self.locals.append(
                Bounce(ins[i], outs[i].at[pl.ds(me * rows, rows)], buffers[i], local_sem.at[i])
            )

    def start(self):
        for copy in self.sends + self.locals:
            copy.start()

    def finish(self):
        for copy in self.locals:
            copy.turn()
        for send, copy in zip(self.sends, self.passes):
            send.wait_recv()
            copy.start()
        for send in self.sends:
            send.wait_send()
        for copy in self.passes + self.locals:
            copy.wait()


def dense_scratch(arrays, fsdp):
    count = len(arrays)
    return (
        [pltpu.VMEM(a.shape, a.dtype) for a in arrays]
        + [pltpu.SemaphoreType.DMA((count,))]
        + [pltpu.SemaphoreType.DMA((count, fsdp - 1)) for unused in range(4)]
    )


class LineGather:
    def __init__(self, ins, outs, sems, chips):
        self.ins, self.outs, self.chips = ins, outs, chips
        self.buffers, self.sems = sems[:-7], sems[-7:]
        self.ctx, self.me, self.chip, core, self.sibling = place()
        self.count = len(ins)

    def to_right(self, i, step):
        outs, chips = self.outs, self.chips
        return remote(
            self.ins[i] if step == 0 else outs[i].at[0, chips - step],
            outs[i].at[0, chips - 1 - step],
            self.sems[1].at[i, step],
            self.sems[2].at[i, step],
            (self.ctx + 2, self.me),
        )

    def to_left(self, i, step):
        outs = self.outs
        return remote(
            self.ins[i] if step == 0 else outs[i].at[0, step],
            outs[i].at[0, step + 1],
            self.sems[3].at[i, step],
            self.sems[4].at[i, step],
            (self.ctx - 2, self.me),
        )

    def across(self, i, slot):
        return remote(
            self.ins[i] if slot == 0 else self.outs[i].at[0, slot],
            self.outs[i].at[1, slot],
            self.sems[5].at[i, slot],
            self.sems[6].at[i, slot],
            (self.sibling, self.me),
        )

    def local(self, i):
        return Bounce(self.ins[i], self.outs[i].at[0, 0], self.buffers[i], self.sems[0].at[i])

    def send(self, step):
        chip, chips, count = self.chip, self.chips, self.count

        @pl.when((chip + 1 < chips) & (chip >= step))
        def _():
            for i in range(count):
                self.to_right(i, step).start()

        @pl.when((chip >= 1) & (chip + step < chips))
        def _():
            for i in range(count):
                self.to_left(i, step).start()

    def receive(self, step):
        chip, chips, count = self.chip, self.chips, self.count

        @pl.when(chip >= step + 1)
        def _():
            for i in range(count):
                self.to_right(i, step).wait_recv()
                self.across(i, chips - 1 - step).start()

        @pl.when(chip + step + 1 < chips)
        def _():
            for i in range(count):
                self.to_left(i, step).wait_recv()
                self.across(i, step + 1).start()

    def own(self):
        for i in range(self.count):
            self.across(i, 0).start()
            self.local(i).start()

    def turn_own(self):
        for i in range(self.count):
            self.local(i).turn()

    def finish_own(self):
        for i in range(self.count):
            self.across(i, 0).wait()
            self.local(i).wait()

    def finish(self, step):
        chip, chips, count = self.chip, self.chips, self.count

        @pl.when((chip + 1 < chips) & (chip >= step))
        def _():
            for i in range(count):
                self.to_right(i, step).wait_send()

        @pl.when((chip >= 1) & (chip + step < chips))
        def _():
            for i in range(count):
                self.to_left(i, step).wait_send()

        @pl.when(chip >= step + 1)
        def _():
            for i in range(count):
                self.across(i, chips - 1 - step).wait()

        @pl.when(chip + step + 1 < chips)
        def _():
            for i in range(count):
                self.across(i, step + 1).wait()


def line_scratch(arrays, chips):
    count = len(arrays)
    return (
        [pltpu.VMEM(a.shape, a.dtype) for a in arrays if a is not None]
        + [pltpu.SemaphoreType.DMA((count,))]
        + [pltpu.SemaphoreType.DMA((count, chips - 1)) for unused in range(4)]
        + [pltpu.SemaphoreType.DMA((count, chips)) for unused in range(2)]
    )


def gather_kernel(dense, line, resumed, steps, fsdp, chips, *refs):
    count = dense + line + resumed
    ins, outs, scratch = refs[:count], refs[count : 2 * count], refs[2 * count :]
    ctx, me, chip, core, sibling = place()
    greet(chips, peers_of(me, fsdp) if dense else [], line > 0)
    split = dense + line
    if dense:
        own, scratch = scratch[: dense + 5], scratch[dense + 5 :]
        first = DenseGather(
            ins[:dense], outs[:dense], (own[:dense],) + tuple(own[dense:]), fsdp
        )
        first.start()
    if line:
        own, scratch = scratch[: line + 7], scratch[line + 7 :]
        second = LineGather(ins[dense:split], outs[dense:split], own, chips)
        for step in range(steps):
            second.send(step)
            if step == 0:
                second.own()
            second.receive(step)
            if step == 0:
                second.turn_own()
    if resumed:
        third = LineGather([None], outs[split:], scratch, chips)
        third.send(chips - 2)
        third.receive(chips - 2)
    if dense:
        first.finish()
    if line:
        second.finish_own()
        for step in range(steps):
            second.finish(step)
    if resumed:
        third.finish(chips - 2)


def gather(dense, line, steps, fsdp, chips, collective_id, resumed=()):
    arrays = list(dense) + list(line) + list(resumed)
    count = len(arrays)
    scratch = (dense_scratch(dense, fsdp) if dense else []) + (
        line_scratch(line, chips) if line else []
    )
    if resumed:
        scratch = scratch + line_scratch([None], chips)
    return pl.pallas_call(
        functools.partial(
            gather_kernel, len(dense), len(line), len(resumed), steps, fsdp, chips
        ),
        out_shape=[jax.ShapeDtypeStruct((fsdp * a.shape[0],) + a.shape[1:], a.dtype) for a in dense]
        + [jax.ShapeDtypeStruct((2, chips) + a.shape, a.dtype) for a in line]
        + [jax.ShapeDtypeStruct(a.shape, a.dtype) for a in resumed],
        in_specs=[pl.BlockSpec(memory_space=pl.ANY)] * count,
        out_specs=[pl.BlockSpec(memory_space=pl.ANY)] * count,
        scratch_shapes=scratch,
        input_output_aliases={count - 1: count - 1} if resumed else {},
        compiler_params=pltpu.CompilerParams(
            collective_id=collective_id, has_side_effects=True, vmem_limit_bytes=VMEM_BYTES
        ),
        name="gather",
    )(*arrays)


def add(*parts):
    total = parts[0].astype(F32)
    for part in parts[1:]:
        total = total + part.astype(F32)
    return total


class LineSum:
    def __init__(self, chips, held, keep, gots, sems):
        self.chips, self.held, self.keep = chips, held, keep
        self.got_right, self.got_left = gots
        self.sems = sems
        self.ctx, self.me, self.chip, core, sibling = place()

    def right(self, step):
        return remote(
            self.keep(self.chips - 1 - step),
            self.got_right.at[step],
            self.sems[0].at[step],
            self.sems[1].at[step],
            (self.ctx + 2, self.me),
        )

    def left(self, step):
        return remote(
            self.keep(step + 1),
            self.got_left.at[step],
            self.sems[2].at[step],
            self.sems[3].at[step],
            (self.ctx - 2, self.me),
        )

    def step(self, step):
        chip, chips = self.chip, self.chips
        far_right, far_left = chips - 1 - step, step + 1

        @pl.when(chip <= step)
        def _():
            parts = self.held(far_right)
            if step == 0:
                self.keep(far_right)[...] = add(*parts()).astype(BF16)
            else:

                @pl.when(chip == 0)
                def _():
                    self.keep(far_right)[...] = add(*parts()).astype(BF16)

                @pl.when(chip >= 1)
                def _():
                    self.right(step - 1).wait_recv()
                    total = add(*parts(), self.got_right[step - 1])
                    self.keep(far_right)[...] = total.astype(BF16)

            self.right(step).start()

        @pl.when(chip >= chips - 1 - step)
        def _():
            parts = self.held(far_left)
            if step == 0:
                self.keep(far_left)[...] = add(*parts()).astype(BF16)
            else:

                @pl.when(chip == chips - 1)
                def _():
                    self.keep(far_left)[...] = add(*parts()).astype(BF16)

                @pl.when(chip < chips - 1)
                def _():
                    self.left(step - 1).wait_recv()
                    total = add(*parts(), self.got_left[step - 1])
                    self.keep(far_left)[...] = total.astype(BF16)

            self.left(step).start()

    def total(self, done):
        chip, chips, last = self.chip, self.chips, self.chips - 2
        parts = self.held(0)

        @pl.when(chip == 0)
        def _():
            self.left(last).wait_recv()
            done(add(*parts(), self.got_left[last]))

        @pl.when(chip == chips - 1)
        def _():
            self.right(last).wait_recv()
            done(add(*parts(), self.got_right[last]))

        @pl.when((chip >= 1) & (chip < chips - 1))
        def _():
            self.left(last).wait_recv()
            self.right(last).wait_recv()
            done(add(*parts(), self.got_left[last], self.got_right[last]))

    def finish(self):
        for step in range(self.chips - 1):

            @pl.when(self.chip <= step)
            def _():
                self.right(step).wait_send()

            @pl.when(self.chip >= self.chips - 1 - step)
            def _():
                self.left(step).wait_send()


def line_reduce_kernel(
    chips, mine_ref, other_ref, out_ref, pair, gr, gl, ps, pr, s0, s1, s2, s3
):
    ctx, me, chip, core, sibling = place()
    greet(chips, [], True)
    swaps = [
        remote(other_ref.at[r], pair.at[r], ps.at[r], pr.at[r], (sibling, me))
        for r in range(chips)
    ]
    order = []
    for step in range(chips - 1):
        for r in (chips - 1 - step, step + 1):
            if r not in order:
                order.append(r)
    for r in order + [0]:
        swaps[r].start()

    def held(r):
        swaps[r].wait_recv()
        return lambda: (mine_ref[r], pair[r])

    line = LineSum(chips, held, lambda r: pair.at[r], (gr, gl), (s0, s1, s2, s3))
    for step in range(chips - 1):
        line.step(step)

    def done(total):
        out_ref[...] = total

    line.total(done)
    line.finish()
    for swap in swaps:
        swap.wait_send()


def line_reduce_now(mine, other, chips, collective_id):
    unused, rows, width = mine.shape
    vmem = pl.BlockSpec(memory_space=pltpu.VMEM)
    return pl.pallas_call(
        functools.partial(line_reduce_kernel, chips),
        out_shape=jax.ShapeDtypeStruct((rows, width), F32),
        in_specs=[vmem, vmem],
        out_specs=vmem,
        scratch_shapes=[pltpu.VMEM((chips, rows, width), BF16)]
        + [pltpu.VMEM((chips - 1, rows, width), BF16) for unused in range(2)]
        + [pltpu.SemaphoreType.DMA((chips,)) for unused in range(2)]
        + [pltpu.SemaphoreType.DMA((chips - 1,)) for unused in range(4)],
        compiler_params=pltpu.CompilerParams(
            collective_id=collective_id, has_side_effects=True, vmem_limit_bytes=VMEM_BYTES
        ),
        name="line_reduce",
    )(mine, other)


DENSE_BUFFERS = 6
DENSE_SEMS = 14


class DenseSum:
    def __init__(self, local, out, buffers, sems, fsdp, chips):
        self.local, self.out = local, out
        self.pair, self.cross, self.sums, got_right, got_left, self.spread = buffers
        self.sems = sems
        self.chips = chips
        self.ctx, self.me, self.chip, self.core, self.sibling = place()
        self.owners = peers_of(self.me, fsdp) + [self.me]
        self.cut = out.shape[2] // chips
        self.line = LineSum(
            chips,
            lambda r: lambda: (self.sums[:, self.columns(r)],),
            lambda r: self.keep_ref(r),
            (got_right, got_left),
            sems[4:8],
        )

    def keep_ref(self, r):
        return self.sums.at[:, self.columns(r)]

    def columns(self, r):
        owner = lax.rem(self.chip + r, self.chips)
        return pl.ds(pl.multiple_of(owner * self.cut, LANES), self.cut)

    def swap(self, j):
        return remote(
            self.local.at[self.owners[j], 1 - self.core],
            self.pair.at[j],
            self.sems[0].at[j],
            self.sems[1].at[j],
            (self.sibling, self.me),
        )

    def crossing(self, j):
        return remote(
            self.pair.at[j],
            self.cross.at[j],
            self.sems[2].at[j],
            self.sems[3].at[j],
            (self.ctx, self.owners[j]),
        )

    def to_right(self, step):
        return remote(
            self.spread.at[0, (self.chips - step) % self.chips],
            self.spread.at[0, self.chips - 1 - step],
            self.sems[8].at[step],
            self.sems[9].at[step],
            (self.ctx + 2, self.me),
        )

    def to_left(self, step):
        return remote(
            self.spread.at[0, step],
            self.spread.at[0, step + 1],
            self.sems[10].at[step],
            self.sems[11].at[step],
            (self.ctx - 2, self.me),
        )

    def across(self, slot):
        return remote(
            self.spread.at[0, slot],
            self.spread.at[1, slot],
            self.sems[12].at[slot],
            self.sems[13].at[slot],
            (self.sibling, self.me),
        )

    def start(self):
        for j in range(len(self.owners)):
            self.swap(j).start()

    def cross_over(self):
        for j, owner in enumerate(self.owners):
            self.swap(j).wait_recv()
            self.pair[j] = add(self.local[owner, self.core], self.pair[j]).astype(BF16)
            if j < len(self.owners) - 1:
                self.crossing(j).start()

    def stages(self):
        chip, chips = self.chip, self.chips

        def open_up():
            for j in range(len(self.owners) - 1):
                self.crossing(j).wait_recv()
            self.sums[...] = add(
                *[self.cross[j] for j in range(len(self.owners) - 1)],
                self.pair[len(self.owners) - 1],
            ).astype(BF16)
            self.line.step(0)

        def summed():
            def done(total):
                self.spread[0, 0] = total.astype(BF16)

            self.line.total(done)
            hand_on(0)

        def hand_on(step):
            @pl.when((chip + 1 < chips) & (chip >= step))
            def _():
                self.to_right(step).start()

            @pl.when((chip >= 1) & (chip + step < chips))
            def _():
                self.to_left(step).start()

            if step == 0:
                self.across(0).start()

        def take(step):
            @pl.when(chip >= step + 1)
            def _():
                self.to_right(step).wait_recv()
                self.across(chips - 1 - step).start()

            @pl.when(chip + step + 1 < chips)
            def _():
                self.to_left(step).wait_recv()
                self.across(step + 1).start()

        def pass_on(step):
            def run():
                take(step - 1)
                hand_on(step)

            return run

        def line_step(step):
            return lambda: self.line.step(step)

        return (
            [open_up]
            + [line_step(step) for step in range(1, chips - 1)]
            + [summed]
            + [pass_on(step) for step in range(1, chips - 1)]
            + [lambda: take(chips - 2)]
        )

    def finish(self):
        chip, chips = self.chip, self.chips
        for r in range(chips):
            self.out[self.core, :, self.columns(r)] = self.spread[0, r]
        for r in range(chips):
            self.across(r).wait()
            self.out[1 - self.core, :, self.columns(r)] = self.spread[1, r]
        for step in range(chips - 1):

            @pl.when((chip + 1 < chips) & (chip >= step))
            def _():
                self.to_right(step).wait_send()

            @pl.when((chip >= 1) & (chip + step < chips))
            def _():
                self.to_left(step).wait_send()

        self.line.finish()
        for j in range(len(self.owners) - 1):
            self.crossing(j).wait_send()
        for j in range(len(self.owners)):
            self.swap(j).wait_send()


def dense_reduce_kernel(fsdp, chips, cuts, *refs):
    count = len(cuts)
    arrays = max(cut[0] for cut in cuts) + 1
    ins, outs, rest = refs[:arrays], refs[arrays : 2 * arrays], refs[2 * arrays :]
    ctx, me, chip, core, sibling = place()
    greet(chips, peers_of(me, fsdp), True)
    sums = []
    for i, (which, start, size) in enumerate(cuts):
        buffers = rest[i * DENSE_BUFFERS : (i + 1) * DENSE_BUFFERS]
        sems = rest[count * DENSE_BUFFERS + i * DENSE_SEMS :][:DENSE_SEMS]
        sums.append(
            DenseSum(
                ins[which].at[:, :, :, pl.ds(start, size)],
                outs[which].at[:, :, pl.ds(start, size)],
                buffers,
                sems,
                fsdp,
                chips,
            )
        )
    for one in sums:
        one.start()
    for one in sums:
        one.cross_over()
    stages = [one.stages() for one in sums]
    lag = chips - 1
    for tick in range(len(stages[0]) + lag * (count - 1)):
        for i in range(count):
            if 0 <= tick - lag * i < len(stages[i]):
                stages[i][tick - lag * i]()
    for one in sums:
        one.finish()


def dense_reduce(arrays, piece, fsdp, chips, collective_id):
    vmem = pl.BlockSpec(memory_space=pltpu.VMEM)
    cuts, buffers = [], []
    for i, a in enumerate(arrays):
        rows, width = a.shape[2:]
        for start in range(0, width, piece):
            size = min(piece, width - start)
            cut = size // chips
            cuts.append((i, start, size))
            buffers += [
                pltpu.VMEM((fsdp, rows, size), BF16),
                pltpu.VMEM((fsdp - 1, rows, size), BF16),
                pltpu.VMEM((rows, size), BF16),
                pltpu.VMEM((chips - 1, rows, cut), BF16),
                pltpu.VMEM((chips - 1, rows, cut), BF16),
                pltpu.VMEM((2, chips, rows, cut), BF16),
            ]
    sems = (
        [pltpu.SemaphoreType.DMA((fsdp,)) for unused in range(2)]
        + [pltpu.SemaphoreType.DMA((fsdp - 1,)) for unused in range(2)]
        + [pltpu.SemaphoreType.DMA((chips - 1,)) for unused in range(8)]
        + [pltpu.SemaphoreType.DMA((chips,)) for unused in range(2)]
    )
    return pl.pallas_call(
        functools.partial(dense_reduce_kernel, fsdp, chips, tuple(cuts)),
        out_shape=[jax.ShapeDtypeStruct(a.shape[1:], BF16) for a in arrays],
        in_specs=[vmem] * len(arrays),
        out_specs=[vmem] * len(arrays),
        scratch_shapes=buffers + sems * len(cuts),
        compiler_params=pltpu.CompilerParams(
            collective_id=collective_id, has_side_effects=True, vmem_limit_bytes=VMEM_BYTES
        ),
        name="dense_reduce",
    )(*arrays)


def after(value, *others):
    return lax.optimization_barrier((value,) + others)[0]


def attention_kernel(
    scale, q_ref, k_ref, v_ref, oq_ref, pq_ref, ok_ref, out_ref, lse_ref, bias, scores
):
    keys = k_ref.shape[0]
    tiles = keys // KEY_TILE
    rows = q_ref.shape[0]

    @pl.when(pl.program_id(0) == 0)
    def _():
        def fill(t, carry):
            tile = pl.ds(pl.multiple_of(t * KEY_TILE, KEY_TILE), KEY_TILE)
            gap = oq_ref[...] - ok_ref[:, tile]
            bias[:, tile] = jnp.where((gap >= 0) & (gap <= pq_ref[...]), 0.0, MASKED)
            return carry

        lax.fori_loop(0, tiles, fill, 0)

    query = q_ref[...]

    def score(t, top):
        tile = pl.ds(pl.multiple_of(t * KEY_TILE, KEY_TILE), KEY_TILE)
        raw = dot(query, k_ref[tile, :], NT) * (scale * LOG2E) + bias[:, tile]
        scores[:, tile] = raw
        for part in range(KEY_TILE // LANES):
            top = jnp.maximum(top, raw[:, part * LANES : (part + 1) * LANES])
        return top

    top = lax.fori_loop(0, tiles, score, jnp.full((rows, LANES), MASKED, F32))
    top = jnp.max(top, axis=1, keepdims=True)

    def weigh(t, carry):
        total, acc = carry
        tile = pl.ds(pl.multiple_of(t * KEY_TILE, KEY_TILE), KEY_TILE)
        probs = jnp.exp2(scores[:, tile] - top)
        for part in range(KEY_TILE // LANES):
            total = total + probs[:, part * LANES : (part + 1) * LANES]
        acc = acc + dot(probs.astype(BF16), v_ref[tile, :], NN)
        return total, acc

    total, acc = lax.fori_loop(
        0, tiles, weigh, (jnp.zeros((rows, LANES), F32), jnp.zeros((rows, HEAD_SIZE), F32))
    )
    total = jnp.sum(total, axis=1, keepdims=True)
    out_ref[...] = (acc / total).astype(BF16)
    lse = jnp.broadcast_to(top + jnp.log2(total), (rows, LANES))
    lse_ref[0] = lse.T[:1, :]


def attention(queries, kv, order_mine, pos_mine, order_keys, group):
    rows = queries.shape[0]
    keys = kv.shape[0]
    per_group = QUERY_HEADS // KVH
    return pl.pallas_call(
        functools.partial(attention_kernel, HEAD_SIZE ** (-0.5)),
        grid=(per_group,),
        out_shape=[
            jax.ShapeDtypeStruct((rows, per_group * HEAD_SIZE), BF16),
            jax.ShapeDtypeStruct((per_group, 1, rows), F32),
        ],
        in_specs=[
            pl.BlockSpec((rows, HEAD_SIZE), lambda h: (0, group * per_group + h)),
            pl.BlockSpec((keys, HEAD_SIZE), lambda h: (0, group)),
            pl.BlockSpec((keys, HEAD_SIZE), lambda h: (0, KVH + group)),
            pl.BlockSpec((rows, 1), lambda h: (0, 0)),
            pl.BlockSpec((rows, 1), lambda h: (0, 0)),
            pl.BlockSpec((1, keys), lambda h: (0, 0)),
        ],
        out_specs=[
            pl.BlockSpec((rows, HEAD_SIZE), lambda h: (0, h)),
            pl.BlockSpec((1, 1, rows), lambda h: (h, 0, 0)),
        ],
        scratch_shapes=[pltpu.VMEM((rows, keys), F32), pltpu.VMEM((rows, keys), F32)],
        compiler_params=pltpu.CompilerParams(vmem_limit_bytes=VMEM_BYTES),
        cost_estimate=pl.CostEstimate(
            flops=4 * rows * keys * HEAD_SIZE * per_group,
            bytes_accessed=4 * rows * per_group * HEAD_SIZE + 4 * keys * HEAD_SIZE,
            transcendentals=rows * keys * per_group,
        ),
        name="attention",
    )(queries, kv, kv, order_mine[:, None], pos_mine[:, None], order_keys[None, :])


def attention_back_kernel(
    scale,
    per_group,
    q_ref,
    k_ref,
    v_ref,
    o_ref,
    do_ref,
    lse_ref,
    oq_ref,
    pq_ref,
    ok_ref,
    dq_ref,
    dk_ref,
    dv_ref,
    bias,
    dk_acc,
    dv_acc,
):
    keys = k_ref.shape[0]
    tiles = keys // KEY_TILE
    rows = q_ref.shape[0]
    head = pl.program_id(0)

    @pl.when(head == 0)
    def _():
        def fill(t, carry):
            tile = pl.ds(pl.multiple_of(t * KEY_TILE, KEY_TILE), KEY_TILE)
            gap = oq_ref[...] - ok_ref[tile, :]
            bias[tile, :] = jnp.where((gap >= 0) & (gap <= pq_ref[...]), 0.0, MASKED)
            return carry

        lax.fori_loop(0, tiles, fill, 0)

    @pl.when(lax.rem(head, per_group) == 0)
    def _():
        dk_acc[...] = jnp.zeros_like(dk_acc)
        dv_acc[...] = jnp.zeros_like(dv_acc)

    query = q_ref[...]
    grad = do_ref[...]
    lse = lse_ref[0]
    product = grad.astype(F32) * o_ref[...].astype(F32)
    delta = jnp.sum(product.T, axis=0, keepdims=True)

    def step(t, acc):
        tile = pl.ds(pl.multiple_of(t * KEY_TILE, KEY_TILE), KEY_TILE)
        key = k_ref[tile, :]
        raw = dot(key, query, NT) * (scale * LOG2E) + bias[tile, :]
        probs = jnp.exp2(raw - lse)
        prob_grad = dot(v_ref[tile, :], grad, NT)
        score_grad = (probs * (prob_grad - delta)).astype(BF16)
        dv_acc[tile, :] += dot(probs.astype(BF16), grad, NN)
        dk_acc[tile, :] += dot(score_grad, query, NN)
        return acc + dot(score_grad, key, TN)

    acc = lax.fori_loop(0, tiles, step, jnp.zeros((rows, HEAD_SIZE), F32))
    dq_ref[...] = acc * scale

    @pl.when(lax.rem(head, per_group) == per_group - 1)
    def _():
        dk_ref[...] = (dk_acc[...] * scale).astype(BF16)
        dv_ref[...] = dv_acc[...].astype(BF16)


def attention_back(
    queries, kv, attended, attended_grad, lse, order_mine, pos_mine, order_keys, group
):
    rows = queries.shape[0]
    keys = kv.shape[0]
    per_group = QUERY_HEADS // KVH
    head_rows = pl.BlockSpec((rows, HEAD_SIZE), lambda h: (0, group * per_group + h))
    group_rows = pl.BlockSpec((rows, HEAD_SIZE), lambda h: (0, h))
    return pl.pallas_call(
        functools.partial(attention_back_kernel, HEAD_SIZE ** (-0.5), per_group),
        grid=(per_group,),
        out_shape=[
            jax.ShapeDtypeStruct((rows, per_group * HEAD_SIZE), F32),
            jax.ShapeDtypeStruct((keys, HEAD_SIZE), BF16),
            jax.ShapeDtypeStruct((keys, HEAD_SIZE), BF16),
        ],
        in_specs=[
            head_rows,
            pl.BlockSpec((keys, HEAD_SIZE), lambda h: (0, group)),
            pl.BlockSpec((keys, HEAD_SIZE), lambda h: (0, KVH + group)),
            group_rows,
            head_rows,
            pl.BlockSpec((1, 1, rows), lambda h: (h, 0, 0)),
            pl.BlockSpec((1, rows), lambda h: (0, 0)),
            pl.BlockSpec((1, rows), lambda h: (0, 0)),
            pl.BlockSpec((keys, 1), lambda h: (0, 0)),
        ],
        out_specs=[
            group_rows,
            pl.BlockSpec((keys, HEAD_SIZE), lambda h: (0, 0)),
            pl.BlockSpec((keys, HEAD_SIZE), lambda h: (0, 0)),
        ],
        scratch_shapes=[
            pltpu.VMEM((keys, rows), F32),
            pltpu.VMEM((keys, HEAD_SIZE), F32),
            pltpu.VMEM((keys, HEAD_SIZE), F32),
        ],
        compiler_params=pltpu.CompilerParams(vmem_limit_bytes=VMEM_BYTES),
        cost_estimate=pl.CostEstimate(
            flops=10 * rows * keys * HEAD_SIZE * per_group,
            bytes_accessed=10 * rows * per_group * HEAD_SIZE + 8 * keys * HEAD_SIZE,
            transcendentals=rows * keys * per_group,
        ),
        name="attention_back",
    )(
        queries,
        kv,
        kv,
        attended,
        attended_grad,
        lse,
        order_mine[None, :],
        pos_mine[None, :],
        order_keys[:, None],
    )


def expert_kernel(
    capacity,
    local_experts,
    expert_count,
    place_ref,
    hidden_ref,
    grad_ref,
    table_ref,
    weight_ref,
    gate_ref,
    up_ref,
    down_ref,
    out_ref,
    rows_mine,
    rows_other,
    save_x,
    save_pg,
    save_inner,
    save_da,
    save_db,
):
    tokens = hidden_ref.shape[2]
    slot_rows = save_x.shape[1] // 2
    core = place_ref[1]
    first = place_ref[2]
    slot = lax.broadcasted_iota(jnp.int32, (slot_rows, tokens), 0).astype(F32) + 1.0
    slot = jnp.where(slot <= capacity, slot, -1.0)
    lane = lax.broadcasted_iota(jnp.int32, (2 * slot_rows, LANES), 1)
    picks = [[], []]
    outs = [[], []]
    backs = [[], []]
    for e in range(local_experts):
        rows_x, rows_g, rows_w = [], [], []
        for q in range(2):
            row = table_ref[q, 0, pl.ds(first + e, 1), :]
            hit = slot == row
            pick = jnp.where(hit, 1.0, 0.0).astype(BF16)
            weight = weight_ref[q, 0, pl.ds(first + e, 1), :]
            rows_w.append(jnp.sum(jnp.where(hit, weight, 0.0), axis=1, keepdims=True))
            rows_x.append(dot(pick, hidden_ref[q, 0], NN).astype(BF16))
            rows_g.append(dot(pick, grad_ref[q, 0], NN))
            picks[q].append(pick)
        x = jnp.concatenate(rows_x, axis=0)
        g = jnp.concatenate(rows_g, axis=0)
        w = jnp.concatenate(rows_w, axis=0)
        pair_grad = (w * g).astype(BF16)
        gate_pre = dot(x, gate_ref[e], NN)
        up_pre = dot(x, up_ref[e], NN)
        sig = jax.nn.sigmoid(gate_pre)
        silu = gate_pre * sig
        inner = (silu * up_pre).astype(BF16)
        expert_out = dot(inner, down_ref[e], NN).astype(BF16).astype(F32)
        gate_grad = jnp.sum(expert_out * g, axis=1, keepdims=True)
        inner_grad = dot(pair_grad, down_ref[e], NT)
        da = (inner_grad * up_pre * sig * (1.0 + gate_pre * (1.0 - sig))).astype(BF16)
        db = (inner_grad * silu).astype(BF16)
        row_grad = (dot(da, gate_ref[e], NT) + dot(db, up_ref[e], NT)).astype(BF16)
        high = gate_grad.astype(BF16).astype(F32)
        extra = jnp.where(lane == first + e, high, 0.0) + jnp.where(
            lane == expert_count + first + e, gate_grad - high, 0.0
        )
        back = jnp.concatenate([row_grad, extra.astype(BF16)], axis=1)
        out_rows = (w * expert_out).astype(BF16)
        for q in range(2):
            part = slice(q * slot_rows, (q + 1) * slot_rows)
            outs[q].append(out_rows[part])
            backs[q].append(back[part])
        save_x[e] = x
        save_pg[e] = pair_grad
        save_inner[e] = inner
        save_da[e] = da
        save_db[e] = db
    for q in range(2):
        pick = jnp.concatenate(picks[q], axis=0)
        rows_ref = rows_mine if q == 0 else rows_other
        out_ref[0, core if q == 0 else 1 - core] = dot(
            pick, jnp.concatenate(outs[q], axis=0), TN
        ).astype(BF16)
        rows_ref[0] = dot(pick, jnp.concatenate(backs[q], axis=0), TN).astype(BF16)


def expert_rows_pass(
    where, hidden, grad, table, weights, gate, up, down, capacity, expert_count
):
    unused, chips, tokens, width = grad.shape
    local_experts, unused, hidden_units = gate.shape
    slots = 2 * SLOT_STEP * -(-capacity // SLOT_STEP)
    total = chips * slots
    once = pl.Buffered(1)

    def whole(shape):
        return pl.BlockSpec(shape, lambda r, s: (0,) * len(shape), pipeline_mode=once)

    def saved(columns):
        return pl.BlockSpec((local_experts, slots, columns), lambda r, s: (0, r, 0))

    chunk = pl.BlockSpec((2, 1, tokens, width), lambda r, s: (0, r, 0, 0))
    placed = pl.BlockSpec(
        (1, 2, tokens, width), lambda r, s: (lax.rem(s[0] + r, chips), 0, 0, 0)
    )
    wide = pl.BlockSpec((1, tokens, width + LANES), lambda r, s: (r, 0, 0))
    small = pl.BlockSpec((2, 1, expert_count, tokens), lambda r, s: (0, r, 0, 0))
    flops = 2 * total * width * hidden_units * local_experts * 6 + 8 * total * tokens * width
    return pl.pallas_call(
        functools.partial(expert_kernel, capacity, local_experts, expert_count),
        grid_spec=pltpu.PrefetchScalarGridSpec(
            num_scalar_prefetch=1,
            grid=(chips,),
            in_specs=[
                chunk,
                chunk,
                small,
                small,
                whole(gate.shape),
                whole(up.shape),
                whole(down.shape),
            ],
            out_specs=[
                placed,
                wide,
                wide,
                saved(width),
                saved(width),
                saved(hidden_units),
                saved(hidden_units),
                saved(hidden_units),
            ],
        ),
        out_shape=[jax.ShapeDtypeStruct((chips, 2, tokens, width), BF16)]
        + [jax.ShapeDtypeStruct((chips, tokens, width + LANES), BF16)] * 2
        + [jax.ShapeDtypeStruct((local_experts, total, width), BF16)] * 2
        + [jax.ShapeDtypeStruct((local_experts, total, hidden_units), BF16)] * 3,
        compiler_params=pltpu.CompilerParams(vmem_limit_bytes=VMEM_BYTES),
        cost_estimate=pl.CostEstimate(
            flops=flops, bytes_accessed=80_000_000, transcendentals=total * hidden_units * 2
        ),
        name="expert_rows",
    )(where, hidden, grad, table, weights, gate, up, down)


def outer_kernel(per, split_left, left_ref, right_ref, out_ref):
    product = dot(left_ref[0], right_ref[0], TN).astype(BF16)
    axis = 0 if split_left else 1
    size = product.shape[axis] // per
    for i in range(per):
        out_ref[i, 0] = lax.slice_in_dim(product, i * size, (i + 1) * size, axis=axis)


def outer_products(left, right, fsdp, split_left):
    experts, total, m = left.shape
    n = right.shape[2]
    per = 1 if ((m if split_left else n) // fsdp) % LANES == 0 else 2
    if split_left:
        m = m // fsdp
    else:
        n = n // fsdp
    return pl.pallas_call(
        functools.partial(outer_kernel, per, split_left),
        grid=(experts, fsdp // per),
        out_shape=jax.ShapeDtypeStruct((fsdp, experts, m, n), BF16),
        in_specs=[
            pl.BlockSpec(
                (1, total, m * per if split_left else m),
                lambda e, f: (e, 0, f if split_left else 0),
            ),
            pl.BlockSpec(
                (1, total, n if split_left else n * per),
                lambda e, f: (e, 0, 0 if split_left else f),
            ),
        ],
        out_specs=pl.BlockSpec((per, 1, m, n), lambda e, f: (f, e, 0, 0)),
        compiler_params=pltpu.CompilerParams(vmem_limit_bytes=VMEM_BYTES),
        cost_estimate=pl.CostEstimate(
            flops=2 * total * m * n * experts * fsdp, bytes_accessed=14_000_000, transcendentals=0
        ),
        name="outer_products",
    )(left, right)


def body(
    tokens,
    grad_out,
    order,
    lengths,
    routes,
    gain_one,
    gain_two,
    w_query,
    w_key,
    w_value,
    w_out,
    w_router,
    w_gate,
    w_up,
    w_down,
):
    fsdp = lax.axis_size("fsdp")
    chips = lax.axis_size("ctx") // 2
    ctx_index = lax.axis_index("ctx")
    chip = ctx_index // 2
    core = lax.rem(ctx_index, 2)
    tok_rows = tokens.shape[1]
    width = tokens.shape[2]
    top_count = routes.shape[2]
    local_experts = w_gate.shape[0]
    expert_count = local_experts * chips * 2
    capacity = 5 * tok_rows * top_count // (4 * expert_count)
    kv_width = KVH * HEAD_SIZE
    shard = gain_one.shape[0]

    small = jnp.concatenate(
        [
            w_router,
            gain_one[:, None],
            gain_two[:, None],
            jnp.zeros((shard, LANES - expert_count - 2), BF16),
        ],
        axis=1,
    )
    qkv_shard = jnp.concatenate([w_query, w_key, w_value], axis=1)
    qkv_full, small_full, grad_all = gather(
        [qkv_shard, small], [grad_out[0]], chips - 2, fsdp, chips, 0
    )

    qkv_full, w_gate, w_up, w_down = lax.optimization_barrier((qkv_full, w_gate, w_up, w_down))
    gate_full, up_full, down_full = (
        lax.all_gather(w_gate, "fsdp", axis=1, tiled=True),
        lax.all_gather(w_up, "fsdp", axis=1, tiled=True),
        lax.all_gather(w_down, "fsdp", axis=2, tiled=True),
    )
    router_full = small_full[:, :expert_count]
    gain_a = small_full[:, expert_count].astype(F32)
    gain_b = small_full[:, expert_count + 1].astype(F32)

    order_row = order[0]
    start_row = ctx_index * tok_rows
    order_mine = lax.dynamic_slice_in_dim(order_row, start_row, tok_rows)
    ends = jnp.cumsum(lengths[0])
    starts = ends - lengths[0]
    past = order_mine[:, None] >= ends[None, :]
    doc_start = jnp.max(jnp.where(past, ends[None, :], starts[:1]), axis=1)
    pos_mine = order_mine - doc_start
    by_chip = jnp.roll(order_row.reshape(chips, 2, tok_rows), -chip, axis=0)
    by_chip = jnp.where(core == 0, by_chip, by_chip[:, ::-1])
    order_keys = jnp.swapaxes(by_chip, 0, 1).reshape(-1)

    route_rows = routes[0]
    route_onehot = (route_rows[:, :, None] == jnp.arange(expert_count)[None, None, :]).astype(F32)
    routed = jnp.sum(route_onehot, axis=1)
    earlier = (order_mine[None, :] < order_mine[:, None]).astype(BF16)
    ranks = jnp.dot(earlier, routed.astype(BF16), preferred_element_type=F32)
    table = jnp.where(routed > 0, jnp.minimum(ranks, capacity) + 1.0, 0.0)

    half_dim = HEAD_SIZE // 2
    freqs = ROPE_BASE ** (-2.0 * jnp.arange(half_dim).astype(F32) / HEAD_SIZE)
    angles = pos_mine.astype(F32)[:, None] * freqs[None, :]
    cosine = jnp.cos(angles)[:, None, :]
    sine = jnp.sin(angles)[:, None, :]

    inputs = tokens[0].astype(F32)
    hidden_one = rms_scale(inputs, gain_a).astype(BF16)
    pre = jnp.dot(hidden_one, qkv_full, preferred_element_type=F32)
    turned = rotate(
        pre[:, : width + kv_width].reshape(tok_rows, QUERY_HEADS + KVH, HEAD_SIZE), cosine, sine
    )
    queries = turned[:, :QUERY_HEADS].astype(BF16).reshape(tok_rows, width)
    kv_mine = jnp.concatenate(
        [
            turned[:, QUERY_HEADS:].astype(BF16).reshape(tok_rows, kv_width),
            pre[:, width + kv_width :].astype(BF16),
        ],
        axis=1,
    )
    out_full, kv_all, table_all, grad_all = gather(
        [w_out], [kv_mine, table.T], chips - 1, fsdp, chips, 1, [grad_all]
    )
    kv_all = kv_all.reshape(-1, 2 * kv_width)
    attended, lse = [], []
    for group in range(KVH):
        part, part_lse = attention(
            after(queries, *attended[-1:]), kv_all, order_mine, pos_mine, order_keys, group
        )
        attended.append(part)
        lse.append(part_lse)
    attended_parts, attended = attended, jnp.concatenate(attended, axis=1)
    middle = inputs + jnp.dot(attended, out_full, preferred_element_type=F32)
    hidden_two = rms_scale(middle, gain_b).astype(BF16)
    logits = jnp.dot(hidden_two, router_full, preferred_element_type=F32)
    chosen = jnp.where(routed > 0, logits, MASKED)
    gate_weights = jnp.where(routed > 0, jax.nn.softmax(chosen, axis=-1), 0.0)

    hidden_all, weights_all = gather([], [hidden_two, gate_weights.T], chips - 1, fsdp, chips, 2)
    where = jnp.stack([chip, core, ctx_index * local_experts]).astype(jnp.int32)
    (
        out_rows,
        rows_mine,
        rows_other,
        save_x,
        save_pg,
        save_inner,
        save_da,
        save_db,
    ) = expert_rows_pass(
        where,
        hidden_all,
        grad_all,
        table_all,
        weights_all,
        gate_full,
        up_full,
        down_full,
        capacity,
        expert_count,
    )
    gate_local = outer_products(save_x, save_da, fsdp, True)
    up_local = outer_products(save_x, save_db, fsdp, True)
    down_local = outer_products(save_inner, save_pg, fsdp, False)
    returned = line_reduce_now(
        after(rows_mine, gate_local, up_local, down_local), rows_other, chips, 5
    )
    out_sum = lax.psum_scatter(
        after(out_rows, returned).reshape(2 * chips, tok_rows, width),
        "ctx",
        scatter_dimension=0,
        tiled=True,
    )
    expert_grads = [
        lax.psum_scatter(part, "fsdp", scatter_dimension=0, tiled=True)
        for part in (gate_local, up_local, down_local)
    ]

    out_grad = grad_out[0].astype(F32)
    extra = returned[:, width:]
    gate_grad = extra[:, :expert_count] + extra[:, expert_count : 2 * expert_count]
    logit_grad = (
        gate_weights * (gate_grad - jnp.sum(gate_weights * gate_grad, axis=-1, keepdims=True))
    ).astype(BF16)
    router_local = jnp.einsum("td,te->de", hidden_two, logit_grad, preferred_element_type=F32)
    hidden_two_grad = returned[:, :width] + jnp.einsum(
        "te,de->td", logit_grad, router_full, preferred_element_type=F32
    )
    unused_two, norm_two_back = jax.vjp(rms_scale, middle, gain_b)
    middle_part, gain_two_local = norm_two_back(hidden_two_grad)
    middle_grad = out_grad + middle_part
    branch_grad = middle_grad.astype(BF16)
    out_local = jnp.einsum("tc,td->cd", attended, branch_grad, preferred_element_type=F32)
    attended_grad = jnp.einsum(
        "td,cd->tc", branch_grad, out_full, preferred_element_type=F32
    ).astype(BF16)

    query_grad, kv_grads = [], [None] * (2 * KVH)
    for group in range(KVH):
        parts = attention_back(
            queries,
            kv_all,
            attended_parts[group],
            after(attended_grad, *query_grad[-1:]),
            lse[group],
            order_mine,
            pos_mine,
            order_keys,
            group,
        )
        query_grad.append(parts[0])
        kv_grads[group], kv_grads[KVH + group] = parts[1:]
    kv_grads = jnp.concatenate(kv_grads, axis=1).reshape(2, chips, tok_rows, 2 * kv_width)
    kv_grad = line_reduce_now(kv_grads[0], kv_grads[1], chips, 3)
    turned_grad = rotate(
        jnp.concatenate(query_grad + [kv_grad[:, :kv_width]], axis=1).reshape(
            tok_rows, QUERY_HEADS + KVH, HEAD_SIZE
        ),
        cosine,
        -sine,
    ).reshape(tok_rows, width + kv_width)
    pre_grad = jnp.concatenate(
        [turned_grad.astype(BF16), kv_grad[:, kv_width:].astype(BF16)], axis=1
    )
    qkv_local = jnp.einsum("td,tc->dc", hidden_one, pre_grad, preferred_element_type=F32)
    hidden_one_grad = jnp.einsum("tc,dc->td", pre_grad, qkv_full, preferred_element_type=F32)
    unused_one, norm_one_back = jax.vjp(rms_scale, inputs, gain_a)
    input_part, gain_one_local = norm_one_back(hidden_one_grad)
    input_grad = (middle_grad + input_part).astype(BF16)

    def halves(local):
        local = local.astype(BF16).reshape(fsdp, 2, shard // 2, local.shape[1])
        pad = -local.shape[3] % (LANES * chips)
        return jnp.pad(local, ((0, 0), (0, 0), (0, 0), (0, pad))) if pad else local

    span = shard * expert_count // 16
    wide = LANES * chips * -(-max(span, shard) // (LANES * chips))
    small_local = jnp.stack(
        [
            jnp.pad(
                router_local.astype(BF16).reshape(fsdp, 16, span),
                ((0, 0), (0, 0), (0, wide - span)),
            ),
            jnp.pad(
                jnp.stack(
                    [gain_one_local.reshape(fsdp, shard), gain_two_local.reshape(fsdp, shard)],
                    axis=1,
                ).astype(BF16),
                ((0, 0), (0, 14), (0, wide - shard)),
            ),
        ],
        axis=1,
    )
    qkv_sum, out_proj_sum, small_sum = dense_reduce(
        [halves(qkv_local), halves(out_local), small_local], DENSE_PIECE, fsdp, chips, 4
    )
    edge = width + 2 * kv_width
    qkv_grads = qkv_sum.reshape(shard, -1)
    out_proj_grad = out_proj_sum.reshape(shard, -1)[:, :width]
    gate_grad_out, up_grad_out, down_grad_out = (
        after(part, pre_grad)[0].astype(F32) for part in expert_grads
    )
    result = middle + after(out_sum, pre_grad)[0].astype(F32)
    return (
        result.astype(BF16)[None],
        input_grad[None],
        small_sum[1, 0, :shard].astype(F32),
        small_sum[1, 1, :shard].astype(F32),
        qkv_grads[:, :width].astype(F32),
        qkv_grads[:, width : width + kv_width].astype(F32),
        qkv_grads[:, width + kv_width : edge].astype(F32),
        out_proj_grad.astype(F32),
        small_sum[0, :, :span].reshape(shard, expert_count).astype(F32),
        gate_grad_out,
        up_grad_out,
        down_grad_out,
    )


def solution(mesh):
    placed = (
        P("fsdp", "ctx", None),
        P("fsdp", "ctx", None),
        P("fsdp", None),
        P("fsdp", None),
        P("fsdp", "ctx", None),
        P("fsdp"),
        P("fsdp"),
        P("fsdp", None),
        P("fsdp", None),
        P("fsdp", None),
        P("fsdp", None),
        P("fsdp", None),
        P("ctx", "fsdp", None),
        P("ctx", "fsdp", None),
        P("ctx", None, "fsdp"),
    )
    return jax.shard_map(
        body,
        mesh=mesh,
        in_specs=placed,
        out_specs=(
            P("fsdp", "ctx", None),
            P("fsdp", "ctx", None),
            P("fsdp"),
            P("fsdp"),
            P("fsdp", None),
            P("fsdp", None),
            P("fsdp", None),
            P("fsdp", None),
            P("fsdp", None),
            P("ctx", "fsdp", None),
            P("ctx", "fsdp", None),
            P("ctx", None, "fsdp"),
        ),
        check_vma=False,
    )
```

```python
import functools

import jax
import jax.numpy as jnp
from jax import lax
from jax.experimental import pallas as pl
from jax.experimental.pallas import tpu as pltpu
from jax.sharding import PartitionSpec as P

QUERY_HEADS = 12
KVH = 2
HEAD_SIZE = 128

EPSILON = 1e-06
ROPE_BASE = 10000.0
MASKED = -1e30
LOG2E = 1.4426950408889634
LANES = 128
SLOT_STEP = 64
DENSE_PIECE = 1024
LINE_TASK = 4
KEY_TILE = 512
VMEM_BYTES = 56 * 1024 * 1024
EXPERT_VMEM_BYTES = 119 * 512 * 1024
MESH = pl.DeviceIdType.MESH
F32 = jnp.float32
BF16 = jnp.bfloat16


def dot(left, right, contract):
    return lax.dot_general(left, right, (contract, ((), ())), preferred_element_type=F32)


NN = ((1,), (0,))
NT = ((1,), (1,))
TN = ((0,), (0,))


def rms_scale(value_rows, gain):
    return (
        value_rows
        * lax.rsqrt(jnp.mean(value_rows * value_rows, axis=-1, keepdims=True) + EPSILON)
        * gain
    )


def rotate(value_rows, cosine, sine):
    half_dim = value_rows.shape[-1] // 2
    first = value_rows[..., :half_dim]
    second = value_rows[..., half_dim:]
    return jnp.concatenate(
        [first * cosine - second * sine, second * cosine + first * sine], axis=-1
    )


def place():
    ctx = lax.axis_index("ctx")
    core = lax.rem(ctx, 2)
    return ctx, lax.axis_index("fsdp"), ctx // 2, core, ctx + 1 - 2 * core


def peers_of(me, fsdp):
    peers = []
    for shift in range(1, fsdp):
        peer = me
        for bit in range(fsdp.bit_length() - 1):
            if (shift >> bit) & 1:
                digit = lax.rem(me // (1 << bit), 2)
                peer = peer + (1 << bit) - (2 << bit) * digit
        peers.append(peer)
    return peers


def greet(chips, peers, line):
    ctx, me, chip, core, sibling = place()
    barrier = pltpu.get_barrier_semaphore()
    for peer in peers:
        pl.semaphore_signal(barrier, inc=1, device_id=(ctx, peer), device_id_type=MESH)
    pl.semaphore_signal(barrier, inc=1, device_id=(sibling, me), device_id_type=MESH)
    known = len(peers) + 1
    if not line:
        pl.semaphore_wait(barrier, known)
        return
    has_right = chip + 1 < chips
    has_left = chip >= 1

    @pl.when(has_right)
    def _():
        pl.semaphore_signal(barrier, inc=1, device_id=(ctx + 2, me), device_id_type=MESH)

    @pl.when(has_left)
    def _():
        pl.semaphore_signal(barrier, inc=1, device_id=(ctx - 2, me), device_id_type=MESH)

    @pl.when(has_right & has_left)
    def _():
        pl.semaphore_wait(barrier, known + 2)

    @pl.when(jnp.logical_not(has_right & has_left))
    def _():
        pl.semaphore_wait(barrier, known + 1)


class Bounce:
    def __init__(self, src, dst, buffer, sem):
        self.inward = pltpu.make_async_copy(src, buffer, sem)
        self.outward = pltpu.make_async_copy(buffer, dst, sem)

    def start(self):
        self.inward.start()

    def turn(self):
        self.inward.wait()
        self.outward.start()

    def wait(self):
        self.outward.wait()


def remote(src, dst, send_sem, recv_sem, device):
    return pltpu.make_async_remote_copy(
        src_ref=src,
        dst_ref=dst,
        send_sem=send_sem,
        recv_sem=recv_sem,
        device_id=device,
        device_id_type=MESH,
    )


class DenseGather:
    def __init__(self, ins, outs, sems, fsdp):
        buffers, local_sem, send_sem, recv_sem, pass_sem, took_sem = sems
        ctx, me, chip, core, sibling = place()
        self.sends, self.passes, self.locals = [], [], []
        for i in range(len(ins)):
            rows = ins[i].shape[0]
            half = rows // 2
            for j, peer in enumerate(peers_of(me, fsdp)):
                self.sends.append(
                    remote(
                        ins[i].at[pl.ds(core * half, half)],
                        outs[i].at[pl.ds(me * rows + core * half, half)],
                        send_sem.at[i, j],
                        recv_sem.at[i, j],
                        (ctx, peer),
                    )
                )
                got = outs[i].at[pl.ds(peer * rows + core * half, half)]
                self.passes.append(
                    remote(got, got, pass_sem.at[i, j], took_sem.at[i, j], (sibling, me))
                )
            self.locals.append(
                Bounce(ins[i], outs[i].at[pl.ds(me * rows, rows)], buffers[i], local_sem.at[i])
            )

    def start(self):
        for copy in self.sends + self.locals:
            copy.start()

    def finish(self):
        for copy in self.locals:
            copy.turn()
        for send, copy in zip(self.sends, self.passes):
            send.wait_recv()
            copy.start()
        for send in self.sends:
            send.wait_send()
        for copy in self.passes + self.locals:
            copy.wait()


def dense_scratch(arrays, fsdp):
    count = len(arrays)
    return (
        [pltpu.VMEM(a.shape, a.dtype) for a in arrays]
        + [pltpu.SemaphoreType.DMA((count,))]
        + [pltpu.SemaphoreType.DMA((count, fsdp - 1)) for unused in range(4)]
    )


class LineGather:
    def __init__(self, ins, outs, sems, chips):
        self.ins, self.outs, self.chips = ins, outs, chips
        self.buffers, self.sems = sems[:-7], sems[-7:]
        self.ctx, self.me, self.chip, core, self.sibling = place()
        self.count = len(ins)

    def to_right(self, i, step):
        outs, chips = self.outs, self.chips
        return remote(
            self.ins[i] if step == 0 else outs[i].at[0, chips - step],
            outs[i].at[0, chips - 1 - step],
            self.sems[1].at[i, step],
            self.sems[2].at[i, step],
            (self.ctx + 2, self.me),
        )

    def to_left(self, i, step):
        outs = self.outs
        return remote(
            self.ins[i] if step == 0 else outs[i].at[0, step],
            outs[i].at[0, step + 1],
            self.sems[3].at[i, step],
            self.sems[4].at[i, step],
            (self.ctx - 2, self.me),
        )

    def across(self, i, slot):
        return remote(
            self.ins[i] if slot == 0 else self.outs[i].at[0, slot],
            self.outs[i].at[1, slot],
            self.sems[5].at[i, slot],
            self.sems[6].at[i, slot],
            (self.sibling, self.me),
        )

    def local(self, i):
        return Bounce(self.ins[i], self.outs[i].at[0, 0], self.buffers[i], self.sems[0].at[i])

    def send(self, step):
        chip, chips, count = self.chip, self.chips, self.count

        @pl.when((chip + 1 < chips) & (chip >= step))
        def _():
            for i in range(count):
                self.to_right(i, step).start()

        @pl.when((chip >= 1) & (chip + step < chips))
        def _():
            for i in range(count):
                self.to_left(i, step).start()

    def receive(self, step):
        chip, chips, count = self.chip, self.chips, self.count

        @pl.when(chip >= step + 1)
        def _():
            for i in range(count):
                self.to_right(i, step).wait_recv()
                self.across(i, chips - 1 - step).start()

        @pl.when(chip + step + 1 < chips)
        def _():
            for i in range(count):
                self.to_left(i, step).wait_recv()
                self.across(i, step + 1).start()

    def own(self):
        for i in range(self.count):
            self.across(i, 0).start()
            self.local(i).start()

    def turn_own(self):
        for i in range(self.count):
            self.local(i).turn()

    def finish_own(self):
        for i in range(self.count):
            self.across(i, 0).wait()
            self.local(i).wait()

    def finish(self, step):
        chip, chips, count = self.chip, self.chips, self.count

        @pl.when((chip + 1 < chips) & (chip >= step))
        def _():
            for i in range(count):
                self.to_right(i, step).wait_send()

        @pl.when((chip >= 1) & (chip + step < chips))
        def _():
            for i in range(count):
                self.to_left(i, step).wait_send()

        @pl.when(chip >= step + 1)
        def _():
            for i in range(count):
                self.across(i, chips - 1 - step).wait()

        @pl.when(chip + step + 1 < chips)
        def _():
            for i in range(count):
                self.across(i, step + 1).wait()


def line_scratch(arrays, chips):
    count = len(arrays)
    return (
        [pltpu.VMEM(a.shape, a.dtype) for a in arrays if a is not None]
        + [pltpu.SemaphoreType.DMA((count,))]
        + [pltpu.SemaphoreType.DMA((count, chips - 1)) for unused in range(4)]
        + [pltpu.SemaphoreType.DMA((count, chips)) for unused in range(2)]
    )


def gather_kernel(dense, line, resumed, steps, fsdp, chips, *refs):
    count = dense + line + resumed
    ins, outs, scratch = refs[:count], refs[count : 2 * count], refs[2 * count :]
    ctx, me, chip, core, sibling = place()
    greet(chips, peers_of(me, fsdp) if dense else [], line > 0)
    split = dense + line
    if dense:
        own, scratch = scratch[: dense + 5], scratch[dense + 5 :]
        first = DenseGather(
            ins[:dense], outs[:dense], (own[:dense],) + tuple(own[dense:]), fsdp
        )
        first.start()
    if line:
        own, scratch = scratch[: line + 7], scratch[line + 7 :]
        second = LineGather(ins[dense:split], outs[dense:split], own, chips)
        for step in range(steps):
            second.send(step)
            if step == 0:
                second.own()
            second.receive(step)
            if step == 0:
                second.turn_own()
    if resumed:
        third = LineGather([None], outs[split:], scratch, chips)
        third.send(chips - 2)
        third.receive(chips - 2)
    if dense:
        first.finish()
    if line:
        second.finish_own()
        for step in range(steps):
            second.finish(step)
    if resumed:
        third.finish(chips - 2)


def gather(dense, line, steps, fsdp, chips, collective_id, resumed=()):
    arrays = list(dense) + list(line) + list(resumed)
    count = len(arrays)
    scratch = (dense_scratch(dense, fsdp) if dense else []) + (
        line_scratch(line, chips) if line else []
    )
    if resumed:
        scratch = scratch + line_scratch([None], chips)
    return pl.pallas_call(
        functools.partial(
            gather_kernel, len(dense), len(line), len(resumed), steps, fsdp, chips
        ),
        out_shape=[jax.ShapeDtypeStruct((fsdp * a.shape[0],) + a.shape[1:], a.dtype) for a in dense]
        + [jax.ShapeDtypeStruct((2, chips) + a.shape, a.dtype) for a in line]
        + [jax.ShapeDtypeStruct(a.shape, a.dtype) for a in resumed],
        in_specs=[pl.BlockSpec(memory_space=pl.ANY)] * count,
        out_specs=[pl.BlockSpec(memory_space=pl.ANY)] * count,
        scratch_shapes=scratch,
        input_output_aliases={count - 1: count - 1} if resumed else {},
        compiler_params=pltpu.CompilerParams(
            collective_id=collective_id, has_side_effects=True, vmem_limit_bytes=VMEM_BYTES
        ),
        name="gather",
    )(*arrays)


def add(*parts):
    total = parts[0].astype(F32)
    for part in parts[1:]:
        total = total + part.astype(F32)
    return total


def add_into(target, parts):
    rows = target.shape[0]
    tile = 32 if rows % 32 == 0 else 16

    def some(t, carry):
        part = pl.ds(pl.multiple_of(t * tile, tile), tile)
        target[part, :] = add(*[ref[part, :] for ref in parts]).astype(target.dtype)
        return carry

    lax.fori_loop(0, rows // tile, some, 0)


class LineSum:
    def __init__(self, chips, held, keep, got, sems):
        self.chips, self.held, self.keep, self.got = chips, held, keep, got
        self.sems = sems
        self.ctx, self.me, self.chip, core, sibling = place()

    def right(self, step):
        return remote(
            self.keep(self.chips - 1 - step),
            self.got.at[step - self.chip],
            self.sems[0].at[step],
            self.sems[1].at[step],
            (self.ctx + 2, self.me),
        )

    def from_left(self, step):
        slot = step + 1 - self.chip
        pltpu.make_async_remote_copy(
            src_ref=self.keep(self.chips - 1 - step),
            dst_ref=self.got.at[slot],
            send_sem=self.sems[0].at[step],
            recv_sem=self.sems[1].at[step],
            device_id=(self.ctx - 2, self.me),
            device_id_type=MESH,
        ).wait_recv()
        return self.got.at[slot]

    def from_right(self, step):
        slot = step + 2
        self.left(step).wait_recv()
        return self.got.at[slot]

    def left(self, step):
        return remote(
            self.keep(step + 1),
            self.got.at[step + 2],
            self.sems[2].at[step],
            self.sems[3].at[step],
            (self.ctx - 2, self.me),
        )

    def step(self, step):
        chip, chips = self.chip, self.chips
        far_right, far_left = chips - 1 - step, step + 1

        @pl.when(chip <= step)
        def _():
            parts = self.held(far_right)
            if step == 0:
                add_into(self.keep(far_right), parts())
            else:

                @pl.when(chip == 0)
                def _():
                    add_into(self.keep(far_right), parts())

                @pl.when(chip >= 1)
                def _():
                    add_into(self.keep(far_right), [self.from_left(step - 1)] + parts())

            self.right(step).start()

        @pl.when(chip >= chips - 1 - step)
        def _():
            parts = self.held(far_left)
            if step == 0:
                add_into(self.keep(far_left), parts())
            else:

                @pl.when(chip == chips - 1)
                def _():
                    add_into(self.keep(far_left), parts())

                @pl.when(chip < chips - 1)
                def _():
                    add_into(self.keep(far_left), [self.from_right(step - 1)] + parts())

            self.left(step).start()

    def total(self, target):
        chip, chips, last = self.chip, self.chips, self.chips - 2
        parts = self.held(0)

        @pl.when(chip == 0)
        def _():
            add_into(target, [self.from_right(last)] + parts())

        @pl.when(chip == chips - 1)
        def _():
            add_into(target, [self.from_left(last)] + parts())

        @pl.when((chip >= 1) & (chip < chips - 1))
        def _():
            add_into(target, [self.from_right(last), self.from_left(last)] + parts())

    def finish(self):
        for step in range(self.chips - 1):

            @pl.when(self.chip <= step)
            def _():
                self.right(step).wait_send()

            @pl.when(self.chip >= self.chips - 1 - step)
            def _():
                self.left(step).wait_send()


def line_reduce_kernel(
    chips, mine_ref, other_ref, out_ref, pair, got, ps, pr, s0, s1, s2, s3
):
    ctx, me, chip, core, sibling = place()
    greet(chips, [], True)
    swaps = [
        remote(other_ref.at[r], pair.at[r], ps.at[r], pr.at[r], (sibling, me))
        for r in range(chips)
    ]
    order = []
    for step in range(chips - 1):
        for r in (chips - 1 - step, step + 1):
            if r not in order:
                order.append(r)
    for r in order + [0]:
        swaps[r].start()

    def held(r):
        swaps[r].wait_recv()
        return lambda: [mine_ref.at[r], pair.at[r]]

    line = LineSum(chips, held, lambda r: pair.at[r], got, (s0, s1, s2, s3))
    for step in range(chips - 1):
        line.step(step)
    line.total(out_ref)
    line.finish()
    for swap in swaps:
        swap.wait_send()


def line_reduce_now(mine, other, chips, collective_id):
    unused, rows, width = mine.shape
    vmem = pl.BlockSpec(memory_space=pltpu.VMEM)
    return pl.pallas_call(
        functools.partial(line_reduce_kernel, chips),
        out_shape=jax.ShapeDtypeStruct((rows, width), F32),
        in_specs=[vmem, vmem],
        out_specs=vmem,
        scratch_shapes=[pltpu.VMEM((chips, rows, width), BF16)]
        + [pltpu.VMEM((chips + 1, rows, width), BF16)]
        + [pltpu.SemaphoreType.DMA((chips,)) for unused in range(2)]
        + [pltpu.SemaphoreType.DMA((chips - 1,)) for unused in range(4)],
        compiler_params=pltpu.CompilerParams(
            collective_id=collective_id, has_side_effects=True, vmem_limit_bytes=VMEM_BYTES
        ),
        name="line_reduce",
    )(mine, other)


DENSE_BUFFERS = 5
DENSE_SEMS = 14


class DenseSum:
    def __init__(self, local, out, buffers, sems, fsdp, chips):
        self.local, self.out = local, out
        self.pair, self.cross, self.sums, got, self.spread = buffers
        self.sems = sems
        self.chips = chips
        self.ctx, self.me, self.chip, self.core, self.sibling = place()
        self.owners = peers_of(self.me, fsdp) + [self.me]
        self.cut = out.shape[2] // chips
        self.line = LineSum(
            chips,
            lambda r: lambda: [self.keep_ref(r)],
            lambda r: self.keep_ref(r),
            got,
            sems[4:8],
        )

    def keep_ref(self, r):
        return self.sums.at[:, self.columns(r)]

    def columns(self, r):
        owner = lax.rem(self.chip + r, self.chips)
        return pl.ds(pl.multiple_of(owner * self.cut, LANES), self.cut)

    def swap(self, j):
        return remote(
            self.local.at[self.owners[j], 1 - self.core],
            self.pair.at[j],
            self.sems[0].at[j],
            self.sems[1].at[j],
            (self.sibling, self.me),
        )

    def crossing(self, j):
        return remote(
            self.pair.at[j],
            self.cross.at[j],
            self.sems[2].at[j],
            self.sems[3].at[j],
            (self.ctx, self.owners[j]),
        )

    def to_right(self, step):
        return remote(
            self.spread.at[0, (self.chips - step) % self.chips],
            self.spread.at[0, self.chips - 1 - step],
            self.sems[8].at[step],
            self.sems[9].at[step],
            (self.ctx + 2, self.me),
        )

    def to_left(self, step):
        return remote(
            self.spread.at[0, step],
            self.spread.at[0, step + 1],
            self.sems[10].at[step],
            self.sems[11].at[step],
            (self.ctx - 2, self.me),
        )

    def across(self, slot):
        return remote(
            self.spread.at[0, slot],
            self.spread.at[1, slot],
            self.sems[12].at[slot],
            self.sems[13].at[slot],
            (self.sibling, self.me),
        )

    def start(self):
        for j in range(len(self.owners)):
            self.swap(j).start()

    def cross_over(self):
        for j, owner in enumerate(self.owners):
            self.swap(j).wait_recv()
            add_into(self.pair.at[j], [self.local.at[owner, self.core], self.pair.at[j]])
            if j < len(self.owners) - 1:
                self.crossing(j).start()

    def stages(self):
        chip, chips = self.chip, self.chips

        def open_up():
            for j in range(len(self.owners) - 1):
                self.crossing(j).wait_recv()
            add_into(
                self.sums,
                [self.cross.at[j] for j in range(len(self.owners) - 1)]
                + [self.pair.at[len(self.owners) - 1]],
            )
            self.line.step(0)

        def summed():
            self.line.total(self.spread.at[0, 0])
            hand_on(0)

        def hand_on(step):
            @pl.when((chip + 1 < chips) & (chip >= step))
            def _():
                self.to_right(step).start()

            @pl.when((chip >= 1) & (chip + step < chips))
            def _():
                self.to_left(step).start()

            if step == 0:
                self.across(0).start()

        def take(step):
            @pl.when(chip >= step + 1)
            def _():
                self.to_right(step).wait_recv()
                self.across(chips - 1 - step).start()

            @pl.when(chip + step + 1 < chips)
            def _():
                self.to_left(step).wait_recv()
                self.across(step + 1).start()

        def pass_on(step):
            def run():
                take(step - 1)
                hand_on(step)

            return run

        def line_step(step):
            return lambda: self.line.step(step)

        return (
            [open_up]
            + [line_step(step) for step in range(1, chips - 1)]
            + [summed]
            + [pass_on(step) for step in range(1, chips - 1)]
            + [lambda: take(chips - 2)]
        )

    def finish(self):
        chip, chips = self.chip, self.chips
        for r in range(chips):
            self.out[self.core, :, self.columns(r)] = self.spread[0, r]
        for r in range(chips):
            self.across(r).wait()
            self.out[1 - self.core, :, self.columns(r)] = self.spread[1, r]
        for step in range(chips - 1):

            @pl.when((chip + 1 < chips) & (chip >= step))
            def _():
                self.to_right(step).wait_send()

            @pl.when((chip >= 1) & (chip + step < chips))
            def _():
                self.to_left(step).wait_send()

        self.line.finish()
        for j in range(len(self.owners) - 1):
            self.crossing(j).wait_send()
        for j in range(len(self.owners)):
            self.swap(j).wait_send()


def dense_reduce_kernel(fsdp, chips, cuts, *refs):
    count = len(cuts)
    arrays = max(cut[0] for cut in cuts) + 1
    ins, outs, rest = refs[:arrays], refs[arrays : 2 * arrays], refs[2 * arrays :]
    ctx, me, chip, core, sibling = place()
    greet(chips, peers_of(me, fsdp), True)
    sums = []
    for i, (which, start, size) in enumerate(cuts):
        buffers = rest[i * DENSE_BUFFERS : (i + 1) * DENSE_BUFFERS]
        sems = rest[count * DENSE_BUFFERS + i * DENSE_SEMS :][:DENSE_SEMS]
        sums.append(
            DenseSum(
                ins[which].at[:, :, :, pl.ds(start, size)],
                outs[which].at[:, :, pl.ds(start, size)],
                buffers,
                sems,
                fsdp,
                chips,
            )
        )
    for one in sums:
        one.start()
    for one in sums:
        one.cross_over()
    stages = [one.stages() for one in sums]
    lag = chips - 1
    for tick in range(len(stages[0]) + lag * (count - 1)):
        for i in range(count):
            if 0 <= tick - lag * i < len(stages[i]):
                stages[i][tick - lag * i]()
    for one in sums:
        one.finish()


def dense_reduce(arrays, piece, fsdp, chips, collective_id):
    vmem = pl.BlockSpec(memory_space=pltpu.VMEM)
    cuts, buffers = [], []
    for i, a in enumerate(arrays):
        rows, width = a.shape[2:]
        for start in range(0, width, piece):
            size = min(piece, width - start)
            cut = size // chips
            cuts.append((i, start, size))
            buffers += [
                pltpu.VMEM((fsdp, rows, size), BF16),
                pltpu.VMEM((fsdp - 1, rows, size), BF16),
                pltpu.VMEM((rows, size), BF16),
                pltpu.VMEM((chips + 1, rows, cut), BF16),
                pltpu.VMEM((2, chips, rows, cut), BF16),
            ]
    sems = (
        [pltpu.SemaphoreType.DMA((fsdp,)) for unused in range(2)]
        + [pltpu.SemaphoreType.DMA((fsdp - 1,)) for unused in range(2)]
        + [pltpu.SemaphoreType.DMA((chips - 1,)) for unused in range(8)]
        + [pltpu.SemaphoreType.DMA((chips,)) for unused in range(2)]
    )
    return pl.pallas_call(
        functools.partial(dense_reduce_kernel, fsdp, chips, tuple(cuts)),
        out_shape=[jax.ShapeDtypeStruct(a.shape[1:], BF16) for a in arrays],
        in_specs=[vmem] * len(arrays),
        out_specs=[vmem] * len(arrays),
        scratch_shapes=buffers + sems * len(cuts),
        compiler_params=pltpu.CompilerParams(
            collective_id=collective_id, has_side_effects=True, vmem_limit_bytes=VMEM_BYTES
        ),
        name="dense_reduce",
    )(*arrays)


def after(value, *others):
    return lax.optimization_barrier((value,) + others)[0]


def attention_kernel(
    scale, q_ref, k_ref, v_ref, oq_ref, pq_ref, ok_ref, out_ref, lse_ref, bias, scores
):
    keys = k_ref.shape[0]
    tiles = keys // KEY_TILE
    rows = q_ref.shape[0]

    @pl.when(pl.program_id(0) == 0)
    def _():
        def fill(t, carry):
            tile = pl.ds(pl.multiple_of(t * KEY_TILE, KEY_TILE), KEY_TILE)
            gap = oq_ref[...] - ok_ref[:, tile]
            bias[:, tile] = jnp.where((gap >= 0) & (gap <= pq_ref[...]), 0.0, MASKED)
            return carry

        lax.fori_loop(0, tiles, fill, 0)

    query = q_ref[...]

    def score(t, top):
        tile = pl.ds(pl.multiple_of(t * KEY_TILE, KEY_TILE), KEY_TILE)
        raw = dot(query, k_ref[tile, :], NT) * (scale * LOG2E) + bias[:, tile]
        scores[:, tile] = raw
        for part in range(KEY_TILE // LANES):
            top = jnp.maximum(top, raw[:, part * LANES : (part + 1) * LANES])
        return top

    top = lax.fori_loop(0, tiles, score, jnp.full((rows, LANES), MASKED, F32))
    top = jnp.max(top, axis=1, keepdims=True)

    def weigh(t, carry):
        total, acc = carry
        tile = pl.ds(pl.multiple_of(t * KEY_TILE, KEY_TILE), KEY_TILE)
        probs = jnp.exp2(scores[:, tile] - top)
        for part in range(KEY_TILE // LANES):
            total = total + probs[:, part * LANES : (part + 1) * LANES]
        acc = acc + dot(probs.astype(BF16), v_ref[tile, :], NN)
        return total, acc

    total, acc = lax.fori_loop(
        0, tiles, weigh, (jnp.zeros((rows, LANES), F32), jnp.zeros((rows, HEAD_SIZE), F32))
    )
    total = jnp.sum(total, axis=1, keepdims=True)
    out_ref[...] = (acc / total).astype(BF16)
    lse = jnp.broadcast_to(top + jnp.log2(total), (rows, LANES))
    lse_ref[0] = lse.T[:1, :]


def attention(queries, kv, order_mine, pos_mine, order_keys, group):
    rows = queries.shape[0]
    keys = kv.shape[0]
    per_group = QUERY_HEADS // KVH
    return pl.pallas_call(
        functools.partial(attention_kernel, HEAD_SIZE ** (-0.5)),
        grid=(per_group,),
        out_shape=[
            jax.ShapeDtypeStruct((rows, per_group * HEAD_SIZE), BF16),
            jax.ShapeDtypeStruct((per_group, 1, rows), F32),
        ],
        in_specs=[
            pl.BlockSpec((rows, HEAD_SIZE), lambda h: (0, group * per_group + h)),
            pl.BlockSpec((keys, HEAD_SIZE), lambda h: (0, group)),
            pl.BlockSpec((keys, HEAD_SIZE), lambda h: (0, KVH + group)),
            pl.BlockSpec((rows, 1), lambda h: (0, 0)),
            pl.BlockSpec((rows, 1), lambda h: (0, 0)),
            pl.BlockSpec((1, keys), lambda h: (0, 0)),
        ],
        out_specs=[
            pl.BlockSpec((rows, HEAD_SIZE), lambda h: (0, h)),
            pl.BlockSpec((1, 1, rows), lambda h: (h, 0, 0)),
        ],
        scratch_shapes=[pltpu.VMEM((rows, keys), F32), pltpu.VMEM((rows, keys), F32)],
        compiler_params=pltpu.CompilerParams(vmem_limit_bytes=VMEM_BYTES),
        cost_estimate=pl.CostEstimate(
            flops=4 * rows * keys * HEAD_SIZE * per_group,
            bytes_accessed=4 * rows * per_group * HEAD_SIZE + 4 * keys * HEAD_SIZE,
            transcendentals=rows * keys * per_group,
        ),
        name="attention",
    )(queries, kv, kv, order_mine[:, None], pos_mine[:, None], order_keys[None, :])


def attention_back_kernel(
    scale,
    per_group,
    q_ref,
    k_ref,
    v_ref,
    o_ref,
    do_ref,
    lse_ref,
    oq_ref,
    pq_ref,
    ok_ref,
    dq_ref,
    dk_ref,
    dv_ref,
    bias,
    dk_acc,
    dv_acc,
):
    keys = k_ref.shape[0]
    tiles = keys // KEY_TILE
    rows = q_ref.shape[0]
    head = pl.program_id(0)

    @pl.when(head == 0)
    def _():
        def fill(t, carry):
            tile = pl.ds(pl.multiple_of(t * KEY_TILE, KEY_TILE), KEY_TILE)
            gap = oq_ref[...] - ok_ref[tile, :]
            bias[tile, :] = jnp.where((gap >= 0) & (gap <= pq_ref[...]), 0.0, MASKED)
            return carry

        lax.fori_loop(0, tiles, fill, 0)

    @pl.when(lax.rem(head, per_group) == 0)
    def _():
        dk_acc[...] = jnp.zeros_like(dk_acc)
        dv_acc[...] = jnp.zeros_like(dv_acc)

    query = q_ref[...]
    grad = do_ref[...]
    lse = lse_ref[0]
    product = grad.astype(F32) * o_ref[...].astype(F32)
    delta = jnp.sum(product.T, axis=0, keepdims=True)

    def step(t, acc):
        tile = pl.ds(pl.multiple_of(t * KEY_TILE, KEY_TILE), KEY_TILE)
        key = k_ref[tile, :]
        raw = dot(key, query, NT) * (scale * LOG2E) + bias[tile, :]
        probs = jnp.exp2(raw - lse)
        prob_grad = dot(v_ref[tile, :], grad, NT)
        score_grad = (probs * (prob_grad - delta)).astype(BF16)
        dv_acc[tile, :] += dot(probs.astype(BF16), grad, NN)
        dk_acc[tile, :] += dot(score_grad, query, NN)
        return acc + dot(score_grad, key, TN)

    acc = lax.fori_loop(0, tiles, step, jnp.zeros((rows, HEAD_SIZE), F32))
    dq_ref[...] = acc * scale

    @pl.when(lax.rem(head, per_group) == per_group - 1)
    def _():
        dk_ref[...] = (dk_acc[...] * scale).astype(BF16)
        dv_ref[...] = dv_acc[...].astype(BF16)


def attention_back(
    queries, kv, attended, attended_grad, lse, order_mine, pos_mine, order_keys, group
):
    rows = queries.shape[0]
    keys = kv.shape[0]
    per_group = QUERY_HEADS // KVH
    head_rows = pl.BlockSpec((rows, HEAD_SIZE), lambda h: (0, group * per_group + h))
    group_rows = pl.BlockSpec((rows, HEAD_SIZE), lambda h: (0, h))
    return pl.pallas_call(
        functools.partial(attention_back_kernel, HEAD_SIZE ** (-0.5), per_group),
        grid=(per_group,),
        out_shape=[
            jax.ShapeDtypeStruct((rows, per_group * HEAD_SIZE), F32),
            jax.ShapeDtypeStruct((keys, HEAD_SIZE), BF16),
            jax.ShapeDtypeStruct((keys, HEAD_SIZE), BF16),
        ],
        in_specs=[
            head_rows,
            pl.BlockSpec((keys, HEAD_SIZE), lambda h: (0, group)),
            pl.BlockSpec((keys, HEAD_SIZE), lambda h: (0, KVH + group)),
            group_rows,
            head_rows,
            pl.BlockSpec((1, 1, rows), lambda h: (h, 0, 0)),
            pl.BlockSpec((1, rows), lambda h: (0, 0)),
            pl.BlockSpec((1, rows), lambda h: (0, 0)),
            pl.BlockSpec((keys, 1), lambda h: (0, 0)),
        ],
        out_specs=[
            group_rows,
            pl.BlockSpec((keys, HEAD_SIZE), lambda h: (0, 0)),
            pl.BlockSpec((keys, HEAD_SIZE), lambda h: (0, 0)),
        ],
        scratch_shapes=[
            pltpu.VMEM((keys, rows), F32),
            pltpu.VMEM((keys, HEAD_SIZE), F32),
            pltpu.VMEM((keys, HEAD_SIZE), F32),
        ],
        compiler_params=pltpu.CompilerParams(vmem_limit_bytes=VMEM_BYTES),
        cost_estimate=pl.CostEstimate(
            flops=10 * rows * keys * HEAD_SIZE * per_group,
            bytes_accessed=10 * rows * per_group * HEAD_SIZE + 8 * keys * HEAD_SIZE,
            transcendentals=rows * keys * per_group,
        ),
        name="attention_back",
    )(
        queries,
        kv,
        kv,
        attended,
        attended_grad,
        lse,
        order_mine[None, :],
        pos_mine[None, :],
        order_keys[:, None],
    )


def chunk_order(chip, i, chips):
    right_half = lax.div(2 * chip, chips)
    near = chip + right_half * (chips - 1 - 2 * chip)
    alone = chips - 1 - 2 * near
    paired = lax.div(i - alone + chips, chips)
    turn = (i - alone) * paired
    odd = lax.rem(turn, 2)
    pair = lax.div(turn, 2)
    distance = (1 - paired) * (chips - 1 - near - i) + paired * (
        (1 - odd) * (near - pair) + odd * (chips - near + pair)
    )
    return lax.rem(distance + right_half * (chips - 2 * distance), chips)


def experts_kernel(
    capacity,
    local_experts,
    expert_count,
    chips,
    fsdp,
    per,
    hidden_ref,
    grad_ref,
    table_ref,
    weight_ref,
    gate_ref,
    up_ref,
    down_ref,
    returned_ref,
    out_ref,
    gate_grad_ref,
    up_grad_ref,
    down_grad_ref,
    x_ref,
    pg_ref,
    inner_ref,
    da_ref,
    db_ref,
    gate_v,
    up_v,
    down_v,
    hidden_v,
    grad_v,
    out_v,
    x_v,
    pg_v,
    g_v,
    inner_v,
    da_v,
    db_v,
    mine_v,
    other_v,
    pair,
    got,
    stage_tall,
    weight_sem,
    load_sem,
    out_sem,
    save_sem,
    swap_send,
    swap_recv,
    right_send,
    right_recv,
    left_send,
    left_recv,
    stage_sem,
):
    ctx, me, chip, core, sibling = place()
    tokens = hidden_v.shape[1]
    width = hidden_v.shape[2]
    slots = x_v.shape[1]
    slot_rows = slots // 2
    units = inner_v.shape[2]
    total_rows = x_ref.shape[1]
    first = ctx * local_experts

    weights_in = [
        pltpu.make_async_copy(src, dst, weight_sem.at[k])
        for k, (src, dst) in enumerate(
            ((gate_ref, gate_v), (up_ref, up_v), (down_ref, down_v))
        )
    ]

    def load(i):
        r = chunk_order(chip, i, chips)
        return [
            pltpu.make_async_copy(hidden_ref.at[:, r], hidden_v, load_sem.at[0]),
            pltpu.make_async_copy(grad_ref.at[:, r], grad_v, load_sem.at[1]),
        ]

    def saves(i):
        rows = pl.ds(i * slots, slots)
        return [
            pltpu.make_async_copy(src, dst.at[:, rows], save_sem.at[k])
            for k, (src, dst) in enumerate(
                ((x_v, x_ref), (pg_v, pg_ref), (inner_v, inner_ref), (da_v, da_ref), (db_v, db_ref))
            )
        ]

    def out_copy(i):
        owner = lax.rem(chip + chunk_order(chip, i, chips), chips)
        return pltpu.make_async_copy(out_v, out_ref.at[owner], out_sem)

    def swap(i):
        r = chunk_order(chip, i, chips)
        return remote(
            other_v.at[lax.rem(i, 2)],
            pair.at[r],
            swap_send.at[r],
            swap_recv.at[r],
            (sibling, me),
        )

    def join(i):
        r = chunk_order(chip, i, chips)
        swap(i).wait_recv()
        add_into(pair.at[r], [pair.at[r], mine_v.at[lax.rem(i, 2)]])

    line = LineSum(
        chips,
        lambda r: lambda: [pair.at[r]],
        lambda r: pair.at[r],
        got,
        (right_send, right_recv, left_send, left_recv),
    )

    for copy in load(0) + weights_in:
        copy.start()
    greet(chips, [], True)

    slot = lax.broadcasted_iota(jnp.int32, (slot_rows, tokens), 0).astype(F32) + 1.0
    slot = jnp.where(slot <= capacity, slot, -1.0)
    lane = lax.broadcasted_iota(jnp.int32, (slots, LANES), 1)

    def chunk(i, carry):
        r = chunk_order(chip, i, chips)
        for copy in load(i):
            copy.wait()

        @pl.when(i >= 1)
        def _():
            for copy in saves(i - 1):
                copy.wait()

        picks = [[], []]
        weight_rows = []
        for e in range(local_experts):
            rows_w = []
            for q in range(2):
                hit = slot == table_ref[q, r, pl.ds(first + e, 1), :]
                pick = jnp.where(hit, 1.0, 0.0).astype(BF16)
                weight = weight_ref[q, r, pl.ds(first + e, 1), :]
                w = jnp.sum(jnp.where(hit, weight, 0.0), axis=1, keepdims=True)
                rows = pl.ds(q * slot_rows, slot_rows)
                x_v[e, rows, :] = dot(pick, hidden_v[q], NN).astype(BF16)
                g = dot(pick, grad_v[q], NN)
                g_v[e, rows, :] = g.astype(BF16)
                pg_v[e, rows, :] = (w * g).astype(BF16)
                picks[q].append(pick)
                rows_w.append(w)
            weight_rows.append(jnp.concatenate(rows_w, axis=0))

        @pl.when(i + 1 < chips)
        def _():
            for copy in load(i + 1):
                copy.start()

        @pl.when(i == 0)
        def _():
            for copy in weights_in:
                copy.wait()

        outs = [[], []]
        backs = [[], []]
        for e in range(local_experts):
            x = x_v[e]
            pair_grad = pg_v[e]
            w = weight_rows[e]
            gate = gate_v[e * width : (e + 1) * width, :]
            up = up_v[e * width : (e + 1) * width, :]
            down = down_v[e * units : (e + 1) * units, :]
            gate_pre = dot(x, gate, NN)
            up_pre = dot(x, up, NN)
            sig = jax.nn.sigmoid(gate_pre)
            silu = gate_pre * sig
            inner = (silu * up_pre).astype(BF16)
            inner_v[e] = inner
            expert_out = dot(inner, down, NN).astype(BF16).astype(F32)
            gate_grad = jnp.sum(expert_out * g_v[e].astype(F32), axis=1, keepdims=True)
            inner_grad = dot(pair_grad, down, NT)
            da = (inner_grad * up_pre * sig * (1.0 + gate_pre * (1.0 - sig))).astype(BF16)
            db = (inner_grad * silu).astype(BF16)
            da_v[e] = da
            db_v[e] = db
            row_grad = (dot(da, gate, NT) + dot(db, up, NT)).astype(BF16)
            high = gate_grad.astype(BF16).astype(F32)
            extra = jnp.where(lane == first + e, high, 0.0) + jnp.where(
                lane == expert_count + first + e, gate_grad - high, 0.0
            )
            back = jnp.concatenate([row_grad, extra.astype(BF16)], axis=1)
            out_rows = (w * expert_out).astype(BF16)
            for q in range(2):
                part = slice(q * slot_rows, (q + 1) * slot_rows)
                outs[q].append(out_rows[part])
                backs[q].append(back[part])

        for copy in saves(i):
            copy.start()

        @pl.when(i >= 1)
        def _():
            out_copy(i - 1).wait()

        @pl.when(i >= 2)
        def _():
            swap(i - 2).wait_send()

        for q in range(2):
            pick = jnp.concatenate(picks[q], axis=0)
            held = other_v if q else mine_v
            held[lax.rem(i, 2)] = dot(pick, jnp.concatenate(backs[q], axis=0), TN).astype(BF16)
            if q:
                swap(i).start()
        for q in range(2):
            pick = jnp.concatenate(picks[q], axis=0)
            out_v[1 - core if q else core] = dot(
                pick, jnp.concatenate(outs[q], axis=0), TN
            ).astype(BF16)
        out_copy(i).start()

        @pl.when(i == 0)
        def _():
            join(0)
            line.step(0)

        @pl.when(i >= 2)
        def _():
            join(i - 1)

        for step in range(1, chips - 1):
            if 2 * step < chips:

                @pl.when(i == 2 * step)
                def _():
                    line.step(step)

        return carry

    lax.fori_loop(0, chips, chunk, 0)
    join(chips - 1)
    for copy in saves(chips - 1):
        copy.wait()
    out_copy(chips - 1).wait()
    for i in range(max(0, chips - 2), chips):
        swap(i).wait_send()

    shard = width // fsdp
    blocks = fsdp // per
    block = per * shard

    def fetch(copies):
        copies = [
            pltpu.make_async_copy(src, dst, save_sem.at[k])
            for k, (src, dst) in enumerate(copies)
        ]
        for copy in copies:
            copy.start()
        for copy in copies:
            copy.wait()

    def products(e, staged, target, product):
        def write(f):
            return [
                pltpu.make_async_copy(
                    staged(lax.rem(f, 2), p),
                    target.at[f * per + p, e],
                    stage_sem.at[lax.rem(f, 2), p],
                )
                for p in range(per)
            ]

        def one(f, carry):
            @pl.when(f >= 2)
            def _():
                for copy in write(f - 2):
                    copy.wait()

            product(f)
            for copy in write(f):
                copy.start()
            return carry

        lax.fori_loop(0, blocks, one, 0)
        for f in range(max(0, blocks - 2), blocks):
            for copy in write(f):
                copy.wait()

    def stage_wide(slot, p):
        return hidden_v.at[slot, pl.ds(p * shard, shard), pl.ds(0, units)]

    def wide(e, held, target):
        def product(f):
            columns = pl.ds(pl.multiple_of(f * block, LANES), block)
            value = dot(
                down_v[:total_rows, columns],
                held[e * total_rows : (e + 1) * total_rows, :],
                TN,
            ).astype(BF16)
            for p in range(per):
                stage_wide(lax.rem(f, 2), p)[...] = value[p * shard : (p + 1) * shard, :]

        products(e, stage_wide, target, product)

    def tall(e, target):
        def product(f):
            columns = pl.ds(pl.multiple_of(f * block, LANES), block)
            value = dot(
                gate_v[e * total_rows : (e + 1) * total_rows, :],
                down_v[:total_rows, columns],
                TN,
            ).astype(BF16)
            for p in range(per):
                stage_tall[lax.rem(f, 2), p] = value[:, p * shard : (p + 1) * shard]

        products(e, lambda slot, p: stage_tall.at[slot, p], target, product)

    work = []
    for e in range(local_experts):
        copies = [(x_ref.at[e], down_v.at[:total_rows])]
        if e == 0:
            for k in range(local_experts):
                held = pl.ds(k * total_rows, total_rows)
                copies += [(da_ref.at[k], gate_v.at[held]), (db_ref.at[k], up_v.at[held])]
        work.append(lambda copies=copies: fetch(copies))
        work.append(lambda e=e: wide(e, gate_v, gate_grad_ref))
        work.append(lambda e=e: wide(e, up_v, up_grad_ref))
    for e in range(local_experts):
        copies = [(pg_ref.at[e], down_v.at[:total_rows])]
        if e == 0:
            for k in range(local_experts):
                copies.append((inner_ref.at[k], gate_v.at[pl.ds(k * total_rows, total_rows)]))
        work.append(lambda copies=copies: fetch(copies))
        work.append(lambda e=e: tall(e, down_grad_ref))
    late = [step for step in range(1, chips - 1) if 2 * step >= chips]
    for n, task in enumerate(work):
        task()
        if n == LINE_TASK or (n > LINE_TASK and late):
            if late:
                line.step(late.pop(0))
    for step in late:
        line.step(step)

    line.total(returned_ref)
    line.finish()


def experts_pass(
    hidden, grad, table, weights, gate, up, down, capacity, expert_count, fsdp, collective_id
):
    unused, chips, tokens, width = grad.shape
    local_experts, unused, units = gate.shape
    slots = 2 * SLOT_STEP * -(-capacity // SLOT_STEP)
    total = chips * slots
    shard = width // fsdp
    per = 1 if shard % LANES == 0 else 2
    wide = width + LANES
    anywhere = pl.BlockSpec(memory_space=pl.ANY)
    vmem = pl.BlockSpec(memory_space=pltpu.VMEM)
    flops = 2 * total * width * units * local_experts * 9 + 8 * total * tokens * width
    saved = [(local_experts, total, width)] * 2 + [(local_experts, total, units)] * 3
    held = [(local_experts, slots, width)] * 3 + [(local_experts, slots, units)] * 3
    outs = pl.pallas_call(
        functools.partial(
            experts_kernel, capacity, local_experts, expert_count, chips, fsdp, per
        ),
        out_shape=[
            jax.ShapeDtypeStruct((tokens, wide), BF16),
            jax.ShapeDtypeStruct((chips, 2, tokens, width), BF16),
            jax.ShapeDtypeStruct((fsdp, local_experts, shard, units), BF16),
            jax.ShapeDtypeStruct((fsdp, local_experts, shard, units), BF16),
            jax.ShapeDtypeStruct((fsdp, local_experts, units, shard), BF16),
        ]
        + [jax.ShapeDtypeStruct(shape, BF16) for shape in saved],
        in_specs=[anywhere, anywhere, vmem, vmem, anywhere, anywhere, anywhere],
        out_specs=[vmem] + [anywhere] * 9,
        scratch_shapes=[
            pltpu.VMEM((local_experts * width, units), BF16),
            pltpu.VMEM((local_experts * width, units), BF16),
            pltpu.VMEM((local_experts * units, width), BF16),
            pltpu.VMEM((2, tokens, width), BF16),
            pltpu.VMEM((2, tokens, width), BF16),
            pltpu.VMEM((2, tokens, width), BF16),
        ]
        + [pltpu.VMEM(shape, BF16) for shape in held]
        + [
            pltpu.VMEM((2, tokens, wide), BF16),
            pltpu.VMEM((2, tokens, wide), BF16),
            pltpu.VMEM((chips, tokens, wide), BF16),
            pltpu.VMEM((chips + 1, tokens, wide), BF16),
            pltpu.VMEM((2, per, units, shard), BF16),
            pltpu.SemaphoreType.DMA((3,)),
            pltpu.SemaphoreType.DMA((2,)),
            pltpu.SemaphoreType.DMA,
            pltpu.SemaphoreType.DMA((5,)),
            pltpu.SemaphoreType.DMA((chips,)),
            pltpu.SemaphoreType.DMA((chips,)),
        ]
        + [pltpu.SemaphoreType.DMA((chips - 1,)) for unused in range(4)]
        + [pltpu.SemaphoreType.DMA((2, per))],
        compiler_params=pltpu.CompilerParams(
            collective_id=collective_id, has_side_effects=True, vmem_limit_bytes=EXPERT_VMEM_BYTES
        ),
        cost_estimate=pl.CostEstimate(
            flops=flops, bytes_accessed=100_000_000, transcendentals=total * units * 2
        ),
        name="experts",
    )(
        hidden,
        grad,
        table,
        weights,
        gate.reshape(local_experts * width, units),
        up.reshape(local_experts * width, units),
        down.reshape(local_experts * units, width),
    )
    return outs[:5]


def body(
    tokens,
    grad_out,
    order,
    lengths,
    routes,
    gain_one,
    gain_two,
    w_query,
    w_key,
    w_value,
    w_out,
    w_router,
    w_gate,
    w_up,
    w_down,
):
    fsdp = lax.axis_size("fsdp")
    chips = lax.axis_size("ctx") // 2
    ctx_index = lax.axis_index("ctx")
    chip = ctx_index // 2
    core = lax.rem(ctx_index, 2)
    tok_rows = tokens.shape[1]
    width = tokens.shape[2]
    top_count = routes.shape[2]
    local_experts = w_gate.shape[0]
    expert_count = local_experts * chips * 2
    capacity = 5 * tok_rows * top_count // (4 * expert_count)
    kv_width = KVH * HEAD_SIZE
    shard = gain_one.shape[0]

    small = jnp.concatenate(
        [
            w_router,
            gain_one[:, None],
            gain_two[:, None],
            jnp.zeros((shard, LANES - expert_count - 2), BF16),
        ],
        axis=1,
    )
    qkv_shard = jnp.concatenate([w_query, w_key, w_value], axis=1)
    qkv_full, small_full, grad_all = gather(
        [qkv_shard, small], [grad_out[0]], chips - 2, fsdp, chips, 0
    )

    qkv_full, w_gate, w_up, w_down = lax.optimization_barrier((qkv_full, w_gate, w_up, w_down))
    gate_full, up_full, down_full = (
        lax.all_gather(w_gate, "fsdp", axis=1, tiled=True),
        lax.all_gather(w_up, "fsdp", axis=1, tiled=True),
        lax.all_gather(w_down, "fsdp", axis=2, tiled=True),
    )
    router_full = small_full[:, :expert_count]
    gain_a = small_full[:, expert_count].astype(F32)
    gain_b = small_full[:, expert_count + 1].astype(F32)

    order_row = order[0]
    start_row = ctx_index * tok_rows
    order_mine = lax.dynamic_slice_in_dim(order_row, start_row, tok_rows)
    ends = jnp.cumsum(lengths[0])
    starts = ends - lengths[0]
    past = order_mine[:, None] >= ends[None, :]
    doc_start = jnp.max(jnp.where(past, ends[None, :], starts[:1]), axis=1)
    pos_mine = order_mine - doc_start
    by_chip = jnp.roll(order_row.reshape(chips, 2, tok_rows), -chip, axis=0)
    by_chip = jnp.where(core == 0, by_chip, by_chip[:, ::-1])
    order_keys = jnp.swapaxes(by_chip, 0, 1).reshape(-1)

    route_rows = routes[0]
    route_onehot = (route_rows[:, :, None] == jnp.arange(expert_count)[None, None, :]).astype(F32)
    routed = jnp.sum(route_onehot, axis=1)
    earlier = (order_mine[None, :] < order_mine[:, None]).astype(BF16)
    ranks = jnp.dot(earlier, routed.astype(BF16), preferred_element_type=F32)
    table = jnp.where(routed > 0, jnp.minimum(ranks, capacity) + 1.0, 0.0)

    half_dim = HEAD_SIZE // 2
    freqs = ROPE_BASE ** (-2.0 * jnp.arange(half_dim).astype(F32) / HEAD_SIZE)
    angles = pos_mine.astype(F32)[:, None] * freqs[None, :]
    cosine = jnp.cos(angles)[:, None, :]
    sine = jnp.sin(angles)[:, None, :]

    inputs = tokens[0].astype(F32)
    hidden_one = rms_scale(inputs, gain_a).astype(BF16)
    pre = jnp.dot(hidden_one, qkv_full, preferred_element_type=F32)
    turned = rotate(
        pre[:, : width + kv_width].reshape(tok_rows, QUERY_HEADS + KVH, HEAD_SIZE), cosine, sine
    )
    queries = turned[:, :QUERY_HEADS].astype(BF16).reshape(tok_rows, width)
    kv_mine = jnp.concatenate(
        [
            turned[:, QUERY_HEADS:].astype(BF16).reshape(tok_rows, kv_width),
            pre[:, width + kv_width :].astype(BF16),
        ],
        axis=1,
    )
    out_full, kv_all, table_all, grad_all = gather(
        [w_out], [kv_mine, table.T], chips - 1, fsdp, chips, 1, [grad_all]
    )
    kv_all = kv_all.reshape(-1, 2 * kv_width)
    attended, lse = [], []
    for group in range(KVH):
        part, part_lse = attention(
            after(queries, *attended[-1:]), kv_all, order_mine, pos_mine, order_keys, group
        )
        attended.append(part)
        lse.append(part_lse)
    attended_parts, attended = attended, jnp.concatenate(attended, axis=1)
    middle = inputs + jnp.dot(attended, out_full, preferred_element_type=F32)
    hidden_two = rms_scale(middle, gain_b).astype(BF16)
    logits = jnp.dot(hidden_two, router_full, preferred_element_type=F32)
    chosen = jnp.where(routed > 0, logits, MASKED)
    gate_weights = jnp.where(routed > 0, jax.nn.softmax(chosen, axis=-1), 0.0)

    hidden_all, weights_all = gather([], [hidden_two, gate_weights.T], chips - 1, fsdp, chips, 2)
    returned, out_rows, gate_local, up_local, down_local = experts_pass(
        hidden_all,
        grad_all,
        table_all,
        weights_all,
        gate_full,
        up_full,
        down_full,
        capacity,
        expert_count,
        fsdp,
        5,
    )
    out_sum = lax.psum_scatter(
        out_rows.reshape(2 * chips, tok_rows, width),
        "ctx",
        scatter_dimension=0,
        tiled=True,
    )
    expert_grads = [
        lax.psum_scatter(part, "fsdp", scatter_dimension=0, tiled=True)
        for part in (gate_local, up_local, down_local)
    ]

    out_grad = grad_out[0].astype(F32)
    returned = returned.astype(F32)
    extra = returned[:, width:]
    gate_grad = extra[:, :expert_count] + extra[:, expert_count : 2 * expert_count]
    logit_grad = (
        gate_weights * (gate_grad - jnp.sum(gate_weights * gate_grad, axis=-1, keepdims=True))
    ).astype(BF16)
    router_local = jnp.einsum("td,te->de", hidden_two, logit_grad, preferred_element_type=F32)
    hidden_two_grad = returned[:, :width] + jnp.einsum(
        "te,de->td", logit_grad, router_full, preferred_element_type=F32
    )
    unused_two, norm_two_back = jax.vjp(rms_scale, middle, gain_b)
    middle_part, gain_two_local = norm_two_back(hidden_two_grad)
    middle_grad = out_grad + middle_part
    branch_grad = middle_grad.astype(BF16)
    out_local = jnp.einsum("tc,td->cd", attended, branch_grad, preferred_element_type=F32)
    attended_grad = jnp.einsum(
        "td,cd->tc", branch_grad, out_full, preferred_element_type=F32
    ).astype(BF16)

    query_grad, kv_grads = [], [None] * (2 * KVH)
    for group in range(KVH):
        parts = attention_back(
            queries,
            kv_all,
            attended_parts[group],
            after(attended_grad, *query_grad[-1:]),
            lse[group],
            order_mine,
            pos_mine,
            order_keys,
            group,
        )
        query_grad.append(parts[0])
        kv_grads[group], kv_grads[KVH + group] = parts[1:]
    kv_grads = jnp.concatenate(kv_grads, axis=1).reshape(2, chips, tok_rows, 2 * kv_width)
    kv_grad = line_reduce_now(kv_grads[0], kv_grads[1], chips, 3)
    turned_grad = rotate(
        jnp.concatenate(query_grad + [kv_grad[:, :kv_width]], axis=1).reshape(
            tok_rows, QUERY_HEADS + KVH, HEAD_SIZE
        ),
        cosine,
        -sine,
    ).reshape(tok_rows, width + kv_width)
    pre_grad = jnp.concatenate(
        [turned_grad.astype(BF16), kv_grad[:, kv_width:].astype(BF16)], axis=1
    )
    qkv_local = jnp.einsum("td,tc->dc", hidden_one, pre_grad, preferred_element_type=F32)
    hidden_one_grad = jnp.einsum("tc,dc->td", pre_grad, qkv_full, preferred_element_type=F32)
    unused_one, norm_one_back = jax.vjp(rms_scale, inputs, gain_a)
    input_part, gain_one_local = norm_one_back(hidden_one_grad)
    input_grad = (middle_grad + input_part).astype(BF16)

    def halves(local):
        local = local.astype(BF16).reshape(fsdp, 2, shard // 2, local.shape[1])
        pad = -local.shape[3] % (LANES * chips)
        return jnp.pad(local, ((0, 0), (0, 0), (0, 0), (0, pad))) if pad else local

    span = shard * expert_count // 16
    wide = LANES * chips * -(-max(span, shard) // (LANES * chips))
    small_local = jnp.stack(
        [
            jnp.pad(
                router_local.astype(BF16).reshape(fsdp, 16, span),
                ((0, 0), (0, 0), (0, wide - span)),
            ),
            jnp.pad(
                jnp.stack(
                    [gain_one_local.reshape(fsdp, shard), gain_two_local.reshape(fsdp, shard)],
                    axis=1,
                ).astype(BF16),
                ((0, 0), (0, 14), (0, wide - shard)),
            ),
        ],
        axis=1,
    )
    qkv_sum, out_proj_sum, small_sum = dense_reduce(
        [halves(qkv_local), halves(out_local), small_local], DENSE_PIECE, fsdp, chips, 4
    )
    edge = width + 2 * kv_width
    qkv_grads = qkv_sum.reshape(shard, -1)
    out_proj_grad = out_proj_sum.reshape(shard, -1)[:, :width]
    gate_grad_out, up_grad_out, down_grad_out = (
        after(part, pre_grad)[0].astype(F32) for part in expert_grads
    )
    result = middle + after(out_sum, pre_grad)[0].astype(F32)
    return (
        result.astype(BF16)[None],
        input_grad[None],
        small_sum[1, 0, :shard].astype(F32),
        small_sum[1, 1, :shard].astype(F32),
        qkv_grads[:, :width].astype(F32),
        qkv_grads[:, width : width + kv_width].astype(F32),
        qkv_grads[:, width + kv_width : edge].astype(F32),
        out_proj_grad.astype(F32),
        small_sum[0, :, :span].reshape(shard, expert_count).astype(F32),
        gate_grad_out,
        up_grad_out,
        down_grad_out,
    )


def solution(mesh):
    placed = (
        P("fsdp", "ctx", None),
        P("fsdp", "ctx", None),
        P("fsdp", None),
        P("fsdp", None),
        P("fsdp", "ctx", None),
        P("fsdp"),
        P("fsdp"),
        P("fsdp", None),
        P("fsdp", None),
        P("fsdp", None),
        P("fsdp", None),
        P("fsdp", None),
        P("ctx", "fsdp", None),
        P("ctx", "fsdp", None),
        P("ctx", None, "fsdp"),
    )
    return jax.shard_map(
        body,
        mesh=mesh,
        in_specs=placed,
        out_specs=(
            P("fsdp", "ctx", None),
            P("fsdp", "ctx", None),
            P("fsdp"),
            P("fsdp"),
            P("fsdp", None),
            P("fsdp", None),
            P("fsdp", None),
            P("fsdp", None),
            P("fsdp", None),
            P("ctx", "fsdp", None),
            P("ctx", "fsdp", None),
            P("ctx", None, "fsdp"),
        ),
        check_vma=False,
    )
```

```python
import functools

import jax
import jax.numpy as jnp
from jax import lax
from jax.experimental import pallas as pl
from jax.experimental.pallas import tpu as pltpu
from jax.sharding import PartitionSpec as P

QUERY_HEADS = 12
KVH = 2
HEAD_SIZE = 128

EPSILON = 1e-06
ROPE_BASE = 10000.0
MASKED = -1e30
LOG2E = 1.4426950408889634
LANES = 128
SLOT_STEP = 64
DENSE_PIECE = 1024
LINE_TASK = 4
KEY_TILE = 512
VMEM_BYTES = 56 * 1024 * 1024
EXPERT_VMEM_BYTES = 119 * 512 * 1024
BACK_VMEM_BYTES = 61 * 1024 * 1024
MESH = pl.DeviceIdType.MESH
F32 = jnp.float32
BF16 = jnp.bfloat16


def dot(left, right, contract):
    return lax.dot_general(left, right, (contract, ((), ())), preferred_element_type=F32)


NN = ((1,), (0,))
NT = ((1,), (1,))
TN = ((0,), (0,))


def rms_scale(value_rows, gain):
    return (
        value_rows
        * lax.rsqrt(jnp.mean(value_rows * value_rows, axis=-1, keepdims=True) + EPSILON)
        * gain
    )


def rotate(value_rows, cosine, sine):
    half_dim = value_rows.shape[-1] // 2
    first = value_rows[..., :half_dim]
    second = value_rows[..., half_dim:]
    return jnp.concatenate(
        [first * cosine - second * sine, second * cosine + first * sine], axis=-1
    )


def place():
    ctx = lax.axis_index("ctx")
    core = lax.rem(ctx, 2)
    return ctx, lax.axis_index("fsdp"), ctx // 2, core, ctx + 1 - 2 * core


def peers_of(me, fsdp):
    peers = []
    for shift in range(1, fsdp):
        peer = me
        for bit in range(fsdp.bit_length() - 1):
            if (shift >> bit) & 1:
                digit = lax.rem(me // (1 << bit), 2)
                peer = peer + (1 << bit) - (2 << bit) * digit
        peers.append(peer)
    return peers


def greet(chips, peers, line):
    ctx, me, chip, core, sibling = place()
    barrier = pltpu.get_barrier_semaphore()
    for peer in peers:
        pl.semaphore_signal(barrier, inc=1, device_id=(ctx, peer), device_id_type=MESH)
    pl.semaphore_signal(barrier, inc=1, device_id=(sibling, me), device_id_type=MESH)
    known = len(peers) + 1
    if not line:
        pl.semaphore_wait(barrier, known)
        return
    has_right = chip + 1 < chips
    has_left = chip >= 1

    @pl.when(has_right)
    def _():
        pl.semaphore_signal(barrier, inc=1, device_id=(ctx + 2, me), device_id_type=MESH)

    @pl.when(has_left)
    def _():
        pl.semaphore_signal(barrier, inc=1, device_id=(ctx - 2, me), device_id_type=MESH)

    @pl.when(has_right & has_left)
    def _():
        pl.semaphore_wait(barrier, known + 2)

    @pl.when(jnp.logical_not(has_right & has_left))
    def _():
        pl.semaphore_wait(barrier, known + 1)


class Bounce:
    def __init__(self, src, dst, buffer, sem):
        self.inward = pltpu.make_async_copy(src, buffer, sem)
        self.outward = pltpu.make_async_copy(buffer, dst, sem)

    def start(self):
        self.inward.start()

    def turn(self):
        self.inward.wait()
        self.outward.start()

    def wait(self):
        self.outward.wait()


def remote(src, dst, send_sem, recv_sem, device):
    return pltpu.make_async_remote_copy(
        src_ref=src,
        dst_ref=dst,
        send_sem=send_sem,
        recv_sem=recv_sem,
        device_id=device,
        device_id_type=MESH,
    )


class DenseGather:
    def __init__(self, ins, outs, sems, fsdp):
        buffers, local_sem, send_sem, recv_sem, pass_sem, took_sem = sems
        ctx, me, chip, core, sibling = place()
        self.sends, self.passes, self.locals = [], [], []
        for i in range(len(ins)):
            rows = ins[i].shape[0]
            half = rows // 2
            for j, peer in enumerate(peers_of(me, fsdp)):
                self.sends.append(
                    remote(
                        ins[i].at[pl.ds(core * half, half)],
                        outs[i].at[pl.ds(me * rows + core * half, half)],
                        send_sem.at[i, j],
                        recv_sem.at[i, j],
                        (ctx, peer),
                    )
                )
                got = outs[i].at[pl.ds(peer * rows + core * half, half)]
                self.passes.append(
                    remote(got, got, pass_sem.at[i, j], took_sem.at[i, j], (sibling, me))
                )
            self.locals.append(
                Bounce(ins[i], outs[i].at[pl.ds(me * rows, rows)], buffers[i], local_sem.at[i])
            )

    def start(self):
        for copy in self.sends + self.locals:
            copy.start()

    def finish(self):
        for copy in self.locals:
            copy.turn()
        for send, copy in zip(self.sends, self.passes):
            send.wait_recv()
            copy.start()
        for send in self.sends:
            send.wait_send()
        for copy in self.passes + self.locals:
            copy.wait()


def dense_scratch(arrays, fsdp):
    count = len(arrays)
    return (
        [pltpu.VMEM(a.shape, a.dtype) for a in arrays]
        + [pltpu.SemaphoreType.DMA((count,))]
        + [pltpu.SemaphoreType.DMA((count, fsdp - 1)) for unused in range(4)]
    )


class LineGather:
    def __init__(self, ins, outs, sems, chips):
        self.ins, self.outs, self.chips = ins, outs, chips
        self.buffers, self.sems = sems[:-7], sems[-7:]
        self.ctx, self.me, self.chip, core, self.sibling = place()
        self.count = len(ins)

    def to_right(self, i, step):
        outs, chips = self.outs, self.chips
        return remote(
            self.ins[i] if step == 0 else outs[i].at[0, chips - step],
            outs[i].at[0, chips - 1 - step],
            self.sems[1].at[i, step],
            self.sems[2].at[i, step],
            (self.ctx + 2, self.me),
        )

    def to_left(self, i, step):
        outs = self.outs
        return remote(
            self.ins[i] if step == 0 else outs[i].at[0, step],
            outs[i].at[0, step + 1],
            self.sems[3].at[i, step],
            self.sems[4].at[i, step],
            (self.ctx - 2, self.me),
        )

    def across(self, i, slot):
        return remote(
            self.ins[i] if slot == 0 else self.outs[i].at[0, slot],
            self.outs[i].at[1, slot],
            self.sems[5].at[i, slot],
            self.sems[6].at[i, slot],
            (self.sibling, self.me),
        )

    def local(self, i):
        return Bounce(self.ins[i], self.outs[i].at[0, 0], self.buffers[i], self.sems[0].at[i])

    def send(self, step):
        chip, chips, count = self.chip, self.chips, self.count

        @pl.when((chip + 1 < chips) & (chip >= step))
        def _():
            for i in range(count):
                self.to_right(i, step).start()

        @pl.when((chip >= 1) & (chip + step < chips))
        def _():
            for i in range(count):
                self.to_left(i, step).start()

    def receive(self, step):
        chip, chips, count = self.chip, self.chips, self.count

        @pl.when(chip >= step + 1)
        def _():
            for i in range(count):
                self.to_right(i, step).wait_recv()
                self.across(i, chips - 1 - step).start()

        @pl.when(chip + step + 1 < chips)
        def _():
            for i in range(count):
                self.to_left(i, step).wait_recv()
                self.across(i, step + 1).start()

    def own(self):
        for i in range(self.count):
            self.across(i, 0).start()
            self.local(i).start()

    def turn_own(self):
        for i in range(self.count):
            self.local(i).turn()

    def finish_own(self):
        for i in range(self.count):
            self.across(i, 0).wait()
            self.local(i).wait()

    def finish(self, step):
        chip, chips, count = self.chip, self.chips, self.count

        @pl.when((chip + 1 < chips) & (chip >= step))
        def _():
            for i in range(count):
                self.to_right(i, step).wait_send()

        @pl.when((chip >= 1) & (chip + step < chips))
        def _():
            for i in range(count):
                self.to_left(i, step).wait_send()

        @pl.when(chip >= step + 1)
        def _():
            for i in range(count):
                self.across(i, chips - 1 - step).wait()

        @pl.when(chip + step + 1 < chips)
        def _():
            for i in range(count):
                self.across(i, step + 1).wait()


def line_scratch(arrays, chips):
    count = len(arrays)
    return (
        [pltpu.VMEM(a.shape, a.dtype) for a in arrays if a is not None]
        + [pltpu.SemaphoreType.DMA((count,))]
        + [pltpu.SemaphoreType.DMA((count, chips - 1)) for unused in range(4)]
        + [pltpu.SemaphoreType.DMA((count, chips)) for unused in range(2)]
    )


def gather_kernel(dense, line, resumed, steps, fsdp, chips, *refs):
    count = dense + line + resumed
    ins, outs, scratch = refs[:count], refs[count : 2 * count], refs[2 * count :]
    ctx, me, chip, core, sibling = place()
    greet(chips, peers_of(me, fsdp) if dense else [], line > 0)
    split = dense + line
    if dense:
        own, scratch = scratch[: dense + 5], scratch[dense + 5 :]
        first = DenseGather(
            ins[:dense], outs[:dense], (own[:dense],) + tuple(own[dense:]), fsdp
        )
        first.start()
    if line:
        own, scratch = scratch[: line + 7], scratch[line + 7 :]
        second = LineGather(ins[dense:split], outs[dense:split], own, chips)
        for step in range(steps):
            second.send(step)
            if step == 0:
                second.own()
            second.receive(step)
            if step == 0:
                second.turn_own()
    if resumed:
        third = LineGather([None], outs[split:], scratch, chips)
        third.send(chips - 2)
        third.receive(chips - 2)
    if dense:
        first.finish()
    if line:
        second.finish_own()
        for step in range(steps):
            second.finish(step)
    if resumed:
        third.finish(chips - 2)


def gather(dense, line, steps, fsdp, chips, collective_id, resumed=()):
    arrays = list(dense) + list(line) + list(resumed)
    count = len(arrays)
    scratch = (dense_scratch(dense, fsdp) if dense else []) + (
        line_scratch(line, chips) if line else []
    )
    if resumed:
        scratch = scratch + line_scratch([None], chips)
    return pl.pallas_call(
        functools.partial(
            gather_kernel, len(dense), len(line), len(resumed), steps, fsdp, chips
        ),
        out_shape=[jax.ShapeDtypeStruct((fsdp * a.shape[0],) + a.shape[1:], a.dtype) for a in dense]
        + [jax.ShapeDtypeStruct((2, chips) + a.shape, a.dtype) for a in line]
        + [jax.ShapeDtypeStruct(a.shape, a.dtype) for a in resumed],
        in_specs=[pl.BlockSpec(memory_space=pl.ANY)] * count,
        out_specs=[pl.BlockSpec(memory_space=pl.ANY)] * count,
        scratch_shapes=scratch,
        input_output_aliases={count - 1: count - 1} if resumed else {},
        compiler_params=pltpu.CompilerParams(
            collective_id=collective_id, has_side_effects=True, vmem_limit_bytes=VMEM_BYTES
        ),
        name="gather",
    )(*arrays)


def add(*parts):
    total = parts[0].astype(F32)
    for part in parts[1:]:
        total = total + part.astype(F32)
    return total


def add_into(target, parts):
    rows = target.shape[0]
    tile = 32 if rows % 32 == 0 else 16

    def some(t, carry):
        part = pl.ds(pl.multiple_of(t * tile, tile), tile)
        target[part, :] = add(*[ref[part, :] for ref in parts]).astype(target.dtype)
        return carry

    lax.fori_loop(0, rows // tile, some, 0)


class LineSum:
    def __init__(self, chips, held, keep, got, sems):
        self.chips, self.held, self.keep, self.got = chips, held, keep, got
        self.sems = sems
        self.ctx, self.me, self.chip, core, sibling = place()

    def right(self, step):
        return remote(
            self.keep(self.chips - 1 - step),
            self.got.at[step - self.chip],
            self.sems[0].at[step],
            self.sems[1].at[step],
            (self.ctx + 2, self.me),
        )

    def from_left(self, step):
        slot = step + 1 - self.chip
        pltpu.make_async_remote_copy(
            src_ref=self.keep(self.chips - 1 - step),
            dst_ref=self.got.at[slot],
            send_sem=self.sems[0].at[step],
            recv_sem=self.sems[1].at[step],
            device_id=(self.ctx - 2, self.me),
            device_id_type=MESH,
        ).wait_recv()
        return self.got.at[slot]

    def from_right(self, step):
        slot = step + 2
        self.left(step).wait_recv()
        return self.got.at[slot]

    def left(self, step):
        return remote(
            self.keep(step + 1),
            self.got.at[step + 2],
            self.sems[2].at[step],
            self.sems[3].at[step],
            (self.ctx - 2, self.me),
        )

    def step(self, step):
        chip, chips = self.chip, self.chips
        far_right, far_left = chips - 1 - step, step + 1

        @pl.when(chip <= step)
        def _():
            parts = self.held(far_right)
            if step == 0:
                add_into(self.keep(far_right), parts())
            else:

                @pl.when(chip == 0)
                def _():
                    add_into(self.keep(far_right), parts())

                @pl.when(chip >= 1)
                def _():
                    add_into(self.keep(far_right), [self.from_left(step - 1)] + parts())

            self.right(step).start()

        @pl.when(chip >= chips - 1 - step)
        def _():
            parts = self.held(far_left)
            if step == 0:
                add_into(self.keep(far_left), parts())
            else:

                @pl.when(chip == chips - 1)
                def _():
                    add_into(self.keep(far_left), parts())

                @pl.when(chip < chips - 1)
                def _():
                    add_into(self.keep(far_left), [self.from_right(step - 1)] + parts())

            self.left(step).start()

    def total(self, target):
        chip, chips, last = self.chip, self.chips, self.chips - 2
        parts = self.held(0)

        @pl.when(chip == 0)
        def _():
            add_into(target, [self.from_right(last)] + parts())

        @pl.when(chip == chips - 1)
        def _():
            add_into(target, [self.from_left(last)] + parts())

        @pl.when((chip >= 1) & (chip < chips - 1))
        def _():
            add_into(target, [self.from_right(last), self.from_left(last)] + parts())

    def finish(self, steps=None):
        for step in range(self.chips - 1 if steps is None else steps):

            @pl.when(self.chip <= step)
            def _():
                self.right(step).wait_send()

            @pl.when(self.chip >= self.chips - 1 - step)
            def _():
                self.left(step).wait_send()


DENSE_BUFFERS = 5
DENSE_SEMS = 14


class DenseSum:
    def __init__(self, local, out, buffers, sems, fsdp, chips):
        self.local, self.out = local, out
        self.pair, self.cross, self.sums, got, self.spread = buffers
        self.sems = sems
        self.chips = chips
        self.ctx, self.me, self.chip, self.core, self.sibling = place()
        self.owners = peers_of(self.me, fsdp) + [self.me]
        self.cut = out.shape[2] // chips
        self.line = LineSum(
            chips,
            lambda r: lambda: [self.keep_ref(r)],
            lambda r: self.keep_ref(r),
            got,
            sems[4:8],
        )

    def keep_ref(self, r):
        return self.sums.at[:, self.columns(r)]

    def columns(self, r):
        owner = lax.rem(self.chip + r, self.chips)
        return pl.ds(pl.multiple_of(owner * self.cut, LANES), self.cut)

    def swap(self, j):
        return remote(
            self.local.at[self.owners[j], 1 - self.core],
            self.pair.at[j],
            self.sems[0].at[j],
            self.sems[1].at[j],
            (self.sibling, self.me),
        )

    def crossing(self, j):
        return remote(
            self.pair.at[j],
            self.cross.at[j],
            self.sems[2].at[j],
            self.sems[3].at[j],
            (self.ctx, self.owners[j]),
        )

    def to_right(self, step):
        return remote(
            self.spread.at[0, (self.chips - step) % self.chips],
            self.spread.at[0, self.chips - 1 - step],
            self.sems[8].at[step],
            self.sems[9].at[step],
            (self.ctx + 2, self.me),
        )

    def to_left(self, step):
        return remote(
            self.spread.at[0, step],
            self.spread.at[0, step + 1],
            self.sems[10].at[step],
            self.sems[11].at[step],
            (self.ctx - 2, self.me),
        )

    def across(self, slot):
        return remote(
            self.spread.at[0, slot],
            self.spread.at[1, slot],
            self.sems[12].at[slot],
            self.sems[13].at[slot],
            (self.sibling, self.me),
        )

    def start(self):
        for j in range(len(self.owners)):
            self.swap(j).start()

    def cross_over(self):
        for j, owner in enumerate(self.owners):
            self.swap(j).wait_recv()
            add_into(self.pair.at[j], [self.local.at[owner, self.core], self.pair.at[j]])
            if j < len(self.owners) - 1:
                self.crossing(j).start()

    def stages(self):
        chip, chips = self.chip, self.chips

        def open_up():
            for j in range(len(self.owners) - 1):
                self.crossing(j).wait_recv()
            add_into(
                self.sums,
                [self.cross.at[j] for j in range(len(self.owners) - 1)]
                + [self.pair.at[len(self.owners) - 1]],
            )
            self.line.step(0)

        def summed():
            self.line.total(self.spread.at[0, 0])
            hand_on(0)

        def hand_on(step):
            @pl.when((chip + 1 < chips) & (chip >= step))
            def _():
                self.to_right(step).start()

            @pl.when((chip >= 1) & (chip + step < chips))
            def _():
                self.to_left(step).start()

            if step == 0:
                self.across(0).start()

        def take(step):
            @pl.when(chip >= step + 1)
            def _():
                self.to_right(step).wait_recv()
                self.across(chips - 1 - step).start()

            @pl.when(chip + step + 1 < chips)
            def _():
                self.to_left(step).wait_recv()
                self.across(step + 1).start()

        def pass_on(step):
            def run():
                take(step - 1)
                hand_on(step)

            return run

        def line_step(step):
            return lambda: self.line.step(step)

        return (
            [open_up]
            + [line_step(step) for step in range(1, chips - 1)]
            + [summed]
            + [pass_on(step) for step in range(1, chips - 1)]
            + [lambda: take(chips - 2)]
        )

    def finish(self):
        chip, chips = self.chip, self.chips
        for r in range(chips):
            self.out[self.core, :, self.columns(r)] = self.spread[0, r]
        for r in range(chips):
            self.across(r).wait()
            self.out[1 - self.core, :, self.columns(r)] = self.spread[1, r]
        for step in range(chips - 1):

            @pl.when((chip + 1 < chips) & (chip >= step))
            def _():
                self.to_right(step).wait_send()

            @pl.when((chip >= 1) & (chip + step < chips))
            def _():
                self.to_left(step).wait_send()

        self.line.finish()
        for j in range(len(self.owners) - 1):
            self.crossing(j).wait_send()
        for j in range(len(self.owners)):
            self.swap(j).wait_send()


def dense_reduce_kernel(fsdp, chips, cuts, *refs):
    count = len(cuts)
    arrays = max(cut[0] for cut in cuts) + 1
    ins, refs = refs[:arrays], refs[arrays:]
    own_ref, right_ref, left_ref = refs[:3]
    outs, total_ref, refs = refs[3 : 3 + arrays], refs[3 + arrays], refs[4 + arrays :]
    from_left, from_right, r_send, r_recv, l_send, l_recv = refs[:6]
    rest = refs[6:]
    ctx, me, chip, core, sibling = place()
    greet(chips, peers_of(me, fsdp), True)

    to_right = remote(right_ref, from_left, r_send, r_recv, (ctx + 2, me))
    to_left = remote(left_ref, from_right, l_send, l_recv, (ctx - 2, me))

    @pl.when(chip + 1 < chips)
    def _():
        to_right.start()

    @pl.when(chip >= 1)
    def _():
        to_left.start()

    sums = []
    for i, (which, start, size) in enumerate(cuts):
        buffers = rest[i * DENSE_BUFFERS : (i + 1) * DENSE_BUFFERS]
        sems = rest[count * DENSE_BUFFERS + i * DENSE_SEMS :][:DENSE_SEMS]
        sums.append(
            DenseSum(
                ins[which].at[:, :, :, pl.ds(start, size)],
                outs[which].at[:, :, pl.ds(start, size)],
                buffers,
                sems,
                fsdp,
                chips,
            )
        )
    for one in sums:
        one.start()
    for one in sums:
        one.cross_over()
    stages = [one.stages() for one in sums]
    lag = chips - 1
    for tick in range(len(stages[0]) + lag * (count - 1)):
        for i in range(count):
            if 0 <= tick - lag * i < len(stages[i]):
                stages[i][tick - lag * i]()
    @pl.when(chip >= 1)
    def _():
        to_right.wait_recv()

    @pl.when(chip + 1 < chips)
    def _():
        to_left.wait_recv()

    @pl.when(chip == 0)
    def _():
        add_into(total_ref, [from_right, own_ref])

    @pl.when(chip == chips - 1)
    def _():
        add_into(total_ref, [from_left, own_ref])

    @pl.when((chip >= 1) & (chip + 1 < chips))
    def _():
        add_into(total_ref, [from_left, from_right, own_ref])

    for one in sums:
        one.finish()

    @pl.when(chip + 1 < chips)
    def _():
        to_right.wait_send()

    @pl.when(chip >= 1)
    def _():
        to_left.wait_send()


def dense_reduce(arrays, own, right, left, piece, fsdp, chips, collective_id):
    vmem = pl.BlockSpec(memory_space=pltpu.VMEM)
    cuts, buffers = [], []
    for i, a in enumerate(arrays):
        rows, width = a.shape[2:]
        for start in range(0, width, piece):
            size = min(piece, width - start)
            cut = size // chips
            cuts.append((i, start, size))
            buffers += [
                pltpu.VMEM((fsdp, rows, size), BF16),
                pltpu.VMEM((fsdp - 1, rows, size), BF16),
                pltpu.VMEM((rows, size), BF16),
                pltpu.VMEM((chips + 1, rows, cut), BF16),
                pltpu.VMEM((2, chips, rows, cut), BF16),
            ]
    sems = (
        [pltpu.SemaphoreType.DMA((fsdp,)) for unused in range(2)]
        + [pltpu.SemaphoreType.DMA((fsdp - 1,)) for unused in range(2)]
        + [pltpu.SemaphoreType.DMA((chips - 1,)) for unused in range(8)]
        + [pltpu.SemaphoreType.DMA((chips,)) for unused in range(2)]
    )
    return pl.pallas_call(
        functools.partial(dense_reduce_kernel, fsdp, chips, tuple(cuts)),
        out_shape=[jax.ShapeDtypeStruct(a.shape[1:], BF16) for a in arrays]
        + [jax.ShapeDtypeStruct(own.shape, F32)],
        in_specs=[vmem] * len(arrays) + [vmem, pl.BlockSpec(memory_space=pl.ANY)]
        + [pl.BlockSpec(memory_space=pl.ANY)],
        out_specs=[vmem] * (len(arrays) + 1),
        scratch_shapes=[pltpu.VMEM(own.shape, BF16)] * 2
        + [pltpu.SemaphoreType.DMA] * 4
        + buffers
        + sems * len(cuts),
        compiler_params=pltpu.CompilerParams(
            collective_id=collective_id, has_side_effects=True, vmem_limit_bytes=VMEM_BYTES
        ),
        name="dense_reduce",
    )(*arrays, own, right, left)


def after(value, *others):
    return lax.optimization_barrier((value,) + others)[0]


def attention_kernel(
    scale, q_ref, k_ref, v_ref, oq_ref, pq_ref, ok_ref, out_ref, lse_ref, bias, scores
):
    keys = k_ref.shape[0]
    tiles = keys // KEY_TILE
    rows = q_ref.shape[0]

    @pl.when(pl.program_id(0) == 0)
    def _():
        def fill(t, carry):
            tile = pl.ds(pl.multiple_of(t * KEY_TILE, KEY_TILE), KEY_TILE)
            gap = oq_ref[...] - ok_ref[:, tile]
            bias[:, tile] = jnp.where((gap >= 0) & (gap <= pq_ref[...]), 0.0, MASKED)
            return carry

        lax.fori_loop(0, tiles, fill, 0)

    query = q_ref[...]

    def score(t, top):
        tile = pl.ds(pl.multiple_of(t * KEY_TILE, KEY_TILE), KEY_TILE)
        raw = dot(query, k_ref[tile, :], NT) * (scale * LOG2E) + bias[:, tile]
        scores[:, tile] = raw
        for part in range(KEY_TILE // LANES):
            top = jnp.maximum(top, raw[:, part * LANES : (part + 1) * LANES])
        return top

    top = lax.fori_loop(0, tiles, score, jnp.full((rows, LANES), MASKED, F32))
    top = jnp.max(top, axis=1, keepdims=True)

    def weigh(t, carry):
        total, acc = carry
        tile = pl.ds(pl.multiple_of(t * KEY_TILE, KEY_TILE), KEY_TILE)
        probs = jnp.exp2(scores[:, tile] - top)
        for part in range(KEY_TILE // LANES):
            total = total + probs[:, part * LANES : (part + 1) * LANES]
        acc = acc + dot(probs.astype(BF16), v_ref[tile, :], NN)
        return total, acc

    total, acc = lax.fori_loop(
        0, tiles, weigh, (jnp.zeros((rows, LANES), F32), jnp.zeros((rows, HEAD_SIZE), F32))
    )
    total = jnp.sum(total, axis=1, keepdims=True)
    out_ref[...] = (acc / total).astype(BF16)
    lse = jnp.broadcast_to(top + jnp.log2(total), (rows, LANES))
    lse_ref[0] = lse.T[:1, :]


def attention(queries, kv, order_mine, pos_mine, order_keys, group):
    rows = queries.shape[0]
    keys = kv.shape[0]
    per_group = QUERY_HEADS // KVH
    return pl.pallas_call(
        functools.partial(attention_kernel, HEAD_SIZE ** (-0.5)),
        grid=(per_group,),
        out_shape=[
            jax.ShapeDtypeStruct((rows, per_group * HEAD_SIZE), BF16),
            jax.ShapeDtypeStruct((per_group, 1, rows), F32),
        ],
        in_specs=[
            pl.BlockSpec((rows, HEAD_SIZE), lambda h: (0, group * per_group + h)),
            pl.BlockSpec((keys, HEAD_SIZE), lambda h: (0, group)),
            pl.BlockSpec((keys, HEAD_SIZE), lambda h: (0, KVH + group)),
            pl.BlockSpec((rows, 1), lambda h: (0, 0)),
            pl.BlockSpec((rows, 1), lambda h: (0, 0)),
            pl.BlockSpec((1, keys), lambda h: (0, 0)),
        ],
        out_specs=[
            pl.BlockSpec((rows, HEAD_SIZE), lambda h: (0, h)),
            pl.BlockSpec((1, 1, rows), lambda h: (h, 0, 0)),
        ],
        scratch_shapes=[pltpu.VMEM((rows, keys), F32), pltpu.VMEM((rows, keys), F32)],
        compiler_params=pltpu.CompilerParams(vmem_limit_bytes=VMEM_BYTES),
        cost_estimate=pl.CostEstimate(
            flops=4 * rows * keys * HEAD_SIZE * per_group,
            bytes_accessed=4 * rows * per_group * HEAD_SIZE + 4 * keys * HEAD_SIZE,
            transcendentals=rows * keys * per_group,
        ),
        name="attention",
    )(queries, kv, kv, order_mine[:, None], pos_mine[:, None], order_keys[None, :])


def attention_back_kernel(
    scale,
    chips,
    q_ref,
    k_ref,
    v_ref,
    o_ref,
    do_ref,
    lse_ref,
    oq_ref,
    pq_ref,
    ok_ref,
    mine_ref,
    other_ref,
    dq_ref,
    kv_ref,
    own_ref,
    right_ref,
    left_ref,
    bias,
    dk_acc,
    dv_acc,
    mine_v,
    pair,
    got,
    kv_v,
    kv_pair,
    kv_got,
    load_sem,
    store_sem,
    swap_send,
    swap_recv,
    r_send,
    r_recv,
    l_send,
    l_recv,
    kv_swap_send,
    kv_swap_recv,
    kr_send,
    kr_recv,
    kl_send,
    kl_recv,
):
    ctx, me, chip, core, sibling = place()
    keys = k_ref.shape[0]
    tiles = keys // KEY_TILE
    rows = q_ref.shape[0]
    per_group = QUERY_HEADS // KVH
    head = pl.program_id(0)

    order = []
    for step in range(chips - 1):
        for r in (chips - 1 - step, step + 1):
            if r not in order:
                order.append(r)
    order.append(0)
    swaps = [
        remote(other_ref.at[r], pair.at[r], swap_send.at[r], swap_recv.at[r], (sibling, me))
        for r in range(chips)
    ]
    loads = [
        pltpu.make_async_copy(mine_ref.at[r], mine_v.at[j % 2], load_sem.at[j % 2])
        for j, r in enumerate(order)
    ]
    line = LineSum(
        chips,
        lambda r: lambda: [pair.at[r]],
        lambda r: pair.at[r],
        got,
        (r_send, r_recv, l_send, l_recv),
    )

    def join(j):
        loads[j].wait()
        swaps[order[j]].wait_recv()
        add_into(pair.at[order[j]], [pair.at[order[j]], mine_v.at[j % 2]])
        if j + 2 < chips:
            loads[j + 2].start()

    def kv_swap(group, r):
        return remote(
            kv_v.at[group, 1, r],
            kv_pair.at[group, r],
            kv_swap_send.at[group, r],
            kv_swap_recv.at[group, r],
            (sibling, me),
        )

    def kv_line(group):
        def held(r):
            kv_swap(group, r).wait_recv()
            return lambda: [kv_v.at[group, 0, r], kv_pair.at[group, r]]

        return LineSum(
            chips,
            held,
            lambda r: kv_pair.at[group, r],
            kv_got.at[group],
            tuple(sem.at[group] for sem in (kr_send, kr_recv, kl_send, kl_recv)),
        )

    def kv_start(group):
        for q in range(2):
            for r in range(chips):
                part = pl.ds((q * chips + r) * rows, rows)
                kv_v[group, q, r, :, :HEAD_SIZE] = (dk_acc[part, :] * scale).astype(BF16)
                kv_v[group, q, r, :, HEAD_SIZE:] = dv_acc[part, :].astype(BF16)
        for r in order:
            kv_swap(group, r).start()

    @pl.when(head == 0)
    def _():
        greet(chips, [], True)
        for r in order:
            swaps[r].start()
        for copy in loads[:2]:
            copy.start()

        def fill(t, carry):
            tile = pl.ds(pl.multiple_of(t * KEY_TILE, KEY_TILE), KEY_TILE)
            gap = oq_ref[...] - ok_ref[tile, :]
            bias[tile, :] = jnp.where((gap >= 0) & (gap <= pq_ref[...]), 0.0, MASKED)
            return carry

        lax.fori_loop(0, tiles, fill, 0)

    @pl.when(lax.rem(head, per_group) == 0)
    def _():
        dk_acc[...] = jnp.zeros_like(dk_acc)
        dv_acc[...] = jnp.zeros_like(dv_acc)

    query = q_ref[...]
    grad = do_ref[...]
    lse = lse_ref[0]
    product = grad.astype(F32) * o_ref[...].astype(F32)
    delta = jnp.sum(product.T, axis=0, keepdims=True)

    def step(t, acc):
        tile = pl.ds(pl.multiple_of(t * KEY_TILE, KEY_TILE), KEY_TILE)
        key = k_ref[tile, :]
        raw = dot(key, query, NT) * (scale * LOG2E) + bias[tile, :]
        probs = jnp.exp2(raw - lse)
        prob_grad = dot(v_ref[tile, :], grad, NT)
        score_grad = (probs * (prob_grad - delta)).astype(BF16)
        dv_acc[tile, :] += dot(probs.astype(BF16), grad, NN)
        dk_acc[tile, :] += dot(score_grad, query, NN)
        return acc + dot(score_grad, key, TN)

    acc = lax.fori_loop(0, tiles, step, jnp.zeros((rows, HEAD_SIZE), F32))
    dq_ref[...] = acc * scale

    last = QUERY_HEADS - 1
    stride = max(1, last // (chips - 2))
    early = {per_group + 2 * s: s for s in range(chips - 1) if per_group + 2 * s < last}
    for h in range(QUERY_HEADS):

        @pl.when(head == h)
        def _():
            if h == 0:
                for j in range(chips):
                    join(j)
            for s in range(chips - 2):
                if h == s * stride:
                    line.step(s)
            if h % per_group == per_group - 1:
                kv_start(h // per_group)
            if h in early:
                kv_line(0).step(early[h])

    @pl.when(head == last)
    def _():
        def store(k, r, target):
            return pltpu.make_async_copy(pair.at[r], target, store_sem.at[k])

        @pl.when((chip >= 1) & (chip + 1 < chips))
        def _():
            add_into(pair.at[1], [pair.at[1], line.from_left(chips - 3)])
            add_into(pair.at[chips - 1], [pair.at[chips - 1], line.from_right(chips - 3)])

        for copy in (
            store(0, 0, own_ref),
            store(1, 1, right_ref),
            store(2, chips - 1, left_ref),
        ):
            copy.start()
        for group in range(KVH):
            one = kv_line(group)
            for s in range(chips - 1):
                if group > 0 or s not in early.values():
                    one.step(s)
            one.total(kv_ref.at[group])
        for group in range(KVH):
            kv_line(group).finish()
            for r in range(chips):
                kv_swap(group, r).wait_send()
        line.finish(chips - 2)
        for swap in swaps:
            swap.wait_send()
        for copy in (
            store(0, 0, own_ref),
            store(1, 1, right_ref),
            store(2, chips - 1, left_ref),
        ):
            copy.wait()


def attention_back(
    queries, kv, attended, attended_grad, lse, order_mine, pos_mine, order_keys, mine, other,
    collective_id
):
    rows = queries.shape[0]
    keys = kv.shape[0]
    chips, unused, width = mine.shape
    per_group = QUERY_HEADS // KVH
    head_rows = pl.BlockSpec((rows, HEAD_SIZE), lambda h: (0, h))
    anywhere = pl.BlockSpec(memory_space=pl.ANY)
    return pl.pallas_call(
        functools.partial(attention_back_kernel, HEAD_SIZE ** (-0.5), chips),
        grid=(QUERY_HEADS,),
        out_shape=[
            jax.ShapeDtypeStruct(queries.shape, F32),
            jax.ShapeDtypeStruct((KVH, rows, 2 * HEAD_SIZE), F32),
        ]
        + [jax.ShapeDtypeStruct((rows, width), BF16)] * 3,
        in_specs=[
            head_rows,
            pl.BlockSpec((keys, HEAD_SIZE), lambda h: (0, h // per_group)),
            pl.BlockSpec((keys, HEAD_SIZE), lambda h: (0, KVH + h // per_group)),
            head_rows,
            head_rows,
            pl.BlockSpec((1, 1, rows), lambda h: (h, 0, 0)),
            pl.BlockSpec((1, rows), lambda h: (0, 0)),
            pl.BlockSpec((1, rows), lambda h: (0, 0)),
            pl.BlockSpec((keys, 1), lambda h: (0, 0)),
            anywhere,
            anywhere,
        ],
        out_specs=[
            head_rows,
            pl.BlockSpec((KVH, rows, 2 * HEAD_SIZE), lambda h: (0, 0, 0)),
            anywhere,
            anywhere,
            anywhere,
        ],
        scratch_shapes=[
            pltpu.VMEM((keys, rows), F32),
            pltpu.VMEM((keys, HEAD_SIZE), F32),
            pltpu.VMEM((keys, HEAD_SIZE), F32),
            pltpu.VMEM((2, rows, width), BF16),
            pltpu.VMEM((chips, rows, width), BF16),
            pltpu.VMEM((chips + 1, rows, width), BF16),
            pltpu.VMEM((KVH, 2, chips, rows, 2 * HEAD_SIZE), BF16),
            pltpu.VMEM((KVH, chips, rows, 2 * HEAD_SIZE), BF16),
            pltpu.VMEM((KVH, chips + 1, rows, 2 * HEAD_SIZE), BF16),
            pltpu.SemaphoreType.DMA((2,)),
            pltpu.SemaphoreType.DMA((3,)),
            pltpu.SemaphoreType.DMA((chips,)),
            pltpu.SemaphoreType.DMA((chips,)),
        ]
        + [pltpu.SemaphoreType.DMA((chips - 1,)) for unused in range(4)]
        + [pltpu.SemaphoreType.DMA((KVH, chips)) for unused in range(2)]
        + [pltpu.SemaphoreType.DMA((KVH, chips - 1)) for unused in range(4)],
        compiler_params=pltpu.CompilerParams(
            collective_id=collective_id, has_side_effects=True, vmem_limit_bytes=BACK_VMEM_BYTES
        ),
        cost_estimate=pl.CostEstimate(
            flops=10 * rows * keys * HEAD_SIZE * QUERY_HEADS,
            bytes_accessed=10 * rows * QUERY_HEADS * HEAD_SIZE + 8 * keys * KVH * HEAD_SIZE,
            transcendentals=rows * keys * QUERY_HEADS,
        ),
        name="attention_back",
    )(
        queries,
        kv,
        kv,
        attended,
        attended_grad,
        lse,
        order_mine[None, :],
        pos_mine[None, :],
        order_keys[:, None],
        mine,
        other,
    )


def chunk_order(chip, i, chips):
    right_half = lax.div(2 * chip, chips)
    near = chip + right_half * (chips - 1 - 2 * chip)
    alone = chips - 1 - 2 * near
    paired = lax.div(i - alone + chips, chips)
    turn = (i - alone) * paired
    odd = lax.rem(turn, 2)
    pair = lax.div(turn, 2)
    distance = (1 - paired) * (chips - 1 - near - i) + paired * (
        (1 - odd) * (near - pair) + odd * (chips - near + pair)
    )
    return lax.rem(distance + right_half * (chips - 2 * distance), chips)


def experts_kernel(
    capacity,
    local_experts,
    expert_count,
    chips,
    fsdp,
    per,
    hidden_ref,
    grad_ref,
    table_ref,
    weight_ref,
    gate_ref,
    up_ref,
    down_ref,
    returned_ref,
    out_mine_ref,
    out_other_ref,
    gate_grad_ref,
    up_grad_ref,
    down_grad_ref,
    x_ref,
    pg_ref,
    inner_ref,
    da_ref,
    db_ref,
    gate_v,
    up_v,
    down_v,
    hidden_v,
    grad_v,
    out_v,
    x_v,
    pg_v,
    g_v,
    inner_v,
    da_v,
    db_v,
    mine_v,
    other_v,
    pair,
    got,
    stage_tall,
    weight_sem,
    load_sem,
    out_sem,
    save_sem,
    swap_send,
    swap_recv,
    right_send,
    right_recv,
    left_send,
    left_recv,
    stage_sem,
):
    ctx, me, chip, core, sibling = place()
    tokens = hidden_v.shape[1]
    width = hidden_v.shape[2]
    slots = x_v.shape[1]
    slot_rows = slots // 2
    units = inner_v.shape[2]
    total_rows = x_ref.shape[1]
    first = ctx * local_experts

    weights_in = [
        pltpu.make_async_copy(src, dst, weight_sem.at[k])
        for k, (src, dst) in enumerate(
            ((gate_ref, gate_v), (up_ref, up_v), (down_ref, down_v))
        )
    ]

    def load(i):
        r = chunk_order(chip, i, chips)
        return [
            pltpu.make_async_copy(hidden_ref.at[:, r], hidden_v, load_sem.at[0]),
            pltpu.make_async_copy(grad_ref.at[:, r], grad_v, load_sem.at[1]),
        ]

    def saves(i):
        rows = pl.ds(i * slots, slots)
        return [
            pltpu.make_async_copy(src, dst.at[:, rows], save_sem.at[k])
            for k, (src, dst) in enumerate(
                ((x_v, x_ref), (pg_v, pg_ref), (inner_v, inner_ref), (da_v, da_ref), (db_v, db_ref))
            )
        ]

    def out_copies(i):
        r = chunk_order(chip, i, chips)
        return [
            pltpu.make_async_copy(out_v.at[0], out_mine_ref.at[r], out_sem.at[0]),
            pltpu.make_async_copy(out_v.at[1], out_other_ref.at[r], out_sem.at[1]),
        ]

    def swap(i):
        r = chunk_order(chip, i, chips)
        return remote(
            other_v.at[lax.rem(i, 2)],
            pair.at[r],
            swap_send.at[r],
            swap_recv.at[r],
            (sibling, me),
        )

    def join(i):
        r = chunk_order(chip, i, chips)
        swap(i).wait_recv()
        add_into(pair.at[r], [pair.at[r], mine_v.at[lax.rem(i, 2)]])

    line = LineSum(
        chips,
        lambda r: lambda: [pair.at[r]],
        lambda r: pair.at[r],
        got,
        (right_send, right_recv, left_send, left_recv),
    )

    for copy in load(0) + weights_in:
        copy.start()
    greet(chips, [], True)

    slot = lax.broadcasted_iota(jnp.int32, (slot_rows, tokens), 0).astype(F32) + 1.0
    slot = jnp.where(slot <= capacity, slot, -1.0)
    lane = lax.broadcasted_iota(jnp.int32, (slots, LANES), 1)

    def chunk(i, carry):
        r = chunk_order(chip, i, chips)
        for copy in load(i):
            copy.wait()

        @pl.when(i >= 1)
        def _():
            for copy in saves(i - 1):
                copy.wait()

        picks = [[], []]
        weight_rows = []
        for e in range(local_experts):
            rows_w = []
            for q in range(2):
                hit = slot == table_ref[q, r, pl.ds(first + e, 1), :]
                pick = jnp.where(hit, 1.0, 0.0).astype(BF16)
                weight = weight_ref[q, r, pl.ds(first + e, 1), :]
                w = jnp.sum(jnp.where(hit, weight, 0.0), axis=1, keepdims=True)
                rows = pl.ds(q * slot_rows, slot_rows)
                x_v[e, rows, :] = dot(pick, hidden_v[q], NN).astype(BF16)
                g = dot(pick, grad_v[q], NN)
                g_v[e, rows, :] = g.astype(BF16)
                pg_v[e, rows, :] = (w * g).astype(BF16)
                picks[q].append(pick)
                rows_w.append(w)
            weight_rows.append(jnp.concatenate(rows_w, axis=0))

        @pl.when(i + 1 < chips)
        def _():
            for copy in load(i + 1):
                copy.start()

        @pl.when(i == 0)
        def _():
            for copy in weights_in:
                copy.wait()

        outs = [[], []]
        backs = [[], []]
        for e in range(local_experts):
            x = x_v[e]
            pair_grad = pg_v[e]
            w = weight_rows[e]
            gate = gate_v[e * width : (e + 1) * width, :]
            up = up_v[e * width : (e + 1) * width, :]
            down = down_v[e * units : (e + 1) * units, :]
            gate_pre = dot(x, gate, NN)
            up_pre = dot(x, up, NN)
            sig = jax.nn.sigmoid(gate_pre)
            silu = gate_pre * sig
            inner = (silu * up_pre).astype(BF16)
            inner_v[e] = inner
            expert_out = dot(inner, down, NN).astype(BF16).astype(F32)
            gate_grad = jnp.sum(expert_out * g_v[e].astype(F32), axis=1, keepdims=True)
            inner_grad = dot(pair_grad, down, NT)
            da = (inner_grad * up_pre * sig * (1.0 + gate_pre * (1.0 - sig))).astype(BF16)
            db = (inner_grad * silu).astype(BF16)
            da_v[e] = da
            db_v[e] = db
            row_grad = (dot(da, gate, NT) + dot(db, up, NT)).astype(BF16)
            high = gate_grad.astype(BF16).astype(F32)
            extra = jnp.where(lane == first + e, high, 0.0) + jnp.where(
                lane == expert_count + first + e, gate_grad - high, 0.0
            )
            back = jnp.concatenate([row_grad, extra.astype(BF16)], axis=1)
            out_rows = (w * expert_out).astype(BF16)
            for q in range(2):
                part = slice(q * slot_rows, (q + 1) * slot_rows)
                outs[q].append(out_rows[part])
                backs[q].append(back[part])

        for copy in saves(i):
            copy.start()

        @pl.when(i >= 1)
        def _():
            for copy in out_copies(i - 1):
                copy.wait()

        @pl.when(i >= 2)
        def _():
            swap(i - 2).wait_send()

        for q in range(2):
            pick = jnp.concatenate(picks[q], axis=0)
            held = other_v if q else mine_v
            held[lax.rem(i, 2)] = dot(pick, jnp.concatenate(backs[q], axis=0), TN).astype(BF16)
            if q:
                swap(i).start()
        for q in range(2):
            pick = jnp.concatenate(picks[q], axis=0)
            out_v[q] = dot(pick, jnp.concatenate(outs[q], axis=0), TN).astype(BF16)
        for copy in out_copies(i):
            copy.start()

        @pl.when(i == 0)
        def _():
            join(0)
            line.step(0)

        @pl.when(i >= 2)
        def _():
            join(i - 1)

        for step in range(1, chips - 1):
            if 2 * step < chips:

                @pl.when(i == 2 * step)
                def _():
                    line.step(step)

        return carry

    lax.fori_loop(0, chips, chunk, 0)
    join(chips - 1)
    for copy in saves(chips - 1):
        copy.wait()
    for copy in out_copies(chips - 1):
        copy.wait()
    for i in range(max(0, chips - 2), chips):
        swap(i).wait_send()

    shard = width // fsdp
    blocks = fsdp // per
    block = per * shard

    def fetch(copies):
        copies = [
            pltpu.make_async_copy(src, dst, save_sem.at[k])
            for k, (src, dst) in enumerate(copies)
        ]
        for copy in copies:
            copy.start()
        for copy in copies:
            copy.wait()

    def products(e, staged, target, product):
        def write(f):
            return [
                pltpu.make_async_copy(
                    staged(lax.rem(f, 2), p),
                    target.at[f * per + p, e],
                    stage_sem.at[lax.rem(f, 2), p],
                )
                for p in range(per)
            ]

        def one(f, carry):
            @pl.when(f >= 2)
            def _():
                for copy in write(f - 2):
                    copy.wait()

            product(f)
            for copy in write(f):
                copy.start()
            return carry

        lax.fori_loop(0, blocks, one, 0)
        for f in range(max(0, blocks - 2), blocks):
            for copy in write(f):
                copy.wait()

    def stage_wide(slot, p):
        return hidden_v.at[slot, pl.ds(p * shard, shard), pl.ds(0, units)]

    def wide(e, held, target):
        def product(f):
            columns = pl.ds(pl.multiple_of(f * block, LANES), block)
            value = dot(
                down_v[:total_rows, columns],
                held[e * total_rows : (e + 1) * total_rows, :],
                TN,
            ).astype(BF16)
            for p in range(per):
                stage_wide(lax.rem(f, 2), p)[...] = value[p * shard : (p + 1) * shard, :]

        products(e, stage_wide, target, product)

    def tall(e, target):
        def product(f):
            columns = pl.ds(pl.multiple_of(f * block, LANES), block)
            value = dot(
                gate_v[e * total_rows : (e + 1) * total_rows, :],
                down_v[:total_rows, columns],
                TN,
            ).astype(BF16)
            for p in range(per):
                stage_tall[lax.rem(f, 2), p] = value[:, p * shard : (p + 1) * shard]

        products(e, lambda slot, p: stage_tall.at[slot, p], target, product)

    work = []
    for e in range(local_experts):
        copies = [(x_ref.at[e], down_v.at[:total_rows])]
        if e == 0:
            for k in range(local_experts):
                held = pl.ds(k * total_rows, total_rows)
                copies += [(da_ref.at[k], gate_v.at[held]), (db_ref.at[k], up_v.at[held])]
        work.append(lambda copies=copies: fetch(copies))
        work.append(lambda e=e: wide(e, gate_v, gate_grad_ref))
        work.append(lambda e=e: wide(e, up_v, up_grad_ref))
    for e in range(local_experts):
        copies = [(pg_ref.at[e], down_v.at[:total_rows])]
        if e == 0:
            for k in range(local_experts):
                copies.append((inner_ref.at[k], gate_v.at[pl.ds(k * total_rows, total_rows)]))
        work.append(lambda copies=copies: fetch(copies))
        work.append(lambda e=e: tall(e, down_grad_ref))
    late = [step for step in range(1, chips - 1) if 2 * step >= chips]
    for n, task in enumerate(work):
        task()
        if n == LINE_TASK or (n > LINE_TASK and late):
            if late:
                line.step(late.pop(0))
    for step in late:
        line.step(step)

    line.total(returned_ref)
    line.finish()


def experts_pass(
    hidden, grad, table, weights, gate, up, down, capacity, expert_count, fsdp, collective_id
):
    unused, chips, tokens, width = grad.shape
    local_experts, unused, units = gate.shape
    slots = 2 * SLOT_STEP * -(-capacity // SLOT_STEP)
    total = chips * slots
    shard = width // fsdp
    per = 1 if shard % LANES == 0 else 2
    wide = width + LANES
    anywhere = pl.BlockSpec(memory_space=pl.ANY)
    vmem = pl.BlockSpec(memory_space=pltpu.VMEM)
    flops = 2 * total * width * units * local_experts * 9 + 8 * total * tokens * width
    saved = [(local_experts, total, width)] * 2 + [(local_experts, total, units)] * 3
    held = [(local_experts, slots, width)] * 3 + [(local_experts, slots, units)] * 3
    outs = pl.pallas_call(
        functools.partial(
            experts_kernel, capacity, local_experts, expert_count, chips, fsdp, per
        ),
        out_shape=[
            jax.ShapeDtypeStruct((tokens, wide), BF16),
            jax.ShapeDtypeStruct((chips, tokens, width), BF16),
            jax.ShapeDtypeStruct((chips, tokens, width), BF16),
            jax.ShapeDtypeStruct((fsdp, local_experts, shard, units), BF16),
            jax.ShapeDtypeStruct((fsdp, local_experts, shard, units), BF16),
            jax.ShapeDtypeStruct((fsdp, local_experts, units, shard), BF16),
        ]
        + [jax.ShapeDtypeStruct(shape, BF16) for shape in saved],
        in_specs=[anywhere, anywhere, vmem, vmem, anywhere, anywhere, anywhere],
        out_specs=[vmem] + [anywhere] * 10,
        scratch_shapes=[
            pltpu.VMEM((local_experts * width, units), BF16),
            pltpu.VMEM((local_experts * width, units), BF16),
            pltpu.VMEM((local_experts * units, width), BF16),
            pltpu.VMEM((2, tokens, width), BF16),
            pltpu.VMEM((2, tokens, width), BF16),
            pltpu.VMEM((2, tokens, width), BF16),
        ]
        + [pltpu.VMEM(shape, BF16) for shape in held]
        + [
            pltpu.VMEM((2, tokens, wide), BF16),
            pltpu.VMEM((2, tokens, wide), BF16),
            pltpu.VMEM((chips, tokens, wide), BF16),
            pltpu.VMEM((chips + 1, tokens, wide), BF16),
            pltpu.VMEM((2, per, units, shard), BF16),
            pltpu.SemaphoreType.DMA((3,)),
            pltpu.SemaphoreType.DMA((2,)),
            pltpu.SemaphoreType.DMA((2,)),
            pltpu.SemaphoreType.DMA((5,)),
            pltpu.SemaphoreType.DMA((chips,)),
            pltpu.SemaphoreType.DMA((chips,)),
        ]
        + [pltpu.SemaphoreType.DMA((chips - 1,)) for unused in range(4)]
        + [pltpu.SemaphoreType.DMA((2, per))],
        compiler_params=pltpu.CompilerParams(
            collective_id=collective_id, has_side_effects=True, vmem_limit_bytes=EXPERT_VMEM_BYTES
        ),
        cost_estimate=pl.CostEstimate(
            flops=flops, bytes_accessed=100_000_000, transcendentals=total * units * 2
        ),
        name="experts",
    )(
        hidden,
        grad,
        table,
        weights,
        gate.reshape(local_experts * width, units),
        up.reshape(local_experts * width, units),
        down.reshape(local_experts * units, width),
    )
    return outs[:6]


def body(
    tokens,
    grad_out,
    order,
    lengths,
    routes,
    gain_one,
    gain_two,
    w_query,
    w_key,
    w_value,
    w_out,
    w_router,
    w_gate,
    w_up,
    w_down,
):
    fsdp = lax.axis_size("fsdp")
    chips = lax.axis_size("ctx") // 2
    ctx_index = lax.axis_index("ctx")
    chip = ctx_index // 2
    core = lax.rem(ctx_index, 2)
    tok_rows = tokens.shape[1]
    width = tokens.shape[2]
    top_count = routes.shape[2]
    local_experts = w_gate.shape[0]
    expert_count = local_experts * chips * 2
    capacity = 5 * tok_rows * top_count // (4 * expert_count)
    kv_width = KVH * HEAD_SIZE
    shard = gain_one.shape[0]

    small = jnp.concatenate(
        [
            w_router,
            gain_one[:, None],
            gain_two[:, None],
            jnp.zeros((shard, LANES - expert_count - 2), BF16),
        ],
        axis=1,
    )
    qkv_shard = jnp.concatenate([w_query, w_key, w_value], axis=1)
    qkv_full, small_full, grad_all = gather(
        [qkv_shard, small], [grad_out[0]], chips - 2, fsdp, chips, 0
    )

    qkv_full, w_gate, w_up, w_down = lax.optimization_barrier((qkv_full, w_gate, w_up, w_down))
    gate_full, up_full, down_full = (
        lax.all_gather(w_gate, "fsdp", axis=1, tiled=True),
        lax.all_gather(w_up, "fsdp", axis=1, tiled=True),
        lax.all_gather(w_down, "fsdp", axis=2, tiled=True),
    )
    router_full = small_full[:, :expert_count]
    gain_a = small_full[:, expert_count].astype(F32)
    gain_b = small_full[:, expert_count + 1].astype(F32)

    order_row = order[0]
    start_row = ctx_index * tok_rows
    order_mine = lax.dynamic_slice_in_dim(order_row, start_row, tok_rows)
    ends = jnp.cumsum(lengths[0])
    starts = ends - lengths[0]
    past = order_mine[:, None] >= ends[None, :]
    doc_start = jnp.max(jnp.where(past, ends[None, :], starts[:1]), axis=1)
    pos_mine = order_mine - doc_start
    by_chip = jnp.roll(order_row.reshape(chips, 2, tok_rows), -chip, axis=0)
    by_chip = jnp.where(core == 0, by_chip, by_chip[:, ::-1])
    order_keys = jnp.swapaxes(by_chip, 0, 1).reshape(-1)

    route_rows = routes[0]
    route_onehot = (route_rows[:, :, None] == jnp.arange(expert_count)[None, None, :]).astype(F32)
    routed = jnp.sum(route_onehot, axis=1)
    earlier = (order_mine[None, :] < order_mine[:, None]).astype(BF16)
    ranks = jnp.dot(earlier, routed.astype(BF16), preferred_element_type=F32)
    table = jnp.where(routed > 0, jnp.minimum(ranks, capacity) + 1.0, 0.0)

    half_dim = HEAD_SIZE // 2
    freqs = ROPE_BASE ** (-2.0 * jnp.arange(half_dim).astype(F32) / HEAD_SIZE)
    angles = pos_mine.astype(F32)[:, None] * freqs[None, :]
    cosine = jnp.cos(angles)[:, None, :]
    sine = jnp.sin(angles)[:, None, :]

    inputs = tokens[0].astype(F32)
    hidden_one = rms_scale(inputs, gain_a).astype(BF16)
    pre = jnp.dot(hidden_one, qkv_full, preferred_element_type=F32)
    turned = rotate(
        pre[:, : width + kv_width].reshape(tok_rows, QUERY_HEADS + KVH, HEAD_SIZE), cosine, sine
    )
    queries = turned[:, :QUERY_HEADS].astype(BF16).reshape(tok_rows, width)
    kv_mine = jnp.concatenate(
        [
            turned[:, QUERY_HEADS:].astype(BF16).reshape(tok_rows, kv_width),
            pre[:, width + kv_width :].astype(BF16),
        ],
        axis=1,
    )
    out_full, kv_all, table_all, grad_all = gather(
        [w_out], [kv_mine, table.T], chips - 1, fsdp, chips, 1, [grad_all]
    )
    kv_all = kv_all.reshape(-1, 2 * kv_width)
    attended, lse = [], []
    for group in range(KVH):
        part, part_lse = attention(
            after(queries, *attended[-1:]), kv_all, order_mine, pos_mine, order_keys, group
        )
        attended.append(part)
        lse.append(part_lse)
    attended_parts, attended = attended, jnp.concatenate(attended, axis=1)
    middle = inputs + jnp.dot(attended, out_full, preferred_element_type=F32)
    hidden_two = rms_scale(middle, gain_b).astype(BF16)
    logits = jnp.dot(hidden_two, router_full, preferred_element_type=F32)
    chosen = jnp.where(routed > 0, logits, MASKED)
    gate_weights = jnp.where(routed > 0, jax.nn.softmax(chosen, axis=-1), 0.0)

    hidden_all, weights_all = gather([], [hidden_two, gate_weights.T], chips - 1, fsdp, chips, 2)
    returned, out_mine, out_other, gate_local, up_local, down_local = experts_pass(
        hidden_all,
        grad_all,
        table_all,
        weights_all,
        gate_full,
        up_full,
        down_full,
        capacity,
        expert_count,
        fsdp,
        5,
    )
    expert_grads = [
        lax.psum_scatter(part, "fsdp", scatter_dimension=0, tiled=True)
        for part in (gate_local, up_local, down_local)
    ]

    out_grad = grad_out[0].astype(F32)
    returned = returned.astype(F32)
    extra = returned[:, width:]
    gate_grad = extra[:, :expert_count] + extra[:, expert_count : 2 * expert_count]
    logit_grad = (
        gate_weights * (gate_grad - jnp.sum(gate_weights * gate_grad, axis=-1, keepdims=True))
    ).astype(BF16)
    router_local = jnp.einsum("td,te->de", hidden_two, logit_grad, preferred_element_type=F32)
    hidden_two_grad = returned[:, :width] + jnp.einsum(
        "te,de->td", logit_grad, router_full, preferred_element_type=F32
    )
    unused_two, norm_two_back = jax.vjp(rms_scale, middle, gain_b)
    middle_part, gain_two_local = norm_two_back(hidden_two_grad)
    middle_grad = out_grad + middle_part
    branch_grad = middle_grad.astype(BF16)
    out_local = jnp.einsum("tc,td->cd", attended, branch_grad, preferred_element_type=F32)
    attended_grad = jnp.einsum(
        "td,cd->tc", branch_grad, out_full, preferred_element_type=F32
    ).astype(BF16)

    query_grad, kv_grad, out_own, out_right, out_left = attention_back(
        queries,
        kv_all,
        attended,
        attended_grad,
        jnp.concatenate(lse, axis=0),
        order_mine,
        pos_mine,
        order_keys,
        out_mine,
        out_other,
        3,
    )
    key_grad = [kv_grad[group, :, :HEAD_SIZE] for group in range(KVH)]
    value_grad = [kv_grad[group, :, HEAD_SIZE:] for group in range(KVH)]
    turned_grad = rotate(
        jnp.concatenate([query_grad] + key_grad, axis=1).reshape(
            tok_rows, QUERY_HEADS + KVH, HEAD_SIZE
        ),
        cosine,
        -sine,
    ).reshape(tok_rows, width + kv_width)
    pre_grad = jnp.concatenate(
        [turned_grad.astype(BF16)] + [part.astype(BF16) for part in value_grad], axis=1
    )
    qkv_local = jnp.einsum("td,tc->dc", hidden_one, pre_grad, preferred_element_type=F32)
    hidden_one_grad = jnp.einsum("tc,dc->td", pre_grad, qkv_full, preferred_element_type=F32)
    unused_one, norm_one_back = jax.vjp(rms_scale, inputs, gain_a)
    input_part, gain_one_local = norm_one_back(hidden_one_grad)
    input_grad = (middle_grad + input_part).astype(BF16)

    def halves(local):
        local = local.astype(BF16).reshape(fsdp, 2, shard // 2, local.shape[1])
        pad = -local.shape[3] % (LANES * chips)
        return jnp.pad(local, ((0, 0), (0, 0), (0, 0), (0, pad))) if pad else local

    span = shard * expert_count // 16
    wide = LANES * chips * -(-max(span, shard) // (LANES * chips))
    small_local = jnp.stack(
        [
            jnp.pad(
                router_local.astype(BF16).reshape(fsdp, 16, span),
                ((0, 0), (0, 0), (0, wide - span)),
            ),
            jnp.pad(
                jnp.stack(
                    [gain_one_local.reshape(fsdp, shard), gain_two_local.reshape(fsdp, shard)],
                    axis=1,
                ).astype(BF16),
                ((0, 0), (0, 14), (0, wide - shard)),
            ),
        ],
        axis=1,
    )
    qkv_sum, out_proj_sum, small_sum, out_sum = dense_reduce(
        [halves(qkv_local), halves(out_local), small_local],
        out_own,
        out_right,
        out_left,
        DENSE_PIECE,
        fsdp,
        chips,
        4,
    )
    edge = width + 2 * kv_width
    qkv_grads = qkv_sum.reshape(shard, -1)
    out_proj_grad = out_proj_sum.reshape(shard, -1)[:, :width]
    gate_grad_out, up_grad_out, down_grad_out = (
        after(part, pre_grad)[0].astype(F32) for part in expert_grads
    )
    result = middle + out_sum
    return (
        result.astype(BF16)[None],
        input_grad[None],
        small_sum[1, 0, :shard].astype(F32),
        small_sum[1, 1, :shard].astype(F32),
        qkv_grads[:, :width].astype(F32),
        qkv_grads[:, width : width + kv_width].astype(F32),
        qkv_grads[:, width + kv_width : edge].astype(F32),
        out_proj_grad.astype(F32),
        small_sum[0, :, :span].reshape(shard, expert_count).astype(F32),
        gate_grad_out,
        up_grad_out,
        down_grad_out,
    )


def solution(mesh):
    placed = (
        P("fsdp", "ctx", None),
        P("fsdp", "ctx", None),
        P("fsdp", None),
        P("fsdp", None),
        P("fsdp", "ctx", None),
        P("fsdp"),
        P("fsdp"),
        P("fsdp", None),
        P("fsdp", None),
        P("fsdp", None),
        P("fsdp", None),
        P("fsdp", None),
        P("ctx", "fsdp", None),
        P("ctx", "fsdp", None),
        P("ctx", None, "fsdp"),
    )
    return jax.shard_map(
        body,
        mesh=mesh,
        in_specs=placed,
        out_specs=(
            P("fsdp", "ctx", None),
            P("fsdp", "ctx", None),
            P("fsdp"),
            P("fsdp"),
            P("fsdp", None),
            P("fsdp", None),
            P("fsdp", None),
            P("fsdp", None),
            P("fsdp", None),
            P("ctx", "fsdp", None),
            P("ctx", "fsdp", None),
            P("ctx", None, "fsdp"),
        ),
        check_vma=False,
    )
```

```python
import functools

import jax
import jax.numpy as jnp
from jax import lax
from jax.experimental import pallas as pl
from jax.experimental.pallas import tpu as pltpu
from jax.sharding import PartitionSpec as P

QUERY_HEADS = 12
KVH = 2
HEAD_SIZE = 128

EPSILON = 1e-06
ROPE_BASE = 10000.0
MASKED = -1e30
LOG2E = 1.4426950408889634
LANES = 128
SLOT_STEP = 64
DENSE_PIECE = 1024
LINE_TASK = 4
KEY_TILE = 512
VMEM_BYTES = 56 * 1024 * 1024
EXPERT_VMEM_BYTES = 119 * 512 * 1024
BACK_VMEM_BYTES = 61 * 1024 * 1024
FRONT_VMEM_BYTES = 40 * 1024 * 1024
MESH = pl.DeviceIdType.MESH
F32 = jnp.float32
BF16 = jnp.bfloat16


def dot(left, right, contract):
    return lax.dot_general(left, right, (contract, ((), ())), preferred_element_type=F32)


NN = ((1,), (0,))
NT = ((1,), (1,))
TN = ((0,), (0,))


def rms_scale(value_rows, gain):
    return (
        value_rows
        * lax.rsqrt(jnp.mean(value_rows * value_rows, axis=-1, keepdims=True) + EPSILON)
        * gain
    )


def rotate(value_rows, cosine, sine):
    half_dim = value_rows.shape[-1] // 2
    first = value_rows[..., :half_dim]
    second = value_rows[..., half_dim:]
    return jnp.concatenate(
        [first * cosine - second * sine, second * cosine + first * sine], axis=-1
    )


def place():
    ctx = lax.axis_index("ctx")
    core = lax.rem(ctx, 2)
    return ctx, lax.axis_index("fsdp"), ctx // 2, core, ctx + 1 - 2 * core


def peers_of(me, fsdp):
    peers = []
    for shift in range(1, fsdp):
        peer = me
        for bit in range(fsdp.bit_length() - 1):
            if (shift >> bit) & 1:
                digit = lax.rem(me // (1 << bit), 2)
                peer = peer + (1 << bit) - (2 << bit) * digit
        peers.append(peer)
    return peers


def greet(chips, peers, line):
    ctx, me, chip, core, sibling = place()
    barrier = pltpu.get_barrier_semaphore()
    for peer in peers:
        pl.semaphore_signal(barrier, inc=1, device_id=(ctx, peer), device_id_type=MESH)
    pl.semaphore_signal(barrier, inc=1, device_id=(sibling, me), device_id_type=MESH)
    known = len(peers) + 1
    if not line:
        pl.semaphore_wait(barrier, known)
        return
    has_right = chip + 1 < chips
    has_left = chip >= 1

    @pl.when(has_right)
    def _():
        pl.semaphore_signal(barrier, inc=1, device_id=(ctx + 2, me), device_id_type=MESH)

    @pl.when(has_left)
    def _():
        pl.semaphore_signal(barrier, inc=1, device_id=(ctx - 2, me), device_id_type=MESH)

    @pl.when(has_right & has_left)
    def _():
        pl.semaphore_wait(barrier, known + 2)

    @pl.when(jnp.logical_not(has_right & has_left))
    def _():
        pl.semaphore_wait(barrier, known + 1)


class Bounce:
    def __init__(self, src, dst, buffer, sem):
        self.inward = pltpu.make_async_copy(src, buffer, sem)
        self.outward = pltpu.make_async_copy(buffer, dst, sem)

    def start(self):
        self.inward.start()

    def turn(self):
        self.inward.wait()
        self.outward.start()

    def wait(self):
        self.outward.wait()


def remote(src, dst, send_sem, recv_sem, device):
    return pltpu.make_async_remote_copy(
        src_ref=src,
        dst_ref=dst,
        send_sem=send_sem,
        recv_sem=recv_sem,
        device_id=device,
        device_id_type=MESH,
    )


class DenseGather:
    def __init__(self, ins, outs, sems, fsdp):
        buffers, local_sem, send_sem, recv_sem, pass_sem, took_sem = sems
        ctx, me, chip, core, sibling = place()
        self.sends, self.passes, self.locals = [], [], []
        for i in range(len(ins)):
            rows = ins[i].shape[0]
            half = rows // 2
            for j, peer in enumerate(peers_of(me, fsdp)):
                self.sends.append(
                    remote(
                        ins[i].at[pl.ds(core * half, half)],
                        outs[i].at[pl.ds(me * rows + core * half, half)],
                        send_sem.at[i, j],
                        recv_sem.at[i, j],
                        (ctx, peer),
                    )
                )
                got = outs[i].at[pl.ds(peer * rows + core * half, half)]
                self.passes.append(
                    remote(got, got, pass_sem.at[i, j], took_sem.at[i, j], (sibling, me))
                )
            self.locals.append(
                Bounce(ins[i], outs[i].at[pl.ds(me * rows, rows)], buffers[i], local_sem.at[i])
            )

    def start(self):
        for copy in self.sends + self.locals:
            copy.start()

    def finish(self):
        for copy in self.locals:
            copy.turn()
        for send, copy in zip(self.sends, self.passes):
            send.wait_recv()
            copy.start()
        for send in self.sends:
            send.wait_send()
        for copy in self.passes + self.locals:
            copy.wait()


def dense_scratch(arrays, fsdp):
    count = len(arrays)
    return (
        [pltpu.VMEM(a.shape, a.dtype) for a in arrays]
        + [pltpu.SemaphoreType.DMA((count,))]
        + [pltpu.SemaphoreType.DMA((count, fsdp - 1)) for unused in range(4)]
    )


class LineGather:
    def __init__(self, ins, outs, sems, chips):
        self.ins, self.outs, self.chips = ins, outs, chips
        self.buffers, self.sems = sems[:-7], sems[-7:]
        self.ctx, self.me, self.chip, core, self.sibling = place()
        self.count = len(ins)

    def to_right(self, i, step):
        outs, chips = self.outs, self.chips
        return remote(
            self.ins[i] if step == 0 else outs[i].at[0, chips - step],
            outs[i].at[0, chips - 1 - step],
            self.sems[1].at[i, step],
            self.sems[2].at[i, step],
            (self.ctx + 2, self.me),
        )

    def to_left(self, i, step):
        outs = self.outs
        return remote(
            self.ins[i] if step == 0 else outs[i].at[0, step],
            outs[i].at[0, step + 1],
            self.sems[3].at[i, step],
            self.sems[4].at[i, step],
            (self.ctx - 2, self.me),
        )

    def across(self, i, slot):
        return remote(
            self.ins[i] if slot == 0 else self.outs[i].at[0, slot],
            self.outs[i].at[1, slot],
            self.sems[5].at[i, slot],
            self.sems[6].at[i, slot],
            (self.sibling, self.me),
        )

    def local(self, i):
        return Bounce(self.ins[i], self.outs[i].at[0, 0], self.buffers[i], self.sems[0].at[i])

    def send(self, step):
        chip, chips, count = self.chip, self.chips, self.count

        @pl.when((chip + 1 < chips) & (chip >= step))
        def _():
            for i in range(count):
                self.to_right(i, step).start()

        @pl.when((chip >= 1) & (chip + step < chips))
        def _():
            for i in range(count):
                self.to_left(i, step).start()

    def receive(self, step):
        chip, chips, count = self.chip, self.chips, self.count

        @pl.when(chip >= step + 1)
        def _():
            for i in range(count):
                self.to_right(i, step).wait_recv()
                self.across(i, chips - 1 - step).start()

        @pl.when(chip + step + 1 < chips)
        def _():
            for i in range(count):
                self.to_left(i, step).wait_recv()
                self.across(i, step + 1).start()

    def own(self):
        for i in range(self.count):
            self.across(i, 0).start()
            self.local(i).start()

    def turn_own(self):
        for i in range(self.count):
            self.local(i).turn()

    def finish_own(self):
        for i in range(self.count):
            self.across(i, 0).wait()
            self.local(i).wait()

    def arrived(self, slot):
        for i in range(self.count):
            remote(
                self.outs[i].at[0, slot],
                self.outs[i].at[1, slot],
                self.sems[5].at[i, slot],
                self.sems[6].at[i, slot],
                (self.sibling, self.me),
            ).wait_recv()

    def sent(self):
        chip, chips, count = self.chip, self.chips, self.count
        for step in range(chips - 1):

            @pl.when((chip + 1 < chips) & (chip >= step))
            def _():
                for i in range(count):
                    self.to_right(i, step).wait_send()

            @pl.when((chip >= 1) & (chip + step < chips))
            def _():
                for i in range(count):
                    self.to_left(i, step).wait_send()

        for slot in range(chips):
            for i in range(count):
                self.across(i, slot).wait_send()

    def finish(self, step):
        chip, chips, count = self.chip, self.chips, self.count

        @pl.when((chip + 1 < chips) & (chip >= step))
        def _():
            for i in range(count):
                self.to_right(i, step).wait_send()

        @pl.when((chip >= 1) & (chip + step < chips))
        def _():
            for i in range(count):
                self.to_left(i, step).wait_send()

        @pl.when(chip >= step + 1)
        def _():
            for i in range(count):
                self.across(i, chips - 1 - step).wait()

        @pl.when(chip + step + 1 < chips)
        def _():
            for i in range(count):
                self.across(i, step + 1).wait()


def line_scratch(arrays, chips):
    count = len(arrays)
    return (
        [pltpu.VMEM(a.shape, a.dtype) for a in arrays if a is not None]
        + [pltpu.SemaphoreType.DMA((count,))]
        + [pltpu.SemaphoreType.DMA((count, chips - 1)) for unused in range(4)]
        + [pltpu.SemaphoreType.DMA((count, chips)) for unused in range(2)]
    )


def gather_kernel(dense, line, resumed, steps, fsdp, chips, *refs):
    count = dense + line + resumed
    ins, outs, scratch = refs[:count], refs[count : 2 * count], refs[2 * count :]
    ctx, me, chip, core, sibling = place()
    greet(chips, peers_of(me, fsdp) if dense else [], line > 0)
    split = dense + line
    if dense:
        own, scratch = scratch[: dense + 5], scratch[dense + 5 :]
        first = DenseGather(
            ins[:dense], outs[:dense], (own[:dense],) + tuple(own[dense:]), fsdp
        )
        first.start()
    if line:
        own, scratch = scratch[: line + 7], scratch[line + 7 :]
        second = LineGather(ins[dense:split], outs[dense:split], own, chips)
        for step in range(steps):
            second.send(step)
            if step == 0:
                second.own()
            second.receive(step)
            if step == 0:
                second.turn_own()
    if resumed:
        third = LineGather([None], outs[split:], scratch, chips)
        third.send(chips - 2)
        third.receive(chips - 2)
    if dense:
        first.finish()
    if line:
        second.finish_own()
        for step in range(steps):
            second.finish(step)
    if resumed:
        third.finish(chips - 2)


def gather(dense, line, steps, fsdp, chips, collective_id, resumed=()):
    arrays = list(dense) + list(line) + list(resumed)
    count = len(arrays)
    scratch = (dense_scratch(dense, fsdp) if dense else []) + (
        line_scratch(line, chips) if line else []
    )
    if resumed:
        scratch = scratch + line_scratch([None], chips)
    return pl.pallas_call(
        functools.partial(
            gather_kernel, len(dense), len(line), len(resumed), steps, fsdp, chips
        ),
        out_shape=[jax.ShapeDtypeStruct((fsdp * a.shape[0],) + a.shape[1:], a.dtype) for a in dense]
        + [jax.ShapeDtypeStruct((2, chips) + a.shape, a.dtype) for a in line]
        + [jax.ShapeDtypeStruct(a.shape, a.dtype) for a in resumed],
        in_specs=[pl.BlockSpec(memory_space=pl.ANY)] * count,
        out_specs=[pl.BlockSpec(memory_space=pl.ANY)] * count,
        scratch_shapes=scratch,
        input_output_aliases={count - 1: count - 1} if resumed else {},
        compiler_params=pltpu.CompilerParams(
            collective_id=collective_id, has_side_effects=True, vmem_limit_bytes=VMEM_BYTES
        ),
        name="gather",
    )(*arrays)


def add(*parts):
    total = parts[0].astype(F32)
    for part in parts[1:]:
        total = total + part.astype(F32)
    return total


def add_into(target, parts):
    rows = target.shape[0]
    tile = 32 if rows % 32 == 0 else 16

    def some(t, carry):
        part = pl.ds(pl.multiple_of(t * tile, tile), tile)
        target[part, :] = add(*[ref[part, :] for ref in parts]).astype(target.dtype)
        return carry

    lax.fori_loop(0, rows // tile, some, 0)


class LineSum:
    def __init__(self, chips, held, keep, got, sems):
        self.chips, self.held, self.keep, self.got = chips, held, keep, got
        self.sems = sems
        self.ctx, self.me, self.chip, core, sibling = place()

    def right(self, step):
        return remote(
            self.keep(self.chips - 1 - step),
            self.got.at[step - self.chip],
            self.sems[0].at[step],
            self.sems[1].at[step],
            (self.ctx + 2, self.me),
        )

    def from_left(self, step):
        slot = step + 1 - self.chip
        pltpu.make_async_remote_copy(
            src_ref=self.keep(self.chips - 1 - step),
            dst_ref=self.got.at[slot],
            send_sem=self.sems[0].at[step],
            recv_sem=self.sems[1].at[step],
            device_id=(self.ctx - 2, self.me),
            device_id_type=MESH,
        ).wait_recv()
        return self.got.at[slot]

    def from_right(self, step):
        slot = step + 2
        self.left(step).wait_recv()
        return self.got.at[slot]

    def left(self, step):
        return remote(
            self.keep(step + 1),
            self.got.at[step + 2],
            self.sems[2].at[step],
            self.sems[3].at[step],
            (self.ctx - 2, self.me),
        )

    def step(self, step):
        chip, chips = self.chip, self.chips
        far_right, far_left = chips - 1 - step, step + 1

        @pl.when(chip <= step)
        def _():
            parts = self.held(far_right)
            if step == 0:
                add_into(self.keep(far_right), parts())
            else:

                @pl.when(chip == 0)
                def _():
                    add_into(self.keep(far_right), parts())

                @pl.when(chip >= 1)
                def _():
                    add_into(self.keep(far_right), [self.from_left(step - 1)] + parts())

            self.right(step).start()

        @pl.when(chip >= chips - 1 - step)
        def _():
            parts = self.held(far_left)
            if step == 0:
                add_into(self.keep(far_left), parts())
            else:

                @pl.when(chip == chips - 1)
                def _():
                    add_into(self.keep(far_left), parts())

                @pl.when(chip < chips - 1)
                def _():
                    add_into(self.keep(far_left), [self.from_right(step - 1)] + parts())

            self.left(step).start()

    def total(self, target):
        chip, chips, last = self.chip, self.chips, self.chips - 2
        parts = self.held(0)

        @pl.when(chip == 0)
        def _():
            add_into(target, [self.from_right(last)] + parts())

        @pl.when(chip == chips - 1)
        def _():
            add_into(target, [self.from_left(last)] + parts())

        @pl.when((chip >= 1) & (chip < chips - 1))
        def _():
            add_into(target, [self.from_right(last), self.from_left(last)] + parts())

    def finish(self, steps=None):
        for step in range(self.chips - 1 if steps is None else steps):

            @pl.when(self.chip <= step)
            def _():
                self.right(step).wait_send()

            @pl.when(self.chip >= self.chips - 1 - step)
            def _():
                self.left(step).wait_send()


DENSE_BUFFERS = 5
DENSE_SEMS = 14


class DenseSum:
    def __init__(self, local, out, buffers, sems, fsdp, chips):
        self.local, self.out = local, out
        self.pair, self.cross, self.sums, got, self.spread = buffers
        self.sems = sems
        self.chips = chips
        self.ctx, self.me, self.chip, self.core, self.sibling = place()
        self.owners = peers_of(self.me, fsdp) + [self.me]
        self.cut = out.shape[2] // chips
        self.line = LineSum(
            chips,
            lambda r: lambda: [self.keep_ref(r)],
            lambda r: self.keep_ref(r),
            got,
            sems[4:8],
        )

    def keep_ref(self, r):
        return self.sums.at[:, self.columns(r)]

    def columns(self, r):
        owner = lax.rem(self.chip + r, self.chips)
        return pl.ds(pl.multiple_of(owner * self.cut, LANES), self.cut)

    def swap(self, j):
        return remote(
            self.local.at[self.owners[j], 1 - self.core],
            self.pair.at[j],
            self.sems[0].at[j],
            self.sems[1].at[j],
            (self.sibling, self.me),
        )

    def crossing(self, j):
        return remote(
            self.pair.at[j],
            self.cross.at[j],
            self.sems[2].at[j],
            self.sems[3].at[j],
            (self.ctx, self.owners[j]),
        )

    def to_right(self, step):
        return remote(
            self.spread.at[0, (self.chips - step) % self.chips],
            self.spread.at[0, self.chips - 1 - step],
            self.sems[8].at[step],
            self.sems[9].at[step],
            (self.ctx + 2, self.me),
        )

    def to_left(self, step):
        return remote(
            self.spread.at[0, step],
            self.spread.at[0, step + 1],
            self.sems[10].at[step],
            self.sems[11].at[step],
            (self.ctx - 2, self.me),
        )

    def across(self, slot):
        return remote(
            self.spread.at[0, slot],
            self.spread.at[1, slot],
            self.sems[12].at[slot],
            self.sems[13].at[slot],
            (self.sibling, self.me),
        )

    def start(self):
        for j in range(len(self.owners)):
            self.swap(j).start()

    def cross_over(self):
        for j, owner in enumerate(self.owners):
            self.swap(j).wait_recv()
            add_into(self.pair.at[j], [self.local.at[owner, self.core], self.pair.at[j]])
            if j < len(self.owners) - 1:
                self.crossing(j).start()

    def stages(self):
        chip, chips = self.chip, self.chips

        def open_up():
            for j in range(len(self.owners) - 1):
                self.crossing(j).wait_recv()
            add_into(
                self.sums,
                [self.cross.at[j] for j in range(len(self.owners) - 1)]
                + [self.pair.at[len(self.owners) - 1]],
            )
            self.line.step(0)

        def summed():
            self.line.total(self.spread.at[0, 0])
            hand_on(0)

        def hand_on(step):
            @pl.when((chip + 1 < chips) & (chip >= step))
            def _():
                self.to_right(step).start()

            @pl.when((chip >= 1) & (chip + step < chips))
            def _():
                self.to_left(step).start()

            if step == 0:
                self.across(0).start()

        def take(step):
            @pl.when(chip >= step + 1)
            def _():
                self.to_right(step).wait_recv()
                self.across(chips - 1 - step).start()

            @pl.when(chip + step + 1 < chips)
            def _():
                self.to_left(step).wait_recv()
                self.across(step + 1).start()

        def pass_on(step):
            def run():
                take(step - 1)
                hand_on(step)

            return run

        def line_step(step):
            return lambda: self.line.step(step)

        return (
            [open_up]
            + [line_step(step) for step in range(1, chips - 1)]
            + [summed]
            + [pass_on(step) for step in range(1, chips - 1)]
            + [lambda: take(chips - 2)]
        )

    def finish(self):
        chip, chips = self.chip, self.chips
        for r in range(chips):
            self.out[self.core, :, self.columns(r)] = self.spread[0, r]
        for r in range(chips):
            self.across(r).wait()
            self.out[1 - self.core, :, self.columns(r)] = self.spread[1, r]
        for step in range(chips - 1):

            @pl.when((chip + 1 < chips) & (chip >= step))
            def _():
                self.to_right(step).wait_send()

            @pl.when((chip >= 1) & (chip + step < chips))
            def _():
                self.to_left(step).wait_send()

        self.line.finish()
        for j in range(len(self.owners) - 1):
            self.crossing(j).wait_send()
        for j in range(len(self.owners)):
            self.swap(j).wait_send()


def dense_reduce_kernel(fsdp, chips, cuts, *refs):
    count = len(cuts)
    arrays = max(cut[0] for cut in cuts) + 1
    ins, refs = refs[:arrays], refs[arrays:]
    own_ref, right_ref, left_ref = refs[:3]
    outs, total_ref, refs = refs[3 : 3 + arrays], refs[3 + arrays], refs[4 + arrays :]
    from_left, from_right, r_send, r_recv, l_send, l_recv = refs[:6]
    rest = refs[6:]
    ctx, me, chip, core, sibling = place()
    greet(chips, peers_of(me, fsdp), True)

    to_right = remote(right_ref, from_left, r_send, r_recv, (ctx + 2, me))
    to_left = remote(left_ref, from_right, l_send, l_recv, (ctx - 2, me))

    @pl.when(chip + 1 < chips)
    def _():
        to_right.start()

    @pl.when(chip >= 1)
    def _():
        to_left.start()

    sums = []
    for i, (which, start, size) in enumerate(cuts):
        buffers = rest[i * DENSE_BUFFERS : (i + 1) * DENSE_BUFFERS]
        sems = rest[count * DENSE_BUFFERS + i * DENSE_SEMS :][:DENSE_SEMS]
        sums.append(
            DenseSum(
                ins[which].at[:, :, :, pl.ds(start, size)],
                outs[which].at[:, :, pl.ds(start, size)],
                buffers,
                sems,
                fsdp,
                chips,
            )
        )
    for one in sums:
        one.start()
    for one in sums:
        one.cross_over()
    stages = [one.stages() for one in sums]
    lag = chips - 1
    for tick in range(len(stages[0]) + lag * (count - 1)):
        for i in range(count):
            if 0 <= tick - lag * i < len(stages[i]):
                stages[i][tick - lag * i]()
    @pl.when(chip >= 1)
    def _():
        to_right.wait_recv()

    @pl.when(chip + 1 < chips)
    def _():
        to_left.wait_recv()

    @pl.when(chip == 0)
    def _():
        add_into(total_ref, [from_right, own_ref])

    @pl.when(chip == chips - 1)
    def _():
        add_into(total_ref, [from_left, own_ref])

    @pl.when((chip >= 1) & (chip + 1 < chips))
    def _():
        add_into(total_ref, [from_left, from_right, own_ref])

    for one in sums:
        one.finish()

    @pl.when(chip + 1 < chips)
    def _():
        to_right.wait_send()

    @pl.when(chip >= 1)
    def _():
        to_left.wait_send()


def dense_reduce(arrays, own, right, left, piece, fsdp, chips, collective_id):
    vmem = pl.BlockSpec(memory_space=pltpu.VMEM)
    cuts, buffers = [], []
    for i, a in enumerate(arrays):
        rows, width = a.shape[2:]
        for start in range(0, width, piece):
            size = min(piece, width - start)
            cut = size // chips
            cuts.append((i, start, size))
            buffers += [
                pltpu.VMEM((fsdp, rows, size), BF16),
                pltpu.VMEM((fsdp - 1, rows, size), BF16),
                pltpu.VMEM((rows, size), BF16),
                pltpu.VMEM((chips + 1, rows, cut), BF16),
                pltpu.VMEM((2, chips, rows, cut), BF16),
            ]
    sems = (
        [pltpu.SemaphoreType.DMA((fsdp,)) for unused in range(2)]
        + [pltpu.SemaphoreType.DMA((fsdp - 1,)) for unused in range(2)]
        + [pltpu.SemaphoreType.DMA((chips - 1,)) for unused in range(8)]
        + [pltpu.SemaphoreType.DMA((chips,)) for unused in range(2)]
    )
    return pl.pallas_call(
        functools.partial(dense_reduce_kernel, fsdp, chips, tuple(cuts)),
        out_shape=[jax.ShapeDtypeStruct(a.shape[1:], BF16) for a in arrays]
        + [jax.ShapeDtypeStruct(own.shape, F32)],
        in_specs=[vmem] * len(arrays) + [vmem, pl.BlockSpec(memory_space=pl.ANY)]
        + [pl.BlockSpec(memory_space=pl.ANY)],
        out_specs=[vmem] * (len(arrays) + 1),
        scratch_shapes=[pltpu.VMEM(own.shape, BF16)] * 2
        + [pltpu.SemaphoreType.DMA] * 4
        + buffers
        + sems * len(cuts),
        compiler_params=pltpu.CompilerParams(
            collective_id=collective_id, has_side_effects=True, vmem_limit_bytes=VMEM_BYTES
        ),
        name="dense_reduce",
    )(*arrays, own, right, left)


def after(value, *others):
    return lax.optimization_barrier((value,) + others)[0]


def chunk_order(chip, i, chips):
    right_half = lax.div(2 * chip, chips)
    near = chip + right_half * (chips - 1 - 2 * chip)
    alone = chips - 1 - 2 * near
    paired = lax.div(i - alone + chips, chips)
    turn = (i - alone) * paired
    odd = lax.rem(turn, 2)
    pair = lax.div(turn, 2)
    distance = (1 - paired) * (chips - 1 - near - i) + paired * (
        (1 - odd) * (near - pair) + odd * (chips - near + pair)
    )
    return lax.rem(distance + right_half * (chips - 2 * distance), chips)


def front_kernel(
    scale,
    chips,
    expert_count,
    tokens_ref,
    gain_a_ref,
    gain_b_ref,
    small_ref,
    cos_ref,
    sin_ref,
    oq_ref,
    pq_ref,
    ok_ref,
    routed_ref,
    table_ref,
    qkv_ref,
    wo_ref,
    passed_ref,
    q_ref,
    normed_ref,
    kv_ref,
    table_all_ref,
    attended_ref,
    lse_ref,
    middle_ref,
    gate_ref,
    weights_ref,
    hidden_all_ref,
    grad_ref,
    qkv_v,
    wo_v,
    hidden_v,
    bias,
    top,
    total,
    acc,
    load_sem,
    own_sem,
    *line_sems,
):
    ctx, me, chip, core, sibling = place()
    rows = tokens_ref.shape[0]
    width = tokens_ref.shape[1]
    half = rows // 2
    kv_width = KVH * HEAD_SIZE
    per_group = QUERY_HEADS // KVH
    parts = [pl.ds(0, half), pl.ds(half, half)]
    loads = [
        pltpu.make_async_copy(src, dst, load_sem.at[k])
        for k, (src, dst) in enumerate(((qkv_ref, qkv_v), (wo_ref, wo_v)))
    ]
    for copy in loads:
        copy.start()
    greet(chips, [], True)
    kv_line = LineGather(
        [kv_ref.at[0, 0], table_all_ref.at[0, 0]], [kv_ref, table_all_ref], line_sems[:7], chips
    )
    grad_line = LineGather([None], [grad_ref], line_sems[7:14], chips)
    hidden_lines = [
        LineGather(
            [hidden_v.at[parts[0]]], [hidden_all_ref.at[:, :, parts[0]]], line_sems[14:21], chips
        ),
        LineGather(
            [hidden_v.at[parts[1]], weights_ref.at[0, 0]],
            [hidden_all_ref.at[:, :, parts[1]], weights_ref],
            line_sems[21:28],
            chips,
        ),
    ]

    def normed(value, gain):
        return value * lax.rsqrt(jnp.mean(value * value, axis=-1, keepdims=True) + EPSILON) * gain

    table_all_ref[0, 0] = table_ref[...]
    for part in parts:
        normed_ref[part, :] = normed(
            tokens_ref[part, :].astype(F32), gain_a_ref[...]
        ).astype(BF16)
    loads[0].wait()
    for part in parts:
        rows_one = normed_ref[part, :]
        cosine, sine = cos_ref[part, :], sin_ref[part, :]
        for h in range(KVH):
            columns = slice(width + h * HEAD_SIZE, width + (h + 1) * HEAD_SIZE)
            value = dot(rows_one, qkv_v[:, columns], NN)
            value = value * cosine + pltpu.roll(value, HEAD_SIZE // 2, 1) * sine
            kv_ref[0, 0, part, h * HEAD_SIZE : (h + 1) * HEAD_SIZE] = value.astype(BF16)
        kv_ref[0, 0, part, kv_width:] = dot(
            rows_one, qkv_v[:, width + kv_width :], NN
        ).astype(BF16)
    kv_line.send(0)
    for i in range(2):
        kv_line.across(i, 0).start()
    for part in parts:
        rows_one = normed_ref[part, :]
        cosine, sine = cos_ref[part, :], sin_ref[part, :]
        for h in range(0, QUERY_HEADS, 2):
            pre = dot(rows_one, qkv_v[:, h * HEAD_SIZE : (h + 2) * HEAD_SIZE], NN)
            for k in range(2):
                value = pre[:, k * HEAD_SIZE : (k + 1) * HEAD_SIZE]
                value = value * cosine + pltpu.roll(value, HEAD_SIZE // 2, 1) * sine
                q_ref[part, (h + k) * HEAD_SIZE : (h + k + 1) * HEAD_SIZE] = value.astype(BF16)

    def turn(index, r):
        part = parts[index]
        for q in range(2):
            gap = oq_ref[part, :] - ok_ref[q * chips + r]
            bias[:, q * rows : (q + 1) * rows] = jnp.where(
                (gap >= 0) & (gap <= pq_ref[part, :]), 0.0, MASKED
            )

        def one(h, carry):
            group = lax.div(h, per_group)
            columns = pl.ds(pl.multiple_of(h * HEAD_SIZE, HEAD_SIZE), HEAD_SIZE)
            key_columns = pl.ds(pl.multiple_of(group * HEAD_SIZE, HEAD_SIZE), HEAD_SIZE)
            value_columns = pl.ds(
                pl.multiple_of(kv_width + group * HEAD_SIZE, HEAD_SIZE), HEAD_SIZE
            )
            query = q_ref[part, columns]
            scores = []
            peak = top[h, part, :]
            for q in range(2):
                raw = dot(query, kv_ref[q, r, :, key_columns], NT) * (scale * LOG2E)
                raw = raw + bias[:, q * rows : (q + 1) * rows]
                scores.append(raw)
            best = scores[0][:, :LANES]
            for q in range(2):
                for k in range(rows // LANES):
                    best = jnp.maximum(best, scores[q][:, k * LANES : (k + 1) * LANES])
            new = jnp.maximum(peak, jnp.max(best, axis=1, keepdims=True))
            fade = jnp.exp2(peak - new)
            wide = jnp.concatenate([new] * (rows // LANES), axis=1)
            mass = total[h] * fade
            out = acc[:, columns] * fade
            for q in range(2):
                probs = jnp.exp2(scores[q] - wide)
                for k in range(rows // LANES):
                    mass = mass + probs[:, k * LANES : (k + 1) * LANES]
                out = out + dot(probs.astype(BF16), kv_ref[q, r, :, value_columns], NN)
            top[h, part, :] = new
            total[h] = mass
            acc[:, columns] = out
            return carry

        lax.fori_loop(0, QUERY_HEADS, one, 0)

    def begin(index):
        top[:, parts[index], :] = jnp.full((QUERY_HEADS, half, LANES), MASKED, F32)
        total[...] = jnp.zeros_like(total)
        acc[...] = jnp.zeros_like(acc)

    def end(index):
        part = parts[index]
        for h in range(QUERY_HEADS):
            columns = slice(h * HEAD_SIZE, (h + 1) * HEAD_SIZE)
            mass = jnp.sum(total[h], axis=1, keepdims=True)
            attended_ref[part, columns] = (acc[:, columns] / mass).astype(BF16)
            top[h, part, :] = top[h, part, :] + jnp.log2(mass)
        if index == 0:
            loads[1].wait()
        middle = tokens_ref[part, :].astype(F32) + dot(attended_ref[part, :], wo_v[...], NN)
        middle_ref[part, :] = middle
        rows_two = normed(middle, gain_b_ref[...]).astype(BF16)
        hidden_v[part, :] = rows_two
        routed = routed_ref[part, :] > 0.0
        logits = jnp.where(routed, dot(rows_two, small_ref[...], NN), MASKED)
        power = jnp.exp(logits - jnp.max(logits, axis=1, keepdims=True))
        power = jnp.where(routed, power, 0.0)
        gate_ref[part, :] = power / jnp.sum(power, axis=1, keepdims=True)
        if index == 1:
            weights_ref[0, 0] = gate_ref[...].T[:expert_count, :]
        line = hidden_lines[index]
        line.send(0)
        for i in range(line.count):
            line.across(i, 0).start()
        own(index).start()

    def own(index):
        return pltpu.make_async_copy(
            hidden_v.at[parts[index]],
            hidden_all_ref.at[0, 0, parts[index]],
            own_sem.at[index],
        )

    begin(0)

    def first_turn(t, carry):
        for k in range(1, chips):

            @pl.when(t == k)
            def _():
                kv_line.receive(k - 1)
                if k < chips - 1:
                    kv_line.send(k)
                else:
                    grad_line.send(chips - 2)

        r = chunk_order(chip, chips - 1 - t, chips)
        kv_line.arrived(r)
        turn(0, r)
        return carry

    lax.fori_loop(0, chips, first_turn, 0)
    end(0)
    begin(1)
    early = [step for step in range(chips - 1) if 2 * step + 2 < chips]

    def second_turn(t, carry):
        for step in early:

            @pl.when(t == 2 * step + 2)
            def _():
                hidden_lines[0].receive(step)
                if step + 1 < chips - 1:
                    hidden_lines[0].send(step + 1)

        turn(1, t)
        return carry

    lax.fori_loop(0, chips, second_turn, 0)
    grad_line.receive(chips - 2)
    late = [step for step in range(chips - 1) if step not in early]
    for step in late[:1]:
        hidden_lines[0].receive(step)
        if step + 1 < chips - 1:
            hidden_lines[0].send(step + 1)
    end(1)
    for h in range(QUERY_HEADS):
        lse_ref[h] = top[h].T[:1, :]
    for step in late[1:]:
        hidden_lines[0].receive(step)
        if step + 1 < chips - 1:
            hidden_lines[0].send(step + 1)
    for step in range(chips - 1):
        hidden_lines[1].receive(step)
        if step + 1 < chips - 1:
            hidden_lines[1].send(step + 1)
    for line in hidden_lines:
        for slot in range(chips):
            line.arrived(slot)
        line.sent()
    kv_line.sent()
    grad_line.finish(chips - 2)
    for index in range(2):
        own(index).wait()


def front(
    tokens,
    gain_a,
    gain_b,
    small,
    cosine,
    sine,
    order_mine,
    pos_mine,
    order_keys,
    routed,
    table,
    qkv,
    w_out,
    grad_all,
    chips,
    collective_id,
):
    rows, width = tokens.shape
    expert_count = table.shape[0]
    kv_width = KVH * HEAD_SIZE
    vmem = pl.BlockSpec(memory_space=pltpu.VMEM)
    anywhere = pl.BlockSpec(memory_space=pl.ANY)
    shapes = [
        ((rows, width), BF16),
        ((rows, width), BF16),
        ((2, chips, rows, 2 * kv_width), BF16),
        ((2, chips, expert_count, rows), F32),
        ((rows, width), BF16),
        ((QUERY_HEADS, 1, rows), F32),
        ((rows, width), F32),
        ((rows, LANES), F32),
        ((2, chips, expert_count, rows), F32),
        ((2, chips, rows, width), BF16),
        (grad_all.shape, BF16),
    ]
    flops = 4 * rows * (2 * chips * rows) * width + 2 * rows * width * (2 * width + 2 * kv_width)
    return pl.pallas_call(
        functools.partial(front_kernel, HEAD_SIZE ** (-0.5), chips, expert_count),
        out_shape=[jax.ShapeDtypeStruct(shape, kind) for shape, kind in shapes],
        in_specs=[vmem] * 11 + [anywhere] * 3,
        out_specs=[vmem] * 9 + [anywhere] * 2,
        scratch_shapes=[
            pltpu.VMEM(qkv.shape, BF16),
            pltpu.VMEM(w_out.shape, BF16),
            pltpu.VMEM((rows, width), BF16),
            pltpu.VMEM((rows // 2, 2 * rows), F32),
            pltpu.VMEM((QUERY_HEADS, rows, LANES), F32),
            pltpu.VMEM((QUERY_HEADS, rows // 2, LANES), F32),
            pltpu.VMEM((rows // 2, width), F32),
            pltpu.SemaphoreType.DMA((2,)),
            pltpu.SemaphoreType.DMA((2,)),
        ]
        + line_scratch([None] * 2, chips)
        + line_scratch([None], chips)
        + line_scratch([None], chips)
        + line_scratch([None] * 2, chips),
        input_output_aliases={13: 10},
        compiler_params=pltpu.CompilerParams(
            collective_id=collective_id, has_side_effects=True, vmem_limit_bytes=FRONT_VMEM_BYTES
        ),
        cost_estimate=pl.CostEstimate(
            flops=flops, bytes_accessed=40_000_000, transcendentals=rows * rows * chips * 24
        ),
        name="front",
    )(
        tokens,
        gain_a[None, :],
        gain_b[None, :],
        small,
        cosine,
        sine,
        order_mine[:, None],
        pos_mine[:, None],
        order_keys.reshape(2 * chips, 1, rows),
        routed,
        table,
        qkv,
        w_out,
        grad_all,
    )


def attention_back_kernel(
    scale,
    chips,
    q_ref,
    k_ref,
    v_ref,
    o_ref,
    do_ref,
    lse_ref,
    oq_ref,
    pq_ref,
    ok_ref,
    mine_ref,
    other_ref,
    dq_ref,
    kv_ref,
    own_ref,
    right_ref,
    left_ref,
    bias,
    dk_acc,
    dv_acc,
    mine_v,
    pair,
    got,
    kv_v,
    kv_pair,
    kv_got,
    load_sem,
    store_sem,
    swap_send,
    swap_recv,
    r_send,
    r_recv,
    l_send,
    l_recv,
    kv_swap_send,
    kv_swap_recv,
    kr_send,
    kr_recv,
    kl_send,
    kl_recv,
):
    ctx, me, chip, core, sibling = place()
    keys = k_ref.shape[0]
    tiles = keys // KEY_TILE
    rows = q_ref.shape[0]
    per_group = QUERY_HEADS // KVH
    head = pl.program_id(0)

    order = []
    for step in range(chips - 1):
        for r in (chips - 1 - step, step + 1):
            if r not in order:
                order.append(r)
    order.append(0)
    swaps = [
        remote(other_ref.at[r], pair.at[r], swap_send.at[r], swap_recv.at[r], (sibling, me))
        for r in range(chips)
    ]
    loads = [
        pltpu.make_async_copy(mine_ref.at[r], mine_v.at[j % 2], load_sem.at[j % 2])
        for j, r in enumerate(order)
    ]
    line = LineSum(
        chips,
        lambda r: lambda: [pair.at[r]],
        lambda r: pair.at[r],
        got,
        (r_send, r_recv, l_send, l_recv),
    )

    def join(j):
        loads[j].wait()
        swaps[order[j]].wait_recv()
        add_into(pair.at[order[j]], [pair.at[order[j]], mine_v.at[j % 2]])
        if j + 2 < chips:
            loads[j + 2].start()

    def kv_swap(group, r):
        return remote(
            kv_v.at[group, 1, r],
            kv_pair.at[group, r],
            kv_swap_send.at[group, r],
            kv_swap_recv.at[group, r],
            (sibling, me),
        )

    def kv_line(group):
        def held(r):
            kv_swap(group, r).wait_recv()
            return lambda: [kv_v.at[group, 0, r], kv_pair.at[group, r]]

        return LineSum(
            chips,
            held,
            lambda r: kv_pair.at[group, r],
            kv_got.at[group],
            tuple(sem.at[group] for sem in (kr_send, kr_recv, kl_send, kl_recv)),
        )

    def kv_start(group):
        for q in range(2):
            for r in range(chips):
                part = pl.ds((q * chips + r) * rows, rows)
                kv_v[group, q, r, :, :HEAD_SIZE] = (dk_acc[part, :] * scale).astype(BF16)
                kv_v[group, q, r, :, HEAD_SIZE:] = dv_acc[part, :].astype(BF16)
        for r in order:
            kv_swap(group, r).start()

    @pl.when(head == 0)
    def _():
        greet(chips, [], True)
        for r in order:
            swaps[r].start()
        for copy in loads[:2]:
            copy.start()

        def fill(t, carry):
            tile = pl.ds(pl.multiple_of(t * KEY_TILE, KEY_TILE), KEY_TILE)
            gap = oq_ref[...] - ok_ref[tile, :]
            bias[tile, :] = jnp.where((gap >= 0) & (gap <= pq_ref[...]), 0.0, MASKED)
            return carry

        lax.fori_loop(0, tiles, fill, 0)

    @pl.when(lax.rem(head, per_group) == 0)
    def _():
        dk_acc[...] = jnp.zeros_like(dk_acc)
        dv_acc[...] = jnp.zeros_like(dv_acc)

    query = q_ref[...]
    grad = do_ref[...]
    lse = lse_ref[0]
    product = grad.astype(F32) * o_ref[...].astype(F32)
    delta = jnp.sum(product.T, axis=0, keepdims=True)

    def step(t, acc):
        tile = pl.ds(pl.multiple_of(t * KEY_TILE, KEY_TILE), KEY_TILE)
        key = k_ref[tile, :]
        raw = dot(key, query, NT) * (scale * LOG2E) + bias[tile, :]
        probs = jnp.exp2(raw - lse)
        prob_grad = dot(v_ref[tile, :], grad, NT)
        score_grad = (probs * (prob_grad - delta)).astype(BF16)
        dv_acc[tile, :] += dot(probs.astype(BF16), grad, NN)
        dk_acc[tile, :] += dot(score_grad, query, NN)
        return acc + dot(score_grad, key, TN)

    acc = lax.fori_loop(0, tiles, step, jnp.zeros((rows, HEAD_SIZE), F32))
    dq_ref[...] = acc * scale

    last = QUERY_HEADS - 1
    stride = max(1, last // (chips - 2))
    early = {per_group + 2 * s: s for s in range(chips - 1) if per_group + 2 * s < last}
    for h in range(QUERY_HEADS):

        @pl.when(head == h)
        def _():
            if h == 0:
                for j in range(chips):
                    join(j)
            for s in range(chips - 2):
                if h == s * stride:
                    line.step(s)
            if h % per_group == per_group - 1:
                kv_start(h // per_group)
            if h in early:
                kv_line(0).step(early[h])

    @pl.when(head == last)
    def _():
        def store(k, r, target):
            return pltpu.make_async_copy(pair.at[r], target, store_sem.at[k])

        @pl.when((chip >= 1) & (chip + 1 < chips))
        def _():
            add_into(pair.at[1], [pair.at[1], line.from_left(chips - 3)])
            add_into(pair.at[chips - 1], [pair.at[chips - 1], line.from_right(chips - 3)])

        for copy in (
            store(0, 0, own_ref),
            store(1, 1, right_ref),
            store(2, chips - 1, left_ref),
        ):
            copy.start()
        for group in range(KVH):
            one = kv_line(group)
            for s in range(chips - 1):
                if group > 0 or s not in early.values():
                    one.step(s)
            one.total(kv_ref.at[group])
        for group in range(KVH):
            kv_line(group).finish()
            for r in range(chips):
                kv_swap(group, r).wait_send()
        line.finish(chips - 2)
        for swap in swaps:
            swap.wait_send()
        for copy in (
            store(0, 0, own_ref),
            store(1, 1, right_ref),
            store(2, chips - 1, left_ref),
        ):
            copy.wait()


def attention_back(
    queries, kv, attended, attended_grad, lse, order_mine, pos_mine, order_keys, mine, other,
    collective_id
):
    rows = queries.shape[0]
    keys = kv.shape[0]
    chips, unused, width = mine.shape
    per_group = QUERY_HEADS // KVH
    head_rows = pl.BlockSpec((rows, HEAD_SIZE), lambda h: (0, h))
    anywhere = pl.BlockSpec(memory_space=pl.ANY)
    return pl.pallas_call(
        functools.partial(attention_back_kernel, HEAD_SIZE ** (-0.5), chips),
        grid=(QUERY_HEADS,),
        out_shape=[
            jax.ShapeDtypeStruct(queries.shape, F32),
            jax.ShapeDtypeStruct((KVH, rows, 2 * HEAD_SIZE), F32),
        ]
        + [jax.ShapeDtypeStruct((rows, width), BF16)] * 3,
        in_specs=[
            head_rows,
            pl.BlockSpec((keys, HEAD_SIZE), lambda h: (0, h // per_group)),
            pl.BlockSpec((keys, HEAD_SIZE), lambda h: (0, KVH + h // per_group)),
            head_rows,
            head_rows,
            pl.BlockSpec((1, 1, rows), lambda h: (h, 0, 0)),
            pl.BlockSpec((1, rows), lambda h: (0, 0)),
            pl.BlockSpec((1, rows), lambda h: (0, 0)),
            pl.BlockSpec((keys, 1), lambda h: (0, 0)),
            anywhere,
            anywhere,
        ],
        out_specs=[
            head_rows,
            pl.BlockSpec((KVH, rows, 2 * HEAD_SIZE), lambda h: (0, 0, 0)),
            anywhere,
            anywhere,
            anywhere,
        ],
        scratch_shapes=[
            pltpu.VMEM((keys, rows), F32),
            pltpu.VMEM((keys, HEAD_SIZE), F32),
            pltpu.VMEM((keys, HEAD_SIZE), F32),
            pltpu.VMEM((2, rows, width), BF16),
            pltpu.VMEM((chips, rows, width), BF16),
            pltpu.VMEM((chips + 1, rows, width), BF16),
            pltpu.VMEM((KVH, 2, chips, rows, 2 * HEAD_SIZE), BF16),
            pltpu.VMEM((KVH, chips, rows, 2 * HEAD_SIZE), BF16),
            pltpu.VMEM((KVH, chips + 1, rows, 2 * HEAD_SIZE), BF16),
            pltpu.SemaphoreType.DMA((2,)),
            pltpu.SemaphoreType.DMA((3,)),
            pltpu.SemaphoreType.DMA((chips,)),
            pltpu.SemaphoreType.DMA((chips,)),
        ]
        + [pltpu.SemaphoreType.DMA((chips - 1,)) for unused in range(4)]
        + [pltpu.SemaphoreType.DMA((KVH, chips)) for unused in range(2)]
        + [pltpu.SemaphoreType.DMA((KVH, chips - 1)) for unused in range(4)],
        compiler_params=pltpu.CompilerParams(
            collective_id=collective_id, has_side_effects=True, vmem_limit_bytes=BACK_VMEM_BYTES
        ),
        cost_estimate=pl.CostEstimate(
            flops=10 * rows * keys * HEAD_SIZE * QUERY_HEADS,
            bytes_accessed=10 * rows * QUERY_HEADS * HEAD_SIZE + 8 * keys * KVH * HEAD_SIZE,
            transcendentals=rows * keys * QUERY_HEADS,
        ),
        name="attention_back",
    )(
        queries,
        kv,
        kv,
        attended,
        attended_grad,
        lse,
        order_mine[None, :],
        pos_mine[None, :],
        order_keys[:, None],
        mine,
        other,
    )


def experts_kernel(
    capacity,
    local_experts,
    expert_count,
    chips,
    fsdp,
    per,
    hidden_ref,
    grad_ref,
    table_ref,
    weight_ref,
    gate_ref,
    up_ref,
    down_ref,
    returned_ref,
    out_mine_ref,
    out_other_ref,
    gate_grad_ref,
    up_grad_ref,
    down_grad_ref,
    x_ref,
    pg_ref,
    inner_ref,
    da_ref,
    db_ref,
    gate_v,
    up_v,
    down_v,
    hidden_v,
    grad_v,
    out_v,
    x_v,
    pg_v,
    g_v,
    inner_v,
    da_v,
    db_v,
    mine_v,
    other_v,
    pair,
    got,
    stage_tall,
    weight_sem,
    load_sem,
    out_sem,
    save_sem,
    swap_send,
    swap_recv,
    right_send,
    right_recv,
    left_send,
    left_recv,
    stage_sem,
):
    ctx, me, chip, core, sibling = place()
    tokens = hidden_v.shape[1]
    width = hidden_v.shape[2]
    slots = x_v.shape[1]
    slot_rows = slots // 2
    units = inner_v.shape[2]
    total_rows = x_ref.shape[1]
    first = ctx * local_experts

    weights_in = [
        pltpu.make_async_copy(src, dst, weight_sem.at[k])
        for k, (src, dst) in enumerate(
            ((gate_ref, gate_v), (up_ref, up_v), (down_ref, down_v))
        )
    ]

    def load(i):
        r = chunk_order(chip, i, chips)
        return [
            pltpu.make_async_copy(hidden_ref.at[:, r], hidden_v, load_sem.at[0]),
            pltpu.make_async_copy(grad_ref.at[:, r], grad_v, load_sem.at[1]),
        ]

    def saves(i):
        rows = pl.ds(i * slots, slots)
        return [
            pltpu.make_async_copy(src, dst.at[:, rows], save_sem.at[k])
            for k, (src, dst) in enumerate(
                ((x_v, x_ref), (pg_v, pg_ref), (inner_v, inner_ref), (da_v, da_ref), (db_v, db_ref))
            )
        ]

    def out_copies(i):
        r = chunk_order(chip, i, chips)
        return [
            pltpu.make_async_copy(out_v.at[0], out_mine_ref.at[r], out_sem.at[0]),
            pltpu.make_async_copy(out_v.at[1], out_other_ref.at[r], out_sem.at[1]),
        ]

    def swap(i):
        r = chunk_order(chip, i, chips)
        return remote(
            other_v.at[lax.rem(i, 2)],
            pair.at[r],
            swap_send.at[r],
            swap_recv.at[r],
            (sibling, me),
        )

    def join(i):
        r = chunk_order(chip, i, chips)
        swap(i).wait_recv()
        add_into(pair.at[r], [pair.at[r], mine_v.at[lax.rem(i, 2)]])

    line = LineSum(
        chips,
        lambda r: lambda: [pair.at[r]],
        lambda r: pair.at[r],
        got,
        (right_send, right_recv, left_send, left_recv),
    )

    for copy in load(0) + weights_in:
        copy.start()
    greet(chips, [], True)

    slot = lax.broadcasted_iota(jnp.int32, (slot_rows, tokens), 0).astype(F32) + 1.0
    slot = jnp.where(slot <= capacity, slot, -1.0)
    lane = lax.broadcasted_iota(jnp.int32, (slots, LANES), 1)

    def chunk(i, carry):
        r = chunk_order(chip, i, chips)
        for copy in load(i):
            copy.wait()

        @pl.when(i >= 1)
        def _():
            for copy in saves(i - 1):
                copy.wait()

        picks = [[], []]
        weight_rows = []
        for e in range(local_experts):
            rows_w = []
            for q in range(2):
                hit = slot == table_ref[q, r, pl.ds(first + e, 1), :]
                pick = jnp.where(hit, 1.0, 0.0).astype(BF16)
                weight = weight_ref[q, r, pl.ds(first + e, 1), :]
                w = jnp.sum(jnp.where(hit, weight, 0.0), axis=1, keepdims=True)
                rows = pl.ds(q * slot_rows, slot_rows)
                x_v[e, rows, :] = dot(pick, hidden_v[q], NN).astype(BF16)
                g = dot(pick, grad_v[q], NN)
                g_v[e, rows, :] = g.astype(BF16)
                pg_v[e, rows, :] = (w * g).astype(BF16)
                picks[q].append(pick)
                rows_w.append(w)
            weight_rows.append(jnp.concatenate(rows_w, axis=0))

        @pl.when(i + 1 < chips)
        def _():
            for copy in load(i + 1):
                copy.start()

        @pl.when(i == 0)
        def _():
            for copy in weights_in:
                copy.wait()

        outs = [[], []]
        backs = [[], []]
        for e in range(local_experts):
            x = x_v[e]
            pair_grad = pg_v[e]
            w = weight_rows[e]
            gate = gate_v[e * width : (e + 1) * width, :]
            up = up_v[e * width : (e + 1) * width, :]
            down = down_v[e * units : (e + 1) * units, :]
            gate_pre = dot(x, gate, NN)
            up_pre = dot(x, up, NN)
            sig = jax.nn.sigmoid(gate_pre)
            silu = gate_pre * sig
            inner = (silu * up_pre).astype(BF16)
            inner_v[e] = inner
            expert_out = dot(inner, down, NN).astype(BF16).astype(F32)
            gate_grad = jnp.sum(expert_out * g_v[e].astype(F32), axis=1, keepdims=True)
            inner_grad = dot(pair_grad, down, NT)
            da = (inner_grad * up_pre * sig * (1.0 + gate_pre * (1.0 - sig))).astype(BF16)
            db = (inner_grad * silu).astype(BF16)
            da_v[e] = da
            db_v[e] = db
            row_grad = (dot(da, gate, NT) + dot(db, up, NT)).astype(BF16)
            high = gate_grad.astype(BF16).astype(F32)
            extra = jnp.where(lane == first + e, high, 0.0) + jnp.where(
                lane == expert_count + first + e, gate_grad - high, 0.0
            )
            back = jnp.concatenate([row_grad, extra.astype(BF16)], axis=1)
            out_rows = (w * expert_out).astype(BF16)
            for q in range(2):
                part = slice(q * slot_rows, (q + 1) * slot_rows)
                outs[q].append(out_rows[part])
                backs[q].append(back[part])

        for copy in saves(i):
            copy.start()

        @pl.when(i >= 1)
        def _():
            for copy in out_copies(i - 1):
                copy.wait()

        @pl.when(i >= 2)
        def _():
            swap(i - 2).wait_send()

        for q in range(2):
            pick = jnp.concatenate(picks[q], axis=0)
            held = other_v if q else mine_v
            held[lax.rem(i, 2)] = dot(pick, jnp.concatenate(backs[q], axis=0), TN).astype(BF16)
            if q:
                swap(i).start()
        for q in range(2):
            pick = jnp.concatenate(picks[q], axis=0)
            out_v[q] = dot(pick, jnp.concatenate(outs[q], axis=0), TN).astype(BF16)
        for copy in out_copies(i):
            copy.start()

        @pl.when(i == 0)
        def _():
            join(0)
            line.step(0)

        @pl.when(i >= 2)
        def _():
            join(i - 1)

        for step in range(1, chips - 1):
            if 2 * step < chips:

                @pl.when(i == 2 * step)
                def _():
                    line.step(step)

        return carry

    lax.fori_loop(0, chips, chunk, 0)
    join(chips - 1)
    for copy in saves(chips - 1):
        copy.wait()
    for copy in out_copies(chips - 1):
        copy.wait()
    for i in range(max(0, chips - 2), chips):
        swap(i).wait_send()

    shard = width // fsdp
    blocks = fsdp // per
    block = per * shard

    def fetch(copies):
        copies = [
            pltpu.make_async_copy(src, dst, save_sem.at[k])
            for k, (src, dst) in enumerate(copies)
        ]
        for copy in copies:
            copy.start()
        for copy in copies:
            copy.wait()

    def products(e, staged, target, product):
        def write(f):
            return [
                pltpu.make_async_copy(
                    staged(lax.rem(f, 2), p),
                    target.at[f * per + p, e],
                    stage_sem.at[lax.rem(f, 2), p],
                )
                for p in range(per)
            ]

        def one(f, carry):
            @pl.when(f >= 2)
            def _():
                for copy in write(f - 2):
                    copy.wait()

            product(f)
            for copy in write(f):
                copy.start()
            return carry

        lax.fori_loop(0, blocks, one, 0)
        for f in range(max(0, blocks - 2), blocks):
            for copy in write(f):
                copy.wait()

    def stage_wide(slot, p):
        return hidden_v.at[slot, pl.ds(p * shard, shard), pl.ds(0, units)]

    def wide(e, held, target):
        def product(f):
            columns = pl.ds(pl.multiple_of(f * block, LANES), block)
            value = dot(
                down_v[:total_rows, columns],
                held[e * total_rows : (e + 1) * total_rows, :],
                TN,
            ).astype(BF16)
            for p in range(per):
                stage_wide(lax.rem(f, 2), p)[...] = value[p * shard : (p + 1) * shard, :]

        products(e, stage_wide, target, product)

    def tall(e, target):
        def product(f):
            columns = pl.ds(pl.multiple_of(f * block, LANES), block)
            value = dot(
                gate_v[e * total_rows : (e + 1) * total_rows, :],
                down_v[:total_rows, columns],
                TN,
            ).astype(BF16)
            for p in range(per):
                stage_tall[lax.rem(f, 2), p] = value[:, p * shard : (p + 1) * shard]

        products(e, lambda slot, p: stage_tall.at[slot, p], target, product)

    work = []
    for e in range(local_experts):
        copies = [(x_ref.at[e], down_v.at[:total_rows])]
        if e == 0:
            for k in range(local_experts):
                held = pl.ds(k * total_rows, total_rows)
                copies += [(da_ref.at[k], gate_v.at[held]), (db_ref.at[k], up_v.at[held])]
        work.append(lambda copies=copies: fetch(copies))
        work.append(lambda e=e: wide(e, gate_v, gate_grad_ref))
        work.append(lambda e=e: wide(e, up_v, up_grad_ref))
    for e in range(local_experts):
        copies = [(pg_ref.at[e], down_v.at[:total_rows])]
        if e == 0:
            for k in range(local_experts):
                copies.append((inner_ref.at[k], gate_v.at[pl.ds(k * total_rows, total_rows)]))
        work.append(lambda copies=copies: fetch(copies))
        work.append(lambda e=e: tall(e, down_grad_ref))
    late = [step for step in range(1, chips - 1) if 2 * step >= chips]
    for n, task in enumerate(work):
        task()
        if n == LINE_TASK or (n > LINE_TASK and late):
            if late:
                line.step(late.pop(0))
    for step in late:
        line.step(step)

    line.total(returned_ref)
    line.finish()


def experts_pass(
    hidden, grad, table, weights, gate, up, down, capacity, expert_count, fsdp, collective_id
):
    unused, chips, tokens, width = grad.shape
    local_experts, unused, units = gate.shape
    slots = 2 * SLOT_STEP * -(-capacity // SLOT_STEP)
    total = chips * slots
    shard = width // fsdp
    per = 1 if shard % LANES == 0 else 2
    wide = width + LANES
    anywhere = pl.BlockSpec(memory_space=pl.ANY)
    vmem = pl.BlockSpec(memory_space=pltpu.VMEM)
    flops = 2 * total * width * units * local_experts * 9 + 8 * total * tokens * width
    saved = [(local_experts, total, width)] * 2 + [(local_experts, total, units)] * 3
    held = [(local_experts, slots, width)] * 3 + [(local_experts, slots, units)] * 3
    outs = pl.pallas_call(
        functools.partial(
            experts_kernel, capacity, local_experts, expert_count, chips, fsdp, per
        ),
        out_shape=[
            jax.ShapeDtypeStruct((tokens, wide), BF16),
            jax.ShapeDtypeStruct((chips, tokens, width), BF16),
            jax.ShapeDtypeStruct((chips, tokens, width), BF16),
            jax.ShapeDtypeStruct((fsdp, local_experts, shard, units), BF16),
            jax.ShapeDtypeStruct((fsdp, local_experts, shard, units), BF16),
            jax.ShapeDtypeStruct((fsdp, local_experts, units, shard), BF16),
        ]
        + [jax.ShapeDtypeStruct(shape, BF16) for shape in saved],
        in_specs=[anywhere, anywhere, vmem, vmem, anywhere, anywhere, anywhere],
        out_specs=[vmem] + [anywhere] * 10,
        scratch_shapes=[
            pltpu.VMEM((local_experts * width, units), BF16),
            pltpu.VMEM((local_experts * width, units), BF16),
            pltpu.VMEM((local_experts * units, width), BF16),
            pltpu.VMEM((2, tokens, width), BF16),
            pltpu.VMEM((2, tokens, width), BF16),
            pltpu.VMEM((2, tokens, width), BF16),
        ]
        + [pltpu.VMEM(shape, BF16) for shape in held]
        + [
            pltpu.VMEM((2, tokens, wide), BF16),
            pltpu.VMEM((2, tokens, wide), BF16),
            pltpu.VMEM((chips, tokens, wide), BF16),
            pltpu.VMEM((chips + 1, tokens, wide), BF16),
            pltpu.VMEM((2, per, units, shard), BF16),
            pltpu.SemaphoreType.DMA((3,)),
            pltpu.SemaphoreType.DMA((2,)),
            pltpu.SemaphoreType.DMA((2,)),
            pltpu.SemaphoreType.DMA((5,)),
            pltpu.SemaphoreType.DMA((chips,)),
            pltpu.SemaphoreType.DMA((chips,)),
        ]
        + [pltpu.SemaphoreType.DMA((chips - 1,)) for unused in range(4)]
        + [pltpu.SemaphoreType.DMA((2, per))],
        compiler_params=pltpu.CompilerParams(
            collective_id=collective_id, has_side_effects=True, vmem_limit_bytes=EXPERT_VMEM_BYTES
        ),
        cost_estimate=pl.CostEstimate(
            flops=flops, bytes_accessed=100_000_000, transcendentals=total * units * 2
        ),
        name="experts",
    )(
        hidden,
        grad,
        table,
        weights,
        gate.reshape(local_experts * width, units),
        up.reshape(local_experts * width, units),
        down.reshape(local_experts * units, width),
    )
    return outs[:6]


def body(
    tokens,
    grad_out,
    order,
    lengths,
    routes,
    gain_one,
    gain_two,
    w_query,
    w_key,
    w_value,
    w_out,
    w_router,
    w_gate,
    w_up,
    w_down,
):
    fsdp = lax.axis_size("fsdp")
    chips = lax.axis_size("ctx") // 2
    ctx_index = lax.axis_index("ctx")
    chip = ctx_index // 2
    core = lax.rem(ctx_index, 2)
    tok_rows = tokens.shape[1]
    width = tokens.shape[2]
    top_count = routes.shape[2]
    local_experts = w_gate.shape[0]
    expert_count = local_experts * chips * 2
    capacity = 5 * tok_rows * top_count // (4 * expert_count)
    kv_width = KVH * HEAD_SIZE
    shard = gain_one.shape[0]

    small = jnp.concatenate(
        [
            w_router,
            gain_one[:, None],
            gain_two[:, None],
            jnp.zeros((shard, LANES - expert_count - 2), BF16),
        ],
        axis=1,
    )
    qkv_shard = jnp.concatenate([w_query, w_key, w_value], axis=1)
    qkv_full, small_full, out_full, grad_all = gather(
        [qkv_shard, small, w_out], [grad_out[0]], chips - 2, fsdp, chips, 0
    )

    qkv_full, w_gate, w_up, w_down = lax.optimization_barrier((qkv_full, w_gate, w_up, w_down))
    gate_full, up_full, down_full = (
        lax.all_gather(w_gate, "fsdp", axis=1, tiled=True),
        lax.all_gather(w_up, "fsdp", axis=1, tiled=True),
        lax.all_gather(w_down, "fsdp", axis=2, tiled=True),
    )
    router_full = small_full[:, :expert_count]
    gain_a = small_full[:, expert_count].astype(F32)
    gain_b = small_full[:, expert_count + 1].astype(F32)

    order_row = order[0]
    start_row = ctx_index * tok_rows
    order_mine = lax.dynamic_slice_in_dim(order_row, start_row, tok_rows)
    ends = jnp.cumsum(lengths[0])
    starts = ends - lengths[0]
    past = order_mine[:, None] >= ends[None, :]
    doc_start = jnp.max(jnp.where(past, ends[None, :], starts[:1]), axis=1)
    pos_mine = order_mine - doc_start
    by_chip = jnp.roll(order_row.reshape(chips, 2, tok_rows), -chip, axis=0)
    by_chip = jnp.where(core == 0, by_chip, by_chip[:, ::-1])
    order_keys = jnp.swapaxes(by_chip, 0, 1).reshape(-1)

    route_rows = routes[0]
    route_onehot = (route_rows[:, :, None] == jnp.arange(expert_count)[None, None, :]).astype(F32)
    routed = jnp.sum(route_onehot, axis=1)
    earlier = (order_mine[None, :] < order_mine[:, None]).astype(BF16)
    ranks = jnp.dot(earlier, routed.astype(BF16), preferred_element_type=F32)
    table = jnp.where(routed > 0, jnp.minimum(ranks, capacity) + 1.0, 0.0)

    half_dim = HEAD_SIZE // 2
    freqs = ROPE_BASE ** (-2.0 * jnp.arange(half_dim).astype(F32) / HEAD_SIZE)
    angles = pos_mine.astype(F32)[:, None] * freqs[None, :]
    cosine = jnp.cos(angles)
    sine = jnp.sin(angles)

    inputs = tokens[0].astype(F32)
    (
        queries,
        hidden_one,
        kv_all,
        table_all,
        attended,
        lse,
        middle,
        gate_weights,
        weights_all,
        hidden_all,
        grad_all,
    ) = front(
        tokens[0],
        gain_a,
        gain_b,
        small_full,
        jnp.concatenate([cosine, cosine], axis=1),
        jnp.concatenate([-sine, sine], axis=1),
        order_mine,
        pos_mine,
        order_keys,
        jnp.pad(routed, ((0, 0), (0, LANES - expert_count))),
        table.T,
        qkv_full,
        out_full,
        grad_all,
        chips,
        1,
    )
    kv_all = kv_all.reshape(-1, 2 * kv_width)
    gate_weights = gate_weights[:, :expert_count]
    hidden_two = hidden_all[0, 0]
    cosine, sine = cosine[:, None, :], sine[:, None, :]

    returned, out_mine, out_other, gate_local, up_local, down_local = experts_pass(
        hidden_all,
        grad_all,
        table_all,
        weights_all,
        gate_full,
        up_full,
        down_full,
        capacity,
        expert_count,
        fsdp,
        5,
    )
    expert_grads = [
        lax.psum_scatter(part, "fsdp", scatter_dimension=0, tiled=True)
        for part in (gate_local, up_local, down_local)
    ]

    out_grad = grad_out[0].astype(F32)
    returned = returned.astype(F32)
    extra = returned[:, width:]
    gate_grad = extra[:, :expert_count] + extra[:, expert_count : 2 * expert_count]
    logit_grad = (
        gate_weights * (gate_grad - jnp.sum(gate_weights * gate_grad, axis=-1, keepdims=True))
    ).astype(BF16)
    router_local = jnp.einsum("td,te->de", hidden_two, logit_grad, preferred_element_type=F32)
    hidden_two_grad = returned[:, :width] + jnp.einsum(
        "te,de->td", logit_grad, router_full, preferred_element_type=F32
    )
    unused_two, norm_two_back = jax.vjp(rms_scale, middle, gain_b)
    middle_part, gain_two_local = norm_two_back(hidden_two_grad)
    middle_grad = out_grad + middle_part
    branch_grad = middle_grad.astype(BF16)
    out_local = jnp.einsum("tc,td->cd", attended, branch_grad, preferred_element_type=F32)
    attended_grad = jnp.einsum(
        "td,cd->tc", branch_grad, out_full, preferred_element_type=F32
    ).astype(BF16)

    query_grad, kv_grad, out_own, out_right, out_left = attention_back(
        queries,
        kv_all,
        attended,
        attended_grad,
        lse,
        order_mine,
        pos_mine,
        order_keys,
        out_mine,
        out_other,
        3,
    )
    key_grad = [kv_grad[group, :, :HEAD_SIZE] for group in range(KVH)]
    value_grad = [kv_grad[group, :, HEAD_SIZE:] for group in range(KVH)]
    turned_grad = rotate(
        jnp.concatenate([query_grad] + key_grad, axis=1).reshape(
            tok_rows, QUERY_HEADS + KVH, HEAD_SIZE
        ),
        cosine,
        -sine,
    ).reshape(tok_rows, width + kv_width)
    pre_grad = jnp.concatenate(
        [turned_grad.astype(BF16)] + [part.astype(BF16) for part in value_grad], axis=1
    )
    qkv_local = jnp.einsum("td,tc->dc", hidden_one, pre_grad, preferred_element_type=F32)
    hidden_one_grad = jnp.einsum("tc,dc->td", pre_grad, qkv_full, preferred_element_type=F32)
    unused_one, norm_one_back = jax.vjp(rms_scale, inputs, gain_a)
    input_part, gain_one_local = norm_one_back(hidden_one_grad)
    input_grad = (middle_grad + input_part).astype(BF16)

    def halves(local):
        local = local.astype(BF16).reshape(fsdp, 2, shard // 2, local.shape[1])
        pad = -local.shape[3] % (LANES * chips)
        return jnp.pad(local, ((0, 0), (0, 0), (0, 0), (0, pad))) if pad else local

    span = shard * expert_count // 16
    wide = LANES * chips * -(-max(span, shard) // (LANES * chips))
    small_local = jnp.stack(
        [
            jnp.pad(
                router_local.astype(BF16).reshape(fsdp, 16, span),
                ((0, 0), (0, 0), (0, wide - span)),
            ),
            jnp.pad(
                jnp.stack(
                    [gain_one_local.reshape(fsdp, shard), gain_two_local.reshape(fsdp, shard)],
                    axis=1,
                ).astype(BF16),
                ((0, 0), (0, 14), (0, wide - shard)),
            ),
        ],
        axis=1,
    )
    qkv_sum, out_proj_sum, small_sum, out_sum = dense_reduce(
        [halves(qkv_local), halves(out_local), small_local],
        out_own,
        out_right,
        out_left,
        DENSE_PIECE,
        fsdp,
        chips,
        4,
    )
    edge = width + 2 * kv_width
    qkv_grads = qkv_sum.reshape(shard, -1)
    out_proj_grad = out_proj_sum.reshape(shard, -1)[:, :width]
    gate_grad_out, up_grad_out, down_grad_out = (
        after(part, pre_grad)[0].astype(F32) for part in expert_grads
    )
    result = middle + out_sum
    return (
        result.astype(BF16)[None],
        input_grad[None],
        small_sum[1, 0, :shard].astype(F32),
        small_sum[1, 1, :shard].astype(F32),
        qkv_grads[:, :width].astype(F32),
        qkv_grads[:, width : width + kv_width].astype(F32),
        qkv_grads[:, width + kv_width : edge].astype(F32),
        out_proj_grad.astype(F32),
        small_sum[0, :, :span].reshape(shard, expert_count).astype(F32),
        gate_grad_out,
        up_grad_out,
        down_grad_out,
    )


def solution(mesh):
    placed = (
        P("fsdp", "ctx", None),
        P("fsdp", "ctx", None),
        P("fsdp", None),
        P("fsdp", None),
        P("fsdp", "ctx", None),
        P("fsdp"),
        P("fsdp"),
        P("fsdp", None),
        P("fsdp", None),
        P("fsdp", None),
        P("fsdp", None),
        P("fsdp", None),
        P("ctx", "fsdp", None),
        P("ctx", "fsdp", None),
        P("ctx", None, "fsdp"),
    )
    return jax.shard_map(
        body,
        mesh=mesh,
        in_specs=placed,
        out_specs=(
            P("fsdp", "ctx", None),
            P("fsdp", "ctx", None),
            P("fsdp"),
            P("fsdp"),
            P("fsdp", None),
            P("fsdp", None),
            P("fsdp", None),
            P("fsdp", None),
            P("fsdp", None),
            P("ctx", "fsdp", None),
            P("ctx", "fsdp", None),
            P("ctx", None, "fsdp"),
        ),
        check_vma=False,
    )
```

```python
import functools

import jax
import jax.numpy as jnp
from jax import lax
from jax.experimental import pallas as pl
from jax.experimental.pallas import tpu as pltpu
from jax.sharding import PartitionSpec as P

QUERY_HEADS = 12
KVH = 2
HEAD_SIZE = 128

EPSILON = 1e-06
ROPE_BASE = 10000.0
MASKED = -1e30
LOG2E = 1.4426950408889634
LANES = 128
SLOT_STEP = 64
DENSE_PIECE = 1024
LINE_TASK = 4
KEY_TILE = 512
VMEM_BYTES = 56 * 1024 * 1024
EXPERT_VMEM_BYTES = 119 * 512 * 1024
BACK_VMEM_BYTES = 61 * 1024 * 1024
FRONT_VMEM_BYTES = 40 * 1024 * 1024
MESH = pl.DeviceIdType.MESH
F32 = jnp.float32
BF16 = jnp.bfloat16


def dot(left, right, contract):
    return lax.dot_general(left, right, (contract, ((), ())), preferred_element_type=F32)


NN = ((1,), (0,))
NT = ((1,), (1,))
TN = ((0,), (0,))


def rms_scale(value_rows, gain):
    return (
        value_rows
        * lax.rsqrt(jnp.mean(value_rows * value_rows, axis=-1, keepdims=True) + EPSILON)
        * gain
    )


def place():
    ctx = lax.axis_index("ctx")
    core = lax.rem(ctx, 2)
    return ctx, lax.axis_index("fsdp"), ctx // 2, core, ctx + 1 - 2 * core


def peers_of(me, fsdp):
    peers = []
    for shift in range(1, fsdp):
        peer = me
        for bit in range(fsdp.bit_length() - 1):
            if (shift >> bit) & 1:
                digit = lax.rem(me // (1 << bit), 2)
                peer = peer + (1 << bit) - (2 << bit) * digit
        peers.append(peer)
    return peers


def greet(chips, peers, line):
    ctx, me, chip, core, sibling = place()
    barrier = pltpu.get_barrier_semaphore()
    for peer in peers:
        pl.semaphore_signal(barrier, inc=1, device_id=(ctx, peer), device_id_type=MESH)
    pl.semaphore_signal(barrier, inc=1, device_id=(sibling, me), device_id_type=MESH)
    known = len(peers) + 1
    if not line:
        pl.semaphore_wait(barrier, known)
        return
    has_right = chip + 1 < chips
    has_left = chip >= 1

    @pl.when(has_right)
    def _():
        pl.semaphore_signal(barrier, inc=1, device_id=(ctx + 2, me), device_id_type=MESH)

    @pl.when(has_left)
    def _():
        pl.semaphore_signal(barrier, inc=1, device_id=(ctx - 2, me), device_id_type=MESH)

    @pl.when(has_right & has_left)
    def _():
        pl.semaphore_wait(barrier, known + 2)

    @pl.when(jnp.logical_not(has_right & has_left))
    def _():
        pl.semaphore_wait(barrier, known + 1)


class Bounce:
    def __init__(self, src, dst, buffer, sem):
        self.inward = pltpu.make_async_copy(src, buffer, sem)
        self.outward = pltpu.make_async_copy(buffer, dst, sem)

    def start(self):
        self.inward.start()

    def turn(self):
        self.inward.wait()
        self.outward.start()

    def wait(self):
        self.outward.wait()


def remote(src, dst, send_sem, recv_sem, device):
    return pltpu.make_async_remote_copy(
        src_ref=src,
        dst_ref=dst,
        send_sem=send_sem,
        recv_sem=recv_sem,
        device_id=device,
        device_id_type=MESH,
    )


class DenseGather:
    def __init__(self, ins, outs, sems, fsdp):
        buffers, local_sem, send_sem, recv_sem, pass_sem, took_sem = sems
        ctx, me, chip, core, sibling = place()
        self.sends, self.passes, self.locals = [], [], []
        for i in range(len(ins)):
            rows = ins[i].shape[0]
            half = rows // 2
            for j, peer in enumerate(peers_of(me, fsdp)):
                self.sends.append(
                    remote(
                        ins[i].at[pl.ds(core * half, half)],
                        outs[i].at[pl.ds(me * rows + core * half, half)],
                        send_sem.at[i, j],
                        recv_sem.at[i, j],
                        (ctx, peer),
                    )
                )
                got = outs[i].at[pl.ds(peer * rows + core * half, half)]
                self.passes.append(
                    remote(got, got, pass_sem.at[i, j], took_sem.at[i, j], (sibling, me))
                )
            self.locals.append(
                Bounce(ins[i], outs[i].at[pl.ds(me * rows, rows)], buffers[i], local_sem.at[i])
            )

    def start(self):
        for copy in self.sends + self.locals:
            copy.start()

    def finish(self):
        for copy in self.locals:
            copy.turn()
        for send, copy in zip(self.sends, self.passes):
            send.wait_recv()
            copy.start()
        for send in self.sends:
            send.wait_send()
        for copy in self.passes + self.locals:
            copy.wait()


def dense_scratch(arrays, fsdp):
    count = len(arrays)
    return (
        [pltpu.VMEM(a.shape, a.dtype) for a in arrays]
        + [pltpu.SemaphoreType.DMA((count,))]
        + [pltpu.SemaphoreType.DMA((count, fsdp - 1)) for unused in range(4)]
    )


class ShardGather:
    def __init__(self, ref, out, buffer, sems, fsdp):
        own_sem, send_sem, recv_sem = sems
        ctx, me, chip, core, sibling = place()
        rows = ref.shape[1]
        mine = out.at[:, pl.ds(me * rows, rows)]
        self.sends = [
            remote(ref, mine, send_sem.at[j], recv_sem.at[j], (ctx, peer))
            for j, peer in enumerate(peers_of(me, fsdp))
        ]
        self.own = Bounce(ref, mine, buffer, own_sem)

    def start(self):
        for copy in self.sends + [self.own]:
            copy.start()

    def finish(self):
        self.own.turn()
        for copy in self.sends:
            copy.wait()
        self.own.wait()


class LineGather:
    def __init__(self, ins, outs, sems, chips):
        self.ins, self.outs, self.chips = ins, outs, chips
        self.buffers, self.sems = sems[:-7], sems[-7:]
        self.ctx, self.me, self.chip, core, self.sibling = place()
        self.count = len(ins)

    def to_right(self, i, step):
        outs, chips = self.outs, self.chips
        return remote(
            self.ins[i] if step == 0 else outs[i].at[0, chips - step],
            outs[i].at[0, chips - 1 - step],
            self.sems[1].at[i, step],
            self.sems[2].at[i, step],
            (self.ctx + 2, self.me),
        )

    def to_left(self, i, step):
        outs = self.outs
        return remote(
            self.ins[i] if step == 0 else outs[i].at[0, step],
            outs[i].at[0, step + 1],
            self.sems[3].at[i, step],
            self.sems[4].at[i, step],
            (self.ctx - 2, self.me),
        )

    def across(self, i, slot):
        return remote(
            self.ins[i] if slot == 0 else self.outs[i].at[0, slot],
            self.outs[i].at[1, slot],
            self.sems[5].at[i, slot],
            self.sems[6].at[i, slot],
            (self.sibling, self.me),
        )

    def local(self, i):
        return Bounce(self.ins[i], self.outs[i].at[0, 0], self.buffers[i], self.sems[0].at[i])

    def send(self, step):
        chip, chips, count = self.chip, self.chips, self.count

        @pl.when((chip + 1 < chips) & (chip >= step))
        def _():
            for i in range(count):
                self.to_right(i, step).start()

        @pl.when((chip >= 1) & (chip + step < chips))
        def _():
            for i in range(count):
                self.to_left(i, step).start()

    def receive(self, step):
        chip, chips, count = self.chip, self.chips, self.count

        @pl.when(chip >= step + 1)
        def _():
            for i in range(count):
                self.to_right(i, step).wait_recv()
                self.across(i, chips - 1 - step).start()

        @pl.when(chip + step + 1 < chips)
        def _():
            for i in range(count):
                self.to_left(i, step).wait_recv()
                self.across(i, step + 1).start()

    def own(self):
        for i in range(self.count):
            self.across(i, 0).start()
            self.local(i).start()

    def turn_own(self):
        for i in range(self.count):
            self.local(i).turn()

    def finish_own(self):
        for i in range(self.count):
            self.across(i, 0).wait()
            self.local(i).wait()

    def arrived(self, slot):
        for i in range(self.count):
            remote(
                self.outs[i].at[0, slot],
                self.outs[i].at[1, slot],
                self.sems[5].at[i, slot],
                self.sems[6].at[i, slot],
                (self.sibling, self.me),
            ).wait_recv()

    def sent(self):
        chip, chips, count = self.chip, self.chips, self.count
        for step in range(chips - 1):

            @pl.when((chip + 1 < chips) & (chip >= step))
            def _():
                for i in range(count):
                    self.to_right(i, step).wait_send()

            @pl.when((chip >= 1) & (chip + step < chips))
            def _():
                for i in range(count):
                    self.to_left(i, step).wait_send()

        for slot in range(chips):
            for i in range(count):
                self.across(i, slot).wait_send()

    def finish(self, step):
        chip, chips, count = self.chip, self.chips, self.count

        @pl.when((chip + 1 < chips) & (chip >= step))
        def _():
            for i in range(count):
                self.to_right(i, step).wait_send()

        @pl.when((chip >= 1) & (chip + step < chips))
        def _():
            for i in range(count):
                self.to_left(i, step).wait_send()

        @pl.when(chip >= step + 1)
        def _():
            for i in range(count):
                self.across(i, chips - 1 - step).wait()

        @pl.when(chip + step + 1 < chips)
        def _():
            for i in range(count):
                self.across(i, step + 1).wait()


def line_scratch(arrays, chips):
    count = len(arrays)
    return (
        [pltpu.VMEM(a.shape, a.dtype) for a in arrays if a is not None]
        + [pltpu.SemaphoreType.DMA((count,))]
        + [pltpu.SemaphoreType.DMA((count, chips - 1)) for unused in range(4)]
        + [pltpu.SemaphoreType.DMA((count, chips)) for unused in range(2)]
    )


def gather_kernel(dense, line, resumed, steps, fsdp, chips, *refs):
    count = dense + line + resumed
    ins, outs, scratch = refs[:count], refs[count : 2 * count], refs[2 * count :]
    ctx, me, chip, core, sibling = place()
    greet(chips, peers_of(me, fsdp) if dense else [], line > 0)
    split = dense + line
    if dense:
        own, scratch = scratch[: dense + 5], scratch[dense + 5 :]
        first = DenseGather(
            ins[:dense], outs[:dense], (own[:dense],) + tuple(own[dense:]), fsdp
        )
        first.start()
    if line:
        own, scratch = scratch[: line + 7], scratch[line + 7 :]
        second = LineGather(ins[dense:split], outs[dense:split], own, chips)
        for step in range(steps):
            second.send(step)
            if step == 0:
                second.own()
            second.receive(step)
            if step == 0:
                second.turn_own()
    if resumed:
        third = LineGather([None], outs[split:], scratch, chips)
        third.send(chips - 2)
        third.receive(chips - 2)
    if dense:
        first.finish()
    if line:
        second.finish_own()
        for step in range(steps):
            second.finish(step)
    if resumed:
        third.finish(chips - 2)


def gather(dense, line, steps, fsdp, chips, collective_id, resumed=()):
    arrays = list(dense) + list(line) + list(resumed)
    count = len(arrays)
    scratch = (dense_scratch(dense, fsdp) if dense else []) + (
        line_scratch(line, chips) if line else []
    )
    if resumed:
        scratch = scratch + line_scratch([None], chips)
    return pl.pallas_call(
        functools.partial(
            gather_kernel, len(dense), len(line), len(resumed), steps, fsdp, chips
        ),
        out_shape=[jax.ShapeDtypeStruct((fsdp * a.shape[0],) + a.shape[1:], a.dtype) for a in dense]
        + [jax.ShapeDtypeStruct((2, chips) + a.shape, a.dtype) for a in line]
        + [jax.ShapeDtypeStruct(a.shape, a.dtype) for a in resumed],
        in_specs=[pl.BlockSpec(memory_space=pl.ANY)] * count,
        out_specs=[pl.BlockSpec(memory_space=pl.ANY)] * count,
        scratch_shapes=scratch,
        input_output_aliases={count - 1: count - 1} if resumed else {},
        compiler_params=pltpu.CompilerParams(
            collective_id=collective_id, has_side_effects=True, vmem_limit_bytes=VMEM_BYTES
        ),
        name="gather",
    )(*arrays)


def add(*parts):
    total = parts[0].astype(F32)
    for part in parts[1:]:
        total = total + part.astype(F32)
    return total


def add_into(target, parts):
    rows = target.shape[0]
    tile = 32 if rows % 32 == 0 else 16

    def some(t, carry):
        part = pl.ds(pl.multiple_of(t * tile, tile), tile)
        target[part, :] = add(*[ref[part, :] for ref in parts]).astype(target.dtype)
        return carry

    lax.fori_loop(0, rows // tile, some, 0)


class LineSum:
    def __init__(self, chips, held, keep, got, sems):
        self.chips, self.held, self.keep, self.got = chips, held, keep, got
        self.sems = sems
        self.ctx, self.me, self.chip, core, sibling = place()

    def right(self, step):
        return remote(
            self.keep(self.chips - 1 - step),
            self.got.at[step - self.chip],
            self.sems[0].at[step],
            self.sems[1].at[step],
            (self.ctx + 2, self.me),
        )

    def from_left(self, step):
        slot = step + 1 - self.chip
        pltpu.make_async_remote_copy(
            src_ref=self.keep(self.chips - 1 - step),
            dst_ref=self.got.at[slot],
            send_sem=self.sems[0].at[step],
            recv_sem=self.sems[1].at[step],
            device_id=(self.ctx - 2, self.me),
            device_id_type=MESH,
        ).wait_recv()
        return self.got.at[slot]

    def from_right(self, step):
        slot = step + 2
        self.left(step).wait_recv()
        return self.got.at[slot]

    def left(self, step):
        return remote(
            self.keep(step + 1),
            self.got.at[step + 2],
            self.sems[2].at[step],
            self.sems[3].at[step],
            (self.ctx - 2, self.me),
        )

    def step(self, step):
        chip, chips = self.chip, self.chips
        far_right, far_left = chips - 1 - step, step + 1

        @pl.when(chip <= step)
        def _():
            parts = self.held(far_right)
            if step == 0:
                add_into(self.keep(far_right), parts())
            else:

                @pl.when(chip == 0)
                def _():
                    add_into(self.keep(far_right), parts())

                @pl.when(chip >= 1)
                def _():
                    add_into(self.keep(far_right), [self.from_left(step - 1)] + parts())

            self.right(step).start()

        @pl.when(chip >= chips - 1 - step)
        def _():
            parts = self.held(far_left)
            if step == 0:
                add_into(self.keep(far_left), parts())
            else:

                @pl.when(chip == chips - 1)
                def _():
                    add_into(self.keep(far_left), parts())

                @pl.when(chip < chips - 1)
                def _():
                    add_into(self.keep(far_left), [self.from_right(step - 1)] + parts())

            self.left(step).start()

    def total(self, target):
        chip, chips, last = self.chip, self.chips, self.chips - 2
        parts = self.held(0)

        @pl.when(chip == 0)
        def _():
            add_into(target, [self.from_right(last)] + parts())

        @pl.when(chip == chips - 1)
        def _():
            add_into(target, [self.from_left(last)] + parts())

        @pl.when((chip >= 1) & (chip < chips - 1))
        def _():
            add_into(target, [self.from_right(last), self.from_left(last)] + parts())

    def finish(self, steps=None):
        for step in range(self.chips - 1 if steps is None else steps):

            @pl.when(self.chip <= step)
            def _():
                self.right(step).wait_send()

            @pl.when(self.chip >= self.chips - 1 - step)
            def _():
                self.left(step).wait_send()


DENSE_BUFFERS = 5
DENSE_SEMS = 14


class DenseSum:
    def __init__(self, local, out, buffers, sems, fsdp, chips):
        self.local, self.out = local, out
        self.pair, self.cross, self.sums, got, self.spread = buffers
        self.sems = sems
        self.chips = chips
        self.ctx, self.me, self.chip, self.core, self.sibling = place()
        self.owners = peers_of(self.me, fsdp) + [self.me]
        self.cut = out.shape[2] // chips
        self.line = LineSum(
            chips,
            lambda r: lambda: [self.keep_ref(r)],
            lambda r: self.keep_ref(r),
            got,
            sems[4:8],
        )

    def keep_ref(self, r):
        return self.sums.at[:, self.columns(r)]

    def columns(self, r):
        owner = lax.rem(self.chip + r, self.chips)
        return pl.ds(pl.multiple_of(owner * self.cut, LANES), self.cut)

    def swap(self, j):
        return remote(
            self.local.at[self.owners[j], 1 - self.core],
            self.pair.at[j],
            self.sems[0].at[j],
            self.sems[1].at[j],
            (self.sibling, self.me),
        )

    def crossing(self, j):
        return remote(
            self.pair.at[j],
            self.cross.at[j],
            self.sems[2].at[j],
            self.sems[3].at[j],
            (self.ctx, self.owners[j]),
        )

    def to_right(self, step):
        return remote(
            self.spread.at[0, (self.chips - step) % self.chips],
            self.spread.at[0, self.chips - 1 - step],
            self.sems[8].at[step],
            self.sems[9].at[step],
            (self.ctx + 2, self.me),
        )

    def to_left(self, step):
        return remote(
            self.spread.at[0, step],
            self.spread.at[0, step + 1],
            self.sems[10].at[step],
            self.sems[11].at[step],
            (self.ctx - 2, self.me),
        )

    def across(self, slot):
        return remote(
            self.spread.at[0, slot],
            self.spread.at[1, slot],
            self.sems[12].at[slot],
            self.sems[13].at[slot],
            (self.sibling, self.me),
        )

    def start(self):
        for j in range(len(self.owners)):
            self.swap(j).start()

    def cross_over(self):
        for j, owner in enumerate(self.owners):
            self.swap(j).wait_recv()
            add_into(self.pair.at[j], [self.local.at[owner, self.core], self.pair.at[j]])
            if j < len(self.owners) - 1:
                self.crossing(j).start()

    def stages(self):
        chip, chips = self.chip, self.chips

        def open_up():
            for j in range(len(self.owners) - 1):
                self.crossing(j).wait_recv()
            add_into(
                self.sums,
                [self.cross.at[j] for j in range(len(self.owners) - 1)]
                + [self.pair.at[len(self.owners) - 1]],
            )
            self.line.step(0)

        def summed():
            self.line.total(self.spread.at[0, 0])
            hand_on(0)

        def hand_on(step):
            @pl.when((chip + 1 < chips) & (chip >= step))
            def _():
                self.to_right(step).start()

            @pl.when((chip >= 1) & (chip + step < chips))
            def _():
                self.to_left(step).start()

            if step == 0:
                self.across(0).start()

        def take(step):
            @pl.when(chip >= step + 1)
            def _():
                self.to_right(step).wait_recv()
                self.across(chips - 1 - step).start()

            @pl.when(chip + step + 1 < chips)
            def _():
                self.to_left(step).wait_recv()
                self.across(step + 1).start()

        def pass_on(step):
            def run():
                take(step - 1)
                hand_on(step)

            return run

        def line_step(step):
            return lambda: self.line.step(step)

        return (
            [open_up]
            + [line_step(step) for step in range(1, chips - 1)]
            + [summed]
            + [pass_on(step) for step in range(1, chips - 1)]
            + [lambda: take(chips - 2)]
        )

    def finish(self):
        chip, chips = self.chip, self.chips
        for r in range(chips):
            self.out[self.core, :, self.columns(r)] = self.spread[0, r]
        for r in range(chips):
            self.across(r).wait()
            self.out[1 - self.core, :, self.columns(r)] = self.spread[1, r]
        for step in range(chips - 1):

            @pl.when((chip + 1 < chips) & (chip >= step))
            def _():
                self.to_right(step).wait_send()

            @pl.when((chip >= 1) & (chip + step < chips))
            def _():
                self.to_left(step).wait_send()

        self.line.finish()
        for j in range(len(self.owners) - 1):
            self.crossing(j).wait_send()
        for j in range(len(self.owners)):
            self.swap(j).wait_send()


def dense_reduce_kernel(fsdp, chips, cuts, *refs):
    count = len(cuts)
    arrays = max(cut[0] for cut in cuts) + 1
    ins, refs = refs[:arrays], refs[arrays:]
    own_ref, right_ref, left_ref = refs[:3]
    outs, total_ref, refs = refs[3 : 3 + arrays], refs[3 + arrays], refs[4 + arrays :]
    from_left, from_right, r_send, r_recv, l_send, l_recv = refs[:6]
    rest = refs[6:]
    ctx, me, chip, core, sibling = place()
    greet(chips, peers_of(me, fsdp), True)

    to_right = remote(right_ref, from_left, r_send, r_recv, (ctx + 2, me))
    to_left = remote(left_ref, from_right, l_send, l_recv, (ctx - 2, me))

    @pl.when(chip + 1 < chips)
    def _():
        to_right.start()

    @pl.when(chip >= 1)
    def _():
        to_left.start()

    sums = []
    for i, (which, start, size) in enumerate(cuts):
        buffers = rest[i * DENSE_BUFFERS : (i + 1) * DENSE_BUFFERS]
        sems = rest[count * DENSE_BUFFERS + i * DENSE_SEMS :][:DENSE_SEMS]
        sums.append(
            DenseSum(
                ins[which].at[:, :, :, pl.ds(start, size)],
                outs[which].at[:, :, pl.ds(start, size)],
                buffers,
                sems,
                fsdp,
                chips,
            )
        )
    for one in sums:
        one.start()
    for one in sums:
        one.cross_over()
    stages = [one.stages() for one in sums]
    lag = chips - 1
    for tick in range(len(stages[0]) + lag * (count - 1)):
        for i in range(count):
            if 0 <= tick - lag * i < len(stages[i]):
                stages[i][tick - lag * i]()
    @pl.when(chip >= 1)
    def _():
        to_right.wait_recv()

    @pl.when(chip + 1 < chips)
    def _():
        to_left.wait_recv()

    @pl.when(chip == 0)
    def _():
        add_into(total_ref, [from_right, own_ref])

    @pl.when(chip == chips - 1)
    def _():
        add_into(total_ref, [from_left, own_ref])

    @pl.when((chip >= 1) & (chip + 1 < chips))
    def _():
        add_into(total_ref, [from_left, from_right, own_ref])

    for one in sums:
        one.finish()

    @pl.when(chip + 1 < chips)
    def _():
        to_right.wait_send()

    @pl.when(chip >= 1)
    def _():
        to_left.wait_send()


def dense_reduce(arrays, own, right, left, piece, fsdp, chips, collective_id):
    vmem = pl.BlockSpec(memory_space=pltpu.VMEM)
    cuts, buffers = [], []
    for i, a in enumerate(arrays):
        rows, width = a.shape[2:]
        for start in range(0, width, piece):
            size = min(piece, width - start)
            cut = size // chips
            cuts.append((i, start, size))
            buffers += [
                pltpu.VMEM((fsdp, rows, size), BF16),
                pltpu.VMEM((fsdp - 1, rows, size), BF16),
                pltpu.VMEM((rows, size), BF16),
                pltpu.VMEM((chips + 1, rows, cut), BF16),
                pltpu.VMEM((2, chips, rows, cut), BF16),
            ]
    sems = (
        [pltpu.SemaphoreType.DMA((fsdp,)) for unused in range(2)]
        + [pltpu.SemaphoreType.DMA((fsdp - 1,)) for unused in range(2)]
        + [pltpu.SemaphoreType.DMA((chips - 1,)) for unused in range(8)]
        + [pltpu.SemaphoreType.DMA((chips,)) for unused in range(2)]
    )
    return pl.pallas_call(
        functools.partial(dense_reduce_kernel, fsdp, chips, tuple(cuts)),
        out_shape=[jax.ShapeDtypeStruct(a.shape[1:], BF16) for a in arrays]
        + [jax.ShapeDtypeStruct(own.shape, F32)],
        in_specs=[vmem] * len(arrays) + [vmem, pl.BlockSpec(memory_space=pl.ANY)]
        + [pl.BlockSpec(memory_space=pl.ANY)],
        out_specs=[vmem] * (len(arrays) + 1),
        scratch_shapes=[pltpu.VMEM(own.shape, BF16)] * 2
        + [pltpu.SemaphoreType.DMA] * 4
        + buffers
        + sems * len(cuts),
        compiler_params=pltpu.CompilerParams(
            collective_id=collective_id, has_side_effects=True, vmem_limit_bytes=VMEM_BYTES
        ),
        name="dense_reduce",
    )(*arrays, own, right, left)


def after(value, *others):
    return lax.optimization_barrier((value,) + others)[0]


def chunk_order(chip, i, chips):
    right_half = lax.div(2 * chip, chips)
    near = chip + right_half * (chips - 1 - 2 * chip)
    alone = chips - 1 - 2 * near
    paired = lax.div(i - alone + chips, chips)
    turn = (i - alone) * paired
    odd = lax.rem(turn, 2)
    pair = lax.div(turn, 2)
    distance = (1 - paired) * (chips - 1 - near - i) + paired * (
        (1 - odd) * (near - pair) + odd * (chips - near + pair)
    )
    return lax.rem(distance + right_half * (chips - 2 * distance), chips)


def front_kernel(
    scale,
    chips,
    fsdp,
    expert_count,
    tokens_ref,
    gain_a_ref,
    gain_b_ref,
    small_ref,
    cos_ref,
    sin_ref,
    oq_ref,
    pq_ref,
    ok_ref,
    routed_ref,
    table_ref,
    qkv_ref,
    wo_ref,
    gate_w_ref,
    passed_ref,
    q_ref,
    normed_ref,
    kv_ref,
    table_all_ref,
    attended_ref,
    lse_ref,
    middle_ref,
    gate_ref,
    weights_ref,
    hidden_all_ref,
    gate_full_ref,
    grad_ref,
    qkv_v,
    wo_v,
    gate_v,
    hidden_v,
    bias,
    top,
    total,
    acc,
    load_sem,
    own_sem,
    gate_own,
    gate_send,
    gate_recv,
    *line_sems,
):
    ctx, me, chip, core, sibling = place()
    rows = tokens_ref.shape[0]
    width = tokens_ref.shape[1]
    half = rows // 2
    kv_width = KVH * HEAD_SIZE
    per_group = QUERY_HEADS // KVH
    parts = [pl.ds(0, half), pl.ds(half, half)]
    loads = [
        pltpu.make_async_copy(src, dst, load_sem.at[k])
        for k, (src, dst) in enumerate(((qkv_ref, qkv_v), (wo_ref, wo_v)))
    ]
    for copy in loads:
        copy.start()
    greet(chips, peers_of(me, fsdp), True)
    gate_gather = ShardGather(
        gate_w_ref, gate_full_ref, gate_v, (gate_own, gate_send, gate_recv), fsdp
    )
    gate_gather.start()
    kv_line = LineGather(
        [kv_ref.at[0, 0], table_all_ref.at[0, 0]], [kv_ref, table_all_ref], line_sems[:7], chips
    )
    grad_line = LineGather([None], [grad_ref], line_sems[7:14], chips)
    hidden_lines = [
        LineGather(
            [hidden_v.at[parts[0]]], [hidden_all_ref.at[:, :, parts[0]]], line_sems[14:21], chips
        ),
        LineGather(
            [hidden_v.at[parts[1]], weights_ref.at[0, 0]],
            [hidden_all_ref.at[:, :, parts[1]], weights_ref],
            line_sems[21:28],
            chips,
        ),
    ]

    def normed(value, gain):
        return value * lax.rsqrt(jnp.mean(value * value, axis=-1, keepdims=True) + EPSILON) * gain

    table_all_ref[0, 0] = table_ref[...]
    for part in parts:
        normed_ref[part, :] = normed(
            tokens_ref[part, :].astype(F32), gain_a_ref[...]
        ).astype(BF16)
    loads[0].wait()
    for part in parts:
        rows_one = normed_ref[part, :]
        cosine, sine = cos_ref[part, :], sin_ref[part, :]
        for h in range(KVH):
            columns = slice(width + h * HEAD_SIZE, width + (h + 1) * HEAD_SIZE)
            value = dot(rows_one, qkv_v[:, columns], NN)
            value = value * cosine + pltpu.roll(value, HEAD_SIZE // 2, 1) * sine
            kv_ref[0, 0, part, h * HEAD_SIZE : (h + 1) * HEAD_SIZE] = value.astype(BF16)
        kv_ref[0, 0, part, kv_width:] = dot(
            rows_one, qkv_v[:, width + kv_width :], NN
        ).astype(BF16)
    kv_line.send(0)
    for i in range(2):
        kv_line.across(i, 0).start()
    for part in parts:
        rows_one = normed_ref[part, :]
        cosine, sine = cos_ref[part, :], sin_ref[part, :]
        for h in range(0, QUERY_HEADS, 2):
            pre = dot(rows_one, qkv_v[:, h * HEAD_SIZE : (h + 2) * HEAD_SIZE], NN)
            for k in range(2):
                value = pre[:, k * HEAD_SIZE : (k + 1) * HEAD_SIZE]
                value = value * cosine + pltpu.roll(value, HEAD_SIZE // 2, 1) * sine
                q_ref[part, (h + k) * HEAD_SIZE : (h + k + 1) * HEAD_SIZE] = value.astype(BF16)

    def turn(index, r):
        part = parts[index]
        for q in range(2):
            gap = oq_ref[part, :] - ok_ref[q * chips + r]
            bias[:, q * rows : (q + 1) * rows] = jnp.where(
                (gap >= 0) & (gap <= pq_ref[part, :]), 0.0, MASKED
            )

        def one(h, carry):
            group = lax.div(h, per_group)
            columns = pl.ds(pl.multiple_of(h * HEAD_SIZE, HEAD_SIZE), HEAD_SIZE)
            key_columns = pl.ds(pl.multiple_of(group * HEAD_SIZE, HEAD_SIZE), HEAD_SIZE)
            value_columns = pl.ds(
                pl.multiple_of(kv_width + group * HEAD_SIZE, HEAD_SIZE), HEAD_SIZE
            )
            query = q_ref[part, columns]
            scores = []
            peak = top[h, part, :]
            for q in range(2):
                raw = dot(query, kv_ref[q, r, :, key_columns], NT) * (scale * LOG2E)
                raw = raw + bias[:, q * rows : (q + 1) * rows]
                scores.append(raw)
            best = scores[0][:, :LANES]
            for q in range(2):
                for k in range(rows // LANES):
                    best = jnp.maximum(best, scores[q][:, k * LANES : (k + 1) * LANES])
            new = jnp.maximum(peak, jnp.max(best, axis=1, keepdims=True))
            fade = jnp.exp2(peak - new)
            wide = jnp.concatenate([new] * (rows // LANES), axis=1)
            mass = total[h] * fade
            out = acc[:, columns] * fade
            for q in range(2):
                probs = jnp.exp2(scores[q] - wide)
                for k in range(rows // LANES):
                    mass = mass + probs[:, k * LANES : (k + 1) * LANES]
                out = out + dot(probs.astype(BF16), kv_ref[q, r, :, value_columns], NN)
            top[h, part, :] = new
            total[h] = mass
            acc[:, columns] = out
            return carry

        lax.fori_loop(0, QUERY_HEADS, one, 0)

    def begin(index):
        top[:, parts[index], :] = jnp.full((QUERY_HEADS, half, LANES), MASKED, F32)
        total[...] = jnp.zeros_like(total)
        acc[...] = jnp.zeros_like(acc)

    def end(index):
        part = parts[index]
        for h in range(QUERY_HEADS):
            columns = slice(h * HEAD_SIZE, (h + 1) * HEAD_SIZE)
            mass = jnp.sum(total[h], axis=1, keepdims=True)
            attended_ref[part, columns] = (acc[:, columns] / mass).astype(BF16)
            top[h, part, :] = top[h, part, :] + jnp.log2(mass)
        if index == 0:
            loads[1].wait()
        middle = tokens_ref[part, :].astype(F32) + dot(attended_ref[part, :], wo_v[...], NN)
        middle_ref[part, :] = middle
        rows_two = normed(middle, gain_b_ref[...]).astype(BF16)
        hidden_v[part, :] = rows_two
        routed = routed_ref[part, :] > 0.0
        logits = jnp.where(routed, dot(rows_two, small_ref[...], NN), MASKED)
        power = jnp.exp(logits - jnp.max(logits, axis=1, keepdims=True))
        power = jnp.where(routed, power, 0.0)
        gate_ref[part, :] = power / jnp.sum(power, axis=1, keepdims=True)
        if index == 1:
            weights_ref[0, 0] = gate_ref[...].T[:expert_count, :]
        line = hidden_lines[index]
        line.send(0)
        for i in range(line.count):
            line.across(i, 0).start()
        own(index).start()

    def own(index):
        return pltpu.make_async_copy(
            hidden_v.at[parts[index]],
            hidden_all_ref.at[0, 0, parts[index]],
            own_sem.at[index],
        )

    begin(0)

    def first_turn(t, carry):
        for k in range(1, chips):

            @pl.when(t == k)
            def _():
                kv_line.receive(k - 1)
                if k < chips - 1:
                    kv_line.send(k)
                else:
                    grad_line.send(chips - 2)

        r = chunk_order(chip, chips - 1 - t, chips)
        kv_line.arrived(r)
        turn(0, r)
        return carry

    lax.fori_loop(0, chips, first_turn, 0)
    end(0)
    begin(1)
    early = [step for step in range(chips - 1) if 2 * step + 2 < chips]

    def second_turn(t, carry):
        for step in early:

            @pl.when(t == 2 * step + 2)
            def _():
                hidden_lines[0].receive(step)
                if step + 1 < chips - 1:
                    hidden_lines[0].send(step + 1)

        turn(1, t)
        return carry

    lax.fori_loop(0, chips, second_turn, 0)
    grad_line.receive(chips - 2)
    late = [step for step in range(chips - 1) if step not in early]
    for step in late[:1]:
        hidden_lines[0].receive(step)
        if step + 1 < chips - 1:
            hidden_lines[0].send(step + 1)
    end(1)
    for h in range(QUERY_HEADS):
        lse_ref[h] = top[h].T[:1, :]
    for step in late[1:]:
        hidden_lines[0].receive(step)
        if step + 1 < chips - 1:
            hidden_lines[0].send(step + 1)
    for step in range(chips - 1):
        hidden_lines[1].receive(step)
        if step + 1 < chips - 1:
            hidden_lines[1].send(step + 1)
    for line in hidden_lines:
        for slot in range(chips):
            line.arrived(slot)
        line.sent()
    kv_line.sent()
    gate_gather.finish()
    grad_line.finish(chips - 2)
    for index in range(2):
        own(index).wait()


def front(
    tokens,
    gain_a,
    gain_b,
    small,
    cosine,
    sine,
    order_mine,
    pos_mine,
    order_keys,
    routed,
    table,
    qkv,
    w_out,
    w_gate,
    grad_all,
    chips,
    fsdp,
    collective_id,
):
    rows, width = tokens.shape
    expert_count = table.shape[0]
    kv_width = KVH * HEAD_SIZE
    vmem = pl.BlockSpec(memory_space=pltpu.VMEM)
    anywhere = pl.BlockSpec(memory_space=pl.ANY)
    shapes = [
        ((rows, width), BF16),
        ((rows, width), BF16),
        ((2, chips, rows, 2 * kv_width), BF16),
        ((2, chips, expert_count, rows), F32),
        ((rows, width), BF16),
        ((QUERY_HEADS, 1, rows), F32),
        ((rows, width), F32),
        ((rows, LANES), F32),
        ((2, chips, expert_count, rows), F32),
        ((2, chips, rows, width), BF16),
        ((w_gate.shape[0], width, w_gate.shape[2]), BF16),
        (grad_all.shape, BF16),
    ]
    flops = 4 * rows * (2 * chips * rows) * width + 2 * rows * width * (2 * width + 2 * kv_width)
    return pl.pallas_call(
        functools.partial(front_kernel, HEAD_SIZE ** (-0.5), chips, fsdp, expert_count),
        out_shape=[jax.ShapeDtypeStruct(shape, kind) for shape, kind in shapes],
        in_specs=[vmem] * 11 + [anywhere] * 4,
        out_specs=[vmem] * 9 + [anywhere] * 3,
        scratch_shapes=[
            pltpu.VMEM(qkv.shape, BF16),
            pltpu.VMEM(w_out.shape, BF16),
            pltpu.VMEM(w_gate.shape, BF16),
            pltpu.VMEM((rows, width), BF16),
            pltpu.VMEM((rows // 2, 2 * rows), F32),
            pltpu.VMEM((QUERY_HEADS, rows, LANES), F32),
            pltpu.VMEM((QUERY_HEADS, rows // 2, LANES), F32),
            pltpu.VMEM((rows // 2, width), F32),
            pltpu.SemaphoreType.DMA((2,)),
            pltpu.SemaphoreType.DMA((2,)),
            pltpu.SemaphoreType.DMA,
            pltpu.SemaphoreType.DMA((fsdp - 1,)),
            pltpu.SemaphoreType.DMA((fsdp - 1,)),
        ]
        + line_scratch([None] * 2, chips)
        + line_scratch([None], chips)
        + line_scratch([None], chips)
        + line_scratch([None] * 2, chips),
        input_output_aliases={14: 11},
        compiler_params=pltpu.CompilerParams(
            collective_id=collective_id, has_side_effects=True, vmem_limit_bytes=FRONT_VMEM_BYTES
        ),
        cost_estimate=pl.CostEstimate(
            flops=flops, bytes_accessed=40_000_000, transcendentals=rows * rows * chips * 24
        ),
        name="front",
    )(
        tokens,
        gain_a[None, :],
        gain_b[None, :],
        small,
        cosine,
        sine,
        order_mine[:, None],
        pos_mine[:, None],
        order_keys.reshape(2 * chips, 1, rows),
        routed,
        table,
        qkv,
        w_out,
        w_gate,
        grad_all,
    )


def attention_back_kernel(
    scale,
    chips,
    q_ref,
    k_ref,
    v_ref,
    o_ref,
    do_ref,
    lse_ref,
    oq_ref,
    pq_ref,
    ok_ref,
    cos_ref,
    sin_ref,
    mine_ref,
    other_ref,
    dq_ref,
    kv_ref,
    own_ref,
    right_ref,
    left_ref,
    bias,
    dk_acc,
    dv_acc,
    kv_total,
    mine_v,
    pair,
    got,
    kv_v,
    kv_pair,
    kv_got,
    load_sem,
    store_sem,
    swap_send,
    swap_recv,
    r_send,
    r_recv,
    l_send,
    l_recv,
    kv_swap_send,
    kv_swap_recv,
    kr_send,
    kr_recv,
    kl_send,
    kl_recv,
):
    ctx, me, chip, core, sibling = place()
    keys = k_ref.shape[0]
    tiles = keys // KEY_TILE
    rows = q_ref.shape[0]
    per_group = QUERY_HEADS // KVH
    head = pl.program_id(0)

    order = []
    for step in range(chips - 1):
        for r in (chips - 1 - step, step + 1):
            if r not in order:
                order.append(r)
    order.append(0)
    swaps = [
        remote(other_ref.at[r], pair.at[r], swap_send.at[r], swap_recv.at[r], (sibling, me))
        for r in range(chips)
    ]
    slots = mine_v.shape[0]
    loads = [
        pltpu.make_async_copy(mine_ref.at[r], mine_v.at[j % slots], load_sem.at[j % slots])
        for j, r in enumerate(order)
    ]
    line = LineSum(
        chips,
        lambda r: lambda: [pair.at[r]],
        lambda r: pair.at[r],
        got,
        (r_send, r_recv, l_send, l_recv),
    )

    def join(j):
        loads[j].wait()
        swaps[order[j]].wait_recv()
        add_into(pair.at[order[j]], [pair.at[order[j]], mine_v.at[j % slots]])
        if j + slots < chips:
            loads[j + slots].start()

    def kv_swap(group, r):
        return remote(
            kv_v.at[group, 1, r],
            kv_pair.at[group, r],
            kv_swap_send.at[group, r],
            kv_swap_recv.at[group, r],
            (sibling, me),
        )

    def kv_line(group):
        def held(r):
            kv_swap(group, r).wait_recv()
            return lambda: [kv_v.at[group, 0, r], kv_pair.at[group, r]]

        return LineSum(
            chips,
            held,
            lambda r: kv_pair.at[group, r],
            kv_got.at[group],
            tuple(sem.at[group] for sem in (kr_send, kr_recv, kl_send, kl_recv)),
        )

    def kv_start(group):
        for q in range(2):
            for r in range(chips):
                part = pl.ds((q * chips + r) * rows, rows)
                kv_v[group, q, r, :, :HEAD_SIZE] = (dk_acc[part, :] * scale).astype(BF16)
                kv_v[group, q, r, :, HEAD_SIZE:] = dv_acc[part, :].astype(BF16)
        for r in order:
            kv_swap(group, r).start()

    @pl.when(head == 0)
    def _():
        greet(chips, [], True)
        for r in order:
            swaps[r].start()
        for copy in loads[:slots]:
            copy.start()

        def fill(t, carry):
            tile = pl.ds(pl.multiple_of(t * KEY_TILE, KEY_TILE), KEY_TILE)
            gap = oq_ref[...] - ok_ref[tile, :]
            bias[tile, :] = jnp.where((gap >= 0) & (gap <= pq_ref[...]), 0.0, MASKED)
            return carry

        lax.fori_loop(0, tiles, fill, 0)

    @pl.when(lax.rem(head, per_group) == 0)
    def _():
        dk_acc[...] = jnp.zeros_like(dk_acc)
        dv_acc[...] = jnp.zeros_like(dv_acc)

    query = q_ref[...]
    grad = do_ref[...]
    lse = lse_ref[0]
    product = grad.astype(F32) * o_ref[...].astype(F32)
    delta = jnp.sum(product.T, axis=0, keepdims=True)

    def step(t, acc):
        tile = pl.ds(pl.multiple_of(t * KEY_TILE, KEY_TILE), KEY_TILE)
        key = k_ref[tile, :]
        raw = dot(key, query, NT) * (scale * LOG2E) + bias[tile, :]
        probs = jnp.exp2(raw - lse)
        prob_grad = dot(v_ref[tile, :], grad, NT)
        score_grad = (probs * (prob_grad - delta)).astype(BF16)
        dv_acc[tile, :] += dot(probs.astype(BF16), grad, NN)
        dk_acc[tile, :] += dot(score_grad, query, NN)
        return acc + dot(score_grad, key, TN)

    acc = lax.fori_loop(0, tiles, step, jnp.zeros((rows, HEAD_SIZE), F32))
    def turn_back(value):
        back = value * cos_ref[...] - pltpu.roll(value, HEAD_SIZE // 2, 1) * sin_ref[...]
        return back.astype(BF16)

    dq_ref[...] = turn_back(acc * scale)

    last = QUERY_HEADS - 1
    stride = max(1, last // (chips - 2))
    early = {per_group + 2 * s: s for s in range(chips - 1) if per_group + 2 * s < last}
    for h in range(QUERY_HEADS):

        @pl.when(head == h)
        def _():
            if h == 0:
                for j in range(chips):
                    join(j)
            for s in range(chips - 2):
                if h == s * stride:
                    line.step(s)
            if h % per_group == per_group - 1:
                kv_start(h // per_group)
            if h in early:
                kv_line(0).step(early[h])

    @pl.when(head == last)
    def _():
        def store(k, r, target):
            return pltpu.make_async_copy(pair.at[r], target, store_sem.at[k])

        @pl.when((chip >= 1) & (chip + 1 < chips))
        def _():
            add_into(pair.at[1], [pair.at[1], line.from_left(chips - 3)])
            add_into(pair.at[chips - 1], [pair.at[chips - 1], line.from_right(chips - 3)])

        for copy in (
            store(0, 0, own_ref),
            store(1, 1, right_ref),
            store(2, chips - 1, left_ref),
        ):
            copy.start()
        for group in range(KVH):
            one = kv_line(group)
            for s in range(chips - 1):
                if group > 0 or s not in early.values():
                    one.step(s)
            one.total(kv_total)
            kv_ref[:, group * HEAD_SIZE : (group + 1) * HEAD_SIZE] = turn_back(
                kv_total[:, :HEAD_SIZE]
            )
            kv_ref[:, (KVH + group) * HEAD_SIZE : (KVH + group + 1) * HEAD_SIZE] = kv_total[
                :, HEAD_SIZE:
            ].astype(BF16)
        for group in range(KVH):
            kv_line(group).finish()
            for r in range(chips):
                kv_swap(group, r).wait_send()
        line.finish(chips - 2)
        for swap in swaps:
            swap.wait_send()
        for copy in (
            store(0, 0, own_ref),
            store(1, 1, right_ref),
            store(2, chips - 1, left_ref),
        ):
            copy.wait()


def attention_back(
    queries,
    kv,
    attended,
    attended_grad,
    lse,
    order_mine,
    pos_mine,
    order_keys,
    cosine,
    sine,
    mine,
    other,
    collective_id,
):
    rows = queries.shape[0]
    keys = kv.shape[0]
    chips, unused, width = mine.shape
    per_group = QUERY_HEADS // KVH
    head_rows = pl.BlockSpec((rows, HEAD_SIZE), lambda h: (0, h))
    anywhere = pl.BlockSpec(memory_space=pl.ANY)
    return pl.pallas_call(
        functools.partial(attention_back_kernel, HEAD_SIZE ** (-0.5), chips),
        grid=(QUERY_HEADS,),
        out_shape=[
            jax.ShapeDtypeStruct(queries.shape, BF16),
            jax.ShapeDtypeStruct((rows, 2 * KVH * HEAD_SIZE), BF16),
        ]
        + [jax.ShapeDtypeStruct((rows, width), BF16)] * 3,
        in_specs=[
            head_rows,
            pl.BlockSpec((keys, HEAD_SIZE), lambda h: (0, h // per_group)),
            pl.BlockSpec((keys, HEAD_SIZE), lambda h: (0, KVH + h // per_group)),
            head_rows,
            head_rows,
            pl.BlockSpec((1, 1, rows), lambda h: (h, 0, 0)),
            pl.BlockSpec((1, rows), lambda h: (0, 0)),
            pl.BlockSpec((1, rows), lambda h: (0, 0)),
            pl.BlockSpec((keys, 1), lambda h: (0, 0)),
            pl.BlockSpec((rows, HEAD_SIZE), lambda h: (0, 0)),
            pl.BlockSpec((rows, HEAD_SIZE), lambda h: (0, 0)),
            anywhere,
            anywhere,
        ],
        out_specs=[
            head_rows,
            pl.BlockSpec((rows, 2 * KVH * HEAD_SIZE), lambda h: (0, 0)),
            anywhere,
            anywhere,
            anywhere,
        ],
        scratch_shapes=[
            pltpu.VMEM((keys, rows), F32),
            pltpu.VMEM((keys, HEAD_SIZE), F32),
            pltpu.VMEM((keys, HEAD_SIZE), F32),
            pltpu.VMEM((rows, 2 * HEAD_SIZE), F32),
            pltpu.VMEM((2 if chips <= 4 else 1, rows, width), BF16),
            pltpu.VMEM((chips, rows, width), BF16),
            pltpu.VMEM((chips + 1, rows, width), BF16),
            pltpu.VMEM((KVH, 2, chips, rows, 2 * HEAD_SIZE), BF16),
            pltpu.VMEM((KVH, chips, rows, 2 * HEAD_SIZE), BF16),
            pltpu.VMEM((KVH, chips + 1, rows, 2 * HEAD_SIZE), BF16),
            pltpu.SemaphoreType.DMA((2,)),
            pltpu.SemaphoreType.DMA((3,)),
            pltpu.SemaphoreType.DMA((chips,)),
            pltpu.SemaphoreType.DMA((chips,)),
        ]
        + [pltpu.SemaphoreType.DMA((chips - 1,)) for unused in range(4)]
        + [pltpu.SemaphoreType.DMA((KVH, chips)) for unused in range(2)]
        + [pltpu.SemaphoreType.DMA((KVH, chips - 1)) for unused in range(4)],
        compiler_params=pltpu.CompilerParams(
            collective_id=collective_id, has_side_effects=True, vmem_limit_bytes=BACK_VMEM_BYTES
        ),
        cost_estimate=pl.CostEstimate(
            flops=10 * rows * keys * HEAD_SIZE * QUERY_HEADS,
            bytes_accessed=10 * rows * QUERY_HEADS * HEAD_SIZE + 8 * keys * KVH * HEAD_SIZE,
            transcendentals=rows * keys * QUERY_HEADS,
        ),
        name="attention_back",
    )(
        queries,
        kv,
        kv,
        attended,
        attended_grad,
        lse,
        order_mine[None, :],
        pos_mine[None, :],
        order_keys[:, None],
        cosine,
        sine,
        mine,
        other,
    )


def experts_kernel(
    capacity,
    local_experts,
    expert_count,
    chips,
    fsdp,
    per,
    hidden_ref,
    grad_ref,
    table_ref,
    weight_ref,
    gate_ref,
    up_ref,
    down_ref,
    returned_ref,
    out_mine_ref,
    out_other_ref,
    gate_grad_ref,
    up_grad_ref,
    down_grad_ref,
    x_ref,
    pg_ref,
    inner_ref,
    da_ref,
    db_ref,
    gate_v,
    up_v,
    down_v,
    hidden_v,
    grad_v,
    out_v,
    x_v,
    pg_v,
    g_v,
    inner_v,
    da_v,
    db_v,
    mine_v,
    other_v,
    pair,
    got,
    stage_tall,
    weight_sem,
    load_sem,
    out_sem,
    save_sem,
    swap_send,
    swap_recv,
    right_send,
    right_recv,
    left_send,
    left_recv,
    stage_sem,
):
    ctx, me, chip, core, sibling = place()
    tokens = hidden_v.shape[1]
    width = hidden_v.shape[2]
    slots = x_v.shape[1]
    slot_rows = slots // 2
    units = inner_v.shape[2]
    total_rows = x_ref.shape[1]
    first = ctx * local_experts

    weights_in = [
        pltpu.make_async_copy(src, dst, weight_sem.at[k])
        for k, (src, dst) in enumerate(
            ((gate_ref, gate_v), (up_ref, up_v), (down_ref, down_v))
        )
    ]

    def load(i):
        r = chunk_order(chip, i, chips)
        return [
            pltpu.make_async_copy(hidden_ref.at[:, r], hidden_v, load_sem.at[0]),
            pltpu.make_async_copy(grad_ref.at[:, r], grad_v, load_sem.at[1]),
        ]

    def saves(i):
        rows = pl.ds(i * slots, slots)
        return [
            pltpu.make_async_copy(src, dst.at[:, rows], save_sem.at[k])
            for k, (src, dst) in enumerate(
                ((x_v, x_ref), (pg_v, pg_ref), (inner_v, inner_ref), (da_v, da_ref), (db_v, db_ref))
            )
        ]

    def out_copies(i):
        r = chunk_order(chip, i, chips)
        return [
            pltpu.make_async_copy(out_v.at[0], out_mine_ref.at[r], out_sem.at[0]),
            pltpu.make_async_copy(out_v.at[1], out_other_ref.at[r], out_sem.at[1]),
        ]

    def swap(i):
        r = chunk_order(chip, i, chips)
        return remote(
            other_v.at[lax.rem(i, 2)],
            pair.at[r],
            swap_send.at[r],
            swap_recv.at[r],
            (sibling, me),
        )

    def join(i):
        r = chunk_order(chip, i, chips)
        swap(i).wait_recv()
        add_into(pair.at[r], [pair.at[r], mine_v.at[lax.rem(i, 2)]])

    line = LineSum(
        chips,
        lambda r: lambda: [pair.at[r]],
        lambda r: pair.at[r],
        got,
        (right_send, right_recv, left_send, left_recv),
    )

    for copy in load(0) + weights_in:
        copy.start()
    greet(chips, [], True)

    slot = lax.broadcasted_iota(jnp.int32, (slot_rows, tokens), 0).astype(F32) + 1.0
    slot = jnp.where(slot <= capacity, slot, -1.0)
    lane = lax.broadcasted_iota(jnp.int32, (slots, LANES), 1)

    def chunk(i, carry):
        r = chunk_order(chip, i, chips)
        for copy in load(i):
            copy.wait()

        @pl.when(i >= 1)
        def _():
            for copy in saves(i - 1):
                copy.wait()

        picks = [[], []]
        weight_rows = []
        for e in range(local_experts):
            rows_w = []
            for q in range(2):
                hit = slot == table_ref[q, r, pl.ds(first + e, 1), :]
                pick = jnp.where(hit, 1.0, 0.0).astype(BF16)
                weight = weight_ref[q, r, pl.ds(first + e, 1), :]
                w = jnp.sum(jnp.where(hit, weight, 0.0), axis=1, keepdims=True)
                rows = pl.ds(q * slot_rows, slot_rows)
                x_v[e, rows, :] = dot(pick, hidden_v[q], NN).astype(BF16)
                g = dot(pick, grad_v[q], NN)
                g_v[e, rows, :] = g.astype(BF16)
                pg_v[e, rows, :] = (w * g).astype(BF16)
                picks[q].append(pick)
                rows_w.append(w)
            weight_rows.append(jnp.concatenate(rows_w, axis=0))

        @pl.when(i + 1 < chips)
        def _():
            for copy in load(i + 1):
                copy.start()

        @pl.when(i == 0)
        def _():
            for copy in weights_in:
                copy.wait()

        outs = [[], []]
        backs = [[], []]
        for e in range(local_experts):
            x = x_v[e]
            pair_grad = pg_v[e]
            w = weight_rows[e]
            gate = gate_v[e * width : (e + 1) * width, :]
            up = up_v[e * width : (e + 1) * width, :]
            down = down_v[e * units : (e + 1) * units, :]
            gate_pre = dot(x, gate, NN)
            up_pre = dot(x, up, NN)
            sig = jax.nn.sigmoid(gate_pre)
            silu = gate_pre * sig
            inner = (silu * up_pre).astype(BF16)
            inner_v[e] = inner
            expert_out = dot(inner, down, NN).astype(BF16).astype(F32)
            gate_grad = jnp.sum(expert_out * g_v[e].astype(F32), axis=1, keepdims=True)
            inner_grad = dot(pair_grad, down, NT)
            da = (inner_grad * up_pre * sig * (1.0 + gate_pre * (1.0 - sig))).astype(BF16)
            db = (inner_grad * silu).astype(BF16)
            da_v[e] = da
            db_v[e] = db
            row_grad = (dot(da, gate, NT) + dot(db, up, NT)).astype(BF16)
            high = gate_grad.astype(BF16).astype(F32)
            extra = jnp.where(lane == first + e, high, 0.0) + jnp.where(
                lane == expert_count + first + e, gate_grad - high, 0.0
            )
            back = jnp.concatenate([row_grad, extra.astype(BF16)], axis=1)
            out_rows = (w * expert_out).astype(BF16)
            for q in range(2):
                part = slice(q * slot_rows, (q + 1) * slot_rows)
                outs[q].append(out_rows[part])
                backs[q].append(back[part])

        for copy in saves(i):
            copy.start()

        @pl.when(i >= 1)
        def _():
            for copy in out_copies(i - 1):
                copy.wait()

        @pl.when(i >= 2)
        def _():
            swap(i - 2).wait_send()

        for q in range(2):
            pick = jnp.concatenate(picks[q], axis=0)
            held = other_v if q else mine_v
            held[lax.rem(i, 2)] = dot(pick, jnp.concatenate(backs[q], axis=0), TN).astype(BF16)
            if q:
                swap(i).start()
        for q in range(2):
            pick = jnp.concatenate(picks[q], axis=0)
            out_v[q] = dot(pick, jnp.concatenate(outs[q], axis=0), TN).astype(BF16)
        for copy in out_copies(i):
            copy.start()

        @pl.when(i == 0)
        def _():
            join(0)
            line.step(0)

        @pl.when(i >= 2)
        def _():
            join(i - 1)

        for step in range(1, chips - 1):
            if 2 * step < chips:

                @pl.when(i == 2 * step)
                def _():
                    line.step(step)

        return carry

    lax.fori_loop(0, chips, chunk, 0)
    join(chips - 1)
    for copy in saves(chips - 1):
        copy.wait()
    for copy in out_copies(chips - 1):
        copy.wait()
    for i in range(max(0, chips - 2), chips):
        swap(i).wait_send()

    shard = width // fsdp
    blocks = fsdp // per
    block = per * shard

    def fetch(copies):
        copies = [
            pltpu.make_async_copy(src, dst, save_sem.at[k])
            for k, (src, dst) in enumerate(copies)
        ]
        for copy in copies:
            copy.start()
        for copy in copies:
            copy.wait()

    def products(e, staged, target, product):
        def write(f):
            return [
                pltpu.make_async_copy(
                    staged(lax.rem(f, 2), p),
                    target.at[f * per + p, e],
                    stage_sem.at[lax.rem(f, 2), p],
                )
                for p in range(per)
            ]

        def one(f, carry):
            @pl.when(f >= 2)
            def _():
                for copy in write(f - 2):
                    copy.wait()

            product(f)
            for copy in write(f):
                copy.start()
            return carry

        lax.fori_loop(0, blocks, one, 0)
        for f in range(max(0, blocks - 2), blocks):
            for copy in write(f):
                copy.wait()

    def stage_wide(slot, p):
        return hidden_v.at[slot, pl.ds(p * shard, shard), pl.ds(0, units)]

    def wide(e, held, target):
        def product(f):
            columns = pl.ds(pl.multiple_of(f * block, LANES), block)
            value = dot(
                down_v[:total_rows, columns],
                held[e * total_rows : (e + 1) * total_rows, :],
                TN,
            ).astype(BF16)
            for p in range(per):
                stage_wide(lax.rem(f, 2), p)[...] = value[p * shard : (p + 1) * shard, :]

        products(e, stage_wide, target, product)

    def tall(e, target):
        def product(f):
            columns = pl.ds(pl.multiple_of(f * block, LANES), block)
            value = dot(
                gate_v[e * total_rows : (e + 1) * total_rows, :],
                down_v[:total_rows, columns],
                TN,
            ).astype(BF16)
            for p in range(per):
                stage_tall[lax.rem(f, 2), p] = value[:, p * shard : (p + 1) * shard]

        products(e, lambda slot, p: stage_tall.at[slot, p], target, product)

    work = []
    for e in range(local_experts):
        copies = [(x_ref.at[e], down_v.at[:total_rows])]
        if e == 0:
            for k in range(local_experts):
                held = pl.ds(k * total_rows, total_rows)
                copies += [(da_ref.at[k], gate_v.at[held]), (db_ref.at[k], up_v.at[held])]
        work.append(lambda copies=copies: fetch(copies))
        work.append(lambda e=e: wide(e, gate_v, gate_grad_ref))
        work.append(lambda e=e: wide(e, up_v, up_grad_ref))
    for e in range(local_experts):
        copies = [(pg_ref.at[e], down_v.at[:total_rows])]
        if e == 0:
            for k in range(local_experts):
                copies.append((inner_ref.at[k], gate_v.at[pl.ds(k * total_rows, total_rows)]))
        work.append(lambda copies=copies: fetch(copies))
        work.append(lambda e=e: tall(e, down_grad_ref))
    late = [step for step in range(1, chips - 1) if 2 * step >= chips]
    for n, task in enumerate(work):
        task()
        if n == LINE_TASK or (n > LINE_TASK and late):
            if late:
                line.step(late.pop(0))
    for step in late:
        line.step(step)

    line.total(returned_ref)
    line.finish()


def experts_pass(
    hidden, grad, table, weights, gate, up, down, capacity, expert_count, fsdp, collective_id
):
    unused, chips, tokens, width = grad.shape
    local_experts, unused, units = gate.shape
    slots = 2 * SLOT_STEP * -(-capacity // SLOT_STEP)
    total = chips * slots
    shard = width // fsdp
    per = 1 if shard % LANES == 0 else 2
    wide = width + LANES
    anywhere = pl.BlockSpec(memory_space=pl.ANY)
    vmem = pl.BlockSpec(memory_space=pltpu.VMEM)
    flops = 2 * total * width * units * local_experts * 9 + 8 * total * tokens * width
    saved = [(local_experts, total, width)] * 2 + [(local_experts, total, units)] * 3
    held = [(local_experts, slots, width)] * 3 + [(local_experts, slots, units)] * 3
    outs = pl.pallas_call(
        functools.partial(
            experts_kernel, capacity, local_experts, expert_count, chips, fsdp, per
        ),
        out_shape=[
            jax.ShapeDtypeStruct((tokens, wide), BF16),
            jax.ShapeDtypeStruct((chips, tokens, width), BF16),
            jax.ShapeDtypeStruct((chips, tokens, width), BF16),
            jax.ShapeDtypeStruct((fsdp, local_experts, shard, units), BF16),
            jax.ShapeDtypeStruct((fsdp, local_experts, shard, units), BF16),
            jax.ShapeDtypeStruct((fsdp, local_experts, units, shard), BF16),
        ]
        + [jax.ShapeDtypeStruct(shape, BF16) for shape in saved],
        in_specs=[anywhere, anywhere, vmem, vmem, anywhere, anywhere, anywhere],
        out_specs=[vmem] + [anywhere] * 10,
        scratch_shapes=[
            pltpu.VMEM((local_experts * width, units), BF16),
            pltpu.VMEM((local_experts * width, units), BF16),
            pltpu.VMEM((local_experts * units, width), BF16),
            pltpu.VMEM((2, tokens, width), BF16),
            pltpu.VMEM((2, tokens, width), BF16),
            pltpu.VMEM((2, tokens, width), BF16),
        ]
        + [pltpu.VMEM(shape, BF16) for shape in held]
        + [
            pltpu.VMEM((2, tokens, wide), BF16),
            pltpu.VMEM((2, tokens, wide), BF16),
            pltpu.VMEM((chips, tokens, wide), BF16),
            pltpu.VMEM((chips + 1, tokens, wide), BF16),
            pltpu.VMEM((2, per, units, shard), BF16),
            pltpu.SemaphoreType.DMA((3,)),
            pltpu.SemaphoreType.DMA((2,)),
            pltpu.SemaphoreType.DMA((2,)),
            pltpu.SemaphoreType.DMA((5,)),
            pltpu.SemaphoreType.DMA((chips,)),
            pltpu.SemaphoreType.DMA((chips,)),
        ]
        + [pltpu.SemaphoreType.DMA((chips - 1,)) for unused in range(4)]
        + [pltpu.SemaphoreType.DMA((2, per))],
        compiler_params=pltpu.CompilerParams(
            collective_id=collective_id, has_side_effects=True, vmem_limit_bytes=EXPERT_VMEM_BYTES
        ),
        cost_estimate=pl.CostEstimate(
            flops=flops, bytes_accessed=100_000_000, transcendentals=total * units * 2
        ),
        name="experts",
    )(
        hidden,
        grad,
        table,
        weights,
        gate.reshape(local_experts * width, units),
        up.reshape(local_experts * width, units),
        down.reshape(local_experts * units, width),
    )
    return outs[:6]


def body(
    tokens,
    grad_out,
    order,
    lengths,
    routes,
    gain_one,
    gain_two,
    w_query,
    w_key,
    w_value,
    w_out,
    w_router,
    w_gate,
    w_up,
    w_down,
):
    fsdp = lax.axis_size("fsdp")
    chips = lax.axis_size("ctx") // 2
    ctx_index = lax.axis_index("ctx")
    chip = ctx_index // 2
    core = lax.rem(ctx_index, 2)
    tok_rows = tokens.shape[1]
    width = tokens.shape[2]
    top_count = routes.shape[2]
    local_experts = w_gate.shape[0]
    expert_count = local_experts * chips * 2
    capacity = 5 * tok_rows * top_count // (4 * expert_count)
    kv_width = KVH * HEAD_SIZE
    shard = gain_one.shape[0]

    small = jnp.concatenate(
        [
            w_router,
            gain_one[:, None],
            gain_two[:, None],
            jnp.zeros((shard, LANES - expert_count - 2), BF16),
        ],
        axis=1,
    )
    qkv_shard = jnp.concatenate([w_query, w_key, w_value], axis=1)
    qkv_full, small_full, out_full, grad_all = gather(
        [qkv_shard, small, w_out], [grad_out[0]], chips - 2, fsdp, chips, 0
    )

    qkv_full, w_up, w_down = lax.optimization_barrier((qkv_full, w_up, w_down))
    up_full, down_full = (
        lax.all_gather(w_up, "fsdp", axis=1, tiled=True),
        lax.all_gather(w_down, "fsdp", axis=2, tiled=True),
    )
    router_full = small_full[:, :expert_count]
    gain_a = small_full[:, expert_count].astype(F32)
    gain_b = small_full[:, expert_count + 1].astype(F32)

    order_row = order[0]
    start_row = ctx_index * tok_rows
    order_mine = lax.dynamic_slice_in_dim(order_row, start_row, tok_rows)
    ends = jnp.cumsum(lengths[0])
    starts = ends - lengths[0]
    past = order_mine[:, None] >= ends[None, :]
    doc_start = jnp.max(jnp.where(past, ends[None, :], starts[:1]), axis=1)
    pos_mine = order_mine - doc_start
    by_chip = jnp.roll(order_row.reshape(chips, 2, tok_rows), -chip, axis=0)
    by_chip = jnp.where(core == 0, by_chip, by_chip[:, ::-1])
    order_keys = jnp.swapaxes(by_chip, 0, 1).reshape(-1)

    route_rows = routes[0]
    route_onehot = (route_rows[:, :, None] == jnp.arange(expert_count)[None, None, :]).astype(F32)
    routed = jnp.sum(route_onehot, axis=1)
    earlier = (order_mine[None, :] < order_mine[:, None]).astype(BF16)
    ranks = jnp.dot(earlier, routed.astype(BF16), preferred_element_type=F32)
    table = jnp.where(routed > 0, jnp.minimum(ranks, capacity) + 1.0, 0.0)

    half_dim = HEAD_SIZE // 2
    freqs = ROPE_BASE ** (-2.0 * jnp.arange(half_dim).astype(F32) / HEAD_SIZE)
    angles = pos_mine.astype(F32)[:, None] * freqs[None, :]
    cosine = jnp.concatenate([jnp.cos(angles), jnp.cos(angles)], axis=1)
    sine = jnp.concatenate([-jnp.sin(angles), jnp.sin(angles)], axis=1)

    inputs = tokens[0].astype(F32)
    (
        queries,
        hidden_one,
        kv_all,
        table_all,
        attended,
        lse,
        middle,
        gate_weights,
        weights_all,
        hidden_all,
        gate_full,
        grad_all,
    ) = front(
        tokens[0],
        gain_a,
        gain_b,
        small_full,
        cosine,
        sine,
        order_mine,
        pos_mine,
        order_keys,
        jnp.pad(routed, ((0, 0), (0, LANES - expert_count))),
        table.T,
        qkv_full,
        out_full,
        w_gate,
        grad_all,
        chips,
        fsdp,
        1,
    )
    kv_all = kv_all.reshape(-1, 2 * kv_width)
    gate_weights = gate_weights[:, :expert_count]
    hidden_two = hidden_all[0, 0]

    returned, out_mine, out_other, gate_local, up_local, down_local = experts_pass(
        hidden_all,
        grad_all,
        table_all,
        weights_all,
        gate_full,
        up_full,
        down_full,
        capacity,
        expert_count,
        fsdp,
        5,
    )
    expert_grads = [
        lax.psum_scatter(part, "fsdp", scatter_dimension=0, tiled=True)
        for part in (gate_local, up_local, down_local)
    ]

    out_grad = grad_out[0].astype(F32)
    returned = returned.astype(F32)
    extra = returned[:, width:]
    gate_grad = extra[:, :expert_count] + extra[:, expert_count : 2 * expert_count]
    logit_grad = (
        gate_weights * (gate_grad - jnp.sum(gate_weights * gate_grad, axis=-1, keepdims=True))
    ).astype(BF16)
    router_local = jnp.einsum("td,te->de", hidden_two, logit_grad, preferred_element_type=F32)
    hidden_two_grad = returned[:, :width] + jnp.einsum(
        "te,de->td", logit_grad, router_full, preferred_element_type=F32
    )
    unused_two, norm_two_back = jax.vjp(rms_scale, middle, gain_b)
    middle_part, gain_two_local = norm_two_back(hidden_two_grad)
    middle_grad = out_grad + middle_part
    branch_grad = middle_grad.astype(BF16)
    out_local = jnp.einsum("tc,td->cd", attended, branch_grad, preferred_element_type=F32)
    attended_grad = jnp.einsum(
        "td,cd->tc", branch_grad, out_full, preferred_element_type=F32
    ).astype(BF16)

    query_grad, kv_grad, out_own, out_right, out_left = attention_back(
        queries,
        kv_all,
        attended,
        attended_grad,
        lse,
        order_mine,
        pos_mine,
        order_keys,
        cosine,
        sine,
        out_mine,
        out_other,
        3,
    )
    pre_grad = jnp.concatenate([query_grad, kv_grad], axis=1)
    qkv_local = jnp.einsum("td,tc->dc", hidden_one, pre_grad, preferred_element_type=F32)
    hidden_one_grad = jnp.einsum("tc,dc->td", pre_grad, qkv_full, preferred_element_type=F32)
    unused_one, norm_one_back = jax.vjp(rms_scale, inputs, gain_a)
    input_part, gain_one_local = norm_one_back(hidden_one_grad)
    input_grad = (middle_grad + input_part).astype(BF16)

    def halves(local):
        local = local.astype(BF16).reshape(fsdp, 2, shard // 2, local.shape[1])
        pad = -local.shape[3] % (LANES * chips)
        return jnp.pad(local, ((0, 0), (0, 0), (0, 0), (0, pad))) if pad else local

    span = shard * expert_count // 16
    wide = LANES * chips * -(-max(span, shard) // (LANES * chips))
    small_local = jnp.stack(
        [
            jnp.pad(
                router_local.astype(BF16).reshape(fsdp, 16, span),
                ((0, 0), (0, 0), (0, wide - span)),
            ),
            jnp.pad(
                jnp.stack(
                    [gain_one_local.reshape(fsdp, shard), gain_two_local.reshape(fsdp, shard)],
                    axis=1,
                ).astype(BF16),
                ((0, 0), (0, 14), (0, wide - shard)),
            ),
        ],
        axis=1,
    )
    qkv_sum, out_proj_sum, small_sum, out_sum = dense_reduce(
        [halves(qkv_local), halves(out_local), small_local],
        out_own,
        out_right,
        out_left,
        DENSE_PIECE,
        fsdp,
        chips,
        4,
    )
    edge = width + 2 * kv_width
    qkv_grads = qkv_sum.reshape(shard, -1)
    out_proj_grad = out_proj_sum.reshape(shard, -1)[:, :width]
    gate_grad_out, up_grad_out, down_grad_out = (
        after(part, pre_grad)[0].astype(F32) for part in expert_grads
    )
    result = middle + out_sum
    return (
        result.astype(BF16)[None],
        input_grad[None],
        small_sum[1, 0, :shard].astype(F32),
        small_sum[1, 1, :shard].astype(F32),
        qkv_grads[:, :width].astype(F32),
        qkv_grads[:, width : width + kv_width].astype(F32),
        qkv_grads[:, width + kv_width : edge].astype(F32),
        out_proj_grad.astype(F32),
        small_sum[0, :, :span].reshape(shard, expert_count).astype(F32),
        gate_grad_out,
        up_grad_out,
        down_grad_out,
    )


def solution(mesh):
    placed = (
        P("fsdp", "ctx", None),
        P("fsdp", "ctx", None),
        P("fsdp", None),
        P("fsdp", None),
        P("fsdp", "ctx", None),
        P("fsdp"),
        P("fsdp"),
        P("fsdp", None),
        P("fsdp", None),
        P("fsdp", None),
        P("fsdp", None),
        P("fsdp", None),
        P("ctx", "fsdp", None),
        P("ctx", "fsdp", None),
        P("ctx", None, "fsdp"),
    )
    return jax.shard_map(
        body,
        mesh=mesh,
        in_specs=placed,
        out_specs=(
            P("fsdp", "ctx", None),
            P("fsdp", "ctx", None),
            P("fsdp"),
            P("fsdp"),
            P("fsdp", None),
            P("fsdp", None),
            P("fsdp", None),
            P("fsdp", None),
            P("fsdp", None),
            P("ctx", "fsdp", None),
            P("ctx", "fsdp", None),
            P("ctx", None, "fsdp"),
        ),
        check_vma=False,
    )
```

```python
import functools

import jax
import jax.numpy as jnp
from jax import lax
from jax.experimental import pallas as pl
from jax.experimental.pallas import tpu as pltpu
from jax.sharding import PartitionSpec as P

QUERY_HEADS = 12
KVH = 2
HEAD_SIZE = 128

EPSILON = 1e-06
ROPE_BASE = 10000.0
MASKED = -1e30
LOG2E = 1.4426950408889634
LANES = 128
SLOT_STEP = 64
DENSE_PIECE = 1024
LINE_TASK = 4
KEY_TILE = 512
VMEM_BYTES = 56 * 1024 * 1024
EXPERT_VMEM_BYTES = 119 * 512 * 1024
BACK_VMEM_BYTES = 61 * 1024 * 1024
FRONT_VMEM_BYTES = 40 * 1024 * 1024
MESH = pl.DeviceIdType.MESH
F32 = jnp.float32
BF16 = jnp.bfloat16


def dot(left, right, contract):
    return lax.dot_general(left, right, (contract, ((), ())), preferred_element_type=F32)


NN = ((1,), (0,))
NT = ((1,), (1,))
TN = ((0,), (0,))


def rms_scale(value_rows, gain):
    return (
        value_rows
        * lax.rsqrt(jnp.mean(value_rows * value_rows, axis=-1, keepdims=True) + EPSILON)
        * gain
    )


def place():
    ctx = lax.axis_index("ctx")
    core = lax.rem(ctx, 2)
    return ctx, lax.axis_index("fsdp"), ctx // 2, core, ctx + 1 - 2 * core


def peers_of(me, fsdp):
    peers = []
    for shift in range(1, fsdp):
        peer = me
        for bit in range(fsdp.bit_length() - 1):
            if (shift >> bit) & 1:
                digit = lax.rem(me // (1 << bit), 2)
                peer = peer + (1 << bit) - (2 << bit) * digit
        peers.append(peer)
    return peers


def greet(chips, peers, line):
    ctx, me, chip, core, sibling = place()
    barrier = pltpu.get_barrier_semaphore()
    for peer in peers:
        pl.semaphore_signal(barrier, inc=1, device_id=(ctx, peer), device_id_type=MESH)
    pl.semaphore_signal(barrier, inc=1, device_id=(sibling, me), device_id_type=MESH)
    known = len(peers) + 1
    if not line:
        pl.semaphore_wait(barrier, known)
        return
    has_right = chip + 1 < chips
    has_left = chip >= 1

    @pl.when(has_right)
    def _():
        pl.semaphore_signal(barrier, inc=1, device_id=(ctx + 2, me), device_id_type=MESH)

    @pl.when(has_left)
    def _():
        pl.semaphore_signal(barrier, inc=1, device_id=(ctx - 2, me), device_id_type=MESH)

    @pl.when(has_right & has_left)
    def _():
        pl.semaphore_wait(barrier, known + 2)

    @pl.when(jnp.logical_not(has_right & has_left))
    def _():
        pl.semaphore_wait(barrier, known + 1)


class Bounce:
    def __init__(self, src, dst, buffer, sem):
        self.inward = pltpu.make_async_copy(src, buffer, sem)
        self.outward = pltpu.make_async_copy(buffer, dst, sem)

    def start(self):
        self.inward.start()

    def turn(self):
        self.inward.wait()
        self.outward.start()

    def wait(self):
        self.outward.wait()


def remote(src, dst, send_sem, recv_sem, device):
    return pltpu.make_async_remote_copy(
        src_ref=src,
        dst_ref=dst,
        send_sem=send_sem,
        recv_sem=recv_sem,
        device_id=device,
        device_id_type=MESH,
    )


class DenseGather:
    def __init__(self, ins, outs, sems, fsdp):
        buffers, local_sem, send_sem, recv_sem, pass_sem, took_sem = sems
        ctx, me, chip, core, sibling = place()
        self.sends, self.passes, self.locals = [], [], []
        for i in range(len(ins)):
            rows = ins[i].shape[0]
            half = rows // 2
            for j, peer in enumerate(peers_of(me, fsdp)):
                self.sends.append(
                    remote(
                        ins[i].at[pl.ds(core * half, half)],
                        outs[i].at[pl.ds(me * rows + core * half, half)],
                        send_sem.at[i, j],
                        recv_sem.at[i, j],
                        (ctx, peer),
                    )
                )
                got = outs[i].at[pl.ds(peer * rows + core * half, half)]
                self.passes.append(
                    remote(got, got, pass_sem.at[i, j], took_sem.at[i, j], (sibling, me))
                )
            self.locals.append(
                Bounce(ins[i], outs[i].at[pl.ds(me * rows, rows)], buffers[i], local_sem.at[i])
            )

    def start(self):
        for copy in self.sends + self.locals:
            copy.start()

    def finish(self):
        for copy in self.locals:
            copy.turn()
        for send, copy in zip(self.sends, self.passes):
            send.wait_recv()
            copy.start()
        for send in self.sends:
            send.wait_send()
        for copy in self.passes + self.locals:
            copy.wait()


def dense_scratch(arrays, fsdp):
    count = len(arrays)
    return (
        [pltpu.VMEM(a.shape, a.dtype) for a in arrays]
        + [pltpu.SemaphoreType.DMA((count,))]
        + [pltpu.SemaphoreType.DMA((count, fsdp - 1)) for unused in range(4)]
    )


class ShardGather:
    def __init__(self, ref, out, buffer, sems, fsdp):
        own_sem, send_sem, recv_sem = sems
        ctx, me, chip, core, sibling = place()
        rows = ref.shape[1]
        mine = out.at[:, pl.ds(me * rows, rows)]
        self.sends = [
            remote(ref, mine, send_sem.at[j], recv_sem.at[j], (ctx, peer))
            for j, peer in enumerate(peers_of(me, fsdp))
        ]
        self.own = Bounce(ref, mine, buffer, own_sem)

    def start(self):
        for copy in self.sends + [self.own]:
            copy.start()

    def finish(self):
        self.own.turn()
        for copy in self.sends:
            copy.wait()
        self.own.wait()


class LineGather:
    def __init__(self, ins, outs, sems, chips):
        self.ins, self.outs, self.chips = ins, outs, chips
        self.buffers, self.sems = sems[:-7], sems[-7:]
        self.ctx, self.me, self.chip, core, self.sibling = place()
        self.count = len(ins)

    def to_right(self, i, step):
        outs, chips = self.outs, self.chips
        return remote(
            self.ins[i] if step == 0 else outs[i].at[0, chips - step],
            outs[i].at[0, chips - 1 - step],
            self.sems[1].at[i, step],
            self.sems[2].at[i, step],
            (self.ctx + 2, self.me),
        )

    def to_left(self, i, step):
        outs = self.outs
        return remote(
            self.ins[i] if step == 0 else outs[i].at[0, step],
            outs[i].at[0, step + 1],
            self.sems[3].at[i, step],
            self.sems[4].at[i, step],
            (self.ctx - 2, self.me),
        )

    def across(self, i, slot):
        return remote(
            self.ins[i] if slot == 0 else self.outs[i].at[0, slot],
            self.outs[i].at[1, slot],
            self.sems[5].at[i, slot],
            self.sems[6].at[i, slot],
            (self.sibling, self.me),
        )

    def local(self, i):
        return Bounce(self.ins[i], self.outs[i].at[0, 0], self.buffers[i], self.sems[0].at[i])

    def send(self, step):
        chip, chips, count = self.chip, self.chips, self.count

        @pl.when((chip + 1 < chips) & (chip >= step))
        def _():
            for i in range(count):
                self.to_right(i, step).start()

        @pl.when((chip >= 1) & (chip + step < chips))
        def _():
            for i in range(count):
                self.to_left(i, step).start()

    def receive(self, step):
        chip, chips, count = self.chip, self.chips, self.count

        @pl.when(chip >= step + 1)
        def _():
            for i in range(count):
                self.to_right(i, step).wait_recv()
                self.across(i, chips - 1 - step).start()

        @pl.when(chip + step + 1 < chips)
        def _():
            for i in range(count):
                self.to_left(i, step).wait_recv()
                self.across(i, step + 1).start()

    def own(self):
        for i in range(self.count):
            self.across(i, 0).start()
            self.local(i).start()

    def turn_own(self):
        for i in range(self.count):
            self.local(i).turn()

    def finish_own(self):
        for i in range(self.count):
            self.across(i, 0).wait()
            self.local(i).wait()

    def arrived(self, slot):
        for i in range(self.count):
            remote(
                self.outs[i].at[0, slot],
                self.outs[i].at[1, slot],
                self.sems[5].at[i, slot],
                self.sems[6].at[i, slot],
                (self.sibling, self.me),
            ).wait_recv()

    def sent(self):
        chip, chips, count = self.chip, self.chips, self.count
        for step in range(chips - 1):

            @pl.when((chip + 1 < chips) & (chip >= step))
            def _():
                for i in range(count):
                    self.to_right(i, step).wait_send()

            @pl.when((chip >= 1) & (chip + step < chips))
            def _():
                for i in range(count):
                    self.to_left(i, step).wait_send()

        for slot in range(chips):
            for i in range(count):
                self.across(i, slot).wait_send()

    def finish(self, step):
        chip, chips, count = self.chip, self.chips, self.count

        @pl.when((chip + 1 < chips) & (chip >= step))
        def _():
            for i in range(count):
                self.to_right(i, step).wait_send()

        @pl.when((chip >= 1) & (chip + step < chips))
        def _():
            for i in range(count):
                self.to_left(i, step).wait_send()

        @pl.when(chip >= step + 1)
        def _():
            for i in range(count):
                self.across(i, chips - 1 - step).wait()

        @pl.when(chip + step + 1 < chips)
        def _():
            for i in range(count):
                self.across(i, step + 1).wait()


def line_scratch(arrays, chips):
    count = len(arrays)
    return (
        [pltpu.VMEM(a.shape, a.dtype) for a in arrays if a is not None]
        + [pltpu.SemaphoreType.DMA((count,))]
        + [pltpu.SemaphoreType.DMA((count, chips - 1)) for unused in range(4)]
        + [pltpu.SemaphoreType.DMA((count, chips)) for unused in range(2)]
    )


def gather_kernel(dense, line, resumed, steps, fsdp, chips, *refs):
    count = dense + line + resumed
    ins, outs, scratch = refs[:count], refs[count : 2 * count], refs[2 * count :]
    ctx, me, chip, core, sibling = place()
    greet(chips, peers_of(me, fsdp) if dense else [], line > 0)
    split = dense + line
    if dense:
        own, scratch = scratch[: dense + 5], scratch[dense + 5 :]
        first = DenseGather(
            ins[:dense], outs[:dense], (own[:dense],) + tuple(own[dense:]), fsdp
        )
        first.start()
    if line:
        own, scratch = scratch[: line + 7], scratch[line + 7 :]
        second = LineGather(ins[dense:split], outs[dense:split], own, chips)
        for step in range(steps):
            second.send(step)
            if step == 0:
                second.own()
            second.receive(step)
            if step == 0:
                second.turn_own()
    if resumed:
        third = LineGather([None], outs[split:], scratch, chips)
        third.send(chips - 2)
        third.receive(chips - 2)
    if dense:
        first.finish()
    if line:
        second.finish_own()
        for step in range(steps):
            second.finish(step)
    if resumed:
        third.finish(chips - 2)


def gather(dense, line, steps, fsdp, chips, collective_id, resumed=()):
    arrays = list(dense) + list(line) + list(resumed)
    count = len(arrays)
    scratch = (dense_scratch(dense, fsdp) if dense else []) + (
        line_scratch(line, chips) if line else []
    )
    if resumed:
        scratch = scratch + line_scratch([None], chips)
    return pl.pallas_call(
        functools.partial(
            gather_kernel, len(dense), len(line), len(resumed), steps, fsdp, chips
        ),
        out_shape=[jax.ShapeDtypeStruct((fsdp * a.shape[0],) + a.shape[1:], a.dtype) for a in dense]
        + [jax.ShapeDtypeStruct((2, chips) + a.shape, a.dtype) for a in line]
        + [jax.ShapeDtypeStruct(a.shape, a.dtype) for a in resumed],
        in_specs=[pl.BlockSpec(memory_space=pl.ANY)] * count,
        out_specs=[pl.BlockSpec(memory_space=pl.ANY)] * count,
        scratch_shapes=scratch,
        input_output_aliases={count - 1: count - 1} if resumed else {},
        compiler_params=pltpu.CompilerParams(
            collective_id=collective_id, has_side_effects=True, vmem_limit_bytes=VMEM_BYTES
        ),
        name="gather",
    )(*arrays)


def add(*parts):
    total = parts[0].astype(F32)
    for part in parts[1:]:
        total = total + part.astype(F32)
    return total


def add_into(target, parts):
    rows = target.shape[0]
    tile = 32 if rows % 32 == 0 else 16

    def some(t, carry):
        part = pl.ds(pl.multiple_of(t * tile, tile), tile)
        target[part, :] = add(*[ref[part, :] for ref in parts]).astype(target.dtype)
        return carry

    lax.fori_loop(0, rows // tile, some, 0)


class LineSum:
    def __init__(self, chips, held, keep, got, sems):
        self.chips, self.held, self.keep, self.got = chips, held, keep, got
        self.sems = sems
        self.ctx, self.me, self.chip, core, sibling = place()

    def right(self, step):
        return remote(
            self.keep(self.chips - 1 - step),
            self.got.at[step - self.chip],
            self.sems[0].at[step],
            self.sems[1].at[step],
            (self.ctx + 2, self.me),
        )

    def from_left(self, step):
        slot = step + 1 - self.chip
        pltpu.make_async_remote_copy(
            src_ref=self.keep(self.chips - 1 - step),
            dst_ref=self.got.at[slot],
            send_sem=self.sems[0].at[step],
            recv_sem=self.sems[1].at[step],
            device_id=(self.ctx - 2, self.me),
            device_id_type=MESH,
        ).wait_recv()
        return self.got.at[slot]

    def from_right(self, step):
        slot = step + 2
        self.left(step).wait_recv()
        return self.got.at[slot]

    def left(self, step):
        return remote(
            self.keep(step + 1),
            self.got.at[step + 2],
            self.sems[2].at[step],
            self.sems[3].at[step],
            (self.ctx - 2, self.me),
        )

    def step(self, step):
        chip, chips = self.chip, self.chips
        far_right, far_left = chips - 1 - step, step + 1

        @pl.when(chip <= step)
        def _():
            parts = self.held(far_right)
            if step == 0:
                add_into(self.keep(far_right), parts())
            else:

                @pl.when(chip == 0)
                def _():
                    add_into(self.keep(far_right), parts())

                @pl.when(chip >= 1)
                def _():
                    add_into(self.keep(far_right), [self.from_left(step - 1)] + parts())

            self.right(step).start()

        @pl.when(chip >= chips - 1 - step)
        def _():
            parts = self.held(far_left)
            if step == 0:
                add_into(self.keep(far_left), parts())
            else:

                @pl.when(chip == chips - 1)
                def _():
                    add_into(self.keep(far_left), parts())

                @pl.when(chip < chips - 1)
                def _():
                    add_into(self.keep(far_left), [self.from_right(step - 1)] + parts())

            self.left(step).start()

    def total(self, target):
        chip, chips, last = self.chip, self.chips, self.chips - 2
        parts = self.held(0)

        @pl.when(chip == 0)
        def _():
            add_into(target, [self.from_right(last)] + parts())

        @pl.when(chip == chips - 1)
        def _():
            add_into(target, [self.from_left(last)] + parts())

        @pl.when((chip >= 1) & (chip < chips - 1))
        def _():
            add_into(target, [self.from_right(last), self.from_left(last)] + parts())

    def finish(self, steps=None):
        for step in range(self.chips - 1 if steps is None else steps):

            @pl.when(self.chip <= step)
            def _():
                self.right(step).wait_send()

            @pl.when(self.chip >= self.chips - 1 - step)
            def _():
                self.left(step).wait_send()


DENSE_BUFFERS = 5
DENSE_SEMS = 14


class DenseSum:
    def __init__(self, local, held, out, buffers, sems, fsdp, chips):
        self.local, self.held, self.out = local, held, out
        self.pair, self.cross, self.sums, got, self.spread = buffers
        self.sems = sems
        self.chips = chips
        self.ctx, self.me, self.chip, self.core, self.sibling = place()
        self.owners = peers_of(self.me, fsdp) + [self.me]
        self.cut = out.shape[2] // chips
        self.line = LineSum(
            chips,
            lambda r: lambda: [self.keep_ref(r)],
            lambda r: self.keep_ref(r),
            got,
            sems[4:8],
        )

    def keep_ref(self, r):
        return self.sums.at[:, self.columns(r)]

    def columns(self, r):
        owner = lax.rem(self.chip + r, self.chips)
        return pl.ds(pl.multiple_of(owner * self.cut, LANES), self.cut)

    def swap(self, j):
        return remote(
            self.local.at[self.owners[j], 1 - self.core],
            self.pair.at[j],
            self.sems[0].at[j],
            self.sems[1].at[j],
            (self.sibling, self.me),
        )

    def crossing(self, j):
        return remote(
            self.pair.at[j],
            self.cross.at[j],
            self.sems[2].at[j],
            self.sems[3].at[j],
            (self.ctx, self.owners[j]),
        )

    def to_right(self, step):
        return remote(
            self.spread.at[0, (self.chips - step) % self.chips],
            self.spread.at[0, self.chips - 1 - step],
            self.sems[8].at[step],
            self.sems[9].at[step],
            (self.ctx + 2, self.me),
        )

    def to_left(self, step):
        return remote(
            self.spread.at[0, step],
            self.spread.at[0, step + 1],
            self.sems[10].at[step],
            self.sems[11].at[step],
            (self.ctx - 2, self.me),
        )

    def across(self, slot):
        return remote(
            self.spread.at[0, slot],
            self.spread.at[1, slot],
            self.sems[12].at[slot],
            self.sems[13].at[slot],
            (self.sibling, self.me),
        )

    def start(self):
        for j in range(len(self.owners)):
            self.swap(j).start()

    def cross_over(self):
        for j, owner in enumerate(self.owners):
            self.swap(j).wait_recv()
            add_into(self.pair.at[j], [self.held(j, owner), self.pair.at[j]])
            if j < len(self.owners) - 1:
                self.crossing(j).start()

    def stages(self):
        chip, chips = self.chip, self.chips

        def open_up():
            for j in range(len(self.owners) - 1):
                self.crossing(j).wait_recv()
            add_into(
                self.sums,
                [self.cross.at[j] for j in range(len(self.owners) - 1)]
                + [self.pair.at[len(self.owners) - 1]],
            )
            self.line.step(0)

        def summed():
            self.line.total(self.spread.at[0, 0])
            hand_on(0)

        def hand_on(step):
            @pl.when((chip + 1 < chips) & (chip >= step))
            def _():
                self.to_right(step).start()

            @pl.when((chip >= 1) & (chip + step < chips))
            def _():
                self.to_left(step).start()

            if step == 0:
                self.across(0).start()

        def take(step):
            @pl.when(chip >= step + 1)
            def _():
                self.to_right(step).wait_recv()
                self.across(chips - 1 - step).start()

            @pl.when(chip + step + 1 < chips)
            def _():
                self.to_left(step).wait_recv()
                self.across(step + 1).start()

        def pass_on(step):
            def run():
                take(step - 1)
                hand_on(step)

            return run

        def line_step(step):
            return lambda: self.line.step(step)

        return (
            [open_up]
            + [line_step(step) for step in range(1, chips - 1)]
            + [summed]
            + [pass_on(step) for step in range(1, chips - 1)]
            + [lambda: take(chips - 2)]
        )

    def finish(self):
        chip, chips = self.chip, self.chips
        for r in range(chips):
            self.out[self.core, :, self.columns(r)] = self.spread[0, r]
        for r in range(chips):
            self.across(r).wait()
            self.out[1 - self.core, :, self.columns(r)] = self.spread[1, r]
        for step in range(chips - 1):

            @pl.when((chip + 1 < chips) & (chip >= step))
            def _():
                self.to_right(step).wait_send()

            @pl.when((chip >= 1) & (chip + step < chips))
            def _():
                self.to_left(step).wait_send()

        self.line.finish()
        for j in range(len(self.owners) - 1):
            self.crossing(j).wait_send()
        for j in range(len(self.owners)):
            self.swap(j).wait_send()


def dense_reduce_kernel(fsdp, chips, cuts, *refs):
    count = len(cuts)
    arrays = max(cut[0] for cut in cuts) + 1
    ins, refs = refs[:arrays], refs[arrays:]
    own_ref, right_ref, left_ref = refs[:3]
    outs, total_ref, refs = refs[3 : 3 + arrays], refs[3 + arrays], refs[4 + arrays :]
    from_left, from_right, r_send, r_recv, l_send, l_recv = refs[:6]
    rest = refs[6:]
    ctx, me, chip, core, sibling = place()
    greet(chips, peers_of(me, fsdp), True)

    to_right = remote(right_ref, from_left, r_send, r_recv, (ctx + 2, me))
    to_left = remote(left_ref, from_right, l_send, l_recv, (ctx - 2, me))

    @pl.when(chip + 1 < chips)
    def _():
        to_right.start()

    @pl.when(chip >= 1)
    def _():
        to_left.start()

    sums = []
    for i, (which, start, size) in enumerate(cuts):
        buffers = rest[i * DENSE_BUFFERS : (i + 1) * DENSE_BUFFERS]
        sems = rest[count * DENSE_BUFFERS + i * DENSE_SEMS :][:DENSE_SEMS]
        local = ins[which].at[:, :, :, pl.ds(start, size)]
        sums.append(
            DenseSum(
                local,
                lambda j, owner, local=local: local.at[owner, core],
                outs[which].at[:, :, pl.ds(start, size)],
                buffers,
                sems,
                fsdp,
                chips,
            )
        )
    for one in sums:
        one.start()
    for one in sums:
        one.cross_over()
    stages = [one.stages() for one in sums]
    lag = chips - 1
    for tick in range(len(stages[0]) + lag * (count - 1)):
        for i in range(count):
            if 0 <= tick - lag * i < len(stages[i]):
                stages[i][tick - lag * i]()
    @pl.when(chip >= 1)
    def _():
        to_right.wait_recv()

    @pl.when(chip + 1 < chips)
    def _():
        to_left.wait_recv()

    @pl.when(chip == 0)
    def _():
        add_into(total_ref, [from_right, own_ref])

    @pl.when(chip == chips - 1)
    def _():
        add_into(total_ref, [from_left, own_ref])

    @pl.when((chip >= 1) & (chip + 1 < chips))
    def _():
        add_into(total_ref, [from_left, from_right, own_ref])

    for one in sums:
        one.finish()

    @pl.when(chip + 1 < chips)
    def _():
        to_right.wait_send()

    @pl.when(chip >= 1)
    def _():
        to_left.wait_send()


def dense_buffers(rows, size, fsdp, chips):
    cut = size // chips
    return [
        pltpu.VMEM((fsdp, rows, size), BF16),
        pltpu.VMEM((fsdp - 1, rows, size), BF16),
        pltpu.VMEM((rows, size), BF16),
        pltpu.VMEM((chips + 1, rows, cut), BF16),
        pltpu.VMEM((2, chips, rows, cut), BF16),
    ]


def dense_sems(fsdp, chips):
    return (
        [pltpu.SemaphoreType.DMA((fsdp,)) for unused in range(2)]
        + [pltpu.SemaphoreType.DMA((fsdp - 1,)) for unused in range(2)]
        + [pltpu.SemaphoreType.DMA((chips - 1,)) for unused in range(8)]
        + [pltpu.SemaphoreType.DMA((chips,)) for unused in range(2)]
    )


def dense_reduce(arrays, own, right, left, piece, fsdp, chips, collective_id):
    vmem = pl.BlockSpec(memory_space=pltpu.VMEM)
    cuts, buffers = [], []
    for i, a in enumerate(arrays):
        rows, width = a.shape[2:]
        for start in range(0, width, piece):
            size = min(piece, width - start)
            cuts.append((i, start, size))
            buffers += dense_buffers(rows, size, fsdp, chips)
    sems = dense_sems(fsdp, chips)
    return pl.pallas_call(
        functools.partial(dense_reduce_kernel, fsdp, chips, tuple(cuts)),
        out_shape=[jax.ShapeDtypeStruct(a.shape[1:], BF16) for a in arrays]
        + [jax.ShapeDtypeStruct(own.shape, F32)],
        in_specs=[vmem] * len(arrays) + [vmem, pl.BlockSpec(memory_space=pl.ANY)]
        + [pl.BlockSpec(memory_space=pl.ANY)],
        out_specs=[vmem] * (len(arrays) + 1),
        scratch_shapes=[pltpu.VMEM(own.shape, BF16)] * 2
        + [pltpu.SemaphoreType.DMA] * 4
        + buffers
        + sems * len(cuts),
        compiler_params=pltpu.CompilerParams(
            collective_id=collective_id, has_side_effects=True, vmem_limit_bytes=VMEM_BYTES
        ),
        name="dense_reduce",
    )(*arrays, own, right, left)


def after(value, *others):
    return lax.optimization_barrier((value,) + others)[0]


def chunk_order(chip, i, chips):
    right_half = lax.div(2 * chip, chips)
    near = chip + right_half * (chips - 1 - 2 * chip)
    alone = chips - 1 - 2 * near
    paired = lax.div(i - alone + chips, chips)
    turn = (i - alone) * paired
    odd = lax.rem(turn, 2)
    pair = lax.div(turn, 2)
    distance = (1 - paired) * (chips - 1 - near - i) + paired * (
        (1 - odd) * (near - pair) + odd * (chips - near + pair)
    )
    return lax.rem(distance + right_half * (chips - 2 * distance), chips)


def front_kernel(
    scale,
    chips,
    fsdp,
    expert_count,
    tokens_ref,
    gain_a_ref,
    gain_b_ref,
    small_ref,
    cos_ref,
    sin_ref,
    oq_ref,
    pq_ref,
    ok_ref,
    routed_ref,
    table_ref,
    qkv_ref,
    wo_ref,
    gate_w_ref,
    passed_ref,
    q_ref,
    normed_ref,
    kv_ref,
    table_all_ref,
    attended_ref,
    lse_ref,
    middle_ref,
    gate_ref,
    weights_ref,
    hidden_all_ref,
    gate_full_ref,
    grad_ref,
    qkv_v,
    wo_v,
    gate_v,
    hidden_v,
    bias,
    top,
    total,
    acc,
    load_sem,
    own_sem,
    gate_own,
    gate_send,
    gate_recv,
    *line_sems,
):
    ctx, me, chip, core, sibling = place()
    rows = tokens_ref.shape[0]
    width = tokens_ref.shape[1]
    half = rows // 2
    kv_width = KVH * HEAD_SIZE
    per_group = QUERY_HEADS // KVH
    parts = [pl.ds(0, half), pl.ds(half, half)]
    loads = [
        pltpu.make_async_copy(src, dst, load_sem.at[k])
        for k, (src, dst) in enumerate(((qkv_ref, qkv_v), (wo_ref, wo_v)))
    ]
    for copy in loads:
        copy.start()
    greet(chips, peers_of(me, fsdp), True)
    gate_gather = ShardGather(
        gate_w_ref, gate_full_ref, gate_v, (gate_own, gate_send, gate_recv), fsdp
    )
    gate_gather.start()
    kv_line = LineGather(
        [kv_ref.at[0, 0], table_all_ref.at[0, 0]], [kv_ref, table_all_ref], line_sems[:7], chips
    )
    grad_line = LineGather([None], [grad_ref], line_sems[7:14], chips)
    hidden_lines = [
        LineGather(
            [hidden_v.at[parts[0]]], [hidden_all_ref.at[:, :, parts[0]]], line_sems[14:21], chips
        ),
        LineGather(
            [hidden_v.at[parts[1]], weights_ref.at[0, 0]],
            [hidden_all_ref.at[:, :, parts[1]], weights_ref],
            line_sems[21:28],
            chips,
        ),
    ]

    def normed(value, gain):
        return value * lax.rsqrt(jnp.mean(value * value, axis=-1, keepdims=True) + EPSILON) * gain

    table_all_ref[0, 0] = table_ref[...]
    for part in parts:
        normed_ref[part, :] = normed(
            tokens_ref[part, :].astype(F32), gain_a_ref[...]
        ).astype(BF16)
    loads[0].wait()
    for part in parts:
        rows_one = normed_ref[part, :]
        cosine, sine = cos_ref[part, :], sin_ref[part, :]
        for h in range(KVH):
            columns = slice(width + h * HEAD_SIZE, width + (h + 1) * HEAD_SIZE)
            value = dot(rows_one, qkv_v[:, columns], NN)
            value = value * cosine + pltpu.roll(value, HEAD_SIZE // 2, 1) * sine
            kv_ref[0, 0, part, h * HEAD_SIZE : (h + 1) * HEAD_SIZE] = value.astype(BF16)
        kv_ref[0, 0, part, kv_width:] = dot(
            rows_one, qkv_v[:, width + kv_width :], NN
        ).astype(BF16)
    kv_line.send(0)
    for i in range(2):
        kv_line.across(i, 0).start()
    for part in parts:
        rows_one = normed_ref[part, :]
        cosine, sine = cos_ref[part, :], sin_ref[part, :]
        for h in range(0, QUERY_HEADS, 2):
            pre = dot(rows_one, qkv_v[:, h * HEAD_SIZE : (h + 2) * HEAD_SIZE], NN)
            for k in range(2):
                value = pre[:, k * HEAD_SIZE : (k + 1) * HEAD_SIZE]
                value = value * cosine + pltpu.roll(value, HEAD_SIZE // 2, 1) * sine
                q_ref[part, (h + k) * HEAD_SIZE : (h + k + 1) * HEAD_SIZE] = value.astype(BF16)

    def turn(index, r):
        part = parts[index]
        for q in range(2):
            gap = oq_ref[part, :] - ok_ref[q * chips + r]
            bias[:, q * rows : (q + 1) * rows] = jnp.where(
                (gap >= 0) & (gap <= pq_ref[part, :]), 0.0, MASKED
            )

        def one(h, carry):
            group = lax.div(h, per_group)
            columns = pl.ds(pl.multiple_of(h * HEAD_SIZE, HEAD_SIZE), HEAD_SIZE)
            key_columns = pl.ds(pl.multiple_of(group * HEAD_SIZE, HEAD_SIZE), HEAD_SIZE)
            value_columns = pl.ds(
                pl.multiple_of(kv_width + group * HEAD_SIZE, HEAD_SIZE), HEAD_SIZE
            )
            query = q_ref[part, columns]
            scores = []
            peak = top[h, part, :]
            for q in range(2):
                raw = dot(query, kv_ref[q, r, :, key_columns], NT) * (scale * LOG2E)
                raw = raw + bias[:, q * rows : (q + 1) * rows]
                scores.append(raw)
            best = scores[0][:, :LANES]
            for q in range(2):
                for k in range(rows // LANES):
                    best = jnp.maximum(best, scores[q][:, k * LANES : (k + 1) * LANES])
            new = jnp.maximum(peak, jnp.max(best, axis=1, keepdims=True))
            fade = jnp.exp2(peak - new)
            wide = jnp.concatenate([new] * (rows // LANES), axis=1)
            mass = total[h] * fade
            out = acc[:, columns] * fade
            for q in range(2):
                probs = jnp.exp2(scores[q] - wide)
                for k in range(rows // LANES):
                    mass = mass + probs[:, k * LANES : (k + 1) * LANES]
                out = out + dot(probs.astype(BF16), kv_ref[q, r, :, value_columns], NN)
            top[h, part, :] = new
            total[h] = mass
            acc[:, columns] = out
            return carry

        lax.fori_loop(0, QUERY_HEADS, one, 0)

    def begin(index):
        top[:, parts[index], :] = jnp.full((QUERY_HEADS, half, LANES), MASKED, F32)
        total[...] = jnp.zeros_like(total)
        acc[...] = jnp.zeros_like(acc)

    def end(index):
        part = parts[index]
        for h in range(QUERY_HEADS):
            columns = slice(h * HEAD_SIZE, (h + 1) * HEAD_SIZE)
            mass = jnp.sum(total[h], axis=1, keepdims=True)
            attended_ref[part, columns] = (acc[:, columns] / mass).astype(BF16)
            top[h, part, :] = top[h, part, :] + jnp.log2(mass)
        if index == 0:
            loads[1].wait()
        middle = tokens_ref[part, :].astype(F32) + dot(attended_ref[part, :], wo_v[...], NN)
        middle_ref[part, :] = middle
        rows_two = normed(middle, gain_b_ref[...]).astype(BF16)
        hidden_v[part, :] = rows_two
        routed = routed_ref[part, :] > 0.0
        logits = jnp.where(routed, dot(rows_two, small_ref[...], NN), MASKED)
        power = jnp.exp(logits - jnp.max(logits, axis=1, keepdims=True))
        power = jnp.where(routed, power, 0.0)
        gate_ref[part, :] = power / jnp.sum(power, axis=1, keepdims=True)
        if index == 1:
            weights_ref[0, 0] = gate_ref[...].T[:expert_count, :]
        line = hidden_lines[index]
        line.send(0)
        for i in range(line.count):
            line.across(i, 0).start()
        own(index).start()

    def own(index):
        return pltpu.make_async_copy(
            hidden_v.at[parts[index]],
            hidden_all_ref.at[0, 0, parts[index]],
            own_sem.at[index],
        )

    begin(0)

    def first_turn(t, carry):
        for k in range(1, chips):

            @pl.when(t == k)
            def _():
                kv_line.receive(k - 1)
                if k < chips - 1:
                    kv_line.send(k)
                else:
                    grad_line.send(chips - 2)

        r = chunk_order(chip, chips - 1 - t, chips)
        kv_line.arrived(r)
        turn(0, r)
        return carry

    lax.fori_loop(0, chips, first_turn, 0)
    end(0)
    begin(1)
    early = [step for step in range(chips - 1) if 2 * step + 2 < chips]

    def second_turn(t, carry):
        for step in early:

            @pl.when(t == 2 * step + 2)
            def _():
                hidden_lines[0].receive(step)
                if step + 1 < chips - 1:
                    hidden_lines[0].send(step + 1)

        turn(1, t)
        return carry

    lax.fori_loop(0, chips, second_turn, 0)
    grad_line.receive(chips - 2)
    late = [step for step in range(chips - 1) if step not in early]
    for step in late[:1]:
        hidden_lines[0].receive(step)
        if step + 1 < chips - 1:
            hidden_lines[0].send(step + 1)
    end(1)
    for h in range(QUERY_HEADS):
        lse_ref[h] = top[h].T[:1, :]
    for step in late[1:]:
        hidden_lines[0].receive(step)
        if step + 1 < chips - 1:
            hidden_lines[0].send(step + 1)
    for step in range(chips - 1):
        hidden_lines[1].receive(step)
        if step + 1 < chips - 1:
            hidden_lines[1].send(step + 1)
    for line in hidden_lines:
        for slot in range(chips):
            line.arrived(slot)
        line.sent()
    kv_line.sent()
    gate_gather.finish()
    grad_line.finish(chips - 2)
    for index in range(2):
        own(index).wait()


def front(
    tokens,
    gain_a,
    gain_b,
    small,
    cosine,
    sine,
    order_mine,
    pos_mine,
    order_keys,
    routed,
    table,
    qkv,
    w_out,
    w_gate,
    grad_all,
    chips,
    fsdp,
    collective_id,
):
    rows, width = tokens.shape
    expert_count = table.shape[0]
    kv_width = KVH * HEAD_SIZE
    vmem = pl.BlockSpec(memory_space=pltpu.VMEM)
    anywhere = pl.BlockSpec(memory_space=pl.ANY)
    shapes = [
        ((rows, width), BF16),
        ((rows, width), BF16),
        ((2, chips, rows, 2 * kv_width), BF16),
        ((2, chips, expert_count, rows), F32),
        ((rows, width), BF16),
        ((QUERY_HEADS, 1, rows), F32),
        ((rows, width), F32),
        ((rows, LANES), F32),
        ((2, chips, expert_count, rows), F32),
        ((2, chips, rows, width), BF16),
        ((w_gate.shape[0], width, w_gate.shape[2]), BF16),
        (grad_all.shape, BF16),
    ]
    flops = 4 * rows * (2 * chips * rows) * width + 2 * rows * width * (2 * width + 2 * kv_width)
    return pl.pallas_call(
        functools.partial(front_kernel, HEAD_SIZE ** (-0.5), chips, fsdp, expert_count),
        out_shape=[jax.ShapeDtypeStruct(shape, kind) for shape, kind in shapes],
        in_specs=[vmem] * 11 + [anywhere] * 4,
        out_specs=[vmem] * 9 + [anywhere] * 3,
        scratch_shapes=[
            pltpu.VMEM(qkv.shape, BF16),
            pltpu.VMEM(w_out.shape, BF16),
            pltpu.VMEM(w_gate.shape, BF16),
            pltpu.VMEM((rows, width), BF16),
            pltpu.VMEM((rows // 2, 2 * rows), F32),
            pltpu.VMEM((QUERY_HEADS, rows, LANES), F32),
            pltpu.VMEM((QUERY_HEADS, rows // 2, LANES), F32),
            pltpu.VMEM((rows // 2, width), F32),
            pltpu.SemaphoreType.DMA((2,)),
            pltpu.SemaphoreType.DMA((2,)),
            pltpu.SemaphoreType.DMA,
            pltpu.SemaphoreType.DMA((fsdp - 1,)),
            pltpu.SemaphoreType.DMA((fsdp - 1,)),
        ]
        + line_scratch([None] * 2, chips)
        + line_scratch([None], chips)
        + line_scratch([None], chips)
        + line_scratch([None] * 2, chips),
        input_output_aliases={14: 11},
        compiler_params=pltpu.CompilerParams(
            collective_id=collective_id, has_side_effects=True, vmem_limit_bytes=FRONT_VMEM_BYTES
        ),
        cost_estimate=pl.CostEstimate(
            flops=flops, bytes_accessed=40_000_000, transcendentals=rows * rows * chips * 24
        ),
        name="front",
    )(
        tokens,
        gain_a[None, :],
        gain_b[None, :],
        small,
        cosine,
        sine,
        order_mine[:, None],
        pos_mine[:, None],
        order_keys.reshape(2 * chips, 1, rows),
        routed,
        table,
        qkv,
        w_out,
        w_gate,
        grad_all,
    )


def attention_back_kernel(
    scale,
    chips,
    fsdp,
    early_dense,
    q_ref,
    k_ref,
    v_ref,
    o_ref,
    do_ref,
    lse_ref,
    oq_ref,
    pq_ref,
    ok_ref,
    cos_ref,
    sin_ref,
    mine_ref,
    other_ref,
    dense_ref,
    dq_ref,
    kv_ref,
    own_ref,
    right_ref,
    left_ref,
    dense_out_ref,
    bias,
    dk_acc,
    dv_acc,
    kv_total,
    mine_v,
    pair,
    got,
    kv_v,
    kv_pair,
    kv_got,
    load_sem,
    store_sem,
    swap_send,
    swap_recv,
    r_send,
    r_recv,
    l_send,
    l_recv,
    kv_swap_send,
    kv_swap_recv,
    kr_send,
    kr_recv,
    kl_send,
    kl_recv,
    *dense_refs,
):
    ctx, me, chip, core, sibling = place()
    keys = k_ref.shape[0]
    tiles = keys // KEY_TILE
    rows = q_ref.shape[0]
    per_group = QUERY_HEADS // KVH
    head = pl.program_id(0)

    order = []
    for step in range(chips - 1):
        for r in (chips - 1 - step, step + 1):
            if r not in order:
                order.append(r)
    order.append(0)
    swaps = [
        remote(other_ref.at[r], pair.at[r], swap_send.at[r], swap_recv.at[r], (sibling, me))
        for r in range(chips)
    ]
    slots = mine_v.shape[0]
    loads = [
        pltpu.make_async_copy(mine_ref.at[r], mine_v.at[j % slots], load_sem.at[j % slots])
        for j, r in enumerate(order)
    ]
    line = LineSum(
        chips,
        lambda r: lambda: [pair.at[r]],
        lambda r: pair.at[r],
        got,
        (r_send, r_recv, l_send, l_recv),
    )

    def join(j):
        loads[j].wait()
        swaps[order[j]].wait_recv()
        add_into(pair.at[order[j]], [pair.at[order[j]], mine_v.at[j % slots]])
        if j + slots < chips:
            loads[j + slots].start()

    if early_dense:
        dense_v, dense_load = dense_refs[:2]
        buffers = dense_refs[2 : 2 + DENSE_BUFFERS]
        dense = DenseSum(
            dense_ref,
            lambda j, owner: dense_v.at[j],
            dense_out_ref,
            buffers,
            dense_refs[2 + DENSE_BUFFERS :],
            fsdp,
            chips,
        )
        dense_loads = [
            pltpu.make_async_copy(dense_ref.at[owner, core], dense_v.at[j], dense_load.at[j])
            for j, owner in enumerate(dense.owners)
        ]
        stages = dense.stages()
        at_head = {QUERY_HEADS - 1 - len(stages) // 2 + k: k for k in range(len(stages) // 2)}

    def kv_swap(group, r):
        return remote(
            kv_v.at[group, 1, r],
            kv_pair.at[group, r],
            kv_swap_send.at[group, r],
            kv_swap_recv.at[group, r],
            (sibling, me),
        )

    def kv_line(group):
        def held(r):
            kv_swap(group, r).wait_recv()
            return lambda: [kv_v.at[group, 0, r], kv_pair.at[group, r]]

        return LineSum(
            chips,
            held,
            lambda r: kv_pair.at[group, r],
            kv_got.at[group],
            tuple(sem.at[group] for sem in (kr_send, kr_recv, kl_send, kl_recv)),
        )

    def kv_start(group):
        for q in range(2):
            for r in range(chips):
                part = pl.ds((q * chips + r) * rows, rows)
                kv_v[group, q, r, :, :HEAD_SIZE] = (dk_acc[part, :] * scale).astype(BF16)
                kv_v[group, q, r, :, HEAD_SIZE:] = dv_acc[part, :].astype(BF16)
        for r in order:
            kv_swap(group, r).start()

    @pl.when(head == 0)
    def _():
        greet(chips, peers_of(me, fsdp) if early_dense else [], True)
        if early_dense:
            for copy in dense_loads:
                copy.start()
            dense.start()
        for r in order:
            swaps[r].start()
        for copy in loads[:slots]:
            copy.start()

        def fill(t, carry):
            tile = pl.ds(pl.multiple_of(t * KEY_TILE, KEY_TILE), KEY_TILE)
            gap = oq_ref[...] - ok_ref[tile, :]
            bias[tile, :] = jnp.where((gap >= 0) & (gap <= pq_ref[...]), 0.0, MASKED)
            return carry

        lax.fori_loop(0, tiles, fill, 0)

    @pl.when(lax.rem(head, per_group) == 0)
    def _():
        dk_acc[...] = jnp.zeros_like(dk_acc)
        dv_acc[...] = jnp.zeros_like(dv_acc)

    query = q_ref[...]
    grad = do_ref[...]
    lse = lse_ref[0]
    product = grad.astype(F32) * o_ref[...].astype(F32)
    delta = jnp.sum(product.T, axis=0, keepdims=True)

    def step(t, acc):
        tile = pl.ds(pl.multiple_of(t * KEY_TILE, KEY_TILE), KEY_TILE)
        key = k_ref[tile, :]
        raw = dot(key, query, NT) * (scale * LOG2E) + bias[tile, :]
        probs = jnp.exp2(raw - lse)
        prob_grad = dot(v_ref[tile, :], grad, NT)
        score_grad = (probs * (prob_grad - delta)).astype(BF16)
        dv_acc[tile, :] += dot(probs.astype(BF16), grad, NN)
        dk_acc[tile, :] += dot(score_grad, query, NN)
        return acc + dot(score_grad, key, TN)

    acc = lax.fori_loop(0, tiles, step, jnp.zeros((rows, HEAD_SIZE), F32))
    def turn_back(value):
        back = value * cos_ref[...] - pltpu.roll(value, HEAD_SIZE // 2, 1) * sin_ref[...]
        return back.astype(BF16)

    dq_ref[...] = turn_back(acc * scale)

    last = QUERY_HEADS - 1
    stride = max(1, last // (chips - 2))
    early = {per_group + 2 * s: s for s in range(chips - 1) if per_group + 2 * s < last}
    for h in range(QUERY_HEADS):

        @pl.when(head == h)
        def _():
            if h == 0:
                for j in range(chips):
                    join(j)
            if early_dense and h == 1:
                for copy in dense_loads:
                    copy.wait()
                dense.cross_over()
            if early_dense and h in at_head:
                stages[at_head[h]]()
            for s in range(chips - 2):
                if h == s * stride:
                    line.step(s)
            if h % per_group == per_group - 1:
                kv_start(h // per_group)
            if h in early:
                kv_line(0).step(early[h])

    @pl.when(head == last)
    def _():
        def store(k, r, target):
            return pltpu.make_async_copy(pair.at[r], target, store_sem.at[k])

        @pl.when((chip >= 1) & (chip + 1 < chips))
        def _():
            add_into(pair.at[1], [pair.at[1], line.from_left(chips - 3)])
            add_into(pair.at[chips - 1], [pair.at[chips - 1], line.from_right(chips - 3)])

        for copy in (
            store(0, 0, own_ref),
            store(1, 1, right_ref),
            store(2, chips - 1, left_ref),
        ):
            copy.start()
        rest = stages[len(stages) // 2 :] if early_dense else []
        for group in range(KVH):
            one = kv_line(group)
            for s in range(chips - 1):
                if group > 0 or s not in early.values():
                    one.step(s)
                    if rest:
                        rest.pop(0)()
            one.total(kv_total)
            kv_ref[:, group * HEAD_SIZE : (group + 1) * HEAD_SIZE] = turn_back(
                kv_total[:, :HEAD_SIZE]
            )
            kv_ref[:, (KVH + group) * HEAD_SIZE : (KVH + group + 1) * HEAD_SIZE] = kv_total[
                :, HEAD_SIZE:
            ].astype(BF16)
        for stage in rest:
            stage()
        if early_dense:
            dense.finish()
        for group in range(KVH):
            kv_line(group).finish()
            for r in range(chips):
                kv_swap(group, r).wait_send()
        line.finish(chips - 2)
        for swap in swaps:
            swap.wait_send()
        for copy in (
            store(0, 0, own_ref),
            store(1, 1, right_ref),
            store(2, chips - 1, left_ref),
        ):
            copy.wait()


def attention_back(
    queries,
    kv,
    attended,
    attended_grad,
    lse,
    order_mine,
    pos_mine,
    order_keys,
    cosine,
    sine,
    mine,
    other,
    dense,
    fsdp,
    early_dense,
    collective_id,
):
    rows = queries.shape[0]
    keys = kv.shape[0]
    chips, unused, width = mine.shape
    per_group = QUERY_HEADS // KVH
    head_rows = pl.BlockSpec((rows, HEAD_SIZE), lambda h: (0, h))
    anywhere = pl.BlockSpec(memory_space=pl.ANY)
    return pl.pallas_call(
        functools.partial(
            attention_back_kernel, HEAD_SIZE ** (-0.5), chips, fsdp, early_dense
        ),
        grid=(QUERY_HEADS,),
        out_shape=[
            jax.ShapeDtypeStruct(queries.shape, BF16),
            jax.ShapeDtypeStruct((rows, 2 * KVH * HEAD_SIZE), BF16),
        ]
        + [jax.ShapeDtypeStruct((rows, width), BF16)] * 3
        + [jax.ShapeDtypeStruct(dense.shape[1:], BF16)],
        in_specs=[
            head_rows,
            pl.BlockSpec((keys, HEAD_SIZE), lambda h: (0, h // per_group)),
            pl.BlockSpec((keys, HEAD_SIZE), lambda h: (0, KVH + h // per_group)),
            head_rows,
            head_rows,
            pl.BlockSpec((1, 1, rows), lambda h: (h, 0, 0)),
            pl.BlockSpec((1, rows), lambda h: (0, 0)),
            pl.BlockSpec((1, rows), lambda h: (0, 0)),
            pl.BlockSpec((keys, 1), lambda h: (0, 0)),
            pl.BlockSpec((rows, HEAD_SIZE), lambda h: (0, 0)),
            pl.BlockSpec((rows, HEAD_SIZE), lambda h: (0, 0)),
            anywhere,
            anywhere,
            anywhere,
        ],
        out_specs=[
            head_rows,
            pl.BlockSpec((rows, 2 * KVH * HEAD_SIZE), lambda h: (0, 0)),
            anywhere,
            anywhere,
            anywhere,
            pl.BlockSpec(dense.shape[1:], lambda h: (0, 0, 0)) if early_dense else anywhere,
        ],
        scratch_shapes=[
            pltpu.VMEM((keys, rows), F32),
            pltpu.VMEM((keys, HEAD_SIZE), F32),
            pltpu.VMEM((keys, HEAD_SIZE), F32),
            pltpu.VMEM((rows, 2 * HEAD_SIZE), F32),
            pltpu.VMEM((2 if chips <= 4 else 1, rows, width), BF16),
            pltpu.VMEM((chips, rows, width), BF16),
            pltpu.VMEM((chips + 1, rows, width), BF16),
            pltpu.VMEM((KVH, 2, chips, rows, 2 * HEAD_SIZE), BF16),
            pltpu.VMEM((KVH, chips, rows, 2 * HEAD_SIZE), BF16),
            pltpu.VMEM((KVH, chips + 1, rows, 2 * HEAD_SIZE), BF16),
            pltpu.SemaphoreType.DMA((2,)),
            pltpu.SemaphoreType.DMA((3,)),
            pltpu.SemaphoreType.DMA((chips,)),
            pltpu.SemaphoreType.DMA((chips,)),
        ]
        + [pltpu.SemaphoreType.DMA((chips - 1,)) for unused in range(4)]
        + [pltpu.SemaphoreType.DMA((KVH, chips)) for unused in range(2)]
        + [pltpu.SemaphoreType.DMA((KVH, chips - 1)) for unused in range(4)]
        + (
            [
                pltpu.VMEM((fsdp,) + dense.shape[2:], BF16),
                pltpu.SemaphoreType.DMA((fsdp,)),
            ]
            + dense_buffers(dense.shape[2], dense.shape[3], fsdp, chips)
            + dense_sems(fsdp, chips)
            if early_dense
            else []
        ),
        compiler_params=pltpu.CompilerParams(
            collective_id=collective_id, has_side_effects=True, vmem_limit_bytes=BACK_VMEM_BYTES
        ),
        cost_estimate=pl.CostEstimate(
            flops=10 * rows * keys * HEAD_SIZE * QUERY_HEADS,
            bytes_accessed=10 * rows * QUERY_HEADS * HEAD_SIZE + 8 * keys * KVH * HEAD_SIZE,
            transcendentals=rows * keys * QUERY_HEADS,
        ),
        name="attention_back",
    )(
        queries,
        kv,
        kv,
        attended,
        attended_grad,
        lse,
        order_mine[None, :],
        pos_mine[None, :],
        order_keys[:, None],
        cosine,
        sine,
        mine,
        other,
        dense,
    )


def experts_kernel(
    capacity,
    local_experts,
    expert_count,
    chips,
    fsdp,
    per,
    hidden_ref,
    grad_ref,
    table_ref,
    weight_ref,
    gate_ref,
    up_ref,
    down_ref,
    returned_ref,
    out_mine_ref,
    out_other_ref,
    gate_grad_ref,
    gate_got_ref,
    up_grad_ref,
    down_grad_ref,
    x_ref,
    pg_ref,
    inner_ref,
    da_ref,
    db_ref,
    gate_v,
    up_v,
    down_v,
    hidden_v,
    grad_v,
    out_v,
    x_v,
    pg_v,
    g_v,
    inner_v,
    da_v,
    db_v,
    mine_v,
    other_v,
    pair,
    got,
    stage_tall,
    weight_sem,
    load_sem,
    out_sem,
    save_sem,
    swap_send,
    swap_recv,
    right_send,
    right_recv,
    left_send,
    left_recv,
    stage_sem,
    tile_own,
    tile_send,
    tile_recv,
):
    ctx, me, chip, core, sibling = place()
    peers = peers_of(me, fsdp)
    tokens = hidden_v.shape[1]
    width = hidden_v.shape[2]
    slots = x_v.shape[1]
    slot_rows = slots // 2
    units = inner_v.shape[2]
    total_rows = x_ref.shape[1]
    first = ctx * local_experts

    weights_in = [
        pltpu.make_async_copy(src, dst, weight_sem.at[k])
        for k, (src, dst) in enumerate(
            ((gate_ref, gate_v), (up_ref, up_v), (down_ref, down_v))
        )
    ]

    def load(i):
        r = chunk_order(chip, i, chips)
        return [
            pltpu.make_async_copy(hidden_ref.at[:, r], hidden_v, load_sem.at[0]),
            pltpu.make_async_copy(grad_ref.at[:, r], grad_v, load_sem.at[1]),
        ]

    def saves(i):
        rows = pl.ds(i * slots, slots)
        return [
            pltpu.make_async_copy(src, dst.at[:, rows], save_sem.at[k])
            for k, (src, dst) in enumerate(
                ((x_v, x_ref), (pg_v, pg_ref), (inner_v, inner_ref), (da_v, da_ref), (db_v, db_ref))
            )
        ]

    def out_copies(i):
        r = chunk_order(chip, i, chips)
        return [
            pltpu.make_async_copy(out_v.at[0], out_mine_ref.at[r], out_sem.at[0]),
            pltpu.make_async_copy(out_v.at[1], out_other_ref.at[r], out_sem.at[1]),
        ]

    def swap(i):
        r = chunk_order(chip, i, chips)
        return remote(
            other_v.at[lax.rem(i, 2)],
            pair.at[r],
            swap_send.at[r],
            swap_recv.at[r],
            (sibling, me),
        )

    def join(i):
        r = chunk_order(chip, i, chips)
        swap(i).wait_recv()
        add_into(pair.at[r], [pair.at[r], mine_v.at[lax.rem(i, 2)]])

    line = LineSum(
        chips,
        lambda r: lambda: [pair.at[r]],
        lambda r: pair.at[r],
        got,
        (right_send, right_recv, left_send, left_recv),
    )

    for copy in load(0) + weights_in:
        copy.start()
    greet(chips, peers if per == 1 else [], True)

    slot = lax.broadcasted_iota(jnp.int32, (slot_rows, tokens), 0).astype(F32) + 1.0
    slot = jnp.where(slot <= capacity, slot, -1.0)
    lane = lax.broadcasted_iota(jnp.int32, (slots, LANES), 1)

    def chunk(i, carry):
        r = chunk_order(chip, i, chips)
        for copy in load(i):
            copy.wait()

        @pl.when(i >= 1)
        def _():
            for copy in saves(i - 1):
                copy.wait()

        picks = [[], []]
        weight_rows = []
        for e in range(local_experts):
            rows_w = []
            for q in range(2):
                hit = slot == table_ref[q, r, pl.ds(first + e, 1), :]
                pick = jnp.where(hit, 1.0, 0.0).astype(BF16)
                weight = weight_ref[q, r, pl.ds(first + e, 1), :]
                w = jnp.sum(jnp.where(hit, weight, 0.0), axis=1, keepdims=True)
                rows = pl.ds(q * slot_rows, slot_rows)
                x_v[e, rows, :] = dot(pick, hidden_v[q], NN).astype(BF16)
                g = dot(pick, grad_v[q], NN)
                g_v[e, rows, :] = g.astype(BF16)
                pg_v[e, rows, :] = (w * g).astype(BF16)
                picks[q].append(pick)
                rows_w.append(w)
            weight_rows.append(jnp.concatenate(rows_w, axis=0))

        @pl.when(i + 1 < chips)
        def _():
            for copy in load(i + 1):
                copy.start()

        @pl.when(i == 0)
        def _():
            for copy in weights_in:
                copy.wait()

        outs = [[], []]
        backs = [[], []]
        for e in range(local_experts):
            x = x_v[e]
            pair_grad = pg_v[e]
            w = weight_rows[e]
            gate = gate_v[e * width : (e + 1) * width, :]
            up = up_v[e * width : (e + 1) * width, :]
            down = down_v[e * units : (e + 1) * units, :]
            gate_pre = dot(x, gate, NN)
            up_pre = dot(x, up, NN)
            sig = jax.nn.sigmoid(gate_pre)
            silu = gate_pre * sig
            inner = (silu * up_pre).astype(BF16)
            inner_v[e] = inner
            expert_out = dot(inner, down, NN).astype(BF16).astype(F32)
            gate_grad = jnp.sum(expert_out * g_v[e].astype(F32), axis=1, keepdims=True)
            inner_grad = dot(pair_grad, down, NT)
            da = (inner_grad * up_pre * sig * (1.0 + gate_pre * (1.0 - sig))).astype(BF16)
            db = (inner_grad * silu).astype(BF16)
            da_v[e] = da
            db_v[e] = db
            row_grad = (dot(da, gate, NT) + dot(db, up, NT)).astype(BF16)
            high = gate_grad.astype(BF16).astype(F32)
            extra = jnp.where(lane == first + e, high, 0.0) + jnp.where(
                lane == expert_count + first + e, gate_grad - high, 0.0
            )
            back = jnp.concatenate([row_grad, extra.astype(BF16)], axis=1)
            out_rows = (w * expert_out).astype(BF16)
            for q in range(2):
                part = slice(q * slot_rows, (q + 1) * slot_rows)
                outs[q].append(out_rows[part])
                backs[q].append(back[part])

        for copy in saves(i):
            copy.start()

        @pl.when(i >= 1)
        def _():
            for copy in out_copies(i - 1):
                copy.wait()

        @pl.when(i >= 2)
        def _():
            swap(i - 2).wait_send()

        for q in range(2):
            pick = jnp.concatenate(picks[q], axis=0)
            held = other_v if q else mine_v
            held[lax.rem(i, 2)] = dot(pick, jnp.concatenate(backs[q], axis=0), TN).astype(BF16)
            if q:
                swap(i).start()
        for q in range(2):
            pick = jnp.concatenate(picks[q], axis=0)
            out_v[q] = dot(pick, jnp.concatenate(outs[q], axis=0), TN).astype(BF16)
        for copy in out_copies(i):
            copy.start()

        @pl.when(i == 0)
        def _():
            join(0)
            line.step(0)

        @pl.when(i >= 2)
        def _():
            join(i - 1)

        for step in range(1, chips - 1):
            if 2 * step < chips:

                @pl.when(i == 2 * step)
                def _():
                    line.step(step)

        return carry

    lax.fori_loop(0, chips, chunk, 0)
    join(chips - 1)
    for copy in saves(chips - 1):
        copy.wait()
    for copy in out_copies(chips - 1):
        copy.wait()
    for i in range(max(0, chips - 2), chips):
        swap(i).wait_send()

    shard = width // fsdp
    blocks = fsdp // per
    block = per * shard

    def fetch(copies):
        copies = [
            pltpu.make_async_copy(src, dst, save_sem.at[k])
            for k, (src, dst) in enumerate(copies)
        ]
        for copy in copies:
            copy.start()
        for copy in copies:
            copy.wait()

    def products(e, staged, target, product):
        def write(f):
            return [
                pltpu.make_async_copy(
                    staged(lax.rem(f, 2), p),
                    target.at[f * per + p, e],
                    stage_sem.at[lax.rem(f, 2), p],
                )
                for p in range(per)
            ]

        def one(f, carry):
            @pl.when(f >= 2)
            def _():
                for copy in write(f - 2):
                    copy.wait()

            product(f)
            for copy in write(f):
                copy.start()
            return carry

        lax.fori_loop(0, blocks, one, 0)
        for f in range(max(0, blocks - 2), blocks):
            for copy in write(f):
                copy.wait()

    def stage_wide(slot, p):
        return hidden_v.at[slot, pl.ds(p * shard, shard), pl.ds(0, units)]

    def wide(e, held, staged, target):
        def product(f):
            columns = pl.ds(pl.multiple_of(f * block, LANES), block)
            value = dot(
                down_v[:total_rows, columns],
                held[e * total_rows : (e + 1) * total_rows, :],
                TN,
            ).astype(BF16)
            for p in range(per):
                staged(lax.rem(f, 2), p)[...] = value[p * shard : (p + 1) * shard, :]

        products(e, staged, target, product)

    def tall(e, target):
        def product(f):
            columns = pl.ds(pl.multiple_of(f * block, LANES), block)
            value = dot(
                gate_v[e * total_rows : (e + 1) * total_rows, :],
                down_v[:total_rows, columns],
                TN,
            ).astype(BF16)
            for p in range(per):
                stage_tall[lax.rem(f, 2), p] = value[:, p * shard : (p + 1) * shard]

        products(e, lambda slot, p: stage_tall.at[slot, p], target, product)

    def tile(e, j):
        held = (hidden_v, grad_v)[e]
        return held.at[j // 2, pl.ds(0, shard), pl.ds((j % 2) * units, units)]

    def tile_copy(e, j):
        if j == len(peers):
            return pltpu.make_async_copy(tile(e, j), gate_grad_ref.at[e], tile_own.at[e])
        return remote(
            tile(e, j),
            gate_got_ref.at[j, e],
            tile_send.at[e, j],
            tile_recv.at[e, j],
            (ctx, peers[j]),
        )

    def gate_tiles(e):
        for j, owner in enumerate(peers + [me]):
            columns = pl.ds(pl.multiple_of(owner * shard, LANES), shard)
            tile(e, j)[...] = dot(
                down_v[:total_rows, columns],
                gate_v[e * total_rows : (e + 1) * total_rows, :],
                TN,
            ).astype(BF16)
            tile_copy(e, j).start()

    def fetch_x(e):
        copies = [(x_ref.at[e], down_v.at[:total_rows])]
        if e == 0:
            for k in range(local_experts):
                held = pl.ds(k * total_rows, total_rows)
                copies += [(da_ref.at[k], gate_v.at[held]), (db_ref.at[k], up_v.at[held])]
        return lambda: fetch(copies)

    def stage_up(slot, p):
        return out_v.at[slot, pl.ds(p * shard, shard), pl.ds(0, units)]

    work = []
    for e in range(local_experts):
        work.append(fetch_x(e))
        if per == 1:
            work.append(lambda e=e: gate_tiles(e))
        else:
            work.append(lambda e=e: wide(e, gate_v, stage_wide, gate_grad_ref))
        if e > 0:
            work.append(lambda e=e: wide(e, up_v, stage_up, up_grad_ref))
    work.append(lambda: fetch([(x_ref.at[0], down_v.at[:total_rows])]))
    work.append(lambda: wide(0, up_v, stage_up, up_grad_ref))
    for e in range(local_experts):
        copies = [(pg_ref.at[e], down_v.at[:total_rows])]
        if e == 0:
            for k in range(local_experts):
                copies.append((inner_ref.at[k], gate_v.at[pl.ds(k * total_rows, total_rows)]))
        work.append(lambda copies=copies: fetch(copies))
        work.append(lambda e=e: tall(e, down_grad_ref))
    late = [step for step in range(1, chips - 1) if 2 * step >= chips]
    for n, task in enumerate(work):
        task()
        if n == LINE_TASK or (n > LINE_TASK and late):
            if late:
                line.step(late.pop(0))
    for step in late:
        line.step(step)

    line.total(returned_ref)
    line.finish()
    if per == 1:
        for e in range(local_experts):
            for j in range(fsdp):
                tile_copy(e, j).wait()


def experts_pass(
    hidden, grad, table, weights, gate, up, down, capacity, expert_count, fsdp, collective_id
):
    unused, chips, tokens, width = grad.shape
    local_experts, unused, units = gate.shape
    slots = 2 * SLOT_STEP * -(-capacity // SLOT_STEP)
    total = chips * slots
    shard = width // fsdp
    per = 1 if shard % LANES == 0 else 2
    wide = width + LANES
    anywhere = pl.BlockSpec(memory_space=pl.ANY)
    vmem = pl.BlockSpec(memory_space=pltpu.VMEM)
    flops = 2 * total * width * units * local_experts * 9 + 8 * total * tokens * width
    saved = [(local_experts, total, width)] * 2 + [(local_experts, total, units)] * 3
    held = [(local_experts, slots, width)] * 3 + [(local_experts, slots, units)] * 3
    outs = pl.pallas_call(
        functools.partial(
            experts_kernel, capacity, local_experts, expert_count, chips, fsdp, per
        ),
        out_shape=[
            jax.ShapeDtypeStruct((tokens, wide), BF16),
            jax.ShapeDtypeStruct((chips, tokens, width), BF16),
            jax.ShapeDtypeStruct((chips, tokens, width), BF16),
            jax.ShapeDtypeStruct(
                ((fsdp,) if per > 1 else ()) + (local_experts, shard, units), BF16
            ),
            jax.ShapeDtypeStruct((fsdp - 1, local_experts, shard, units), BF16),
            jax.ShapeDtypeStruct((fsdp, local_experts, shard, units), BF16),
            jax.ShapeDtypeStruct((fsdp, local_experts, units, shard), BF16),
        ]
        + [jax.ShapeDtypeStruct(shape, BF16) for shape in saved],
        in_specs=[anywhere, anywhere, vmem, vmem, anywhere, anywhere, anywhere],
        out_specs=[vmem] + [anywhere] * 11,
        scratch_shapes=[
            pltpu.VMEM((local_experts * width, units), BF16),
            pltpu.VMEM((local_experts * width, units), BF16),
            pltpu.VMEM((local_experts * units, width), BF16),
            pltpu.VMEM((2, tokens, width), BF16),
            pltpu.VMEM((2, tokens, width), BF16),
            pltpu.VMEM((2, tokens, width), BF16),
        ]
        + [pltpu.VMEM(shape, BF16) for shape in held]
        + [
            pltpu.VMEM((2, tokens, wide), BF16),
            pltpu.VMEM((2, tokens, wide), BF16),
            pltpu.VMEM((chips, tokens, wide), BF16),
            pltpu.VMEM((chips + 1, tokens, wide), BF16),
            pltpu.VMEM((2, per, units, shard), BF16),
            pltpu.SemaphoreType.DMA((3,)),
            pltpu.SemaphoreType.DMA((2,)),
            pltpu.SemaphoreType.DMA((2,)),
            pltpu.SemaphoreType.DMA((5,)),
            pltpu.SemaphoreType.DMA((chips,)),
            pltpu.SemaphoreType.DMA((chips,)),
        ]
        + [pltpu.SemaphoreType.DMA((chips - 1,)) for unused in range(4)]
        + [pltpu.SemaphoreType.DMA((2, per)), pltpu.SemaphoreType.DMA((local_experts,))]
        + [pltpu.SemaphoreType.DMA((local_experts, fsdp - 1)) for unused in range(2)],
        compiler_params=pltpu.CompilerParams(
            collective_id=collective_id, has_side_effects=True, vmem_limit_bytes=EXPERT_VMEM_BYTES
        ),
        cost_estimate=pl.CostEstimate(
            flops=flops, bytes_accessed=100_000_000, transcendentals=total * units * 2
        ),
        name="experts",
    )(
        hidden,
        grad,
        table,
        weights,
        gate.reshape(local_experts * width, units),
        up.reshape(local_experts * width, units),
        down.reshape(local_experts * units, width),
    )
    return outs[:7]


def body(
    tokens,
    grad_out,
    order,
    lengths,
    routes,
    gain_one,
    gain_two,
    w_query,
    w_key,
    w_value,
    w_out,
    w_router,
    w_gate,
    w_up,
    w_down,
):
    fsdp = lax.axis_size("fsdp")
    chips = lax.axis_size("ctx") // 2
    ctx_index = lax.axis_index("ctx")
    chip = ctx_index // 2
    core = lax.rem(ctx_index, 2)
    tok_rows = tokens.shape[1]
    width = tokens.shape[2]
    top_count = routes.shape[2]
    local_experts = w_gate.shape[0]
    expert_count = local_experts * chips * 2
    capacity = 5 * tok_rows * top_count // (4 * expert_count)
    kv_width = KVH * HEAD_SIZE
    shard = gain_one.shape[0]

    small = jnp.concatenate(
        [
            w_router,
            gain_one[:, None],
            gain_two[:, None],
            jnp.zeros((shard, LANES - expert_count - 2), BF16),
        ],
        axis=1,
    )
    qkv_shard = jnp.concatenate([w_query, w_key, w_value], axis=1)
    qkv_full, small_full, out_full, grad_all = gather(
        [qkv_shard, small, w_out], [grad_out[0]], chips - 2, fsdp, chips, 0
    )

    qkv_full, w_up, w_down = lax.optimization_barrier((qkv_full, w_up, w_down))
    up_full, down_full = (
        lax.all_gather(w_up, "fsdp", axis=1, tiled=True),
        lax.all_gather(w_down, "fsdp", axis=2, tiled=True),
    )
    router_full = small_full[:, :expert_count]
    gain_a = small_full[:, expert_count].astype(F32)
    gain_b = small_full[:, expert_count + 1].astype(F32)

    order_row = order[0]
    start_row = ctx_index * tok_rows
    order_mine = lax.dynamic_slice_in_dim(order_row, start_row, tok_rows)
    ends = jnp.cumsum(lengths[0])
    starts = ends - lengths[0]
    past = order_mine[:, None] >= ends[None, :]
    doc_start = jnp.max(jnp.where(past, ends[None, :], starts[:1]), axis=1)
    pos_mine = order_mine - doc_start
    by_chip = jnp.roll(order_row.reshape(chips, 2, tok_rows), -chip, axis=0)
    by_chip = jnp.where(core == 0, by_chip, by_chip[:, ::-1])
    order_keys = jnp.swapaxes(by_chip, 0, 1).reshape(-1)

    route_rows = routes[0]
    route_onehot = (route_rows[:, :, None] == jnp.arange(expert_count)[None, None, :]).astype(F32)
    routed = jnp.sum(route_onehot, axis=1)
    earlier = (order_mine[None, :] < order_mine[:, None]).astype(BF16)
    ranks = jnp.dot(earlier, routed.astype(BF16), preferred_element_type=F32)
    table = jnp.where(routed > 0, jnp.minimum(ranks, capacity) + 1.0, 0.0)

    half_dim = HEAD_SIZE // 2
    freqs = ROPE_BASE ** (-2.0 * jnp.arange(half_dim).astype(F32) / HEAD_SIZE)
    angles = pos_mine.astype(F32)[:, None] * freqs[None, :]
    cosine = jnp.concatenate([jnp.cos(angles), jnp.cos(angles)], axis=1)
    sine = jnp.concatenate([-jnp.sin(angles), jnp.sin(angles)], axis=1)

    inputs = tokens[0].astype(F32)
    (
        queries,
        hidden_one,
        kv_all,
        table_all,
        attended,
        lse,
        middle,
        gate_weights,
        weights_all,
        hidden_all,
        gate_full,
        grad_all,
    ) = front(
        tokens[0],
        gain_a,
        gain_b,
        small_full,
        cosine,
        sine,
        order_mine,
        pos_mine,
        order_keys,
        jnp.pad(routed, ((0, 0), (0, LANES - expert_count))),
        table.T,
        qkv_full,
        out_full,
        w_gate,
        grad_all,
        chips,
        fsdp,
        1,
    )
    kv_all = kv_all.reshape(-1, 2 * kv_width)
    gate_weights = gate_weights[:, :expert_count]
    hidden_two = hidden_all[0, 0]

    returned, out_mine, out_other, gate_local, gate_got, up_local, down_local = experts_pass(
        hidden_all,
        grad_all,
        table_all,
        weights_all,
        gate_full,
        up_full,
        down_full,
        capacity,
        expert_count,
        fsdp,
        5,
    )
    direct = gate_local.ndim == 3
    if not direct:
        gate_local = lax.psum_scatter(gate_local, "fsdp", scatter_dimension=0, tiled=True)[0]
    up_sum, down_sum = (
        lax.psum_scatter(part, "fsdp", scatter_dimension=0, tiled=True)
        for part in (up_local, down_local)
    )

    out_grad = grad_out[0].astype(F32)
    returned = returned.astype(F32)
    extra = returned[:, width:]
    gate_grad = extra[:, :expert_count] + extra[:, expert_count : 2 * expert_count]
    logit_grad = (
        gate_weights * (gate_grad - jnp.sum(gate_weights * gate_grad, axis=-1, keepdims=True))
    ).astype(BF16)
    router_local = jnp.einsum("td,te->de", hidden_two, logit_grad, preferred_element_type=F32)
    hidden_two_grad = returned[:, :width] + jnp.einsum(
        "te,de->td", logit_grad, router_full, preferred_element_type=F32
    )
    unused_two, norm_two_back = jax.vjp(rms_scale, middle, gain_b)
    middle_part, gain_two_local = norm_two_back(hidden_two_grad)
    middle_grad = out_grad + middle_part
    branch_grad = middle_grad.astype(BF16)
    out_local = jnp.einsum("tc,td->cd", attended, branch_grad, preferred_element_type=F32)
    attended_grad = jnp.einsum(
        "td,cd->tc", branch_grad, out_full, preferred_element_type=F32
    ).astype(BF16)

    def halves(local):
        local = local.astype(BF16).reshape(fsdp, 2, shard // 2, local.shape[1])
        pad = -local.shape[3] % (LANES * chips)
        return jnp.pad(local, ((0, 0), (0, 0), (0, 0), (0, pad))) if pad else local

    early_dense = chips <= 4
    query_grad, kv_grad, out_own, out_right, out_left, out_proj_sum = attention_back(
        queries,
        kv_all,
        attended,
        attended_grad,
        lse,
        order_mine,
        pos_mine,
        order_keys,
        cosine,
        sine,
        out_mine,
        out_other,
        halves(out_local),
        fsdp,
        early_dense,
        3,
    )
    pre_grad = jnp.concatenate([query_grad, kv_grad], axis=1)
    qkv_local = jnp.einsum("td,tc->dc", hidden_one, pre_grad, preferred_element_type=F32)
    hidden_one_grad = jnp.einsum("tc,dc->td", pre_grad, qkv_full, preferred_element_type=F32)
    unused_one, norm_one_back = jax.vjp(rms_scale, inputs, gain_a)
    input_part, gain_one_local = norm_one_back(hidden_one_grad)
    input_grad = (middle_grad + input_part).astype(BF16)

    span = shard * expert_count // 16
    wide = LANES * chips * -(-max(span, shard) // (LANES * chips))
    small_local = jnp.stack(
        [
            jnp.pad(
                router_local.astype(BF16).reshape(fsdp, 16, span),
                ((0, 0), (0, 0), (0, wide - span)),
            ),
            jnp.pad(
                jnp.stack(
                    [gain_one_local.reshape(fsdp, shard), gain_two_local.reshape(fsdp, shard)],
                    axis=1,
                ).astype(BF16),
                ((0, 0), (0, 14), (0, wide - shard)),
            ),
        ],
        axis=1,
    )
    *sums, out_sum = dense_reduce(
        [halves(qkv_local), small_local] + ([] if early_dense else [halves(out_local)]),
        out_own,
        out_right,
        out_left,
        DENSE_PIECE,
        fsdp,
        chips,
        4,
    )
    qkv_sum, small_sum = sums[:2]
    if not early_dense:
        out_proj_sum = sums[2]
    edge = width + 2 * kv_width
    qkv_grads = qkv_sum.reshape(shard, -1)
    out_proj_grad = out_proj_sum.reshape(shard, -1)[:, :width]
    up_grad_out, down_grad_out = (
        after(part, pre_grad)[0].astype(F32) for part in (up_sum, down_sum)
    )
    if direct:
        gate_local, gate_got = lax.optimization_barrier((gate_local, gate_got, pre_grad))[:2]
        gate_grad_out = add(gate_local, *[gate_got[j] for j in range(fsdp - 1)])
    else:
        gate_grad_out = after(gate_local, pre_grad).astype(F32)
    result = middle + out_sum
    return (
        result.astype(BF16)[None],
        input_grad[None],
        small_sum[1, 0, :shard].astype(F32),
        small_sum[1, 1, :shard].astype(F32),
        qkv_grads[:, :width].astype(F32),
        qkv_grads[:, width : width + kv_width].astype(F32),
        qkv_grads[:, width + kv_width : edge].astype(F32),
        out_proj_grad.astype(F32),
        small_sum[0, :, :span].reshape(shard, expert_count).astype(F32),
        gate_grad_out,
        up_grad_out,
        down_grad_out,
    )


def solution(mesh):
    placed = (
        P("fsdp", "ctx", None),
        P("fsdp", "ctx", None),
        P("fsdp", None),
        P("fsdp", None),
        P("fsdp", "ctx", None),
        P("fsdp"),
        P("fsdp"),
        P("fsdp", None),
        P("fsdp", None),
        P("fsdp", None),
        P("fsdp", None),
        P("fsdp", None),
        P("ctx", "fsdp", None),
        P("ctx", "fsdp", None),
        P("ctx", None, "fsdp"),
    )
    return jax.shard_map(
        body,
        mesh=mesh,
        in_specs=placed,
        out_specs=(
            P("fsdp", "ctx", None),
            P("fsdp", "ctx", None),
            P("fsdp"),
            P("fsdp"),
            P("fsdp", None),
            P("fsdp", None),
            P("fsdp", None),
            P("fsdp", None),
            P("fsdp", None),
            P("ctx", "fsdp", None),
            P("ctx", "fsdp", None),
            P("ctx", None, "fsdp"),
        ),
        check_vma=False,
    )
```

```python
import functools

import jax
import jax.numpy as jnp
from jax import lax
from jax.experimental import pallas as pl
from jax.experimental.pallas import tpu as pltpu
from jax.sharding import PartitionSpec as P

QUERY_HEADS = 12
KVH = 2
HEAD_SIZE = 128

EPSILON = 1e-06
ROPE_BASE = 10000.0
MASKED = -1e30
LOG2E = 1.4426950408889634
LANES = 128
SLOT_STEP = 64
DENSE_PIECE = 1024
LINE_TASK = 4
KEY_TILE = 512
VMEM_BYTES = 56 * 1024 * 1024
EXPERT_VMEM_BYTES = 119 * 512 * 1024
BACK_VMEM_BYTES = 61 * 1024 * 1024
FRONT_VMEM_BYTES = 50 * 1024 * 1024
MESH = pl.DeviceIdType.MESH
F32 = jnp.float32
BF16 = jnp.bfloat16


def dot(left, right, contract):
    return lax.dot_general(left, right, (contract, ((), ())), preferred_element_type=F32)


NN = ((1,), (0,))
NT = ((1,), (1,))
TN = ((0,), (0,))


def rms_scale(value_rows, gain):
    return (
        value_rows
        * lax.rsqrt(jnp.mean(value_rows * value_rows, axis=-1, keepdims=True) + EPSILON)
        * gain
    )


def place():
    ctx = lax.axis_index("ctx")
    core = lax.rem(ctx, 2)
    return ctx, lax.axis_index("fsdp"), ctx // 2, core, ctx + 1 - 2 * core


def peers_of(me, fsdp):
    peers = []
    for shift in range(1, fsdp):
        peer = me
        for bit in range(fsdp.bit_length() - 1):
            if (shift >> bit) & 1:
                digit = lax.rem(me // (1 << bit), 2)
                peer = peer + (1 << bit) - (2 << bit) * digit
        peers.append(peer)
    return peers


def greet(chips, peers, line):
    ctx, me, chip, core, sibling = place()
    barrier = pltpu.get_barrier_semaphore()
    for peer in peers:
        pl.semaphore_signal(barrier, inc=1, device_id=(ctx, peer), device_id_type=MESH)
    pl.semaphore_signal(barrier, inc=1, device_id=(sibling, me), device_id_type=MESH)
    known = len(peers) + 1
    if not line:
        pl.semaphore_wait(barrier, known)
        return
    has_right = chip + 1 < chips
    has_left = chip >= 1

    @pl.when(has_right)
    def _():
        pl.semaphore_signal(barrier, inc=1, device_id=(ctx + 2, me), device_id_type=MESH)

    @pl.when(has_left)
    def _():
        pl.semaphore_signal(barrier, inc=1, device_id=(ctx - 2, me), device_id_type=MESH)

    @pl.when(has_right & has_left)
    def _():
        pl.semaphore_wait(barrier, known + 2)

    @pl.when(jnp.logical_not(has_right & has_left))
    def _():
        pl.semaphore_wait(barrier, known + 1)


class Bounce:
    def __init__(self, src, dst, buffer, sem):
        self.inward = pltpu.make_async_copy(src, buffer, sem)
        self.outward = pltpu.make_async_copy(buffer, dst, sem)

    def start(self):
        self.inward.start()

    def turn(self):
        self.inward.wait()
        self.outward.start()

    def wait(self):
        self.outward.wait()


def remote(src, dst, send_sem, recv_sem, device):
    return pltpu.make_async_remote_copy(
        src_ref=src,
        dst_ref=dst,
        send_sem=send_sem,
        recv_sem=recv_sem,
        device_id=device,
        device_id_type=MESH,
    )


class Spread:
    def __init__(self, block, place_of, size, sems, fsdp):
        send_sem, recv_sem, on_send, on_recv = sems
        ctx, me, chip, core, sibling = place()
        self.peers = peers_of(me, fsdp)
        self.square = fsdp == 4
        near = self.peers[:2] if self.square else self.peers
        self.sends = [
            remote(block, place_of(me, 0, size), send_sem.at[j], recv_sem.at[j], (ctx, peer))
            for j, peer in enumerate(near)
        ]
        self.on, self.last = [], []
        if self.square:
            half = size // 2
            across_x, across_y, far = self.peers
            for k, (owner, target) in enumerate(((across_x, across_y), (across_y, across_x))):
                part = place_of(owner, k * half, half)
                self.on.append(remote(part, part, on_send.at[k], on_recv.at[k], (ctx, target)))
                part = place_of(far, k * half, half)
                self.last.append(remote(part, part, on_send.at[k], on_recv.at[k], (ctx, target)))

    def start(self):
        for copy in self.sends:
            copy.start()

    def hand_on(self, also=lambda j: None):
        for j, copy in enumerate(self.sends):
            copy.wait_recv()
            if self.square:
                self.on[j].start()
            also(j)

    def finish(self, also=lambda j: None):
        for copy in self.last:
            copy.wait_recv()
        if self.square:
            also(2)
        for copy in self.sends + self.on:
            copy.wait_send()


def spread_sems(fsdp):
    return [pltpu.SemaphoreType.DMA((fsdp - 1,)) for unused in range(4)]


class DenseGather:
    def __init__(self, ins, outs, sems, fsdp):
        buffers, local_sem, pass_sem, took_sem, spread_refs = sems
        ctx, me, chip, core, sibling = place()
        peers = peers_of(me, fsdp)
        self.spreads, self.passes, self.locals = [], [], []
        for i in range(len(ins)):
            rows = ins[i].shape[0]
            half = rows // 2

            def place_of(owner, begin, size, i=i, rows=rows, half=half):
                return outs[i].at[pl.ds(owner * rows + core * half + begin, size)]

            self.spreads.append(
                Spread(
                    ins[i].at[pl.ds(core * half, half)],
                    place_of,
                    half,
                    spread_refs[4 * i : 4 * i + 4],
                    fsdp,
                )
            )
            self.passes.append([])
            for j, peer in enumerate(peers):
                got = place_of(peer, 0, half)
                self.passes[i].append(
                    remote(got, got, pass_sem.at[i, j], took_sem.at[i, j], (sibling, me))
                )
            self.locals.append(
                Bounce(ins[i], outs[i].at[pl.ds(me * rows, rows)], buffers[i], local_sem.at[i])
            )

    def start(self):
        for spread in self.spreads:
            spread.start()
        for copy in self.locals:
            copy.start()

    def hand_on(self):
        for copy in self.locals:
            copy.turn()
        for i, spread in enumerate(self.spreads):
            spread.hand_on(lambda j, i=i: self.passes[i][j].start())

    def finish(self):
        for i, spread in enumerate(self.spreads):
            spread.finish(lambda j, i=i: self.passes[i][j].start())
        for passes in self.passes:
            for copy in passes:
                copy.wait()
        for copy in self.locals:
            copy.wait()


def dense_scratch(arrays, fsdp):
    count = len(arrays)
    return (
        [pltpu.VMEM(a.shape, a.dtype) for a in arrays]
        + [pltpu.SemaphoreType.DMA((count,))]
        + [pltpu.SemaphoreType.DMA((count, fsdp - 1)) for unused in range(2)]
        + spread_sems(fsdp) * count
    )


class ShardGather:
    def __init__(self, ref, out, buffer, sems, fsdp):
        ctx, me, chip, core, sibling = place()
        rows = ref.shape[1]

        def place_of(owner, begin, size):
            return out.at[:, pl.ds(owner * rows + begin, size)]

        self.spread = Spread(ref, place_of, rows, sems[1:], fsdp)
        self.own = Bounce(ref, place_of(me, 0, rows), buffer, sems[0])

    def start(self):
        self.spread.start()
        self.own.start()

    def hand_on(self):
        self.spread.hand_on()
        self.own.turn()

    def finish(self):
        self.spread.finish()
        self.own.wait()


class LineGather:
    def __init__(self, ins, outs, sems, chips):
        self.ins, self.outs, self.chips = ins, outs, chips
        self.buffers, self.sems = sems[:-7], sems[-7:]
        self.ctx, self.me, self.chip, core, self.sibling = place()
        self.count = len(ins)

    def to_right(self, i, step):
        outs, chips = self.outs, self.chips
        return remote(
            self.ins[i] if step == 0 else outs[i].at[0, chips - step],
            outs[i].at[0, chips - 1 - step],
            self.sems[1].at[i, step],
            self.sems[2].at[i, step],
            (self.ctx + 2, self.me),
        )

    def to_left(self, i, step):
        outs = self.outs
        return remote(
            self.ins[i] if step == 0 else outs[i].at[0, step],
            outs[i].at[0, step + 1],
            self.sems[3].at[i, step],
            self.sems[4].at[i, step],
            (self.ctx - 2, self.me),
        )

    def across(self, i, slot):
        return remote(
            self.ins[i] if slot == 0 else self.outs[i].at[0, slot],
            self.outs[i].at[1, slot],
            self.sems[5].at[i, slot],
            self.sems[6].at[i, slot],
            (self.sibling, self.me),
        )

    def local(self, i):
        return Bounce(self.ins[i], self.outs[i].at[0, 0], self.buffers[i], self.sems[0].at[i])

    def send(self, step):
        chip, chips, count = self.chip, self.chips, self.count

        @pl.when((chip + 1 < chips) & (chip >= step))
        def _():
            for i in range(count):
                self.to_right(i, step).start()

        @pl.when((chip >= 1) & (chip + step < chips))
        def _():
            for i in range(count):
                self.to_left(i, step).start()

    def receive(self, step):
        chip, chips, count = self.chip, self.chips, self.count

        @pl.when(chip >= step + 1)
        def _():
            for i in range(count):
                self.to_right(i, step).wait_recv()
                self.across(i, chips - 1 - step).start()

        @pl.when(chip + step + 1 < chips)
        def _():
            for i in range(count):
                self.to_left(i, step).wait_recv()
                self.across(i, step + 1).start()

    def own(self):
        for i in range(self.count):
            self.across(i, 0).start()
            self.local(i).start()

    def turn_own(self):
        for i in range(self.count):
            self.local(i).turn()

    def finish_own(self):
        for i in range(self.count):
            self.across(i, 0).wait()
            self.local(i).wait()

    def arrived(self, slot):
        for i in range(self.count):
            remote(
                self.outs[i].at[0, slot],
                self.outs[i].at[1, slot],
                self.sems[5].at[i, slot],
                self.sems[6].at[i, slot],
                (self.sibling, self.me),
            ).wait_recv()

    def sent(self):
        chip, chips, count = self.chip, self.chips, self.count
        for step in range(chips - 1):

            @pl.when((chip + 1 < chips) & (chip >= step))
            def _():
                for i in range(count):
                    self.to_right(i, step).wait_send()

            @pl.when((chip >= 1) & (chip + step < chips))
            def _():
                for i in range(count):
                    self.to_left(i, step).wait_send()

        for slot in range(chips):
            for i in range(count):
                self.across(i, slot).wait_send()

    def finish(self, step):
        chip, chips, count = self.chip, self.chips, self.count

        @pl.when((chip + 1 < chips) & (chip >= step))
        def _():
            for i in range(count):
                self.to_right(i, step).wait_send()

        @pl.when((chip >= 1) & (chip + step < chips))
        def _():
            for i in range(count):
                self.to_left(i, step).wait_send()

        @pl.when(chip >= step + 1)
        def _():
            for i in range(count):
                self.across(i, chips - 1 - step).wait()

        @pl.when(chip + step + 1 < chips)
        def _():
            for i in range(count):
                self.across(i, step + 1).wait()


def line_scratch(arrays, chips):
    count = len(arrays)
    return (
        [pltpu.VMEM(a.shape, a.dtype) for a in arrays if a is not None]
        + [pltpu.SemaphoreType.DMA((count,))]
        + [pltpu.SemaphoreType.DMA((count, chips - 1)) for unused in range(4)]
        + [pltpu.SemaphoreType.DMA((count, chips)) for unused in range(2)]
    )


def gather_kernel(dense, line, resumed, steps, fsdp, chips, *refs):
    count = dense + line + resumed
    ins, outs, scratch = refs[:count], refs[count : 2 * count], refs[2 * count :]
    ctx, me, chip, core, sibling = place()
    greet(chips, peers_of(me, fsdp) if dense else [], line > 0)
    split = dense + line
    if dense:
        own, scratch = scratch[: 5 * dense + 3], scratch[5 * dense + 3 :]
        first = DenseGather(
            ins[:dense],
            outs[:dense],
            (own[:dense],) + tuple(own[dense : dense + 3]) + (own[dense + 3 :],),
            fsdp,
        )
        first.start()
    if line:
        own, scratch = scratch[: line + 7], scratch[line + 7 :]
        second = LineGather(ins[dense:split], outs[dense:split], own, chips)
        for step in range(steps):
            second.send(step)
            if step == 0:
                second.own()
            if step == steps - 1 and dense:
                first.hand_on()
            second.receive(step)
            if step == 0:
                second.turn_own()
    if resumed:
        third = LineGather([None], outs[split:], scratch, chips)
        third.send(chips - 2)
        third.receive(chips - 2)
    if dense:
        first.finish()
    if line:
        second.finish_own()
        for step in range(steps):
            second.finish(step)
    if resumed:
        third.finish(chips - 2)


def gather(dense, line, steps, fsdp, chips, collective_id, resumed=()):
    arrays = list(dense) + list(line) + list(resumed)
    count = len(arrays)
    scratch = (dense_scratch(dense, fsdp) if dense else []) + (
        line_scratch(line, chips) if line else []
    )
    if resumed:
        scratch = scratch + line_scratch([None], chips)
    return pl.pallas_call(
        functools.partial(
            gather_kernel, len(dense), len(line), len(resumed), steps, fsdp, chips
        ),
        out_shape=[jax.ShapeDtypeStruct((fsdp * a.shape[0],) + a.shape[1:], a.dtype) for a in dense]
        + [jax.ShapeDtypeStruct((2, chips) + a.shape, a.dtype) for a in line]
        + [jax.ShapeDtypeStruct(a.shape, a.dtype) for a in resumed],
        in_specs=[pl.BlockSpec(memory_space=pl.ANY)] * count,
        out_specs=[pl.BlockSpec(memory_space=pl.ANY)] * count,
        scratch_shapes=scratch,
        input_output_aliases={count - 1: count - 1} if resumed else {},
        compiler_params=pltpu.CompilerParams(
            collective_id=collective_id, has_side_effects=True, vmem_limit_bytes=VMEM_BYTES
        ),
        name="gather",
    )(*arrays)


def add(*parts):
    total = parts[0].astype(F32)
    for part in parts[1:]:
        total = total + part.astype(F32)
    return total


def add_into(target, parts):
    rows = target.shape[0]
    tile = 32 if rows % 32 == 0 else 16

    def some(t, carry):
        part = pl.ds(pl.multiple_of(t * tile, tile), tile)
        target[part, :] = add(*[ref[part, :] for ref in parts]).astype(target.dtype)
        return carry

    lax.fori_loop(0, rows // tile, some, 0)


class LineSum:
    def __init__(self, chips, held, keep, got, sems):
        self.chips, self.held, self.keep, self.got = chips, held, keep, got
        self.sems = sems
        self.ctx, self.me, self.chip, core, sibling = place()

    def right(self, step):
        return remote(
            self.keep(self.chips - 1 - step),
            self.got.at[step - self.chip],
            self.sems[0].at[step],
            self.sems[1].at[step],
            (self.ctx + 2, self.me),
        )

    def from_left(self, step):
        slot = step + 1 - self.chip
        pltpu.make_async_remote_copy(
            src_ref=self.keep(self.chips - 1 - step),
            dst_ref=self.got.at[slot],
            send_sem=self.sems[0].at[step],
            recv_sem=self.sems[1].at[step],
            device_id=(self.ctx - 2, self.me),
            device_id_type=MESH,
        ).wait_recv()
        return self.got.at[slot]

    def from_right(self, step):
        slot = step + 2
        self.left(step).wait_recv()
        return self.got.at[slot]

    def left(self, step):
        return remote(
            self.keep(step + 1),
            self.got.at[step + 2],
            self.sems[2].at[step],
            self.sems[3].at[step],
            (self.ctx - 2, self.me),
        )

    def step(self, step):
        chip, chips = self.chip, self.chips
        far_right, far_left = chips - 1 - step, step + 1

        @pl.when(chip <= step)
        def _():
            parts = self.held(far_right)
            if step == 0:
                add_into(self.keep(far_right), parts())
            else:

                @pl.when(chip == 0)
                def _():
                    add_into(self.keep(far_right), parts())

                @pl.when(chip >= 1)
                def _():
                    add_into(self.keep(far_right), [self.from_left(step - 1)] + parts())

            self.right(step).start()

        @pl.when(chip >= chips - 1 - step)
        def _():
            parts = self.held(far_left)
            if step == 0:
                add_into(self.keep(far_left), parts())
            else:

                @pl.when(chip == chips - 1)
                def _():
                    add_into(self.keep(far_left), parts())

                @pl.when(chip < chips - 1)
                def _():
                    add_into(self.keep(far_left), [self.from_right(step - 1)] + parts())

            self.left(step).start()

    def total(self, target):
        chip, chips, last = self.chip, self.chips, self.chips - 2
        parts = self.held(0)

        @pl.when(chip == 0)
        def _():
            add_into(target, [self.from_right(last)] + parts())

        @pl.when(chip == chips - 1)
        def _():
            add_into(target, [self.from_left(last)] + parts())

        @pl.when((chip >= 1) & (chip < chips - 1))
        def _():
            add_into(target, [self.from_right(last), self.from_left(last)] + parts())

    def finish(self, steps=None):
        for step in range(self.chips - 1 if steps is None else steps):

            @pl.when(self.chip <= step)
            def _():
                self.right(step).wait_send()

            @pl.when(self.chip >= self.chips - 1 - step)
            def _():
                self.left(step).wait_send()


DENSE_BUFFERS = 5
DENSE_SEMS = 14


class DenseSum:
    def __init__(self, local, held, out, buffers, sems, fsdp, chips):
        self.local, self.held, self.out = local, held, out
        self.pair, self.cross, self.sums, got, self.spread = buffers
        self.sems = sems
        self.chips = chips
        self.ctx, self.me, self.chip, self.core, self.sibling = place()
        self.owners = peers_of(self.me, fsdp) + [self.me]
        self.cut = out.shape[2] // chips
        self.line = LineSum(
            chips,
            lambda r: lambda: [self.keep_ref(r)],
            lambda r: self.keep_ref(r),
            got,
            sems[4:8],
        )

    def keep_ref(self, r):
        return self.sums.at[:, self.columns(r)]

    def columns(self, r):
        owner = lax.rem(self.chip + r, self.chips)
        return pl.ds(pl.multiple_of(owner * self.cut, LANES), self.cut)

    def swap(self, j):
        return remote(
            self.local.at[self.owners[j], 1 - self.core],
            self.pair.at[j],
            self.sems[0].at[j],
            self.sems[1].at[j],
            (self.sibling, self.me),
        )

    def crossing(self, j):
        return remote(
            self.pair.at[j],
            self.cross.at[j],
            self.sems[2].at[j],
            self.sems[3].at[j],
            (self.ctx, self.owners[j]),
        )

    def to_right(self, step):
        return remote(
            self.spread.at[0, (self.chips - step) % self.chips],
            self.spread.at[0, self.chips - 1 - step],
            self.sems[8].at[step],
            self.sems[9].at[step],
            (self.ctx + 2, self.me),
        )

    def to_left(self, step):
        return remote(
            self.spread.at[0, step],
            self.spread.at[0, step + 1],
            self.sems[10].at[step],
            self.sems[11].at[step],
            (self.ctx - 2, self.me),
        )

    def across(self, slot):
        return remote(
            self.spread.at[0, slot],
            self.spread.at[1, slot],
            self.sems[12].at[slot],
            self.sems[13].at[slot],
            (self.sibling, self.me),
        )

    def start(self):
        for j in range(len(self.owners)):
            self.swap(j).start()

    def cross_over(self):
        for j, owner in enumerate(self.owners):
            self.swap(j).wait_recv()
            add_into(self.pair.at[j], [self.held(j, owner), self.pair.at[j]])
            if j < len(self.owners) - 1:
                self.crossing(j).start()

    def stages(self):
        chip, chips = self.chip, self.chips

        def open_up():
            for j in range(len(self.owners) - 1):
                self.crossing(j).wait_recv()
            add_into(
                self.sums,
                [self.cross.at[j] for j in range(len(self.owners) - 1)]
                + [self.pair.at[len(self.owners) - 1]],
            )
            self.line.step(0)

        def summed():
            self.line.total(self.spread.at[0, 0])
            hand_on(0)

        def hand_on(step):
            @pl.when((chip + 1 < chips) & (chip >= step))
            def _():
                self.to_right(step).start()

            @pl.when((chip >= 1) & (chip + step < chips))
            def _():
                self.to_left(step).start()

            if step == 0:
                self.across(0).start()

        def take(step):
            @pl.when(chip >= step + 1)
            def _():
                self.to_right(step).wait_recv()
                self.across(chips - 1 - step).start()

            @pl.when(chip + step + 1 < chips)
            def _():
                self.to_left(step).wait_recv()
                self.across(step + 1).start()

        def pass_on(step):
            def run():
                take(step - 1)
                hand_on(step)

            return run

        def line_step(step):
            return lambda: self.line.step(step)

        return (
            [open_up]
            + [line_step(step) for step in range(1, chips - 1)]
            + [summed]
            + [pass_on(step) for step in range(1, chips - 1)]
            + [lambda: take(chips - 2)]
        )

    def finish(self):
        chip, chips = self.chip, self.chips
        for r in range(chips):
            self.out[self.core, :, self.columns(r)] = self.spread[0, r]
        for r in range(chips):
            self.across(r).wait()
            self.out[1 - self.core, :, self.columns(r)] = self.spread[1, r]
        for step in range(chips - 1):

            @pl.when((chip + 1 < chips) & (chip >= step))
            def _():
                self.to_right(step).wait_send()

            @pl.when((chip >= 1) & (chip + step < chips))
            def _():
                self.to_left(step).wait_send()

        self.line.finish()
        for j in range(len(self.owners) - 1):
            self.crossing(j).wait_send()
        for j in range(len(self.owners)):
            self.swap(j).wait_send()


def dense_reduce_kernel(fsdp, chips, cuts, *refs):
    count = len(cuts)
    arrays = max(cut[0] for cut in cuts) + 1
    ins, refs = refs[:arrays], refs[arrays:]
    own_ref, right_ref, left_ref = refs[:3]
    outs, total_ref, refs = refs[3 : 3 + arrays], refs[3 + arrays], refs[4 + arrays :]
    from_left, from_right, r_send, r_recv, l_send, l_recv = refs[:6]
    rest = refs[6:]
    ctx, me, chip, core, sibling = place()
    greet(chips, peers_of(me, fsdp), True)

    to_right = remote(right_ref, from_left, r_send, r_recv, (ctx + 2, me))
    to_left = remote(left_ref, from_right, l_send, l_recv, (ctx - 2, me))

    @pl.when(chip + 1 < chips)
    def _():
        to_right.start()

    @pl.when(chip >= 1)
    def _():
        to_left.start()

    sums = []
    for i, (which, start, size) in enumerate(cuts):
        buffers = rest[i * DENSE_BUFFERS : (i + 1) * DENSE_BUFFERS]
        sems = rest[count * DENSE_BUFFERS + i * DENSE_SEMS :][:DENSE_SEMS]
        local = ins[which].at[:, :, :, pl.ds(start, size)]
        sums.append(
            DenseSum(
                local,
                lambda j, owner, local=local: local.at[owner, core],
                outs[which].at[:, :, pl.ds(start, size)],
                buffers,
                sems,
                fsdp,
                chips,
            )
        )
    for one in sums:
        one.start()
    for one in sums:
        one.cross_over()
    stages = [one.stages() for one in sums]
    lag = chips - 1
    for tick in range(len(stages[0]) + lag * (count - 1)):
        for i in range(count):
            if 0 <= tick - lag * i < len(stages[i]):
                stages[i][tick - lag * i]()
    @pl.when(chip >= 1)
    def _():
        to_right.wait_recv()

    @pl.when(chip + 1 < chips)
    def _():
        to_left.wait_recv()

    @pl.when(chip == 0)
    def _():
        add_into(total_ref, [from_right, own_ref])

    @pl.when(chip == chips - 1)
    def _():
        add_into(total_ref, [from_left, own_ref])

    @pl.when((chip >= 1) & (chip + 1 < chips))
    def _():
        add_into(total_ref, [from_left, from_right, own_ref])

    for one in sums:
        one.finish()

    @pl.when(chip + 1 < chips)
    def _():
        to_right.wait_send()

    @pl.when(chip >= 1)
    def _():
        to_left.wait_send()


def dense_buffers(rows, size, fsdp, chips):
    cut = size // chips
    return [
        pltpu.VMEM((fsdp, rows, size), BF16),
        pltpu.VMEM((fsdp - 1, rows, size), BF16),
        pltpu.VMEM((rows, size), BF16),
        pltpu.VMEM((chips + 1, rows, cut), BF16),
        pltpu.VMEM((2, chips, rows, cut), BF16),
    ]


def dense_sems(fsdp, chips):
    return (
        [pltpu.SemaphoreType.DMA((fsdp,)) for unused in range(2)]
        + [pltpu.SemaphoreType.DMA((fsdp - 1,)) for unused in range(2)]
        + [pltpu.SemaphoreType.DMA((chips - 1,)) for unused in range(8)]
        + [pltpu.SemaphoreType.DMA((chips,)) for unused in range(2)]
    )


def dense_reduce(arrays, own, right, left, piece, fsdp, chips, collective_id):
    vmem = pl.BlockSpec(memory_space=pltpu.VMEM)
    cuts, buffers = [], []
    for i, a in enumerate(arrays):
        rows, width = a.shape[2:]
        for start in range(0, width, piece):
            size = min(piece, width - start)
            cuts.append((i, start, size))
            buffers += dense_buffers(rows, size, fsdp, chips)
    sems = dense_sems(fsdp, chips)
    return pl.pallas_call(
        functools.partial(dense_reduce_kernel, fsdp, chips, tuple(cuts)),
        out_shape=[jax.ShapeDtypeStruct(a.shape[1:], BF16) for a in arrays]
        + [jax.ShapeDtypeStruct(own.shape, F32)],
        in_specs=[vmem] * len(arrays) + [vmem, pl.BlockSpec(memory_space=pl.ANY)]
        + [pl.BlockSpec(memory_space=pl.ANY)],
        out_specs=[vmem] * (len(arrays) + 1),
        scratch_shapes=[pltpu.VMEM(own.shape, BF16)] * 2
        + [pltpu.SemaphoreType.DMA] * 4
        + buffers
        + sems * len(cuts),
        compiler_params=pltpu.CompilerParams(
            collective_id=collective_id, has_side_effects=True, vmem_limit_bytes=VMEM_BYTES
        ),
        name="dense_reduce",
    )(*arrays, own, right, left)


def after(value, *others):
    return lax.optimization_barrier((value,) + others)[0]


def chunk_order(chip, i, chips):
    right_half = lax.div(2 * chip, chips)
    near = chip + right_half * (chips - 1 - 2 * chip)
    alone = chips - 1 - 2 * near
    paired = lax.div(i - alone + chips, chips)
    turn = (i - alone) * paired
    odd = lax.rem(turn, 2)
    pair = lax.div(turn, 2)
    distance = (1 - paired) * (chips - 1 - near - i) + paired * (
        (1 - odd) * (near - pair) + odd * (chips - near + pair)
    )
    return lax.rem(distance + right_half * (chips - 2 * distance), chips)


def front_kernel(
    scale,
    chips,
    fsdp,
    expert_count,
    tokens_ref,
    gain_a_ref,
    gain_b_ref,
    small_ref,
    cos_ref,
    sin_ref,
    oq_ref,
    pq_ref,
    ok_ref,
    routed_ref,
    table_ref,
    qkv_ref,
    wo_ref,
    gate_w_ref,
    passed_ref,
    table_all_ref,
    lse_ref,
    gate_ref,
    weights_ref,
    q_hbm,
    normed_hbm,
    kv_hbm,
    attended_hbm,
    middle_hbm,
    hidden_all_ref,
    gate_full_ref,
    grad_ref,
    q_ref,
    normed_ref,
    kv_ref,
    attended_ref,
    middle_ref,
    qkv_v,
    wo_v,
    gate_v,
    hidden_v,
    bias,
    top,
    total,
    acc,
    load_sem,
    own_sem,
    gate_own,
    gate_s0,
    gate_s1,
    gate_s2,
    gate_s3,
    keep_sem,
    *line_sems,
):
    ctx, me, chip, core, sibling = place()
    rows = tokens_ref.shape[0]
    width = tokens_ref.shape[1]
    half = rows // 2
    kv_width = KVH * HEAD_SIZE
    per_group = QUERY_HEADS // KVH
    parts = [pl.ds(0, half), pl.ds(half, half)]
    loads = [
        pltpu.make_async_copy(src, dst, load_sem.at[k])
        for k, (src, dst) in enumerate(((qkv_ref, qkv_v), (wo_ref, wo_v)))
    ]
    for copy in loads:
        copy.start()
    greet(chips, peers_of(me, fsdp), True)
    gate_gather = ShardGather(
        gate_w_ref,
        gate_full_ref,
        gate_v,
        (gate_own, gate_s0, gate_s1, gate_s2, gate_s3),
        fsdp,
    )
    gate_gather.start()
    kv_line = LineGather(
        [kv_ref.at[0, 0], table_all_ref.at[0, 0]], [kv_ref, table_all_ref], line_sems[:7], chips
    )
    grad_line = LineGather([None], [grad_ref], line_sems[7:14], chips)
    hidden_lines = [
        LineGather(
            [hidden_v.at[parts[0]]], [hidden_all_ref.at[:, :, parts[0]]], line_sems[14:21], chips
        ),
        LineGather(
            [hidden_v.at[parts[1]], weights_ref.at[0, 0]],
            [hidden_all_ref.at[:, :, parts[1]], weights_ref],
            line_sems[21:28],
            chips,
        ),
    ]

    def normed(value, gain):
        return value * lax.rsqrt(jnp.mean(value * value, axis=-1, keepdims=True) + EPSILON) * gain

    table_all_ref[0, 0] = table_ref[...]
    for part in parts:
        normed_ref[part, :] = normed(
            tokens_ref[part, :].astype(F32), gain_a_ref[...]
        ).astype(BF16)
    loads[0].wait()
    for part in parts:
        rows_one = normed_ref[part, :]
        cosine, sine = cos_ref[part, :], sin_ref[part, :]
        for h in range(KVH):
            columns = slice(width + h * HEAD_SIZE, width + (h + 1) * HEAD_SIZE)
            value = dot(rows_one, qkv_v[:, columns], NN)
            value = value * cosine + pltpu.roll(value, HEAD_SIZE // 2, 1) * sine
            kv_ref[0, 0, part, h * HEAD_SIZE : (h + 1) * HEAD_SIZE] = value.astype(BF16)
        kv_ref[0, 0, part, kv_width:] = dot(
            rows_one, qkv_v[:, width + kv_width :], NN
        ).astype(BF16)
    kv_line.send(0)
    for i in range(2):
        kv_line.across(i, 0).start()
    for part in parts:
        rows_one = normed_ref[part, :]
        cosine, sine = cos_ref[part, :], sin_ref[part, :]
        for h in range(0, QUERY_HEADS, 2):
            pre = dot(rows_one, qkv_v[:, h * HEAD_SIZE : (h + 2) * HEAD_SIZE], NN)
            for k in range(2):
                value = pre[:, k * HEAD_SIZE : (k + 1) * HEAD_SIZE]
                value = value * cosine + pltpu.roll(value, HEAD_SIZE // 2, 1) * sine
                q_ref[part, (h + k) * HEAD_SIZE : (h + k + 1) * HEAD_SIZE] = value.astype(BF16)

    def turn(index, r):
        part = parts[index]
        for q in range(2):
            gap = oq_ref[part, :] - ok_ref[q * chips + r]
            bias[:, q * rows : (q + 1) * rows] = jnp.where(
                (gap >= 0) & (gap <= pq_ref[part, :]), 0.0, MASKED
            )

        def one(h, carry):
            group = lax.div(h, per_group)
            columns = pl.ds(pl.multiple_of(h * HEAD_SIZE, HEAD_SIZE), HEAD_SIZE)
            key_columns = pl.ds(pl.multiple_of(group * HEAD_SIZE, HEAD_SIZE), HEAD_SIZE)
            value_columns = pl.ds(
                pl.multiple_of(kv_width + group * HEAD_SIZE, HEAD_SIZE), HEAD_SIZE
            )
            query = q_ref[part, columns]
            scores = []
            peak = top[h, part, :]
            for q in range(2):
                raw = dot(query, kv_ref[q, r, :, key_columns], NT) * (scale * LOG2E)
                raw = raw + bias[:, q * rows : (q + 1) * rows]
                scores.append(raw)
            best = scores[0][:, :LANES]
            for q in range(2):
                for k in range(rows // LANES):
                    best = jnp.maximum(best, scores[q][:, k * LANES : (k + 1) * LANES])
            new = jnp.maximum(peak, jnp.max(best, axis=1, keepdims=True))
            fade = jnp.exp2(peak - new)
            wide = jnp.concatenate([new] * (rows // LANES), axis=1)
            mass = total[h] * fade
            out = acc[:, columns] * fade
            for q in range(2):
                probs = jnp.exp2(scores[q] - wide)
                for k in range(rows // LANES):
                    mass = mass + probs[:, k * LANES : (k + 1) * LANES]
                out = out + dot(probs.astype(BF16), kv_ref[q, r, :, value_columns], NN)
            top[h, part, :] = new
            total[h] = mass
            acc[:, columns] = out
            return carry

        lax.fori_loop(0, QUERY_HEADS, one, 0)

    def begin(index):
        top[:, parts[index], :] = jnp.full((QUERY_HEADS, half, LANES), MASKED, F32)
        total[...] = jnp.zeros_like(total)
        acc[...] = jnp.zeros_like(acc)

    def end(index):
        part = parts[index]
        for h in range(QUERY_HEADS):
            columns = slice(h * HEAD_SIZE, (h + 1) * HEAD_SIZE)
            mass = jnp.sum(total[h], axis=1, keepdims=True)
            attended_ref[part, columns] = (acc[:, columns] / mass).astype(BF16)
            top[h, part, :] = top[h, part, :] + jnp.log2(mass)
        if index == 0:
            loads[1].wait()
        middle = tokens_ref[part, :].astype(F32) + dot(attended_ref[part, :], wo_v[...], NN)
        middle_ref[part, :] = middle
        rows_two = normed(middle, gain_b_ref[...]).astype(BF16)
        hidden_v[part, :] = rows_two
        routed = routed_ref[part, :] > 0.0
        logits = jnp.where(routed, dot(rows_two, small_ref[...], NN), MASKED)
        power = jnp.exp(logits - jnp.max(logits, axis=1, keepdims=True))
        power = jnp.where(routed, power, 0.0)
        gate_ref[part, :] = power / jnp.sum(power, axis=1, keepdims=True)
        if index == 1:
            weights_ref[0, 0] = gate_ref[...].T[:expert_count, :]
        line = hidden_lines[index]
        line.send(0)
        for i in range(line.count):
            line.across(i, 0).start()
        own(index).start()

    def keep(k, src, dst):
        return pltpu.make_async_copy(src, dst, keep_sem.at[k])

    def own(index):
        return pltpu.make_async_copy(
            hidden_v.at[parts[index]],
            hidden_all_ref.at[0, 0, parts[index]],
            own_sem.at[index],
        )

    begin(0)
    keep(0, q_ref, q_hbm).start()
    keep(1, normed_ref, normed_hbm).start()

    def first_turn(t, carry):
        for k in range(1, chips):

            @pl.when(t == k)
            def _():
                kv_line.receive(k - 1)
                if k < chips - 1:
                    kv_line.send(k)
                else:
                    grad_line.send(chips - 2)

        r = chunk_order(chip, chips - 1 - t, chips)
        kv_line.arrived(r)
        turn(0, r)
        return carry

    lax.fori_loop(0, chips, first_turn, 0)
    end(0)
    begin(1)
    gate_gather.hand_on()
    keep(2, kv_ref, kv_hbm).start()
    early = [step for step in range(chips - 1) if 2 * step + 2 < chips]

    def second_turn(t, carry):
        for step in early:

            @pl.when(t == 2 * step + 2)
            def _():
                hidden_lines[0].receive(step)
                if step + 1 < chips - 1:
                    hidden_lines[0].send(step + 1)

        turn(1, t)
        return carry

    lax.fori_loop(0, chips, second_turn, 0)
    grad_line.receive(chips - 2)
    late = [step for step in range(chips - 1) if step not in early]
    for step in late[:1]:
        hidden_lines[0].receive(step)
        if step + 1 < chips - 1:
            hidden_lines[0].send(step + 1)
    end(1)
    keep(3, attended_ref, attended_hbm).start()
    keep(4, middle_ref, middle_hbm).start()
    for h in range(QUERY_HEADS):
        lse_ref[h] = top[h].T[:1, :]
    for step in late[1:]:
        hidden_lines[0].receive(step)
        if step + 1 < chips - 1:
            hidden_lines[0].send(step + 1)
    for step in range(chips - 1):
        hidden_lines[1].receive(step)
        if step + 1 < chips - 1:
            hidden_lines[1].send(step + 1)
    for line in hidden_lines:
        for slot in range(chips):
            line.arrived(slot)
        line.sent()
    kv_line.sent()
    gate_gather.finish()
    grad_line.finish(chips - 2)
    for index in range(2):
        own(index).wait()
    for k, (src, dst) in enumerate(
        (
            (q_ref, q_hbm),
            (normed_ref, normed_hbm),
            (kv_ref, kv_hbm),
            (attended_ref, attended_hbm),
            (middle_ref, middle_hbm),
        )
    ):
        keep(k, src, dst).wait()


def front(
    tokens,
    gain_a,
    gain_b,
    small,
    cosine,
    sine,
    order_mine,
    pos_mine,
    order_keys,
    routed,
    table,
    qkv,
    w_out,
    w_gate,
    grad_all,
    chips,
    fsdp,
    collective_id,
):
    rows, width = tokens.shape
    expert_count = table.shape[0]
    kv_width = KVH * HEAD_SIZE
    vmem = pl.BlockSpec(memory_space=pltpu.VMEM)
    anywhere = pl.BlockSpec(memory_space=pl.ANY)
    shapes = [
        ((2, chips, expert_count, rows), F32),
        ((QUERY_HEADS, 1, rows), F32),
        ((rows, LANES), F32),
        ((2, chips, expert_count, rows), F32),
    ]
    kept = [
        ((rows, width), BF16),
        ((rows, width), BF16),
        ((2, chips, rows, 2 * kv_width), BF16),
        ((rows, width), BF16),
        ((rows, width), F32),
    ]
    gathered = [
        ((2, chips, rows, width), BF16),
        ((w_gate.shape[0], width, w_gate.shape[2]), BF16),
        (grad_all.shape, BF16),
    ]
    flops = 4 * rows * (2 * chips * rows) * width + 2 * rows * width * (2 * width + 2 * kv_width)
    return pl.pallas_call(
        functools.partial(front_kernel, HEAD_SIZE ** (-0.5), chips, fsdp, expert_count),
        out_shape=[
            jax.ShapeDtypeStruct(shape, kind) for shape, kind in shapes + kept + gathered
        ],
        in_specs=[vmem] * 11 + [anywhere] * 4,
        out_specs=[vmem] * 4 + [anywhere] * 8,
        scratch_shapes=[pltpu.VMEM(shape, kind) for shape, kind in kept]
        + [
            pltpu.VMEM(qkv.shape, BF16),
            pltpu.VMEM(w_out.shape, BF16),
            pltpu.VMEM(w_gate.shape, BF16),
            pltpu.VMEM((rows, width), BF16),
            pltpu.VMEM((rows // 2, 2 * rows), F32),
            pltpu.VMEM((QUERY_HEADS, rows, LANES), F32),
            pltpu.VMEM((QUERY_HEADS, rows // 2, LANES), F32),
            pltpu.VMEM((rows // 2, width), F32),
            pltpu.SemaphoreType.DMA((2,)),
            pltpu.SemaphoreType.DMA((2,)),
            pltpu.SemaphoreType.DMA,
        ]
        + spread_sems(fsdp)
        + [pltpu.SemaphoreType.DMA((5,))]
        + line_scratch([None] * 2, chips)
        + line_scratch([None], chips)
        + line_scratch([None], chips)
        + line_scratch([None] * 2, chips),
        input_output_aliases={14: 11},
        compiler_params=pltpu.CompilerParams(
            collective_id=collective_id, has_side_effects=True, vmem_limit_bytes=FRONT_VMEM_BYTES
        ),
        cost_estimate=pl.CostEstimate(
            flops=flops, bytes_accessed=40_000_000, transcendentals=rows * rows * chips * 24
        ),
        name="front",
    )(
        tokens,
        gain_a[None, :],
        gain_b[None, :],
        small,
        cosine,
        sine,
        order_mine[:, None],
        pos_mine[:, None],
        order_keys.reshape(2 * chips, 1, rows),
        routed,
        table,
        qkv,
        w_out,
        w_gate,
        grad_all,
    )


def attention_back_kernel(
    scale,
    chips,
    fsdp,
    early_dense,
    q_ref,
    k_ref,
    v_ref,
    o_ref,
    do_ref,
    lse_ref,
    oq_ref,
    pq_ref,
    ok_ref,
    cos_ref,
    sin_ref,
    mine_ref,
    other_ref,
    dense_ref,
    dq_ref,
    kv_ref,
    own_ref,
    right_ref,
    left_ref,
    dense_out_ref,
    bias,
    dk_acc,
    dv_acc,
    kv_total,
    mine_v,
    pair,
    got,
    kv_v,
    kv_pair,
    kv_got,
    load_sem,
    store_sem,
    swap_send,
    swap_recv,
    r_send,
    r_recv,
    l_send,
    l_recv,
    kv_swap_send,
    kv_swap_recv,
    kr_send,
    kr_recv,
    kl_send,
    kl_recv,
    *dense_refs,
):
    ctx, me, chip, core, sibling = place()
    keys = k_ref.shape[0]
    tiles = keys // KEY_TILE
    rows = q_ref.shape[0]
    per_group = QUERY_HEADS // KVH
    head = pl.program_id(0)

    order = []
    for step in range(chips - 1):
        for r in (chips - 1 - step, step + 1):
            if r not in order:
                order.append(r)
    order.append(0)
    swaps = [
        remote(other_ref.at[r], pair.at[r], swap_send.at[r], swap_recv.at[r], (sibling, me))
        for r in range(chips)
    ]
    slots = mine_v.shape[0]
    loads = [
        pltpu.make_async_copy(mine_ref.at[r], mine_v.at[j % slots], load_sem.at[j % slots])
        for j, r in enumerate(order)
    ]
    line = LineSum(
        chips,
        lambda r: lambda: [pair.at[r]],
        lambda r: pair.at[r],
        got,
        (r_send, r_recv, l_send, l_recv),
    )

    def join(j):
        loads[j].wait()
        swaps[order[j]].wait_recv()
        add_into(pair.at[order[j]], [pair.at[order[j]], mine_v.at[j % slots]])
        if j + slots < chips:
            loads[j + slots].start()

    if early_dense:
        dense_v, dense_load = dense_refs[:2]
        buffers = dense_refs[2 : 2 + DENSE_BUFFERS]
        dense = DenseSum(
            dense_ref,
            lambda j, owner: dense_v.at[j],
            dense_out_ref,
            buffers,
            dense_refs[2 + DENSE_BUFFERS :],
            fsdp,
            chips,
        )
        dense_loads = [
            pltpu.make_async_copy(dense_ref.at[owner, core], dense_v.at[j], dense_load.at[j])
            for j, owner in enumerate(dense.owners)
        ]
        stages = dense.stages()
        at_head = {QUERY_HEADS - 1 - len(stages) // 2 + k: k for k in range(len(stages) // 2)}

    def kv_swap(group, r):
        return remote(
            kv_v.at[group, 1, r],
            kv_pair.at[group, r],
            kv_swap_send.at[group, r],
            kv_swap_recv.at[group, r],
            (sibling, me),
        )

    def kv_line(group):
        def held(r):
            kv_swap(group, r).wait_recv()
            return lambda: [kv_v.at[group, 0, r], kv_pair.at[group, r]]

        return LineSum(
            chips,
            held,
            lambda r: kv_pair.at[group, r],
            kv_got.at[group],
            tuple(sem.at[group] for sem in (kr_send, kr_recv, kl_send, kl_recv)),
        )

    def kv_start(group):
        for q in range(2):
            for r in range(chips):
                part = pl.ds((q * chips + r) * rows, rows)
                kv_v[group, q, r, :, :HEAD_SIZE] = (dk_acc[part, :] * scale).astype(BF16)
                kv_v[group, q, r, :, HEAD_SIZE:] = dv_acc[part, :].astype(BF16)
        for r in order:
            kv_swap(group, r).start()

    @pl.when(head == 0)
    def _():
        greet(chips, peers_of(me, fsdp) if early_dense else [], True)
        if early_dense:
            for copy in dense_loads:
                copy.start()
            dense.start()
        for r in order:
            swaps[r].start()
        for copy in loads[:slots]:
            copy.start()

        def fill(t, carry):
            tile = pl.ds(pl.multiple_of(t * KEY_TILE, KEY_TILE), KEY_TILE)
            key_order = jnp.broadcast_to(ok_ref[:, tile], (8, KEY_TILE)).T[:, :1]
            gap = oq_ref[...] - key_order
            bias[tile, :] = jnp.where((gap >= 0) & (gap <= pq_ref[...]), 0.0, MASKED)
            return carry

        lax.fori_loop(0, tiles, fill, 0)

    @pl.when(lax.rem(head, per_group) == 0)
    def _():
        dk_acc[...] = jnp.zeros_like(dk_acc)
        dv_acc[...] = jnp.zeros_like(dv_acc)

    query = q_ref[...]
    grad = do_ref[...]
    lse = lse_ref[0]
    product = grad.astype(F32) * o_ref[...].astype(F32)
    delta = jnp.sum(product.T, axis=0, keepdims=True)

    def step(t, acc):
        tile = pl.ds(pl.multiple_of(t * KEY_TILE, KEY_TILE), KEY_TILE)
        key = k_ref[tile, :]
        raw = dot(key, query, NT) * (scale * LOG2E) + bias[tile, :]
        probs = jnp.exp2(raw - lse)
        prob_grad = dot(v_ref[tile, :], grad, NT)
        score_grad = (probs * (prob_grad - delta)).astype(BF16)
        dv_acc[tile, :] += dot(probs.astype(BF16), grad, NN)
        dk_acc[tile, :] += dot(score_grad, query, NN)
        return acc + dot(score_grad, key, TN)

    acc = lax.fori_loop(0, tiles, step, jnp.zeros((rows, HEAD_SIZE), F32))
    def turn_back(value):
        back = value * cos_ref[...] - pltpu.roll(value, HEAD_SIZE // 2, 1) * sin_ref[...]
        return back.astype(BF16)

    dq_ref[...] = turn_back(acc * scale)

    last = QUERY_HEADS - 1
    stride = max(1, last // (chips - 2))
    early = {per_group + 2 * s: s for s in range(chips - 1) if per_group + 2 * s < last}
    for h in range(QUERY_HEADS):

        @pl.when(head == h)
        def _():
            if h == 0:
                for j in range(min(2, chips)):
                    join(j)
            if h == 1:
                for j in range(2, chips):
                    join(j)
            if early_dense and h == 1:
                for copy in dense_loads:
                    copy.wait()
                dense.cross_over()
            if early_dense and h in at_head:
                stages[at_head[h]]()
            for s in range(chips - 2):
                if h == (s * stride if s == 0 else max(1, s * stride)):
                    line.step(s)
            if h % per_group == per_group - 1:
                kv_start(h // per_group)
            if h in early:
                kv_line(0).step(early[h])

    @pl.when(head == last)
    def _():
        def store(k, r, target):
            return pltpu.make_async_copy(pair.at[r], target, store_sem.at[k])

        @pl.when((chip >= 1) & (chip + 1 < chips))
        def _():
            add_into(pair.at[1], [pair.at[1], line.from_left(chips - 3)])
            add_into(pair.at[chips - 1], [pair.at[chips - 1], line.from_right(chips - 3)])

        for copy in (
            store(0, 0, own_ref),
            store(1, 1, right_ref),
            store(2, chips - 1, left_ref),
        ):
            copy.start()
        rest = stages[len(stages) // 2 :] if early_dense else []
        for group in range(KVH):
            one = kv_line(group)
            for s in range(chips - 1):
                if group > 0 or s not in early.values():
                    one.step(s)
                    if rest:
                        rest.pop(0)()
            one.total(kv_total)
            kv_ref[:, group * HEAD_SIZE : (group + 1) * HEAD_SIZE] = turn_back(
                kv_total[:, :HEAD_SIZE]
            )
            kv_ref[:, (KVH + group) * HEAD_SIZE : (KVH + group + 1) * HEAD_SIZE] = kv_total[
                :, HEAD_SIZE:
            ].astype(BF16)
        for stage in rest:
            stage()
        if early_dense:
            dense.finish()
        for group in range(KVH):
            kv_line(group).finish()
            for r in range(chips):
                kv_swap(group, r).wait_send()
        line.finish(chips - 2)
        for swap in swaps:
            swap.wait_send()
        for copy in (
            store(0, 0, own_ref),
            store(1, 1, right_ref),
            store(2, chips - 1, left_ref),
        ):
            copy.wait()


def attention_back(
    queries,
    kv,
    attended,
    attended_grad,
    lse,
    order_mine,
    pos_mine,
    order_keys,
    cosine,
    sine,
    mine,
    other,
    dense,
    fsdp,
    early_dense,
    collective_id,
):
    rows = queries.shape[0]
    keys = kv.shape[0]
    chips, unused, width = mine.shape
    per_group = QUERY_HEADS // KVH
    head_rows = pl.BlockSpec((rows, HEAD_SIZE), lambda h: (0, h))
    anywhere = pl.BlockSpec(memory_space=pl.ANY)
    return pl.pallas_call(
        functools.partial(
            attention_back_kernel, HEAD_SIZE ** (-0.5), chips, fsdp, early_dense
        ),
        grid=(QUERY_HEADS,),
        out_shape=[
            jax.ShapeDtypeStruct(queries.shape, BF16),
            jax.ShapeDtypeStruct((rows, 2 * KVH * HEAD_SIZE), BF16),
        ]
        + [jax.ShapeDtypeStruct((rows, width), BF16)] * 3
        + [jax.ShapeDtypeStruct(dense.shape[1:], BF16)],
        in_specs=[
            head_rows,
            pl.BlockSpec((keys, HEAD_SIZE), lambda h: (0, h // per_group)),
            pl.BlockSpec((keys, HEAD_SIZE), lambda h: (0, KVH + h // per_group)),
            head_rows,
            head_rows,
            pl.BlockSpec((1, 1, rows), lambda h: (h, 0, 0)),
            pl.BlockSpec((1, rows), lambda h: (0, 0)),
            pl.BlockSpec((1, rows), lambda h: (0, 0)),
            pl.BlockSpec((1, keys), lambda h: (0, 0)),
            pl.BlockSpec((rows, HEAD_SIZE), lambda h: (0, 0)),
            pl.BlockSpec((rows, HEAD_SIZE), lambda h: (0, 0)),
            anywhere,
            anywhere,
            anywhere,
        ],
        out_specs=[
            head_rows,
            pl.BlockSpec((rows, 2 * KVH * HEAD_SIZE), lambda h: (0, 0)),
            anywhere,
            anywhere,
            anywhere,
            pl.BlockSpec(dense.shape[1:], lambda h: (0, 0, 0)) if early_dense else anywhere,
        ],
        scratch_shapes=[
            pltpu.VMEM((keys, rows), F32),
            pltpu.VMEM((keys, HEAD_SIZE), F32),
            pltpu.VMEM((keys, HEAD_SIZE), F32),
            pltpu.VMEM((rows, 2 * HEAD_SIZE), F32),
            pltpu.VMEM((2 if chips <= 4 else 1, rows, width), BF16),
            pltpu.VMEM((chips, rows, width), BF16),
            pltpu.VMEM((chips + 1, rows, width), BF16),
            pltpu.VMEM((KVH, 2, chips, rows, 2 * HEAD_SIZE), BF16),
            pltpu.VMEM((KVH, chips, rows, 2 * HEAD_SIZE), BF16),
            pltpu.VMEM((KVH, chips + 1, rows, 2 * HEAD_SIZE), BF16),
            pltpu.SemaphoreType.DMA((2,)),
            pltpu.SemaphoreType.DMA((3,)),
            pltpu.SemaphoreType.DMA((chips,)),
            pltpu.SemaphoreType.DMA((chips,)),
        ]
        + [pltpu.SemaphoreType.DMA((chips - 1,)) for unused in range(4)]
        + [pltpu.SemaphoreType.DMA((KVH, chips)) for unused in range(2)]
        + [pltpu.SemaphoreType.DMA((KVH, chips - 1)) for unused in range(4)]
        + (
            [
                pltpu.VMEM((fsdp,) + dense.shape[2:], BF16),
                pltpu.SemaphoreType.DMA((fsdp,)),
            ]
            + dense_buffers(dense.shape[2], dense.shape[3], fsdp, chips)
            + dense_sems(fsdp, chips)
            if early_dense
            else []
        ),
        compiler_params=pltpu.CompilerParams(
            collective_id=collective_id, has_side_effects=True, vmem_limit_bytes=BACK_VMEM_BYTES
        ),
        cost_estimate=pl.CostEstimate(
            flops=10 * rows * keys * HEAD_SIZE * QUERY_HEADS,
            bytes_accessed=10 * rows * QUERY_HEADS * HEAD_SIZE + 8 * keys * KVH * HEAD_SIZE,
            transcendentals=rows * keys * QUERY_HEADS,
        ),
        name="attention_back",
    )(
        queries,
        kv,
        kv,
        attended,
        attended_grad,
        lse,
        order_mine[None, :],
        pos_mine[None, :],
        order_keys[None, :],
        cosine,
        sine,
        mine,
        other,
        dense,
    )


def experts_kernel(
    capacity,
    local_experts,
    expert_count,
    chips,
    fsdp,
    per,
    hidden_ref,
    grad_ref,
    table_ref,
    weight_ref,
    gate_ref,
    up_ref,
    down_ref,
    returned_ref,
    out_mine_ref,
    out_other_ref,
    gate_grad_ref,
    gate_got_ref,
    up_grad_ref,
    down_grad_ref,
    x_ref,
    pg_ref,
    inner_ref,
    da_ref,
    db_ref,
    gate_v,
    up_v,
    down_v,
    hidden_v,
    grad_v,
    out_v,
    x_v,
    pg_v,
    g_v,
    inner_v,
    da_v,
    db_v,
    mine_v,
    other_v,
    pair,
    got,
    stage_tall,
    weight_sem,
    load_sem,
    out_sem,
    save_sem,
    swap_send,
    swap_recv,
    right_send,
    right_recv,
    left_send,
    left_recv,
    stage_sem,
    tile_own,
    tile_send,
    tile_recv,
):
    ctx, me, chip, core, sibling = place()
    peers = peers_of(me, fsdp)
    tokens = hidden_v.shape[1]
    width = hidden_v.shape[2]
    slots = x_v.shape[1]
    slot_rows = slots // 2
    units = inner_v.shape[2]
    total_rows = x_ref.shape[1]
    first = ctx * local_experts

    weights_in = [
        pltpu.make_async_copy(src, dst, weight_sem.at[k])
        for k, (src, dst) in enumerate(
            ((gate_ref, gate_v), (up_ref, up_v), (down_ref, down_v))
        )
    ]

    def load(i):
        r = chunk_order(chip, i, chips)
        return [
            pltpu.make_async_copy(hidden_ref.at[:, r], hidden_v, load_sem.at[0]),
            pltpu.make_async_copy(grad_ref.at[:, r], grad_v, load_sem.at[1]),
        ]

    def saves(i):
        rows = pl.ds(i * slots, slots)
        return [
            pltpu.make_async_copy(src, dst.at[:, rows], save_sem.at[k])
            for k, (src, dst) in enumerate(
                ((x_v, x_ref), (pg_v, pg_ref), (inner_v, inner_ref), (da_v, da_ref), (db_v, db_ref))
            )
        ]

    def out_copies(i):
        r = chunk_order(chip, i, chips)
        return [
            pltpu.make_async_copy(out_v.at[0], out_mine_ref.at[r], out_sem.at[0]),
            pltpu.make_async_copy(out_v.at[1], out_other_ref.at[r], out_sem.at[1]),
        ]

    def swap(i):
        r = chunk_order(chip, i, chips)
        return remote(
            other_v.at[lax.rem(i, 2)],
            pair.at[r],
            swap_send.at[r],
            swap_recv.at[r],
            (sibling, me),
        )

    def join(i):
        r = chunk_order(chip, i, chips)
        swap(i).wait_recv()
        add_into(pair.at[r], [pair.at[r], mine_v.at[lax.rem(i, 2)]])

    line = LineSum(
        chips,
        lambda r: lambda: [pair.at[r]],
        lambda r: pair.at[r],
        got,
        (right_send, right_recv, left_send, left_recv),
    )

    for copy in load(0) + weights_in:
        copy.start()
    greet(chips, peers if per == 1 else [], True)

    slot = lax.broadcasted_iota(jnp.int32, (slot_rows, tokens), 0).astype(F32) + 1.0
    slot = jnp.where(slot <= capacity, slot, -1.0)
    lane = lax.broadcasted_iota(jnp.int32, (slots, LANES), 1)

    def chunk(i, carry):
        r = chunk_order(chip, i, chips)
        for copy in load(i):
            copy.wait()

        @pl.when(i >= 1)
        def _():
            for copy in saves(i - 1):
                copy.wait()

        picks = [[], []]
        weight_rows = []
        for e in range(local_experts):
            rows_w = []
            for q in range(2):
                hit = slot == table_ref[q, r, pl.ds(first + e, 1), :]
                pick = jnp.where(hit, 1.0, 0.0).astype(BF16)
                weight = weight_ref[q, r, pl.ds(first + e, 1), :]
                w = jnp.sum(jnp.where(hit, weight, 0.0), axis=1, keepdims=True)
                rows = pl.ds(q * slot_rows, slot_rows)
                x_v[e, rows, :] = dot(pick, hidden_v[q], NN).astype(BF16)
                g = dot(pick, grad_v[q], NN)
                g_v[e, rows, :] = g.astype(BF16)
                pg_v[e, rows, :] = (w * g).astype(BF16)
                picks[q].append(pick)
                rows_w.append(w)
            weight_rows.append(jnp.concatenate(rows_w, axis=0))

        @pl.when(i + 1 < chips)
        def _():
            for copy in load(i + 1):
                copy.start()

        @pl.when(i == 0)
        def _():
            for copy in weights_in:
                copy.wait()

        outs = [[], []]
        backs = [[], []]
        for e in range(local_experts):
            x = x_v[e]
            pair_grad = pg_v[e]
            w = weight_rows[e]
            gate = gate_v[e * width : (e + 1) * width, :]
            up = up_v[e * width : (e + 1) * width, :]
            down = down_v[e * units : (e + 1) * units, :]
            gate_pre = dot(x, gate, NN)
            up_pre = dot(x, up, NN)
            sig = jax.nn.sigmoid(gate_pre)
            silu = gate_pre * sig
            inner = (silu * up_pre).astype(BF16)
            inner_v[e] = inner
            expert_out = dot(inner, down, NN).astype(BF16).astype(F32)
            gate_grad = jnp.sum(expert_out * g_v[e].astype(F32), axis=1, keepdims=True)
            inner_grad = dot(pair_grad, down, NT)
            da = (inner_grad * up_pre * sig * (1.0 + gate_pre * (1.0 - sig))).astype(BF16)
            db = (inner_grad * silu).astype(BF16)
            da_v[e] = da
            db_v[e] = db
            row_grad = (dot(da, gate, NT) + dot(db, up, NT)).astype(BF16)
            high = gate_grad.astype(BF16).astype(F32)
            extra = jnp.where(lane == first + e, high, 0.0) + jnp.where(
                lane == expert_count + first + e, gate_grad - high, 0.0
            )
            back = jnp.concatenate([row_grad, extra.astype(BF16)], axis=1)
            out_rows = (w * expert_out).astype(BF16)
            for q in range(2):
                part = slice(q * slot_rows, (q + 1) * slot_rows)
                outs[q].append(out_rows[part])
                backs[q].append(back[part])

        for copy in saves(i):
            copy.start()

        @pl.when(i >= 1)
        def _():
            for copy in out_copies(i - 1):
                copy.wait()

        @pl.when(i >= 2)
        def _():
            swap(i - 2).wait_send()

        for q in range(2):
            pick = jnp.concatenate(picks[q], axis=0)
            held = other_v if q else mine_v
            held[lax.rem(i, 2)] = dot(pick, jnp.concatenate(backs[q], axis=0), TN).astype(BF16)
            if q:
                swap(i).start()
        for q in range(2):
            pick = jnp.concatenate(picks[q], axis=0)
            out_v[q] = dot(pick, jnp.concatenate(outs[q], axis=0), TN).astype(BF16)
        for copy in out_copies(i):
            copy.start()

        @pl.when(i == 0)
        def _():
            join(0)
            line.step(0)

        @pl.when(i >= 2)
        def _():
            join(i - 1)

        for step in range(1, chips - 1):
            if 2 * step < chips:

                @pl.when(i == 2 * step)
                def _():
                    line.step(step)

        return carry

    lax.fori_loop(0, chips, chunk, 0)
    join(chips - 1)
    for copy in saves(chips - 1):
        copy.wait()
    for copy in out_copies(chips - 1):
        copy.wait()
    for i in range(max(0, chips - 2), chips):
        swap(i).wait_send()

    shard = width // fsdp
    blocks = fsdp // per
    block = per * shard

    def fetch(copies):
        copies = [
            pltpu.make_async_copy(src, dst, save_sem.at[k])
            for k, (src, dst) in enumerate(copies)
        ]
        for copy in copies:
            copy.start()
        for copy in copies:
            copy.wait()

    def products(e, staged, target, product):
        def write(f):
            return [
                pltpu.make_async_copy(
                    staged(lax.rem(f, 2), p),
                    target.at[f * per + p, e],
                    stage_sem.at[lax.rem(f, 2), p],
                )
                for p in range(per)
            ]

        def one(f, carry):
            @pl.when(f >= 2)
            def _():
                for copy in write(f - 2):
                    copy.wait()

            product(f)
            for copy in write(f):
                copy.start()
            return carry

        lax.fori_loop(0, blocks, one, 0)
        for f in range(max(0, blocks - 2), blocks):
            for copy in write(f):
                copy.wait()

    def stage_wide(slot, p):
        return hidden_v.at[slot, pl.ds(p * shard, shard), pl.ds(0, units)]

    def wide(e, held, staged, target):
        def product(f):
            columns = pl.ds(pl.multiple_of(f * block, LANES), block)
            value = dot(
                down_v[:total_rows, columns],
                held[e * total_rows : (e + 1) * total_rows, :],
                TN,
            ).astype(BF16)
            for p in range(per):
                staged(lax.rem(f, 2), p)[...] = value[p * shard : (p + 1) * shard, :]

        products(e, staged, target, product)

    def tall(e, target):
        def product(f):
            columns = pl.ds(pl.multiple_of(f * block, LANES), block)
            value = dot(
                gate_v[e * total_rows : (e + 1) * total_rows, :],
                down_v[:total_rows, columns],
                TN,
            ).astype(BF16)
            for p in range(per):
                stage_tall[lax.rem(f, 2), p] = value[:, p * shard : (p + 1) * shard]

        products(e, lambda slot, p: stage_tall.at[slot, p], target, product)

    def tile(e, j):
        held = (hidden_v, grad_v)[e]
        return held.at[j // 2, pl.ds(0, shard), pl.ds((j % 2) * units, units)]

    def tile_copy(e, j):
        if j == len(peers):
            return pltpu.make_async_copy(tile(e, j), gate_grad_ref.at[e], tile_own.at[e])
        return remote(
            tile(e, j),
            gate_got_ref.at[j, e],
            tile_send.at[e, j],
            tile_recv.at[e, j],
            (ctx, peers[j]),
        )

    def gate_tiles(e):
        for j, owner in enumerate(peers + [me]):
            columns = pl.ds(pl.multiple_of(owner * shard, LANES), shard)
            tile(e, j)[...] = dot(
                down_v[:total_rows, columns],
                gate_v[e * total_rows : (e + 1) * total_rows, :],
                TN,
            ).astype(BF16)
            tile_copy(e, j).start()

    def fetch_x(e):
        copies = [(x_ref.at[e], down_v.at[:total_rows])]
        if e == 0:
            for k in range(local_experts):
                held = pl.ds(k * total_rows, total_rows)
                copies += [(da_ref.at[k], gate_v.at[held]), (db_ref.at[k], up_v.at[held])]
        return lambda: fetch(copies)

    def stage_up(slot, p):
        return out_v.at[slot, pl.ds(p * shard, shard), pl.ds(0, units)]

    work = []
    for e in range(local_experts):
        work.append(fetch_x(e))
        if per == 1:
            work.append(lambda e=e: gate_tiles(e))
        else:
            work.append(lambda e=e: wide(e, gate_v, stage_wide, gate_grad_ref))
        if e > 0:
            work.append(lambda e=e: wide(e, up_v, stage_up, up_grad_ref))
    work.append(lambda: fetch([(x_ref.at[0], down_v.at[:total_rows])]))
    work.append(lambda: wide(0, up_v, stage_up, up_grad_ref))
    for e in range(local_experts):
        copies = [(pg_ref.at[e], down_v.at[:total_rows])]
        if e == 0:
            for k in range(local_experts):
                copies.append((inner_ref.at[k], gate_v.at[pl.ds(k * total_rows, total_rows)]))
        work.append(lambda copies=copies: fetch(copies))
        work.append(lambda e=e: tall(e, down_grad_ref))
    late = [step for step in range(1, chips - 1) if 2 * step >= chips]
    for n, task in enumerate(work):
        task()
        if n == LINE_TASK or (n > LINE_TASK and late):
            if late:
                line.step(late.pop(0))
    for step in late:
        line.step(step)

    line.total(returned_ref)
    line.finish()
    if per == 1:
        for e in range(local_experts):
            for j in range(fsdp):
                tile_copy(e, j).wait()


def experts_pass(
    hidden, grad, table, weights, gate, up, down, capacity, expert_count, fsdp, collective_id
):
    unused, chips, tokens, width = grad.shape
    local_experts, unused, units = gate.shape
    slots = 2 * SLOT_STEP * -(-capacity // SLOT_STEP)
    total = chips * slots
    shard = width // fsdp
    per = 1 if shard % LANES == 0 else 2
    wide = width + LANES
    anywhere = pl.BlockSpec(memory_space=pl.ANY)
    vmem = pl.BlockSpec(memory_space=pltpu.VMEM)
    flops = 2 * total * width * units * local_experts * 9 + 8 * total * tokens * width
    saved = [(local_experts, total, width)] * 2 + [(local_experts, total, units)] * 3
    held = [(local_experts, slots, width)] * 3 + [(local_experts, slots, units)] * 3
    outs = pl.pallas_call(
        functools.partial(
            experts_kernel, capacity, local_experts, expert_count, chips, fsdp, per
        ),
        out_shape=[
            jax.ShapeDtypeStruct((tokens, wide), BF16),
            jax.ShapeDtypeStruct((chips, tokens, width), BF16),
            jax.ShapeDtypeStruct((chips, tokens, width), BF16),
            jax.ShapeDtypeStruct(
                ((fsdp,) if per > 1 else ()) + (local_experts, shard, units), BF16
            ),
            jax.ShapeDtypeStruct(
                (fsdp - 1 if per == 1 else 1, local_experts, shard, units), BF16
            ),
            jax.ShapeDtypeStruct((fsdp, local_experts, shard, units), BF16),
            jax.ShapeDtypeStruct((fsdp, local_experts, units, shard), BF16),
        ]
        + [jax.ShapeDtypeStruct(shape, BF16) for shape in saved],
        in_specs=[anywhere, anywhere, vmem, vmem, anywhere, anywhere, anywhere],
        out_specs=[vmem] + [anywhere] * 11,
        scratch_shapes=[
            pltpu.VMEM((local_experts * width, units), BF16),
            pltpu.VMEM((local_experts * width, units), BF16),
            pltpu.VMEM((local_experts * units, width), BF16),
            pltpu.VMEM((2, tokens, width), BF16),
            pltpu.VMEM((2, tokens, width), BF16),
            pltpu.VMEM((2, tokens, width), BF16),
        ]
        + [pltpu.VMEM(shape, BF16) for shape in held]
        + [
            pltpu.VMEM((2, tokens, wide), BF16),
            pltpu.VMEM((2, tokens, wide), BF16),
            pltpu.VMEM((chips, tokens, wide), BF16),
            pltpu.VMEM((chips + 1, tokens, wide), BF16),
            pltpu.VMEM((2, per, units, shard), BF16),
            pltpu.SemaphoreType.DMA((3,)),
            pltpu.SemaphoreType.DMA((2,)),
            pltpu.SemaphoreType.DMA((2,)),
            pltpu.SemaphoreType.DMA((5,)),
            pltpu.SemaphoreType.DMA((chips,)),
            pltpu.SemaphoreType.DMA((chips,)),
        ]
        + [pltpu.SemaphoreType.DMA((chips - 1,)) for unused in range(4)]
        + [pltpu.SemaphoreType.DMA((2, per)), pltpu.SemaphoreType.DMA((local_experts,))]
        + [pltpu.SemaphoreType.DMA((local_experts, fsdp - 1)) for unused in range(2)],
        compiler_params=pltpu.CompilerParams(
            collective_id=collective_id, has_side_effects=True, vmem_limit_bytes=EXPERT_VMEM_BYTES
        ),
        cost_estimate=pl.CostEstimate(
            flops=flops, bytes_accessed=100_000_000, transcendentals=total * units * 2
        ),
        name="experts",
    )(
        hidden,
        grad,
        table,
        weights,
        gate.reshape(local_experts * width, units),
        up.reshape(local_experts * width, units),
        down.reshape(local_experts * units, width),
    )
    return outs[:7]


def body(
    tokens,
    grad_out,
    order,
    lengths,
    routes,
    gain_one,
    gain_two,
    w_query,
    w_key,
    w_value,
    w_out,
    w_router,
    w_gate,
    w_up,
    w_down,
):
    fsdp = lax.axis_size("fsdp")
    chips = lax.axis_size("ctx") // 2
    ctx_index = lax.axis_index("ctx")
    chip = ctx_index // 2
    core = lax.rem(ctx_index, 2)
    tok_rows = tokens.shape[1]
    width = tokens.shape[2]
    top_count = routes.shape[2]
    local_experts = w_gate.shape[0]
    expert_count = local_experts * chips * 2
    capacity = 5 * tok_rows * top_count // (4 * expert_count)
    kv_width = KVH * HEAD_SIZE
    shard = gain_one.shape[0]

    small = jnp.concatenate(
        [
            w_router,
            gain_one[:, None],
            gain_two[:, None],
            jnp.zeros((shard, LANES - expert_count - 2), BF16),
        ],
        axis=1,
    )
    qkv_shard = jnp.concatenate([w_query, w_key, w_value], axis=1)
    qkv_full, small_full, out_full, grad_all = gather(
        [qkv_shard, small, w_out], [grad_out[0]], chips - 2, fsdp, chips, 0
    )

    qkv_full, w_up, w_down = lax.optimization_barrier((qkv_full, w_up, w_down))
    up_full, down_full = (
        lax.all_gather(w_up, "fsdp", axis=1, tiled=True),
        lax.all_gather(w_down, "fsdp", axis=2, tiled=True),
    )
    router_full = small_full[:, :expert_count]
    gain_a = small_full[:, expert_count].astype(F32)
    gain_b = small_full[:, expert_count + 1].astype(F32)

    order_row = order[0]
    start_row = ctx_index * tok_rows
    order_mine = lax.dynamic_slice_in_dim(order_row, start_row, tok_rows)
    ends = jnp.cumsum(lengths[0])
    starts = ends - lengths[0]
    past = order_mine[:, None] >= ends[None, :]
    doc_start = jnp.max(jnp.where(past, ends[None, :], starts[:1]), axis=1)
    pos_mine = order_mine - doc_start
    by_chip = jnp.roll(order_row.reshape(chips, 2, tok_rows), -chip, axis=0)
    by_chip = jnp.where(core == 0, by_chip, by_chip[:, ::-1])
    order_keys = jnp.swapaxes(by_chip, 0, 1).reshape(-1)

    route_rows = routes[0]
    route_onehot = (route_rows[:, :, None] == jnp.arange(expert_count)[None, None, :]).astype(F32)
    routed = jnp.sum(route_onehot, axis=1)
    earlier = (order_mine[None, :] < order_mine[:, None]).astype(BF16)
    ranks = jnp.dot(earlier, routed.astype(BF16), preferred_element_type=F32)
    table = jnp.where(routed > 0, jnp.minimum(ranks, capacity) + 1.0, 0.0)

    half_dim = HEAD_SIZE // 2
    freqs = ROPE_BASE ** (-2.0 * jnp.arange(half_dim).astype(F32) / HEAD_SIZE)
    angles = pos_mine.astype(F32)[:, None] * freqs[None, :]
    cosine = jnp.concatenate([jnp.cos(angles), jnp.cos(angles)], axis=1)
    sine = jnp.concatenate([-jnp.sin(angles), jnp.sin(angles)], axis=1)

    inputs = tokens[0].astype(F32)
    (
        table_all,
        lse,
        gate_weights,
        weights_all,
        queries,
        hidden_one,
        kv_all,
        attended,
        middle,
        hidden_all,
        gate_full,
        grad_all,
    ) = front(
        tokens[0],
        gain_a,
        gain_b,
        small_full,
        cosine,
        sine,
        order_mine,
        pos_mine,
        order_keys,
        jnp.pad(routed, ((0, 0), (0, LANES - expert_count))),
        table.T,
        qkv_full,
        out_full,
        w_gate,
        grad_all,
        chips,
        fsdp,
        1,
    )
    kv_all = kv_all.reshape(-1, 2 * kv_width)
    gate_weights = gate_weights[:, :expert_count]
    hidden_two = hidden_all[0, 0]

    returned, out_mine, out_other, gate_local, gate_got, up_local, down_local = experts_pass(
        hidden_all,
        grad_all,
        table_all,
        weights_all,
        gate_full,
        up_full,
        down_full,
        capacity,
        expert_count,
        fsdp,
        5,
    )
    direct = gate_local.ndim == 3
    if not direct:
        gate_local = lax.psum_scatter(gate_local, "fsdp", scatter_dimension=0, tiled=True)[0]
    up_sum, down_sum = (
        lax.psum_scatter(part, "fsdp", scatter_dimension=0, tiled=True)
        for part in (up_local, down_local)
    )

    out_grad = grad_out[0].astype(F32)
    returned = returned.astype(F32)
    extra = returned[:, width:]
    gate_grad = extra[:, :expert_count] + extra[:, expert_count : 2 * expert_count]
    logit_grad = (
        gate_weights * (gate_grad - jnp.sum(gate_weights * gate_grad, axis=-1, keepdims=True))
    ).astype(BF16)
    router_local = jnp.einsum("td,te->de", hidden_two, logit_grad, preferred_element_type=F32)
    hidden_two_grad = returned[:, :width] + jnp.einsum(
        "te,de->td", logit_grad, router_full, preferred_element_type=F32
    )
    unused_two, norm_two_back = jax.vjp(rms_scale, middle, gain_b)
    middle_part, gain_two_local = norm_two_back(hidden_two_grad)
    middle_grad = out_grad + middle_part
    branch_grad = middle_grad.astype(BF16)
    out_local = jnp.einsum("tc,td->cd", attended, branch_grad, preferred_element_type=F32)
    attended_grad = jnp.einsum(
        "td,cd->tc", branch_grad, out_full, preferred_element_type=F32
    ).astype(BF16)

    def halves(local):
        local = local.astype(BF16).reshape(fsdp, 2, shard // 2, local.shape[1])
        pad = -local.shape[3] % (LANES * chips)
        return jnp.pad(local, ((0, 0), (0, 0), (0, 0), (0, pad))) if pad else local

    early_dense = chips <= 4
    query_grad, kv_grad, out_own, out_right, out_left, out_proj_sum = attention_back(
        queries,
        kv_all,
        attended,
        attended_grad,
        lse,
        order_mine,
        pos_mine,
        order_keys,
        cosine,
        sine,
        out_mine,
        out_other,
        halves(out_local),
        fsdp,
        early_dense,
        3,
    )
    pre_grad = jnp.concatenate([query_grad, kv_grad], axis=1)
    qkv_local = jnp.einsum("td,tc->dc", hidden_one, pre_grad, preferred_element_type=F32)
    hidden_one_grad = jnp.einsum("tc,dc->td", pre_grad, qkv_full, preferred_element_type=F32)
    unused_one, norm_one_back = jax.vjp(rms_scale, inputs, gain_a)
    input_part, gain_one_local = norm_one_back(hidden_one_grad)
    input_grad = (middle_grad + input_part).astype(BF16)

    span = shard * expert_count // 16
    wide = LANES * chips * -(-max(span, shard) // (LANES * chips))
    small_local = jnp.stack(
        [
            jnp.pad(
                router_local.astype(BF16).reshape(fsdp, 16, span),
                ((0, 0), (0, 0), (0, wide - span)),
            ),
            jnp.pad(
                jnp.stack(
                    [gain_one_local.reshape(fsdp, shard), gain_two_local.reshape(fsdp, shard)],
                    axis=1,
                ).astype(BF16),
                ((0, 0), (0, 14), (0, wide - shard)),
            ),
        ],
        axis=1,
    )
    *sums, out_sum = dense_reduce(
        [halves(qkv_local), small_local] + ([] if early_dense else [halves(out_local)]),
        out_own,
        out_right,
        out_left,
        DENSE_PIECE,
        fsdp,
        chips,
        4,
    )
    qkv_sum, small_sum = sums[:2]
    if not early_dense:
        out_proj_sum = sums[2]
    edge = width + 2 * kv_width
    qkv_grads = qkv_sum.reshape(shard, -1)
    out_proj_grad = out_proj_sum.reshape(shard, -1)[:, :width]
    up_grad_out, down_grad_out = (
        after(part, pre_grad)[0].astype(F32) for part in (up_sum, down_sum)
    )
    if direct:
        gate_local, gate_got = lax.optimization_barrier((gate_local, gate_got, pre_grad))[:2]
        gate_grad_out = add(gate_local, *[gate_got[j] for j in range(fsdp - 1)])
    else:
        gate_grad_out = after(gate_local, pre_grad).astype(F32)
    result = middle + out_sum
    return (
        result.astype(BF16)[None],
        input_grad[None],
        small_sum[1, 0, :shard].astype(F32),
        small_sum[1, 1, :shard].astype(F32),
        qkv_grads[:, :width].astype(F32),
        qkv_grads[:, width : width + kv_width].astype(F32),
        qkv_grads[:, width + kv_width : edge].astype(F32),
        out_proj_grad.astype(F32),
        small_sum[0, :, :span].reshape(shard, expert_count).astype(F32),
        gate_grad_out,
        up_grad_out,
        down_grad_out,
    )


def solution(mesh):
    placed = (
        P("fsdp", "ctx", None),
        P("fsdp", "ctx", None),
        P("fsdp", None),
        P("fsdp", None),
        P("fsdp", "ctx", None),
        P("fsdp"),
        P("fsdp"),
        P("fsdp", None),
        P("fsdp", None),
        P("fsdp", None),
        P("fsdp", None),
        P("fsdp", None),
        P("ctx", "fsdp", None),
        P("ctx", "fsdp", None),
        P("ctx", None, "fsdp"),
    )
    return jax.shard_map(
        body,
        mesh=mesh,
        in_specs=placed,
        out_specs=(
            P("fsdp", "ctx", None),
            P("fsdp", "ctx", None),
            P("fsdp"),
            P("fsdp"),
            P("fsdp", None),
            P("fsdp", None),
            P("fsdp", None),
            P("fsdp", None),
            P("fsdp", None),
            P("ctx", "fsdp", None),
            P("ctx", "fsdp", None),
            P("ctx", None, "fsdp"),
        ),
        check_vma=False,
    )
```

```python
import functools

import jax
import jax.numpy as jnp
from jax import lax
from jax.experimental import pallas as pl
from jax.experimental.pallas import tpu as pltpu
from jax.sharding import PartitionSpec as P

QUERY_HEADS = 12
KVH = 2
HEAD_SIZE = 128

EPSILON = 1e-06
ROPE_BASE = 10000.0
MASKED = -1e30
LOG2E = 1.4426950408889634
LANES = 128
SLOT_STEP = 64
DENSE_PIECE = 1024
LINE_TASK = 4
KEY_TILE = 512
VMEM_BYTES = 56 * 1024 * 1024
EXPERT_VMEM_BYTES = 119 * 512 * 1024
BACK_VMEM_BYTES = 61 * 1024 * 1024
FRONT_VMEM_BYTES = 50 * 1024 * 1024
DENSE_VMEM_BYTES = 40 * 1024 * 1024
MESH = pl.DeviceIdType.MESH
F32 = jnp.float32
BF16 = jnp.bfloat16


def dot(left, right, contract):
    return lax.dot_general(left, right, (contract, ((), ())), preferred_element_type=F32)


NN = ((1,), (0,))
NT = ((1,), (1,))
TN = ((0,), (0,))


def rms_scale(value_rows, gain):
    return (
        value_rows
        * lax.rsqrt(jnp.mean(value_rows * value_rows, axis=-1, keepdims=True) + EPSILON)
        * gain
    )


def place():
    ctx = lax.axis_index("ctx")
    core = lax.rem(ctx, 2)
    return ctx, lax.axis_index("fsdp"), ctx // 2, core, ctx + 1 - 2 * core


def peers_of(me, fsdp):
    peers = []
    for shift in range(1, fsdp):
        peer = me
        for bit in range(fsdp.bit_length() - 1):
            if (shift >> bit) & 1:
                digit = lax.rem(me // (1 << bit), 2)
                peer = peer + (1 << bit) - (2 << bit) * digit
        peers.append(peer)
    return peers


def greet(chips, peers, line):
    ctx, me, chip, core, sibling = place()
    barrier = pltpu.get_barrier_semaphore()
    for peer in peers:
        pl.semaphore_signal(barrier, inc=1, device_id=(ctx, peer), device_id_type=MESH)
    pl.semaphore_signal(barrier, inc=1, device_id=(sibling, me), device_id_type=MESH)
    known = len(peers) + 1
    if not line:
        pl.semaphore_wait(barrier, known)
        return
    has_right = chip + 1 < chips
    has_left = chip >= 1

    @pl.when(has_right)
    def _():
        pl.semaphore_signal(barrier, inc=1, device_id=(ctx + 2, me), device_id_type=MESH)

    @pl.when(has_left)
    def _():
        pl.semaphore_signal(barrier, inc=1, device_id=(ctx - 2, me), device_id_type=MESH)

    @pl.when(has_right & has_left)
    def _():
        pl.semaphore_wait(barrier, known + 2)

    @pl.when(jnp.logical_not(has_right & has_left))
    def _():
        pl.semaphore_wait(barrier, known + 1)


class Bounce:
    def __init__(self, src, dst, buffer, sem):
        self.inward = pltpu.make_async_copy(src, buffer, sem)
        self.outward = pltpu.make_async_copy(buffer, dst, sem)

    def start(self):
        self.inward.start()

    def turn(self):
        self.inward.wait()
        self.outward.start()

    def wait(self):
        self.outward.wait()


def remote(src, dst, send_sem, recv_sem, device):
    return pltpu.make_async_remote_copy(
        src_ref=src,
        dst_ref=dst,
        send_sem=send_sem,
        recv_sem=recv_sem,
        device_id=device,
        device_id_type=MESH,
    )


class Spread:
    def __init__(self, block, place_of, size, sems, fsdp):
        send_sem, recv_sem, on_send, on_recv = sems
        ctx, me, chip, core, sibling = place()
        self.peers = peers_of(me, fsdp)
        self.square = fsdp == 4
        near = self.peers[:2] if self.square else self.peers
        self.sends = [
            remote(block, place_of(me, 0, size), send_sem.at[j], recv_sem.at[j], (ctx, peer))
            for j, peer in enumerate(near)
        ]
        self.on, self.last = [], []
        if self.square:
            half = size // 2
            across_x, across_y, far = self.peers
            for k, (owner, target) in enumerate(((across_x, across_y), (across_y, across_x))):
                part = place_of(owner, k * half, half)
                self.on.append(remote(part, part, on_send.at[k], on_recv.at[k], (ctx, target)))
                part = place_of(far, k * half, half)
                self.last.append(remote(part, part, on_send.at[k], on_recv.at[k], (ctx, target)))

    def start(self):
        for copy in self.sends:
            copy.start()

    def hand_on(self, also=lambda j: None):
        for j, copy in enumerate(self.sends):
            copy.wait_recv()
            if self.square:
                self.on[j].start()
            also(j)

    def finish(self, also=lambda j: None):
        for copy in self.last:
            copy.wait_recv()
        if self.square:
            also(2)
        for copy in self.sends + self.on:
            copy.wait_send()


def spread_sems(fsdp):
    return [pltpu.SemaphoreType.DMA((fsdp - 1,)) for unused in range(4)]


class DenseGather:
    def __init__(self, ins, outs, sems, fsdp):
        buffers, local_sem, pass_sem, took_sem, spread_refs = sems
        ctx, me, chip, core, sibling = place()
        peers = peers_of(me, fsdp)
        self.spreads, self.passes, self.locals = [], [], []
        for i in range(len(ins)):
            rows = ins[i].shape[0]
            half = rows // 2

            def place_of(owner, begin, size, i=i, rows=rows, half=half):
                return outs[i].at[pl.ds(owner * rows + core * half + begin, size)]

            self.spreads.append(
                Spread(
                    ins[i].at[pl.ds(core * half, half)],
                    place_of,
                    half,
                    spread_refs[4 * i : 4 * i + 4],
                    fsdp,
                )
            )
            self.passes.append([])
            for j, peer in enumerate(peers):
                got = place_of(peer, 0, half)
                self.passes[i].append(
                    remote(got, got, pass_sem.at[i, j], took_sem.at[i, j], (sibling, me))
                )
            self.locals.append(
                Bounce(ins[i], outs[i].at[pl.ds(me * rows, rows)], buffers[i], local_sem.at[i])
            )

    def start(self):
        for spread in self.spreads:
            spread.start()
        for copy in self.locals:
            copy.start()

    def hand_on(self):
        for copy in self.locals:
            copy.turn()
        for i, spread in enumerate(self.spreads):
            spread.hand_on(lambda j, i=i: self.passes[i][j].start())

    def finish(self):
        for i, spread in enumerate(self.spreads):
            spread.finish(lambda j, i=i: self.passes[i][j].start())
        for passes in self.passes:
            for copy in passes:
                copy.wait()
        for copy in self.locals:
            copy.wait()


def dense_scratch(arrays, fsdp):
    count = len(arrays)
    return (
        [pltpu.VMEM(a.shape, a.dtype) for a in arrays]
        + [pltpu.SemaphoreType.DMA((count,))]
        + [pltpu.SemaphoreType.DMA((count, fsdp - 1)) for unused in range(2)]
        + spread_sems(fsdp) * count
    )


class ShardGather:
    def __init__(self, ref, out, buffer, sems, fsdp):
        ctx, me, chip, core, sibling = place()
        rows = ref.shape[1]

        def place_of(owner, begin, size):
            return out.at[:, pl.ds(owner * rows + begin, size)]

        self.spread = Spread(ref, place_of, rows, sems[1:], fsdp)
        self.own = Bounce(ref, place_of(me, 0, rows), buffer, sems[0])

    def start(self):
        self.spread.start()
        self.own.start()

    def hand_on(self):
        self.spread.hand_on()
        self.own.turn()

    def finish(self):
        self.spread.finish()
        self.own.wait()


class LineGather:
    def __init__(self, ins, outs, sems, chips):
        self.ins, self.outs, self.chips = ins, outs, chips
        self.buffers, self.sems = sems[:-7], sems[-7:]
        self.ctx, self.me, self.chip, core, self.sibling = place()
        self.count = len(ins)

    def to_right(self, i, step):
        outs, chips = self.outs, self.chips
        return remote(
            self.ins[i] if step == 0 else outs[i].at[0, chips - step],
            outs[i].at[0, chips - 1 - step],
            self.sems[1].at[i, step],
            self.sems[2].at[i, step],
            (self.ctx + 2, self.me),
        )

    def to_left(self, i, step):
        outs = self.outs
        return remote(
            self.ins[i] if step == 0 else outs[i].at[0, step],
            outs[i].at[0, step + 1],
            self.sems[3].at[i, step],
            self.sems[4].at[i, step],
            (self.ctx - 2, self.me),
        )

    def across(self, i, slot):
        return remote(
            self.ins[i] if slot == 0 else self.outs[i].at[0, slot],
            self.outs[i].at[1, slot],
            self.sems[5].at[i, slot],
            self.sems[6].at[i, slot],
            (self.sibling, self.me),
        )

    def local(self, i):
        return Bounce(self.ins[i], self.outs[i].at[0, 0], self.buffers[i], self.sems[0].at[i])

    def send(self, step):
        chip, chips, count = self.chip, self.chips, self.count

        @pl.when((chip + 1 < chips) & (chip >= step))
        def _():
            for i in range(count):
                self.to_right(i, step).start()

        @pl.when((chip >= 1) & (chip + step < chips))
        def _():
            for i in range(count):
                self.to_left(i, step).start()

    def receive(self, step):
        chip, chips, count = self.chip, self.chips, self.count

        @pl.when(chip >= step + 1)
        def _():
            for i in range(count):
                self.to_right(i, step).wait_recv()
                self.across(i, chips - 1 - step).start()

        @pl.when(chip + step + 1 < chips)
        def _():
            for i in range(count):
                self.to_left(i, step).wait_recv()
                self.across(i, step + 1).start()

    def own(self):
        for i in range(self.count):
            self.across(i, 0).start()
            self.local(i).start()

    def turn_own(self):
        for i in range(self.count):
            self.local(i).turn()

    def finish_own(self):
        for i in range(self.count):
            self.across(i, 0).wait()
            self.local(i).wait()

    def arrived(self, slot):
        for i in range(self.count):
            remote(
                self.outs[i].at[0, slot],
                self.outs[i].at[1, slot],
                self.sems[5].at[i, slot],
                self.sems[6].at[i, slot],
                (self.sibling, self.me),
            ).wait_recv()

    def sent(self):
        chip, chips, count = self.chip, self.chips, self.count
        for step in range(chips - 1):

            @pl.when((chip + 1 < chips) & (chip >= step))
            def _():
                for i in range(count):
                    self.to_right(i, step).wait_send()

            @pl.when((chip >= 1) & (chip + step < chips))
            def _():
                for i in range(count):
                    self.to_left(i, step).wait_send()

        for slot in range(chips):
            for i in range(count):
                self.across(i, slot).wait_send()

    def finish(self, step):
        chip, chips, count = self.chip, self.chips, self.count

        @pl.when((chip + 1 < chips) & (chip >= step))
        def _():
            for i in range(count):
                self.to_right(i, step).wait_send()

        @pl.when((chip >= 1) & (chip + step < chips))
        def _():
            for i in range(count):
                self.to_left(i, step).wait_send()

        @pl.when(chip >= step + 1)
        def _():
            for i in range(count):
                self.across(i, chips - 1 - step).wait()

        @pl.when(chip + step + 1 < chips)
        def _():
            for i in range(count):
                self.across(i, step + 1).wait()


def line_scratch(arrays, chips):
    count = len(arrays)
    return (
        [pltpu.VMEM(a.shape, a.dtype) for a in arrays if a is not None]
        + [pltpu.SemaphoreType.DMA((count,))]
        + [pltpu.SemaphoreType.DMA((count, chips - 1)) for unused in range(4)]
        + [pltpu.SemaphoreType.DMA((count, chips)) for unused in range(2)]
    )


def gather_kernel(dense, line, merged, steps, fsdp, chips, *refs):
    count = dense + line
    ins, refs = refs[:count], refs[count:]
    outs, scratch = list(refs[: count - merged + 1]), refs[count - merged + 1 :]
    columns, start = [], 0
    for ref in ins[:merged]:
        columns.append(outs[0].at[:, pl.ds(start, ref.shape[1])])
        start += ref.shape[1]
    outs = columns + outs[1:]
    ctx, me, chip, core, sibling = place()
    greet(chips, peers_of(me, fsdp) if dense else [], line > 0)
    if dense:
        own, scratch = scratch[: 5 * dense + 3], scratch[5 * dense + 3 :]
        first = DenseGather(
            ins[:dense],
            outs[:dense],
            (own[:dense],) + tuple(own[dense : dense + 3]) + (own[dense + 3 :],),
            fsdp,
        )
        first.start()
    if line:
        own, scratch = scratch[: line + 7], scratch[line + 7 :]
        second = LineGather(ins[dense:], outs[dense:], own, chips)
        for step in range(steps):
            second.send(step)
            if step == 0:
                second.own()
            if step == steps - 1 and dense:
                first.hand_on()
            second.receive(step)
            if step == 0:
                second.turn_own()
    if dense:
        first.finish()
    if line:
        second.finish_own()
        for step in range(steps):
            second.finish(step)


def gather(dense, merged, line, steps, fsdp, chips, collective_id):
    arrays = list(dense) + list(line)
    joined = sum(a.shape[1] for a in dense[:merged])
    shapes = [(fsdp * dense[0].shape[0], joined)]
    shapes += [(fsdp * a.shape[0],) + a.shape[1:] for a in dense[merged:]]
    shapes += [(2, chips) + a.shape for a in line]
    return pl.pallas_call(
        functools.partial(gather_kernel, len(dense), len(line), merged, steps, fsdp, chips),
        out_shape=[jax.ShapeDtypeStruct(shape, BF16) for shape in shapes],
        in_specs=[pl.BlockSpec(memory_space=pl.ANY)] * len(arrays),
        out_specs=[pl.BlockSpec(memory_space=pl.ANY)] * len(shapes),
        scratch_shapes=dense_scratch(dense, fsdp) + line_scratch(line, chips),
        compiler_params=pltpu.CompilerParams(
            collective_id=collective_id, has_side_effects=True, vmem_limit_bytes=VMEM_BYTES
        ),
        name="gather",
    )(*arrays)


def add(*parts):
    total = parts[0].astype(F32)
    for part in parts[1:]:
        total = total + part.astype(F32)
    return total


def add_into(target, parts):
    rows = target.shape[0]
    tile = 32 if rows % 32 == 0 else 16

    def some(t, carry):
        part = pl.ds(pl.multiple_of(t * tile, tile), tile)
        target[part, :] = add(*[ref[part, :] for ref in parts]).astype(target.dtype)
        return carry

    lax.fori_loop(0, rows // tile, some, 0)


class LineSum:
    def __init__(self, chips, held, keep, got, sems):
        self.chips, self.held, self.keep, self.got = chips, held, keep, got
        self.sems = sems
        self.ctx, self.me, self.chip, core, sibling = place()

    def right(self, step):
        return remote(
            self.keep(self.chips - 1 - step),
            self.got.at[step - self.chip],
            self.sems[0].at[step],
            self.sems[1].at[step],
            (self.ctx + 2, self.me),
        )

    def from_left(self, step):
        slot = step + 1 - self.chip
        pltpu.make_async_remote_copy(
            src_ref=self.keep(self.chips - 1 - step),
            dst_ref=self.got.at[slot],
            send_sem=self.sems[0].at[step],
            recv_sem=self.sems[1].at[step],
            device_id=(self.ctx - 2, self.me),
            device_id_type=MESH,
        ).wait_recv()
        return self.got.at[slot]

    def from_right(self, step):
        slot = step + 2
        self.left(step).wait_recv()
        return self.got.at[slot]

    def left(self, step):
        return remote(
            self.keep(step + 1),
            self.got.at[step + 2],
            self.sems[2].at[step],
            self.sems[3].at[step],
            (self.ctx - 2, self.me),
        )

    def step(self, step):
        chip, chips = self.chip, self.chips
        far_right, far_left = chips - 1 - step, step + 1

        @pl.when(chip <= step)
        def _():
            parts = self.held(far_right)
            if step == 0:
                add_into(self.keep(far_right), parts())
            else:

                @pl.when(chip == 0)
                def _():
                    add_into(self.keep(far_right), parts())

                @pl.when(chip >= 1)
                def _():
                    add_into(self.keep(far_right), [self.from_left(step - 1)] + parts())

            self.right(step).start()

        @pl.when(chip >= chips - 1 - step)
        def _():
            parts = self.held(far_left)
            if step == 0:
                add_into(self.keep(far_left), parts())
            else:

                @pl.when(chip == chips - 1)
                def _():
                    add_into(self.keep(far_left), parts())

                @pl.when(chip < chips - 1)
                def _():
                    add_into(self.keep(far_left), [self.from_right(step - 1)] + parts())

            self.left(step).start()

    def total(self, target):
        chip, chips, last = self.chip, self.chips, self.chips - 2
        parts = self.held(0)

        @pl.when(chip == 0)
        def _():
            add_into(target, [self.from_right(last)] + parts())

        @pl.when(chip == chips - 1)
        def _():
            add_into(target, [self.from_left(last)] + parts())

        @pl.when((chip >= 1) & (chip < chips - 1))
        def _():
            add_into(target, [self.from_right(last), self.from_left(last)] + parts())

    def finish(self, steps=None):
        for step in range(self.chips - 1 if steps is None else steps):

            @pl.when(self.chip <= step)
            def _():
                self.right(step).wait_send()

            @pl.when(self.chip >= self.chips - 1 - step)
            def _():
                self.left(step).wait_send()


DENSE_BUFFERS = 5
DENSE_SEMS = 14


class DenseSum:
    def __init__(self, local, held, out, buffers, sems, fsdp, chips):
        self.local, self.held, self.out = local, held, out
        self.pair, self.cross, self.sums, got, self.spread = buffers
        self.sems = sems
        self.chips = chips
        self.ctx, self.me, self.chip, self.core, self.sibling = place()
        self.owners = peers_of(self.me, fsdp) + [self.me]
        self.cut = out.shape[2] // chips
        self.line = LineSum(
            chips,
            lambda r: lambda: [self.keep_ref(r)],
            lambda r: self.keep_ref(r),
            got,
            sems[4:8],
        )

    def keep_ref(self, r):
        return self.sums.at[:, self.columns(r)]

    def columns(self, r):
        owner = lax.rem(self.chip + r, self.chips)
        return pl.ds(pl.multiple_of(owner * self.cut, LANES), self.cut)

    def swap(self, j):
        return remote(
            self.local.at[self.owners[j], 1 - self.core],
            self.pair.at[j],
            self.sems[0].at[j],
            self.sems[1].at[j],
            (self.sibling, self.me),
        )

    def crossing(self, j):
        return remote(
            self.pair.at[j],
            self.cross.at[j],
            self.sems[2].at[j],
            self.sems[3].at[j],
            (self.ctx, self.owners[j]),
        )

    def to_right(self, step):
        return remote(
            self.spread.at[0, (self.chips - step) % self.chips],
            self.spread.at[0, self.chips - 1 - step],
            self.sems[8].at[step],
            self.sems[9].at[step],
            (self.ctx + 2, self.me),
        )

    def to_left(self, step):
        return remote(
            self.spread.at[0, step],
            self.spread.at[0, step + 1],
            self.sems[10].at[step],
            self.sems[11].at[step],
            (self.ctx - 2, self.me),
        )

    def across(self, slot):
        return remote(
            self.spread.at[0, slot],
            self.spread.at[1, slot],
            self.sems[12].at[slot],
            self.sems[13].at[slot],
            (self.sibling, self.me),
        )

    def start(self):
        for j in range(len(self.owners)):
            self.swap(j).start()

    def cross_over(self):
        for j, owner in enumerate(self.owners):
            self.swap(j).wait_recv()
            add_into(self.pair.at[j], [self.held(j, owner), self.pair.at[j]])
            if j < len(self.owners) - 1:
                self.crossing(j).start()

    def stages(self):
        chip, chips = self.chip, self.chips

        def open_up():
            for j in range(len(self.owners) - 1):
                self.crossing(j).wait_recv()
            add_into(
                self.sums,
                [self.cross.at[j] for j in range(len(self.owners) - 1)]
                + [self.pair.at[len(self.owners) - 1]],
            )
            self.line.step(0)

        def summed():
            self.line.total(self.spread.at[0, 0])
            hand_on(0)

        def hand_on(step):
            @pl.when((chip + 1 < chips) & (chip >= step))
            def _():
                self.to_right(step).start()

            @pl.when((chip >= 1) & (chip + step < chips))
            def _():
                self.to_left(step).start()

            if step == 0:
                self.across(0).start()

        def take(step):
            @pl.when(chip >= step + 1)
            def _():
                self.to_right(step).wait_recv()
                self.across(chips - 1 - step).start()

            @pl.when(chip + step + 1 < chips)
            def _():
                self.to_left(step).wait_recv()
                self.across(step + 1).start()

        def pass_on(step):
            def run():
                take(step - 1)
                hand_on(step)

            return run

        def line_step(step):
            return lambda: self.line.step(step)

        return (
            [open_up]
            + [line_step(step) for step in range(1, chips - 1)]
            + [summed]
            + [pass_on(step) for step in range(1, chips - 1)]
            + [lambda: take(chips - 2)]
        )

    def finish(self):
        chip, chips = self.chip, self.chips
        for r in range(chips):
            self.out[self.core, :, self.columns(r)] = self.spread[0, r]
        for r in range(chips):
            self.across(r).wait()
            self.out[1 - self.core, :, self.columns(r)] = self.spread[1, r]
        for step in range(chips - 1):

            @pl.when((chip + 1 < chips) & (chip >= step))
            def _():
                self.to_right(step).wait_send()

            @pl.when((chip >= 1) & (chip + step < chips))
            def _():
                self.to_left(step).wait_send()

        self.line.finish()
        for j in range(len(self.owners) - 1):
            self.crossing(j).wait_send()
        for j in range(len(self.owners)):
            self.swap(j).wait_send()


def dense_reduce_kernel(fsdp, chips, cuts, *refs):
    count = len(cuts)
    arrays = max(cut[0] for cut in cuts) + 1
    ins, refs = refs[:arrays], refs[arrays:]
    own_ref, right_ref, left_ref, pre_ref, tokens_ref, middle_ref, gain_ref, qkv_ref = refs[:8]
    refs = refs[8:]
    outs, total_ref, input_ref, refs = (
        refs[:arrays],
        refs[arrays],
        refs[arrays + 1],
        refs[arrays + 2 :],
    )
    from_left, from_right, r_send, r_recv, l_send, l_recv, small_v, qkv_v, qkv_sem = refs[:9]
    rest = refs[9:]
    qkv_load = pltpu.make_async_copy(qkv_ref, qkv_v, qkv_sem)
    qkv_load.start()
    ctx, me, chip, core, sibling = place()
    greet(chips, peers_of(me, fsdp), True)

    to_right = remote(right_ref, from_left, r_send, r_recv, (ctx + 2, me))
    to_left = remote(left_ref, from_right, l_send, l_recv, (ctx - 2, me))

    @pl.when(chip + 1 < chips)
    def _():
        to_right.start()

    @pl.when(chip >= 1)
    def _():
        to_left.start()

    sums = []
    for i, (which, start, size) in enumerate(cuts):
        buffers = rest[i * DENSE_BUFFERS : (i + 1) * DENSE_BUFFERS]
        sems = rest[count * DENSE_BUFFERS + i * DENSE_SEMS :][:DENSE_SEMS]
        local = (small_v if which == 1 else ins[which]).at[:, :, :, pl.ds(start, size)]
        sums.append(
            DenseSum(
                local,
                lambda j, owner, local=local: local.at[owner, core],
                outs[which].at[:, :, pl.ds(start, size)],
                buffers,
                sems,
                fsdp,
                chips,
            )
        )
    large = [one for one, cut in zip(sums, cuts) if cut[0] != 1]
    small = [one for one, cut in zip(sums, cuts) if cut[0] == 1]
    for one in large:
        one.start()
    for one in large:
        one.cross_over()

    rows, width = tokens_ref.shape
    qkv_load.wait()
    gain_grad = jnp.zeros((1, width), F32)
    for part in (pl.ds(0, rows // 2), pl.ds(rows // 2, rows // 2)):
        grad = dot(pre_ref[part, :], qkv_v[...], NT)
        value = tokens_ref[part, :].astype(F32)
        scale = lax.rsqrt(jnp.mean(value * value, axis=-1, keepdims=True) + EPSILON)
        unit = value * scale
        scaled = grad * gain_ref[...]
        slope = jnp.mean(scaled * unit, axis=-1, keepdims=True)
        input_ref[part, :] = (middle_ref[part, :] + scale * (scaled - unit * slope)).astype(BF16)
        gain_grad = gain_grad + jnp.sum(grad * unit, axis=0, keepdims=True)
    small_v[...] = ins[1][...]
    shard = width // fsdp
    first_row = lax.broadcasted_iota(jnp.int32, (small_v.shape[2], shard), 0) == 0
    for f in range(fsdp):
        held = small_v[f, 1, :, :shard].astype(F32)
        mine = jnp.broadcast_to(gain_grad[:, f * shard : (f + 1) * shard], held.shape)
        small_v[f, 1, :, :shard] = jnp.where(first_row, mine, held).astype(BF16)
    for one in small:
        one.start()
    for one in small:
        one.cross_over()

    stages = [one.stages() for one in sums]
    lag = chips - 1
    offsets = []
    for which, start, size in cuts:
        turn = sum(1 for other in cuts[: len(offsets)] if other[0] != 1)
        offsets.append(lag * (max(0, turn - 1) if which == 1 else turn))
    for tick in range(len(stages[0]) + max(offsets)):
        for i in range(count):
            if 0 <= tick - offsets[i] < len(stages[i]):
                stages[i][tick - offsets[i]]()
    @pl.when(chip >= 1)
    def _():
        to_right.wait_recv()

    @pl.when(chip + 1 < chips)
    def _():
        to_left.wait_recv()

    @pl.when(chip == 0)
    def _():
        add_into(total_ref, [from_right, own_ref])

    @pl.when(chip == chips - 1)
    def _():
        add_into(total_ref, [from_left, own_ref])

    @pl.when((chip >= 1) & (chip + 1 < chips))
    def _():
        add_into(total_ref, [from_left, from_right, own_ref])

    for one in sums:
        one.finish()

    @pl.when(chip + 1 < chips)
    def _():
        to_right.wait_send()

    @pl.when(chip >= 1)
    def _():
        to_left.wait_send()


def dense_buffers(rows, size, fsdp, chips):
    cut = size // chips
    return [
        pltpu.VMEM((fsdp, rows, size), BF16),
        pltpu.VMEM((fsdp - 1, rows, size), BF16),
        pltpu.VMEM((rows, size), BF16),
        pltpu.VMEM((chips + 1, rows, cut), BF16),
        pltpu.VMEM((2, chips, rows, cut), BF16),
    ]


def dense_sems(fsdp, chips):
    return (
        [pltpu.SemaphoreType.DMA((fsdp,)) for unused in range(2)]
        + [pltpu.SemaphoreType.DMA((fsdp - 1,)) for unused in range(2)]
        + [pltpu.SemaphoreType.DMA((chips - 1,)) for unused in range(8)]
        + [pltpu.SemaphoreType.DMA((chips,)) for unused in range(2)]
    )


def dense_reduce(
    arrays,
    own,
    right,
    left,
    pre_grad,
    tokens,
    middle_grad,
    gain,
    qkv,
    piece,
    fsdp,
    chips,
    collective_id,
):
    vmem = pl.BlockSpec(memory_space=pltpu.VMEM)
    cuts, buffers = [], []
    for i, a in enumerate(arrays):
        rows, width = a.shape[2:]
        for start in range(0, width, piece):
            size = min(piece, width - start)
            cuts.append((i, start, size))
            buffers += dense_buffers(rows, size, fsdp, chips)
    sems = dense_sems(fsdp, chips)
    anywhere = pl.BlockSpec(memory_space=pl.ANY)
    return pl.pallas_call(
        functools.partial(dense_reduce_kernel, fsdp, chips, tuple(cuts)),
        out_shape=[jax.ShapeDtypeStruct(a.shape[1:], BF16) for a in arrays]
        + [jax.ShapeDtypeStruct(own.shape, F32), jax.ShapeDtypeStruct(tokens.shape, BF16)],
        in_specs=[vmem] * len(arrays)
        + [vmem, anywhere, anywhere, vmem, vmem, vmem, vmem, anywhere],
        out_specs=[vmem] * (len(arrays) + 2),
        scratch_shapes=[pltpu.VMEM(own.shape, BF16)] * 2
        + [pltpu.SemaphoreType.DMA] * 4
        + [
            pltpu.VMEM(arrays[1].shape, BF16),
            pltpu.VMEM(qkv.shape, BF16),
            pltpu.SemaphoreType.DMA,
        ]
        + buffers
        + sems * len(cuts),
        compiler_params=pltpu.CompilerParams(
            collective_id=collective_id, has_side_effects=True, vmem_limit_bytes=DENSE_VMEM_BYTES
        ),
        name="dense_reduce",
    )(*arrays, own, right, left, pre_grad, tokens, middle_grad, gain[None, :], qkv)


def after(value, *others):
    return lax.optimization_barrier((value,) + others)[0]


def chunk_order(chip, i, chips):
    right_half = lax.div(2 * chip, chips)
    near = chip + right_half * (chips - 1 - 2 * chip)
    alone = chips - 1 - 2 * near
    paired = lax.div(i - alone + chips, chips)
    turn = (i - alone) * paired
    odd = lax.rem(turn, 2)
    pair = lax.div(turn, 2)
    distance = (1 - paired) * (chips - 1 - near - i) + paired * (
        (1 - odd) * (near - pair) + odd * (chips - near + pair)
    )
    return lax.rem(distance + right_half * (chips - 2 * distance), chips)


def front_kernel(
    scale,
    chips,
    fsdp,
    expert_count,
    tokens_ref,
    gain_a_ref,
    gain_b_ref,
    small_ref,
    cos_ref,
    sin_ref,
    oq_ref,
    pq_ref,
    ok_ref,
    routed_ref,
    table_ref,
    qkv_ref,
    wo_ref,
    gate_w_ref,
    passed_ref,
    table_all_ref,
    lse_ref,
    gate_ref,
    weights_ref,
    q_hbm,
    normed_hbm,
    kv_hbm,
    attended_hbm,
    middle_hbm,
    hidden_hbm,
    hidden_all_ref,
    gate_full_ref,
    grad_ref,
    q_ref,
    normed_ref,
    kv_ref,
    attended_ref,
    middle_ref,
    qkv_v,
    wo_v,
    gate_v,
    hidden_v,
    bias,
    top,
    total,
    acc,
    load_sem,
    own_sem,
    gate_own,
    gate_s0,
    gate_s1,
    gate_s2,
    gate_s3,
    keep_sem,
    *line_sems,
):
    ctx, me, chip, core, sibling = place()
    rows = tokens_ref.shape[0]
    width = tokens_ref.shape[1]
    half = rows // 2
    kv_width = KVH * HEAD_SIZE
    per_group = QUERY_HEADS // KVH
    parts = [pl.ds(0, half), pl.ds(half, half)]
    loads = [
        pltpu.make_async_copy(src, dst, load_sem.at[k])
        for k, (src, dst) in enumerate(((qkv_ref, qkv_v), (wo_ref, wo_v)))
    ]
    for copy in loads:
        copy.start()
    greet(chips, peers_of(me, fsdp), True)
    gate_gather = ShardGather(
        gate_w_ref,
        gate_full_ref,
        gate_v,
        (gate_own, gate_s0, gate_s1, gate_s2, gate_s3),
        fsdp,
    )
    gate_gather.start()
    kv_line = LineGather(
        [kv_ref.at[0, 0], table_all_ref.at[0, 0]], [kv_ref, table_all_ref], line_sems[:7], chips
    )
    grad_line = LineGather([None], [grad_ref], line_sems[7:14], chips)
    hidden_lines = [
        LineGather(
            [hidden_v.at[parts[0]]], [hidden_all_ref.at[:, :, parts[0]]], line_sems[14:21], chips
        ),
        LineGather(
            [hidden_v.at[parts[1]], weights_ref.at[0, 0]],
            [hidden_all_ref.at[:, :, parts[1]], weights_ref],
            line_sems[21:28],
            chips,
        ),
    ]

    def normed(value, gain):
        return value * lax.rsqrt(jnp.mean(value * value, axis=-1, keepdims=True) + EPSILON) * gain

    table_all_ref[0, 0] = table_ref[...]
    for part in parts:
        normed_ref[part, :] = normed(
            tokens_ref[part, :].astype(F32), gain_a_ref[...]
        ).astype(BF16)
    loads[0].wait()
    for part in parts:
        rows_one = normed_ref[part, :]
        cosine, sine = cos_ref[part, :], sin_ref[part, :]
        for h in range(KVH):
            columns = slice(width + h * HEAD_SIZE, width + (h + 1) * HEAD_SIZE)
            value = dot(rows_one, qkv_v[:, columns], NN)
            value = value * cosine + pltpu.roll(value, HEAD_SIZE // 2, 1) * sine
            kv_ref[0, 0, part, h * HEAD_SIZE : (h + 1) * HEAD_SIZE] = value.astype(BF16)
        kv_ref[0, 0, part, kv_width:] = dot(
            rows_one, qkv_v[:, width + kv_width :], NN
        ).astype(BF16)
    kv_line.send(0)
    for i in range(2):
        kv_line.across(i, 0).start()
    for part in parts:
        rows_one = normed_ref[part, :]
        cosine, sine = cos_ref[part, :], sin_ref[part, :]
        for h in range(0, QUERY_HEADS, 2):
            pre = dot(rows_one, qkv_v[:, h * HEAD_SIZE : (h + 2) * HEAD_SIZE], NN)
            for k in range(2):
                value = pre[:, k * HEAD_SIZE : (k + 1) * HEAD_SIZE]
                value = value * cosine + pltpu.roll(value, HEAD_SIZE // 2, 1) * sine
                q_ref[part, (h + k) * HEAD_SIZE : (h + k + 1) * HEAD_SIZE] = value.astype(BF16)

    def turn(index, r):
        part = parts[index]
        for q in range(2):
            gap = oq_ref[part, :] - ok_ref[q * chips + r]
            bias[:, q * rows : (q + 1) * rows] = jnp.where(
                (gap >= 0) & (gap <= pq_ref[part, :]), 0.0, MASKED
            )

        def one(h, carry):
            group = lax.div(h, per_group)
            columns = pl.ds(pl.multiple_of(h * HEAD_SIZE, HEAD_SIZE), HEAD_SIZE)
            key_columns = pl.ds(pl.multiple_of(group * HEAD_SIZE, HEAD_SIZE), HEAD_SIZE)
            value_columns = pl.ds(
                pl.multiple_of(kv_width + group * HEAD_SIZE, HEAD_SIZE), HEAD_SIZE
            )
            query = q_ref[part, columns]
            scores = []
            peak = top[h, part, :]
            for q in range(2):
                raw = dot(query, kv_ref[q, r, :, key_columns], NT) * (scale * LOG2E)
                raw = raw + bias[:, q * rows : (q + 1) * rows]
                scores.append(raw)
            best = scores[0][:, :LANES]
            for q in range(2):
                for k in range(rows // LANES):
                    best = jnp.maximum(best, scores[q][:, k * LANES : (k + 1) * LANES])
            new = jnp.maximum(peak, jnp.max(best, axis=1, keepdims=True))
            fade = jnp.exp2(peak - new)
            wide = jnp.concatenate([new] * (rows // LANES), axis=1)
            mass = total[h] * fade
            out = acc[:, columns] * fade
            for q in range(2):
                probs = jnp.exp2(scores[q] - wide)
                for k in range(rows // LANES):
                    mass = mass + probs[:, k * LANES : (k + 1) * LANES]
                out = out + dot(probs.astype(BF16), kv_ref[q, r, :, value_columns], NN)
            top[h, part, :] = new
            total[h] = mass
            acc[:, columns] = out
            return carry

        lax.fori_loop(0, QUERY_HEADS, one, 0)

    def begin(index):
        top[:, parts[index], :] = jnp.full((QUERY_HEADS, half, LANES), MASKED, F32)
        total[...] = jnp.zeros_like(total)
        acc[...] = jnp.zeros_like(acc)

    def end(index):
        part = parts[index]
        for h in range(QUERY_HEADS):
            columns = slice(h * HEAD_SIZE, (h + 1) * HEAD_SIZE)
            mass = jnp.sum(total[h], axis=1, keepdims=True)
            attended_ref[part, columns] = (acc[:, columns] / mass).astype(BF16)
            top[h, part, :] = top[h, part, :] + jnp.log2(mass)
        if index == 0:
            loads[1].wait()
        middle = tokens_ref[part, :].astype(F32) + dot(attended_ref[part, :], wo_v[...], NN)
        middle_ref[part, :] = middle
        rows_two = normed(middle, gain_b_ref[...]).astype(BF16)
        hidden_v[part, :] = rows_two
        routed = routed_ref[part, :] > 0.0
        logits = jnp.where(routed, dot(rows_two, small_ref[...], NN), MASKED)
        power = jnp.exp(logits - jnp.max(logits, axis=1, keepdims=True))
        power = jnp.where(routed, power, 0.0)
        gate_ref[part, :] = power / jnp.sum(power, axis=1, keepdims=True)
        if index == 1:
            weights_ref[0, 0] = gate_ref[...].T[:expert_count, :]
        line = hidden_lines[index]
        line.send(0)
        for i in range(line.count):
            line.across(i, 0).start()
        own(index).start()

    def keep(k, src, dst):
        return pltpu.make_async_copy(src, dst, keep_sem.at[k])

    def own(index):
        return pltpu.make_async_copy(
            hidden_v.at[parts[index]],
            hidden_all_ref.at[0, 0, parts[index]],
            own_sem.at[index],
        )

    begin(0)
    keep(0, q_ref, q_hbm).start()
    keep(1, normed_ref, normed_hbm).start()

    def first_turn(t, carry):
        for k in range(1, chips):

            @pl.when(t == k)
            def _():
                kv_line.receive(k - 1)
                if k < chips - 1:
                    kv_line.send(k)
                else:
                    grad_line.send(chips - 2)

        r = chunk_order(chip, chips - 1 - t, chips)
        kv_line.arrived(r)
        turn(0, r)
        return carry

    lax.fori_loop(0, chips, first_turn, 0)
    end(0)
    begin(1)
    gate_gather.hand_on()
    keep(2, kv_ref, kv_hbm).start()
    early = [step for step in range(chips - 1) if 2 * step + 2 < chips]

    def second_turn(t, carry):
        for step in early:

            @pl.when(t == 2 * step + 2)
            def _():
                hidden_lines[0].receive(step)
                if step + 1 < chips - 1:
                    hidden_lines[0].send(step + 1)

        turn(1, t)
        return carry

    lax.fori_loop(0, chips, second_turn, 0)
    grad_line.receive(chips - 2)
    late = [step for step in range(chips - 1) if step not in early]
    for step in late[:1]:
        hidden_lines[0].receive(step)
        if step + 1 < chips - 1:
            hidden_lines[0].send(step + 1)
    end(1)
    keep(3, attended_ref, attended_hbm).start()
    keep(4, middle_ref, middle_hbm).start()
    keep(5, hidden_v, hidden_hbm).start()
    for h in range(QUERY_HEADS):
        lse_ref[h] = top[h].T[:1, :]
    for step in late[1:]:
        hidden_lines[0].receive(step)
        if step + 1 < chips - 1:
            hidden_lines[0].send(step + 1)
    for step in range(chips - 1):
        hidden_lines[1].receive(step)
        if step + 1 < chips - 1:
            hidden_lines[1].send(step + 1)
    for line in hidden_lines:
        for slot in range(chips):
            line.arrived(slot)
        line.sent()
    kv_line.sent()
    gate_gather.finish()
    grad_line.finish(chips - 2)
    for index in range(2):
        own(index).wait()
    for k, (src, dst) in enumerate(
        (
            (q_ref, q_hbm),
            (normed_ref, normed_hbm),
            (kv_ref, kv_hbm),
            (attended_ref, attended_hbm),
            (middle_ref, middle_hbm),
            (hidden_v, hidden_hbm),
        )
    ):
        keep(k, src, dst).wait()


def front(
    tokens,
    gain_a,
    gain_b,
    small,
    cosine,
    sine,
    order_mine,
    pos_mine,
    order_keys,
    routed,
    table,
    qkv,
    w_out,
    w_gate,
    grad_all,
    chips,
    fsdp,
    collective_id,
):
    rows, width = tokens.shape
    expert_count = table.shape[0]
    kv_width = KVH * HEAD_SIZE
    vmem = pl.BlockSpec(memory_space=pltpu.VMEM)
    anywhere = pl.BlockSpec(memory_space=pl.ANY)
    shapes = [
        ((2, chips, expert_count, rows), F32),
        ((QUERY_HEADS, 1, rows), F32),
        ((rows, LANES), F32),
        ((2, chips, expert_count, rows), F32),
    ]
    kept = [
        ((rows, width), BF16),
        ((rows, width), BF16),
        ((2, chips, rows, 2 * kv_width), BF16),
        ((rows, width), BF16),
        ((rows, width), F32),
    ]
    gathered = [
        ((rows, width), BF16),
        ((2, chips, rows, width), BF16),
        ((w_gate.shape[0], width, w_gate.shape[2]), BF16),
        (grad_all.shape, BF16),
    ]
    flops = 4 * rows * (2 * chips * rows) * width + 2 * rows * width * (2 * width + 2 * kv_width)
    return pl.pallas_call(
        functools.partial(front_kernel, HEAD_SIZE ** (-0.5), chips, fsdp, expert_count),
        out_shape=[
            jax.ShapeDtypeStruct(shape, kind) for shape, kind in shapes + kept + gathered
        ],
        in_specs=[vmem] * 11 + [anywhere] * 4,
        out_specs=[vmem] * 4 + [anywhere] * 9,
        scratch_shapes=[pltpu.VMEM(shape, kind) for shape, kind in kept]
        + [
            pltpu.VMEM(qkv.shape, BF16),
            pltpu.VMEM(w_out.shape, BF16),
            pltpu.VMEM(w_gate.shape, BF16),
            pltpu.VMEM((rows, width), BF16),
            pltpu.VMEM((rows // 2, 2 * rows), F32),
            pltpu.VMEM((QUERY_HEADS, rows, LANES), F32),
            pltpu.VMEM((QUERY_HEADS, rows // 2, LANES), F32),
            pltpu.VMEM((rows // 2, width), F32),
            pltpu.SemaphoreType.DMA((2,)),
            pltpu.SemaphoreType.DMA((2,)),
            pltpu.SemaphoreType.DMA,
        ]
        + spread_sems(fsdp)
        + [pltpu.SemaphoreType.DMA((6,))]
        + line_scratch([None] * 2, chips)
        + line_scratch([None], chips)
        + line_scratch([None], chips)
        + line_scratch([None] * 2, chips),
        input_output_aliases={14: 12},
        compiler_params=pltpu.CompilerParams(
            collective_id=collective_id, has_side_effects=True, vmem_limit_bytes=FRONT_VMEM_BYTES
        ),
        cost_estimate=pl.CostEstimate(
            flops=flops, bytes_accessed=40_000_000, transcendentals=rows * rows * chips * 24
        ),
        name="front",
    )(
        tokens,
        gain_a[None, :],
        gain_b[None, :],
        small,
        cosine,
        sine,
        order_mine[:, None],
        pos_mine[:, None],
        order_keys.reshape(2 * chips, 1, rows),
        routed,
        table,
        qkv,
        w_out,
        w_gate,
        grad_all,
    )


def attention_back_kernel(
    scale,
    chips,
    fsdp,
    early_dense,
    q_ref,
    k_ref,
    v_ref,
    o_ref,
    do_ref,
    lse_ref,
    oq_ref,
    pq_ref,
    ok_ref,
    cos_ref,
    sin_ref,
    rows_ref,
    dense_ref,
    dq_ref,
    kv_ref,
    own_ref,
    right_ref,
    left_ref,
    dense_out_ref,
    bias,
    dk_acc,
    dv_acc,
    kv_total,
    mine_v,
    pair,
    got,
    kv_v,
    kv_pair,
    kv_got,
    load_sem,
    store_sem,
    swap_send,
    swap_recv,
    r_send,
    r_recv,
    l_send,
    l_recv,
    kv_swap_send,
    kv_swap_recv,
    kr_send,
    kr_recv,
    kl_send,
    kl_recv,
    *dense_refs,
):
    ctx, me, chip, core, sibling = place()
    keys = k_ref.shape[0]
    tiles = keys // KEY_TILE
    rows = q_ref.shape[0]
    per_group = QUERY_HEADS // KVH
    head = pl.program_id(0)

    order = []
    for step in range(chips - 1):
        for r in (chips - 1 - step, step + 1):
            if r not in order:
                order.append(r)
    order.append(0)
    swaps = [
        remote(rows_ref.at[1, r], pair.at[r], swap_send.at[r], swap_recv.at[r], (sibling, me))
        for r in range(chips)
    ]
    slots = mine_v.shape[0]
    loads = [
        pltpu.make_async_copy(rows_ref.at[0, r], mine_v.at[j % slots], load_sem.at[j % slots])
        for j, r in enumerate(order)
    ]
    line = LineSum(
        chips,
        lambda r: lambda: [pair.at[r]],
        lambda r: pair.at[r],
        got,
        (r_send, r_recv, l_send, l_recv),
    )

    def join(j):
        loads[j].wait()
        swaps[order[j]].wait_recv()
        add_into(pair.at[order[j]], [pair.at[order[j]], mine_v.at[j % slots]])
        if j + slots < chips:
            loads[j + slots].start()

    if early_dense:
        dense_v, dense_load = dense_refs[:2]
        buffers = dense_refs[2 : 2 + DENSE_BUFFERS]
        dense = DenseSum(
            dense_ref,
            lambda j, owner: dense_v.at[j],
            dense_out_ref,
            buffers,
            dense_refs[2 + DENSE_BUFFERS :],
            fsdp,
            chips,
        )
        dense_loads = [
            pltpu.make_async_copy(dense_ref.at[owner, core], dense_v.at[j], dense_load.at[j])
            for j, owner in enumerate(dense.owners)
        ]
        stages = dense.stages()
        at_head = {QUERY_HEADS - 1 - len(stages) // 2 + k: k for k in range(len(stages) // 2)}

    def kv_swap(group, r):
        return remote(
            kv_v.at[group, 1, r],
            kv_pair.at[group, r],
            kv_swap_send.at[group, r],
            kv_swap_recv.at[group, r],
            (sibling, me),
        )

    def kv_line(group):
        def held(r):
            kv_swap(group, r).wait_recv()
            return lambda: [kv_v.at[group, 0, r], kv_pair.at[group, r]]

        return LineSum(
            chips,
            held,
            lambda r: kv_pair.at[group, r],
            kv_got.at[group],
            tuple(sem.at[group] for sem in (kr_send, kr_recv, kl_send, kl_recv)),
        )

    def kv_start(group):
        for q in range(2):
            for r in range(chips):
                part = pl.ds((q * chips + r) * rows, rows)
                kv_v[group, q, r, :, :HEAD_SIZE] = (dk_acc[part, :] * scale).astype(BF16)
                kv_v[group, q, r, :, HEAD_SIZE:] = dv_acc[part, :].astype(BF16)
        for r in order:
            kv_swap(group, r).start()

    @pl.when(head == 0)
    def _():
        greet(chips, peers_of(me, fsdp) if early_dense else [], True)
        if early_dense:
            for copy in dense_loads:
                copy.start()
            dense.start()
        for r in order:
            swaps[r].start()
        for copy in loads[:slots]:
            copy.start()

        def fill(t, carry):
            tile = pl.ds(pl.multiple_of(t * KEY_TILE, KEY_TILE), KEY_TILE)
            key_order = jnp.broadcast_to(ok_ref[:, tile], (8, KEY_TILE)).T[:, :1]
            gap = oq_ref[...] - key_order
            bias[tile, :] = jnp.where((gap >= 0) & (gap <= pq_ref[...]), 0.0, MASKED)
            return carry

        lax.fori_loop(0, tiles, fill, 0)

    @pl.when(lax.rem(head, per_group) == 0)
    def _():
        dk_acc[...] = jnp.zeros_like(dk_acc)
        dv_acc[...] = jnp.zeros_like(dv_acc)

    query = q_ref[...]
    grad = do_ref[...]
    lse = lse_ref[0]
    product = grad.astype(F32) * o_ref[...].astype(F32)
    delta = jnp.sum(product.T, axis=0, keepdims=True)

    def step(t, acc):
        tile = pl.ds(pl.multiple_of(t * KEY_TILE, KEY_TILE), KEY_TILE)
        key = k_ref[tile, :]
        raw = dot(key, query, NT) * (scale * LOG2E) + bias[tile, :]
        probs = jnp.exp2(raw - lse)
        prob_grad = dot(v_ref[tile, :], grad, NT)
        score_grad = (probs * (prob_grad - delta)).astype(BF16)
        dv_acc[tile, :] += dot(probs.astype(BF16), grad, NN)
        dk_acc[tile, :] += dot(score_grad, query, NN)
        return acc + dot(score_grad, key, TN)

    acc = lax.fori_loop(0, tiles, step, jnp.zeros((rows, HEAD_SIZE), F32))
    def turn_back(value):
        back = value * cos_ref[...] - pltpu.roll(value, HEAD_SIZE // 2, 1) * sin_ref[...]
        return back.astype(BF16)

    dq_ref[...] = turn_back(acc * scale)

    last = QUERY_HEADS - 1
    stride = max(1, last // (chips - 2))
    early = {per_group + 2 * s: s for s in range(chips - 1) if per_group + 2 * s < last}
    for h in range(QUERY_HEADS):

        @pl.when(head == h)
        def _():
            if h == 0:
                for j in range(min(2, chips)):
                    join(j)
            if h == 1:
                for j in range(2, chips):
                    join(j)
            if early_dense and h == 1:
                for copy in dense_loads:
                    copy.wait()
                dense.cross_over()
            if early_dense and h in at_head:
                stages[at_head[h]]()
            for s in range(chips - 2):
                if h == (s * stride if s == 0 else max(1, s * stride)):
                    line.step(s)
            if h % per_group == per_group - 1:
                kv_start(h // per_group)
            if h in early:
                kv_line(0).step(early[h])

    @pl.when(head == last)
    def _():
        def store(k, r, target):
            return pltpu.make_async_copy(pair.at[r], target, store_sem.at[k])

        @pl.when((chip >= 1) & (chip + 1 < chips))
        def _():
            add_into(pair.at[1], [pair.at[1], line.from_left(chips - 3)])
            add_into(pair.at[chips - 1], [pair.at[chips - 1], line.from_right(chips - 3)])

        for copy in (
            store(0, 0, own_ref),
            store(1, 1, right_ref),
            store(2, chips - 1, left_ref),
        ):
            copy.start()
        rest = stages[len(stages) // 2 :] if early_dense else []
        for group in range(KVH):
            one = kv_line(group)
            for s in range(chips - 1):
                if group > 0 or s not in early.values():
                    one.step(s)
                    if rest:
                        rest.pop(0)()
            one.total(kv_total)
            kv_ref[:, group * HEAD_SIZE : (group + 1) * HEAD_SIZE] = turn_back(
                kv_total[:, :HEAD_SIZE]
            )
            kv_ref[:, (KVH + group) * HEAD_SIZE : (KVH + group + 1) * HEAD_SIZE] = kv_total[
                :, HEAD_SIZE:
            ].astype(BF16)
        for stage in rest:
            stage()
        if early_dense:
            dense.finish()
        for group in range(KVH):
            kv_line(group).finish()
            for r in range(chips):
                kv_swap(group, r).wait_send()
        line.finish(chips - 2)
        for swap in swaps:
            swap.wait_send()
        for copy in (
            store(0, 0, own_ref),
            store(1, 1, right_ref),
            store(2, chips - 1, left_ref),
        ):
            copy.wait()


def attention_back(
    queries,
    kv,
    attended,
    attended_grad,
    lse,
    order_mine,
    pos_mine,
    order_keys,
    cosine,
    sine,
    out_rows,
    dense,
    fsdp,
    early_dense,
    collective_id,
):
    rows = queries.shape[0]
    keys = kv.shape[0]
    unused, chips, unused, width = out_rows.shape
    per_group = QUERY_HEADS // KVH
    head_rows = pl.BlockSpec((rows, HEAD_SIZE), lambda h: (0, h))
    anywhere = pl.BlockSpec(memory_space=pl.ANY)
    return pl.pallas_call(
        functools.partial(
            attention_back_kernel, HEAD_SIZE ** (-0.5), chips, fsdp, early_dense
        ),
        grid=(QUERY_HEADS,),
        out_shape=[
            jax.ShapeDtypeStruct(queries.shape, BF16),
            jax.ShapeDtypeStruct((rows, 2 * KVH * HEAD_SIZE), BF16),
        ]
        + [jax.ShapeDtypeStruct((rows, width), BF16)] * 3
        + [jax.ShapeDtypeStruct(dense.shape[1:] if early_dense else (16, LANES), BF16)],
        in_specs=[
            head_rows,
            pl.BlockSpec((keys, HEAD_SIZE), lambda h: (0, h // per_group)),
            pl.BlockSpec((keys, HEAD_SIZE), lambda h: (0, KVH + h // per_group)),
            head_rows,
            head_rows,
            pl.BlockSpec((1, 1, rows), lambda h: (h, 0, 0)),
            pl.BlockSpec((1, rows), lambda h: (0, 0)),
            pl.BlockSpec((1, rows), lambda h: (0, 0)),
            pl.BlockSpec((1, keys), lambda h: (0, 0)),
            pl.BlockSpec((rows, HEAD_SIZE), lambda h: (0, 0)),
            pl.BlockSpec((rows, HEAD_SIZE), lambda h: (0, 0)),
            anywhere,
            anywhere,
        ],
        out_specs=[
            head_rows,
            pl.BlockSpec((rows, 2 * KVH * HEAD_SIZE), lambda h: (0, 0)),
            anywhere,
            anywhere,
            anywhere,
            pl.BlockSpec(dense.shape[1:], lambda h: (0, 0, 0)) if early_dense else anywhere,
        ],
        scratch_shapes=[
            pltpu.VMEM((keys, rows), F32),
            pltpu.VMEM((keys, HEAD_SIZE), F32),
            pltpu.VMEM((keys, HEAD_SIZE), F32),
            pltpu.VMEM((rows, 2 * HEAD_SIZE), F32),
            pltpu.VMEM((2 if chips <= 4 else 1, rows, width), BF16),
            pltpu.VMEM((chips, rows, width), BF16),
            pltpu.VMEM((chips + 1, rows, width), BF16),
            pltpu.VMEM((KVH, 2, chips, rows, 2 * HEAD_SIZE), BF16),
            pltpu.VMEM((KVH, chips, rows, 2 * HEAD_SIZE), BF16),
            pltpu.VMEM((KVH, chips + 1, rows, 2 * HEAD_SIZE), BF16),
            pltpu.SemaphoreType.DMA((2,)),
            pltpu.SemaphoreType.DMA((3,)),
            pltpu.SemaphoreType.DMA((chips,)),
            pltpu.SemaphoreType.DMA((chips,)),
        ]
        + [pltpu.SemaphoreType.DMA((chips - 1,)) for unused in range(4)]
        + [pltpu.SemaphoreType.DMA((KVH, chips)) for unused in range(2)]
        + [pltpu.SemaphoreType.DMA((KVH, chips - 1)) for unused in range(4)]
        + (
            [
                pltpu.VMEM((fsdp,) + dense.shape[2:], BF16),
                pltpu.SemaphoreType.DMA((fsdp,)),
            ]
            + dense_buffers(dense.shape[2], dense.shape[3], fsdp, chips)
            + dense_sems(fsdp, chips)
            if early_dense
            else []
        ),
        compiler_params=pltpu.CompilerParams(
            collective_id=collective_id, has_side_effects=True, vmem_limit_bytes=BACK_VMEM_BYTES
        ),
        cost_estimate=pl.CostEstimate(
            flops=10 * rows * keys * HEAD_SIZE * QUERY_HEADS,
            bytes_accessed=10 * rows * QUERY_HEADS * HEAD_SIZE + 8 * keys * KVH * HEAD_SIZE,
            transcendentals=rows * keys * QUERY_HEADS,
        ),
        name="attention_back",
    )(
        queries,
        kv,
        kv,
        attended,
        attended_grad,
        lse,
        order_mine[None, :],
        pos_mine[None, :],
        order_keys[None, :],
        cosine,
        sine,
        out_rows,
        dense,
    )


def experts_kernel(
    capacity,
    local_experts,
    expert_count,
    chips,
    fsdp,
    per,
    hidden_ref,
    grad_ref,
    table_ref,
    weight_ref,
    gate_ref,
    up_ref,
    down_ref,
    returned_ref,
    out_ref,
    gate_grad_ref,
    gate_got_ref,
    up_grad_ref,
    down_grad_ref,
    x_ref,
    pg_ref,
    inner_ref,
    da_ref,
    db_ref,
    gate_v,
    up_v,
    down_v,
    hidden_v,
    grad_v,
    out_v,
    x_v,
    pg_v,
    g_v,
    inner_v,
    da_v,
    db_v,
    mine_v,
    other_v,
    pair,
    got,
    stage_tall,
    weight_sem,
    load_sem,
    out_sem,
    save_sem,
    swap_send,
    swap_recv,
    right_send,
    right_recv,
    left_send,
    left_recv,
    stage_sem,
    tile_own,
    tile_send,
    tile_recv,
):
    ctx, me, chip, core, sibling = place()
    peers = peers_of(me, fsdp)
    tokens = hidden_v.shape[1]
    width = hidden_v.shape[2]
    slots = x_v.shape[1]
    slot_rows = slots // 2
    units = inner_v.shape[2]
    total_rows = x_ref.shape[1]
    first = ctx * local_experts

    weights_in = [
        pltpu.make_async_copy(src, dst, weight_sem.at[k])
        for k, (src, dst) in enumerate(
            ((gate_ref, gate_v), (up_ref, up_v), (down_ref, down_v))
        )
    ]

    def load(i):
        r = chunk_order(chip, i, chips)
        return [
            pltpu.make_async_copy(hidden_ref.at[:, r], hidden_v, load_sem.at[0]),
            pltpu.make_async_copy(grad_ref.at[:, r], grad_v, load_sem.at[1]),
        ]

    def saves(i):
        rows = pl.ds(i * slots, slots)
        return [
            pltpu.make_async_copy(src, dst.at[:, rows], save_sem.at[k])
            for k, (src, dst) in enumerate(
                ((x_v, x_ref), (pg_v, pg_ref), (inner_v, inner_ref), (da_v, da_ref), (db_v, db_ref))
            )
        ]

    def out_copies(i):
        r = chunk_order(chip, i, chips)
        return [
            pltpu.make_async_copy(out_v.at[q], out_ref.at[q, r], out_sem.at[q]) for q in range(2)
        ]

    def swap(i):
        r = chunk_order(chip, i, chips)
        return remote(
            other_v.at[lax.rem(i, 2)],
            pair.at[r],
            swap_send.at[r],
            swap_recv.at[r],
            (sibling, me),
        )

    def join(i):
        r = chunk_order(chip, i, chips)
        swap(i).wait_recv()
        add_into(pair.at[r], [pair.at[r], mine_v.at[lax.rem(i, 2)]])

    line = LineSum(
        chips,
        lambda r: lambda: [pair.at[r]],
        lambda r: pair.at[r],
        got,
        (right_send, right_recv, left_send, left_recv),
    )

    for copy in load(0) + weights_in:
        copy.start()
    greet(chips, peers if per == 1 else [], True)

    slot = lax.broadcasted_iota(jnp.int32, (slot_rows, tokens), 0).astype(F32) + 1.0
    slot = jnp.where(slot <= capacity, slot, -1.0)
    lane = lax.broadcasted_iota(jnp.int32, (slots, LANES), 1)

    def chunk(i, carry):
        r = chunk_order(chip, i, chips)
        for copy in load(i):
            copy.wait()

        @pl.when(i >= 1)
        def _():
            for copy in saves(i - 1):
                copy.wait()

        picks = [[], []]
        weight_rows = []
        for e in range(local_experts):
            rows_w = []
            for q in range(2):
                hit = slot == table_ref[q, r, pl.ds(first + e, 1), :]
                pick = jnp.where(hit, 1.0, 0.0).astype(BF16)
                weight = weight_ref[q, r, pl.ds(first + e, 1), :]
                w = jnp.sum(jnp.where(hit, weight, 0.0), axis=1, keepdims=True)
                rows = pl.ds(q * slot_rows, slot_rows)
                x_v[e, rows, :] = dot(pick, hidden_v[q], NN).astype(BF16)
                g = dot(pick, grad_v[q], NN)
                g_v[e, rows, :] = g.astype(BF16)
                pg_v[e, rows, :] = (w * g).astype(BF16)
                picks[q].append(pick)
                rows_w.append(w)
            weight_rows.append(jnp.concatenate(rows_w, axis=0))

        @pl.when(i + 1 < chips)
        def _():
            for copy in load(i + 1):
                copy.start()

        @pl.when(i == 0)
        def _():
            for copy in weights_in:
                copy.wait()

        outs = [[], []]
        backs = [[], []]
        for e in range(local_experts):
            x = x_v[e]
            pair_grad = pg_v[e]
            w = weight_rows[e]
            gate = gate_v[e * width : (e + 1) * width, :]
            up = up_v[e * width : (e + 1) * width, :]
            down = down_v[e * units : (e + 1) * units, :]
            gate_pre = dot(x, gate, NN)
            up_pre = dot(x, up, NN)
            sig = jax.nn.sigmoid(gate_pre)
            silu = gate_pre * sig
            inner = (silu * up_pre).astype(BF16)
            inner_v[e] = inner
            expert_out = dot(inner, down, NN).astype(BF16).astype(F32)
            gate_grad = jnp.sum(expert_out * g_v[e].astype(F32), axis=1, keepdims=True)
            inner_grad = dot(pair_grad, down, NT)
            da = (inner_grad * up_pre * sig * (1.0 + gate_pre * (1.0 - sig))).astype(BF16)
            db = (inner_grad * silu).astype(BF16)
            da_v[e] = da
            db_v[e] = db
            row_grad = (dot(da, gate, NT) + dot(db, up, NT)).astype(BF16)
            high = gate_grad.astype(BF16).astype(F32)
            extra = jnp.where(lane == first + e, high, 0.0) + jnp.where(
                lane == expert_count + first + e, gate_grad - high, 0.0
            )
            back = jnp.concatenate([row_grad, extra.astype(BF16)], axis=1)
            out_rows = (w * expert_out).astype(BF16)
            for q in range(2):
                part = slice(q * slot_rows, (q + 1) * slot_rows)
                outs[q].append(out_rows[part])
                backs[q].append(back[part])

        for copy in saves(i):
            copy.start()

        @pl.when(i >= 1)
        def _():
            for copy in out_copies(i - 1):
                copy.wait()

        @pl.when(i >= 2)
        def _():
            swap(i - 2).wait_send()

        for q in range(2):
            pick = jnp.concatenate(picks[q], axis=0)
            held = other_v if q else mine_v
            held[lax.rem(i, 2)] = dot(pick, jnp.concatenate(backs[q], axis=0), TN).astype(BF16)
            if q:
                swap(i).start()
        for q in range(2):
            pick = jnp.concatenate(picks[q], axis=0)
            out_v[q] = dot(pick, jnp.concatenate(outs[q], axis=0), TN).astype(BF16)
        for copy in out_copies(i):
            copy.start()

        @pl.when(i == 0)
        def _():
            join(0)
            line.step(0)

        @pl.when(i >= 2)
        def _():
            join(i - 1)

        for step in range(1, chips - 1):
            if 2 * step < chips:

                @pl.when(i == 2 * step)
                def _():
                    line.step(step)

        return carry

    lax.fori_loop(0, chips, chunk, 0)
    join(chips - 1)
    for copy in saves(chips - 1):
        copy.wait()
    for copy in out_copies(chips - 1):
        copy.wait()
    for i in range(max(0, chips - 2), chips):
        swap(i).wait_send()

    shard = width // fsdp
    blocks = fsdp // per
    block = per * shard

    def fetch(copies):
        copies = [
            pltpu.make_async_copy(src, dst, save_sem.at[k])
            for k, (src, dst) in enumerate(copies)
        ]
        for copy in copies:
            copy.start()
        for copy in copies:
            copy.wait()

    def products(e, staged, target, product):
        def write(f):
            return [
                pltpu.make_async_copy(
                    staged(lax.rem(f, 2), p),
                    target.at[f * per + p, e],
                    stage_sem.at[lax.rem(f, 2), p],
                )
                for p in range(per)
            ]

        def one(f, carry):
            @pl.when(f >= 2)
            def _():
                for copy in write(f - 2):
                    copy.wait()

            product(f)
            for copy in write(f):
                copy.start()
            return carry

        lax.fori_loop(0, blocks, one, 0)
        for f in range(max(0, blocks - 2), blocks):
            for copy in write(f):
                copy.wait()

    def stage_wide(slot, p):
        return hidden_v.at[slot, pl.ds(p * shard, shard), pl.ds(0, units)]

    def wide(e, held, staged, target):
        def product(f):
            columns = pl.ds(pl.multiple_of(f * block, LANES), block)
            value = dot(
                down_v[:total_rows, columns],
                held[e * total_rows : (e + 1) * total_rows, :],
                TN,
            ).astype(BF16)
            for p in range(per):
                staged(lax.rem(f, 2), p)[...] = value[p * shard : (p + 1) * shard, :]

        products(e, staged, target, product)

    def tall(e, target):
        def product(f):
            columns = pl.ds(pl.multiple_of(f * block, LANES), block)
            value = dot(
                gate_v[e * total_rows : (e + 1) * total_rows, :],
                down_v[:total_rows, columns],
                TN,
            ).astype(BF16)
            for p in range(per):
                stage_tall[lax.rem(f, 2), p] = value[:, p * shard : (p + 1) * shard]

        products(e, lambda slot, p: stage_tall.at[slot, p], target, product)

    def tile(e, j):
        held = (hidden_v, grad_v)[e]
        return held.at[j // 2, pl.ds(0, shard), pl.ds((j % 2) * units, units)]

    def tile_copy(e, j):
        if j == len(peers):
            return pltpu.make_async_copy(tile(e, j), gate_grad_ref.at[e], tile_own.at[e])
        return remote(
            tile(e, j),
            gate_got_ref.at[j, e],
            tile_send.at[e, j],
            tile_recv.at[e, j],
            (ctx, peers[j]),
        )

    def gate_tiles(e):
        for j, owner in enumerate(peers + [me]):
            columns = pl.ds(pl.multiple_of(owner * shard, LANES), shard)
            tile(e, j)[...] = dot(
                down_v[:total_rows, columns],
                gate_v[e * total_rows : (e + 1) * total_rows, :],
                TN,
            ).astype(BF16)
            tile_copy(e, j).start()

    def fetch_x(e):
        copies = [(x_ref.at[e], down_v.at[:total_rows])]
        if e == 0:
            for k in range(local_experts):
                held = pl.ds(k * total_rows, total_rows)
                copies += [(da_ref.at[k], gate_v.at[held]), (db_ref.at[k], up_v.at[held])]
        return lambda: fetch(copies)

    def stage_up(slot, p):
        return out_v.at[slot, pl.ds(p * shard, shard), pl.ds(0, units)]

    work = []
    for e in range(local_experts):
        work.append(fetch_x(e))
        if per == 1:
            work.append(lambda e=e: gate_tiles(e))
        else:
            work.append(lambda e=e: wide(e, gate_v, stage_wide, gate_grad_ref))
        if e > 0:
            work.append(lambda e=e: wide(e, up_v, stage_up, up_grad_ref))
    work.append(lambda: fetch([(x_ref.at[0], down_v.at[:total_rows])]))
    work.append(lambda: wide(0, up_v, stage_up, up_grad_ref))
    for e in range(local_experts):
        copies = [(pg_ref.at[e], down_v.at[:total_rows])]
        if e == 0:
            for k in range(local_experts):
                copies.append((inner_ref.at[k], gate_v.at[pl.ds(k * total_rows, total_rows)]))
        work.append(lambda copies=copies: fetch(copies))
        work.append(lambda e=e: tall(e, down_grad_ref))
    late = [step for step in range(1, chips - 1) if 2 * step >= chips]
    for n, task in enumerate(work):
        task()
        if n == LINE_TASK or (n > LINE_TASK and late):
            if late:
                line.step(late.pop(0))
    for step in late:
        line.step(step)

    line.total(returned_ref)
    line.finish()
    if per == 1:
        for e in range(local_experts):
            for j in range(fsdp):
                tile_copy(e, j).wait()


def experts_pass(
    hidden, grad, table, weights, gate, up, down, capacity, expert_count, fsdp, collective_id
):
    unused, chips, tokens, width = grad.shape
    local_experts, unused, units = gate.shape
    slots = 2 * SLOT_STEP * -(-capacity // SLOT_STEP)
    total = chips * slots
    shard = width // fsdp
    per = 1 if shard % LANES == 0 else 2
    wide = width + LANES
    anywhere = pl.BlockSpec(memory_space=pl.ANY)
    vmem = pl.BlockSpec(memory_space=pltpu.VMEM)
    flops = 2 * total * width * units * local_experts * 9 + 8 * total * tokens * width
    saved = [(local_experts, total, width)] * 2 + [(local_experts, total, units)] * 3
    held = [(local_experts, slots, width)] * 3 + [(local_experts, slots, units)] * 3
    outs = pl.pallas_call(
        functools.partial(
            experts_kernel, capacity, local_experts, expert_count, chips, fsdp, per
        ),
        out_shape=[
            jax.ShapeDtypeStruct((tokens, wide), BF16),
            jax.ShapeDtypeStruct(hidden.shape, BF16),
            jax.ShapeDtypeStruct(
                ((fsdp,) if per > 1 else ()) + (local_experts, shard, units), BF16
            ),
            jax.ShapeDtypeStruct(
                (fsdp - 1, local_experts, shard, units) if per == 1 else (1, 1, 16, LANES), BF16
            ),
            jax.ShapeDtypeStruct((fsdp, local_experts, shard, units), BF16),
            jax.ShapeDtypeStruct((fsdp, local_experts, units, shard), BF16),
        ]
        + [jax.ShapeDtypeStruct(shape, BF16) for shape in saved],
        in_specs=[anywhere, anywhere, vmem, vmem, anywhere, anywhere, anywhere],
        out_specs=[vmem] + [anywhere] * 10,
        input_output_aliases={0: 1},
        scratch_shapes=[
            pltpu.VMEM((local_experts * width, units), BF16),
            pltpu.VMEM((local_experts * width, units), BF16),
            pltpu.VMEM((local_experts * units, width), BF16),
            pltpu.VMEM((2, tokens, width), BF16),
            pltpu.VMEM((2, tokens, width), BF16),
            pltpu.VMEM((2, tokens, width), BF16),
        ]
        + [pltpu.VMEM(shape, BF16) for shape in held]
        + [
            pltpu.VMEM((2, tokens, wide), BF16),
            pltpu.VMEM((2, tokens, wide), BF16),
            pltpu.VMEM((chips, tokens, wide), BF16),
            pltpu.VMEM((chips + 1, tokens, wide), BF16),
            pltpu.VMEM((2, per, units, shard), BF16),
            pltpu.SemaphoreType.DMA((3,)),
            pltpu.SemaphoreType.DMA((2,)),
            pltpu.SemaphoreType.DMA((2,)),
            pltpu.SemaphoreType.DMA((5,)),
            pltpu.SemaphoreType.DMA((chips,)),
            pltpu.SemaphoreType.DMA((chips,)),
        ]
        + [pltpu.SemaphoreType.DMA((chips - 1,)) for unused in range(4)]
        + [pltpu.SemaphoreType.DMA((2, per)), pltpu.SemaphoreType.DMA((local_experts,))]
        + [pltpu.SemaphoreType.DMA((local_experts, fsdp - 1)) for unused in range(2)],
        compiler_params=pltpu.CompilerParams(
            collective_id=collective_id, has_side_effects=True, vmem_limit_bytes=EXPERT_VMEM_BYTES
        ),
        cost_estimate=pl.CostEstimate(
            flops=flops, bytes_accessed=100_000_000, transcendentals=total * units * 2
        ),
        name="experts",
    )(
        hidden,
        grad,
        table,
        weights,
        gate.reshape(local_experts * width, units),
        up.reshape(local_experts * width, units),
        down.reshape(local_experts * units, width),
    )
    return outs[:6]


def body(
    tokens,
    grad_out,
    order,
    lengths,
    routes,
    gain_one,
    gain_two,
    w_query,
    w_key,
    w_value,
    w_out,
    w_router,
    w_gate,
    w_up,
    w_down,
):
    fsdp = lax.axis_size("fsdp")
    chips = lax.axis_size("ctx") // 2
    ctx_index = lax.axis_index("ctx")
    chip = ctx_index // 2
    core = lax.rem(ctx_index, 2)
    tok_rows = tokens.shape[1]
    width = tokens.shape[2]
    top_count = routes.shape[2]
    local_experts = w_gate.shape[0]
    expert_count = local_experts * chips * 2
    capacity = 5 * tok_rows * top_count // (4 * expert_count)
    kv_width = KVH * HEAD_SIZE
    shard = gain_one.shape[0]

    small = jnp.concatenate(
        [
            w_router,
            gain_one[:, None],
            gain_two[:, None],
            jnp.zeros((shard, LANES - expert_count - 2), BF16),
        ],
        axis=1,
    )
    qkv_full, small_full, out_full, grad_all = gather(
        [w_query, w_key, w_value, small, w_out], 3, [grad_out[0]], chips - 2, fsdp, chips, 0
    )

    qkv_full, w_up, w_down = lax.optimization_barrier((qkv_full, w_up, w_down))
    up_full, down_full = (
        lax.all_gather(w_up, "fsdp", axis=1, tiled=True),
        lax.all_gather(w_down, "fsdp", axis=2, tiled=True),
    )
    router_full = small_full[:, :expert_count]
    gain_a = small_full[:, expert_count].astype(F32)
    gain_b = small_full[:, expert_count + 1].astype(F32)

    order_row = order[0]
    start_row = ctx_index * tok_rows
    order_mine = lax.dynamic_slice_in_dim(order_row, start_row, tok_rows)
    ends = jnp.cumsum(lengths[0])
    starts = ends - lengths[0]
    past = order_mine[:, None] >= ends[None, :]
    doc_start = jnp.max(jnp.where(past, ends[None, :], starts[:1]), axis=1)
    pos_mine = order_mine - doc_start
    by_chip = jnp.roll(order_row.reshape(chips, 2, tok_rows), -chip, axis=0)
    by_chip = jnp.where(core == 0, by_chip, by_chip[:, ::-1])
    order_keys = jnp.swapaxes(by_chip, 0, 1).reshape(-1)

    route_rows = routes[0]
    route_onehot = (route_rows[:, :, None] == jnp.arange(expert_count)[None, None, :]).astype(F32)
    routed = jnp.sum(route_onehot, axis=1)
    earlier = (order_mine[None, :] < order_mine[:, None]).astype(BF16)
    ranks = jnp.dot(earlier, routed.astype(BF16), preferred_element_type=F32)
    table = jnp.where(routed > 0, jnp.minimum(ranks, capacity) + 1.0, 0.0)

    half_dim = HEAD_SIZE // 2
    freqs = ROPE_BASE ** (-2.0 * jnp.arange(half_dim).astype(F32) / HEAD_SIZE)
    angles = pos_mine.astype(F32)[:, None] * freqs[None, :]
    cosine = jnp.concatenate([jnp.cos(angles), jnp.cos(angles)], axis=1)
    sine = jnp.concatenate([-jnp.sin(angles), jnp.sin(angles)], axis=1)

    inputs = tokens[0].astype(F32)
    (
        table_all,
        lse,
        gate_weights,
        weights_all,
        queries,
        hidden_one,
        kv_all,
        attended,
        middle,
        hidden_two,
        hidden_all,
        gate_full,
        grad_all,
    ) = front(
        tokens[0],
        gain_a,
        gain_b,
        small_full,
        cosine,
        sine,
        order_mine,
        pos_mine,
        order_keys,
        jnp.pad(routed, ((0, 0), (0, LANES - expert_count))),
        table.T,
        qkv_full,
        out_full,
        w_gate,
        grad_all,
        chips,
        fsdp,
        1,
    )
    kv_all = kv_all.reshape(-1, 2 * kv_width)
    gate_weights = gate_weights[:, :expert_count]

    returned, out_rows, gate_local, gate_got, up_local, down_local = experts_pass(
        hidden_all,
        grad_all,
        table_all,
        weights_all,
        gate_full,
        up_full,
        down_full,
        capacity,
        expert_count,
        fsdp,
        5,
    )
    direct = gate_local.ndim == 3
    if not direct:
        gate_local = lax.psum_scatter(gate_local, "fsdp", scatter_dimension=0, tiled=True)[0]
    up_sum, down_sum = (
        lax.psum_scatter(part, "fsdp", scatter_dimension=0, tiled=True)
        for part in (up_local, down_local)
    )

    out_grad = grad_out[0].astype(F32)
    returned = returned.astype(F32)
    extra = returned[:, width:]
    gate_grad = extra[:, :expert_count] + extra[:, expert_count : 2 * expert_count]
    logit_grad = (
        gate_weights * (gate_grad - jnp.sum(gate_weights * gate_grad, axis=-1, keepdims=True))
    ).astype(BF16)
    router_local = jnp.einsum("td,te->de", hidden_two, logit_grad, preferred_element_type=F32)
    hidden_two_grad = returned[:, :width] + jnp.einsum(
        "te,de->td", logit_grad, router_full, preferred_element_type=F32
    )
    unused_two, norm_two_back = jax.vjp(rms_scale, middle, gain_b)
    middle_part, gain_two_local = norm_two_back(hidden_two_grad)
    middle_grad = out_grad + middle_part
    branch_grad = middle_grad.astype(BF16)
    out_local = jnp.einsum("tc,td->cd", attended, branch_grad, preferred_element_type=F32)
    attended_grad = jnp.einsum(
        "td,cd->tc", branch_grad, out_full, preferred_element_type=F32
    ).astype(BF16)

    def halves(local):
        local = local.astype(BF16).reshape(fsdp, 2, shard // 2, local.shape[1])
        pad = -local.shape[3] % (LANES * chips)
        return jnp.pad(local, ((0, 0), (0, 0), (0, 0), (0, pad))) if pad else local

    early_dense = chips <= 4
    query_grad, kv_grad, out_own, out_right, out_left, out_proj_sum = attention_back(
        queries,
        kv_all,
        attended,
        attended_grad,
        lse,
        order_mine,
        pos_mine,
        order_keys,
        cosine,
        sine,
        out_rows,
        halves(out_local) if early_dense else out_local[:16, :LANES].astype(BF16),
        fsdp,
        early_dense,
        3,
    )
    pre_grad = jnp.concatenate([query_grad, kv_grad], axis=1)
    qkv_local = jnp.einsum("td,tc->dc", hidden_one, pre_grad, preferred_element_type=F32)
    span = shard * expert_count // 16
    wide = LANES * chips * -(-max(span, shard) // (LANES * chips))
    small_local = jnp.stack(
        [
            jnp.pad(
                router_local.astype(BF16).reshape(fsdp, 16, span),
                ((0, 0), (0, 0), (0, wide - span)),
            ),
            jnp.pad(
                gain_two_local.reshape(fsdp, 1, shard).astype(BF16),
                ((0, 0), (1, 14), (0, wide - shard)),
            ),
        ],
        axis=1,
    )
    *sums, out_sum, input_grad = dense_reduce(
        [halves(qkv_local), small_local] + ([] if early_dense else [halves(out_local)]),
        out_own,
        out_right,
        out_left,
        pre_grad,
        tokens[0],
        middle_grad,
        gain_a,
        qkv_full,
        DENSE_PIECE,
        fsdp,
        chips,
        4,
    )
    qkv_sum, small_sum = sums[:2]
    if not early_dense:
        out_proj_sum = sums[2]
    edge = width + 2 * kv_width
    qkv_grads = qkv_sum.reshape(shard, -1)
    out_proj_grad = out_proj_sum.reshape(shard, -1)[:, :width]
    up_grad_out, down_grad_out = (
        after(part, pre_grad)[0].astype(F32) for part in (up_sum, down_sum)
    )
    if direct:
        gate_local, gate_got = lax.optimization_barrier((gate_local, gate_got, pre_grad))[:2]
        gate_grad_out = add(gate_local, *[gate_got[j] for j in range(fsdp - 1)])
    else:
        gate_grad_out = after(gate_local, pre_grad).astype(F32)
    result = middle + out_sum
    return (
        result.astype(BF16)[None],
        input_grad[None],
        small_sum[1, 0, :shard].astype(F32),
        small_sum[1, 1, :shard].astype(F32),
        qkv_grads[:, :width].astype(F32),
        qkv_grads[:, width : width + kv_width].astype(F32),
        qkv_grads[:, width + kv_width : edge].astype(F32),
        out_proj_grad.astype(F32),
        small_sum[0, :, :span].reshape(shard, expert_count).astype(F32),
        gate_grad_out,
        up_grad_out,
        down_grad_out,
    )


def solution(mesh):
    placed = (
        P("fsdp", "ctx", None),
        P("fsdp", "ctx", None),
        P("fsdp", None),
        P("fsdp", None),
        P("fsdp", "ctx", None),
        P("fsdp"),
        P("fsdp"),
        P("fsdp", None),
        P("fsdp", None),
        P("fsdp", None),
        P("fsdp", None),
        P("fsdp", None),
        P("ctx", "fsdp", None),
        P("ctx", "fsdp", None),
        P("ctx", None, "fsdp"),
    )
    return jax.shard_map(
        body,
        mesh=mesh,
        in_specs=placed,
        out_specs=(
            P("fsdp", "ctx", None),
            P("fsdp", "ctx", None),
            P("fsdp"),
            P("fsdp"),
            P("fsdp", None),
            P("fsdp", None),
            P("fsdp", None),
            P("fsdp", None),
            P("fsdp", None),
            P("ctx", "fsdp", None),
            P("ctx", "fsdp", None),
            P("ctx", None, "fsdp"),
        ),
        check_vma=False,
    )
```

```python
import functools

import jax
import jax.numpy as jnp
from jax import lax
from jax.experimental import pallas as pl
from jax.experimental.pallas import tpu as pltpu
from jax.sharding import PartitionSpec as P

QUERY_HEADS = 12
KVH = 2
HEAD_SIZE = 128

EPSILON = 1e-06
ROPE_BASE = 10000.0
MASKED = -1e30
LOG2E = 1.4426950408889634
LANES = 128
SLOT_STEP = 64
DENSE_PIECE = 1024
LINE_TASK = 4
KEY_TILE = 512
VMEM_BYTES = 56 * 1024 * 1024
EXPERT_VMEM_BYTES = 119 * 512 * 1024
BACK_VMEM_BYTES = 61 * 1024 * 1024
FRONT_VMEM_BYTES = 50 * 1024 * 1024
DENSE_VMEM_BYTES = 50 * 1024 * 1024
MESH = pl.DeviceIdType.MESH
F32 = jnp.float32
BF16 = jnp.bfloat16


def dot(left, right, contract):
    return lax.dot_general(left, right, (contract, ((), ())), preferred_element_type=F32)


NN = ((1,), (0,))
NT = ((1,), (1,))
TN = ((0,), (0,))


def rms_scale(value_rows, gain):
    return (
        value_rows
        * lax.rsqrt(jnp.mean(value_rows * value_rows, axis=-1, keepdims=True) + EPSILON)
        * gain
    )


def place():
    ctx = lax.axis_index("ctx")
    core = lax.rem(ctx, 2)
    return ctx, lax.axis_index("fsdp"), ctx // 2, core, ctx + 1 - 2 * core


def peers_of(me, fsdp):
    peers = []
    for shift in range(1, fsdp):
        peer = me
        for bit in range(fsdp.bit_length() - 1):
            if (shift >> bit) & 1:
                digit = lax.rem(me // (1 << bit), 2)
                peer = peer + (1 << bit) - (2 << bit) * digit
        peers.append(peer)
    return peers


def greet(chips, peers, line):
    ctx, me, chip, core, sibling = place()
    barrier = pltpu.get_barrier_semaphore()
    for peer in peers:
        pl.semaphore_signal(barrier, inc=1, device_id=(ctx, peer), device_id_type=MESH)
    pl.semaphore_signal(barrier, inc=1, device_id=(sibling, me), device_id_type=MESH)
    known = len(peers) + 1
    if not line:
        pl.semaphore_wait(barrier, known)
        return
    has_right = chip + 1 < chips
    has_left = chip >= 1

    @pl.when(has_right)
    def _():
        pl.semaphore_signal(barrier, inc=1, device_id=(ctx + 2, me), device_id_type=MESH)

    @pl.when(has_left)
    def _():
        pl.semaphore_signal(barrier, inc=1, device_id=(ctx - 2, me), device_id_type=MESH)

    @pl.when(has_right & has_left)
    def _():
        pl.semaphore_wait(barrier, known + 2)

    @pl.when(jnp.logical_not(has_right & has_left))
    def _():
        pl.semaphore_wait(barrier, known + 1)


class Bounce:
    def __init__(self, src, dst, buffer, sem):
        self.inward = pltpu.make_async_copy(src, buffer, sem)
        self.outward = pltpu.make_async_copy(buffer, dst, sem)

    def start(self):
        self.inward.start()

    def turn(self):
        self.inward.wait()
        self.outward.start()

    def wait(self):
        self.outward.wait()


def remote(src, dst, send_sem, recv_sem, device):
    return pltpu.make_async_remote_copy(
        src_ref=src,
        dst_ref=dst,
        send_sem=send_sem,
        recv_sem=recv_sem,
        device_id=device,
        device_id_type=MESH,
    )


class Spread:
    def __init__(self, block, place_of, size, sems, fsdp):
        send_sem, recv_sem, on_send, on_recv = sems
        ctx, me, chip, core, sibling = place()
        self.peers = peers_of(me, fsdp)
        self.square = fsdp == 4
        near = self.peers[:2] if self.square else self.peers
        self.sends = [
            remote(block, place_of(me, 0, size), send_sem.at[j], recv_sem.at[j], (ctx, peer))
            for j, peer in enumerate(near)
        ]
        self.on, self.last = [], []
        if self.square:
            half = size // 2
            across_x, across_y, far = self.peers
            for k, (owner, target) in enumerate(((across_x, across_y), (across_y, across_x))):
                part = place_of(owner, k * half, half)
                self.on.append(remote(part, part, on_send.at[k], on_recv.at[k], (ctx, target)))
                part = place_of(far, k * half, half)
                self.last.append(remote(part, part, on_send.at[k], on_recv.at[k], (ctx, target)))

    def start(self):
        for copy in self.sends:
            copy.start()

    def hand_on(self, also=lambda j: None):
        for j, copy in enumerate(self.sends):
            copy.wait_recv()
            if self.square:
                self.on[j].start()
            also(j)

    def finish(self, also=lambda j: None):
        for copy in self.last:
            copy.wait_recv()
        if self.square:
            also(2)
        for copy in self.sends + self.on:
            copy.wait_send()


def spread_sems(fsdp):
    return [pltpu.SemaphoreType.DMA((fsdp - 1,)) for unused in range(4)]


class DenseGather:
    def __init__(self, ins, outs, sems, fsdp):
        buffers, local_sem, pass_sem, took_sem, spread_refs = sems
        ctx, me, chip, core, sibling = place()
        peers = peers_of(me, fsdp)
        self.spreads, self.passes, self.locals = [], [], []
        for i in range(len(ins)):
            rows = ins[i].shape[0]
            half = rows // 2

            def place_of(owner, begin, size, i=i, rows=rows, half=half):
                return outs[i].at[pl.ds(owner * rows + core * half + begin, size)]

            self.spreads.append(
                Spread(
                    ins[i].at[pl.ds(core * half, half)],
                    place_of,
                    half,
                    spread_refs[4 * i : 4 * i + 4],
                    fsdp,
                )
            )
            self.passes.append([])
            for j, peer in enumerate(peers):
                got = place_of(peer, 0, half)
                self.passes[i].append(
                    remote(got, got, pass_sem.at[i, j], took_sem.at[i, j], (sibling, me))
                )
            self.locals.append(
                Bounce(ins[i], outs[i].at[pl.ds(me * rows, rows)], buffers[i], local_sem.at[i])
            )

    def start(self):
        for spread in self.spreads:
            spread.start()
        for copy in self.locals:
            copy.start()

    def hand_on(self):
        for copy in self.locals:
            copy.turn()
        for i, spread in enumerate(self.spreads):
            spread.hand_on(lambda j, i=i: self.passes[i][j].start())

    def finish(self):
        for i, spread in enumerate(self.spreads):
            spread.finish(lambda j, i=i: self.passes[i][j].start())
        for passes in self.passes:
            for copy in passes:
                copy.wait()
        for copy in self.locals:
            copy.wait()


def dense_scratch(arrays, fsdp):
    count = len(arrays)
    return (
        [pltpu.VMEM(a.shape, a.dtype) for a in arrays]
        + [pltpu.SemaphoreType.DMA((count,))]
        + [pltpu.SemaphoreType.DMA((count, fsdp - 1)) for unused in range(2)]
        + spread_sems(fsdp) * count
    )


class ShardGather:
    def __init__(self, ref, out, buffer, sems, fsdp):
        ctx, me, chip, core, sibling = place()
        rows = ref.shape[1]

        def place_of(owner, begin, size):
            return out.at[:, pl.ds(owner * rows + begin, size)]

        self.spread = Spread(ref, place_of, rows, sems[1:], fsdp)
        self.own = Bounce(ref, place_of(me, 0, rows), buffer, sems[0])

    def start(self):
        self.spread.start()
        self.own.start()

    def hand_on(self):
        self.spread.hand_on()
        self.own.turn()

    def finish(self):
        self.spread.finish()
        self.own.wait()


class LineGather:
    def __init__(self, ins, outs, sems, chips):
        self.ins, self.outs, self.chips = ins, outs, chips
        self.buffers, self.sems = sems[:-7], sems[-7:]
        self.ctx, self.me, self.chip, core, self.sibling = place()
        self.count = len(ins)

    def to_right(self, i, step):
        outs, chips = self.outs, self.chips
        return remote(
            self.ins[i] if step == 0 else outs[i].at[0, chips - step],
            outs[i].at[0, chips - 1 - step],
            self.sems[1].at[i, step],
            self.sems[2].at[i, step],
            (self.ctx + 2, self.me),
        )

    def to_left(self, i, step):
        outs = self.outs
        return remote(
            self.ins[i] if step == 0 else outs[i].at[0, step],
            outs[i].at[0, step + 1],
            self.sems[3].at[i, step],
            self.sems[4].at[i, step],
            (self.ctx - 2, self.me),
        )

    def across(self, i, slot):
        return remote(
            self.ins[i] if slot == 0 else self.outs[i].at[0, slot],
            self.outs[i].at[1, slot],
            self.sems[5].at[i, slot],
            self.sems[6].at[i, slot],
            (self.sibling, self.me),
        )

    def local(self, i):
        return Bounce(self.ins[i], self.outs[i].at[0, 0], self.buffers[i], self.sems[0].at[i])

    def send(self, step):
        chip, chips, count = self.chip, self.chips, self.count

        @pl.when((chip + 1 < chips) & (chip >= step))
        def _():
            for i in range(count):
                self.to_right(i, step).start()

        @pl.when((chip >= 1) & (chip + step < chips))
        def _():
            for i in range(count):
                self.to_left(i, step).start()

    def receive(self, step):
        chip, chips, count = self.chip, self.chips, self.count

        @pl.when(chip >= step + 1)
        def _():
            for i in range(count):
                self.to_right(i, step).wait_recv()
                self.across(i, chips - 1 - step).start()

        @pl.when(chip + step + 1 < chips)
        def _():
            for i in range(count):
                self.to_left(i, step).wait_recv()
                self.across(i, step + 1).start()

    def own(self):
        for i in range(self.count):
            self.across(i, 0).start()
            self.local(i).start()

    def turn_own(self):
        for i in range(self.count):
            self.local(i).turn()

    def finish_own(self):
        for i in range(self.count):
            self.across(i, 0).wait()
            self.local(i).wait()

    def arrived(self, slot):
        for i in range(self.count):
            remote(
                self.outs[i].at[0, slot],
                self.outs[i].at[1, slot],
                self.sems[5].at[i, slot],
                self.sems[6].at[i, slot],
                (self.sibling, self.me),
            ).wait_recv()

    def sent(self):
        chip, chips, count = self.chip, self.chips, self.count
        for step in range(chips - 1):

            @pl.when((chip + 1 < chips) & (chip >= step))
            def _():
                for i in range(count):
                    self.to_right(i, step).wait_send()

            @pl.when((chip >= 1) & (chip + step < chips))
            def _():
                for i in range(count):
                    self.to_left(i, step).wait_send()

        for slot in range(chips):
            for i in range(count):
                self.across(i, slot).wait_send()

    def finish(self, step):
        chip, chips, count = self.chip, self.chips, self.count

        @pl.when((chip + 1 < chips) & (chip >= step))
        def _():
            for i in range(count):
                self.to_right(i, step).wait_send()

        @pl.when((chip >= 1) & (chip + step < chips))
        def _():
            for i in range(count):
                self.to_left(i, step).wait_send()

        @pl.when(chip >= step + 1)
        def _():
            for i in range(count):
                self.across(i, chips - 1 - step).wait()

        @pl.when(chip + step + 1 < chips)
        def _():
            for i in range(count):
                self.across(i, step + 1).wait()


def line_scratch(arrays, chips):
    count = len(arrays)
    return (
        [pltpu.VMEM(a.shape, a.dtype) for a in arrays if a is not None]
        + [pltpu.SemaphoreType.DMA((count,))]
        + [pltpu.SemaphoreType.DMA((count, chips - 1)) for unused in range(4)]
        + [pltpu.SemaphoreType.DMA((count, chips)) for unused in range(2)]
    )


def gather_kernel(dense, line, merged, steps, fsdp, chips, *refs):
    count = dense + line
    ins, refs = refs[:count], refs[count:]
    outs, scratch = list(refs[: count - merged + 1]), refs[count - merged + 1 :]
    columns, start = [], 0
    for ref in ins[:merged]:
        columns.append(outs[0].at[:, pl.ds(start, ref.shape[1])])
        start += ref.shape[1]
    outs = columns + outs[1:]
    ctx, me, chip, core, sibling = place()
    greet(chips, peers_of(me, fsdp) if dense else [], line > 0)
    if dense:
        own, scratch = scratch[: 5 * dense + 3], scratch[5 * dense + 3 :]
        first = DenseGather(
            ins[:dense],
            outs[:dense],
            (own[:dense],) + tuple(own[dense : dense + 3]) + (own[dense + 3 :],),
            fsdp,
        )
        first.start()
    if line:
        own, scratch = scratch[: line + 7], scratch[line + 7 :]
        second = LineGather(ins[dense:], outs[dense:], own, chips)
        for step in range(steps):
            second.send(step)
            if step == 0:
                second.own()
            if step == steps - 1 and dense:
                first.hand_on()
            second.receive(step)
            if step == 0:
                second.turn_own()
    if dense:
        first.finish()
    if line:
        second.finish_own()
        for step in range(steps):
            second.finish(step)


def gather(dense, merged, line, steps, fsdp, chips, collective_id):
    arrays = list(dense) + list(line)
    joined = sum(a.shape[1] for a in dense[:merged])
    shapes = [(fsdp * dense[0].shape[0], joined)]
    shapes += [(fsdp * a.shape[0],) + a.shape[1:] for a in dense[merged:]]
    shapes += [(2, chips) + a.shape for a in line]
    return pl.pallas_call(
        functools.partial(gather_kernel, len(dense), len(line), merged, steps, fsdp, chips),
        out_shape=[jax.ShapeDtypeStruct(shape, BF16) for shape in shapes],
        in_specs=[pl.BlockSpec(memory_space=pl.ANY)] * len(arrays),
        out_specs=[pl.BlockSpec(memory_space=pl.ANY)] * len(shapes),
        scratch_shapes=dense_scratch(dense, fsdp) + line_scratch(line, chips),
        compiler_params=pltpu.CompilerParams(
            collective_id=collective_id, has_side_effects=True, vmem_limit_bytes=VMEM_BYTES
        ),
        name="gather",
    )(*arrays)


def add(*parts):
    total = parts[0].astype(F32)
    for part in parts[1:]:
        total = total + part.astype(F32)
    return total


def add_into(target, parts):
    rows = target.shape[0]
    tile = 32 if rows % 32 == 0 else 16

    def some(t, carry):
        part = pl.ds(pl.multiple_of(t * tile, tile), tile)
        target[part, :] = add(*[ref[part, :] for ref in parts]).astype(target.dtype)
        return carry

    lax.fori_loop(0, rows // tile, some, 0)


class LineSum:
    def __init__(self, chips, held, keep, got, sems):
        self.chips, self.held, self.keep, self.got = chips, held, keep, got
        self.sems = sems
        self.ctx, self.me, self.chip, core, sibling = place()

    def right(self, step):
        return remote(
            self.keep(self.chips - 1 - step),
            self.got.at[step - self.chip],
            self.sems[0].at[step],
            self.sems[1].at[step],
            (self.ctx + 2, self.me),
        )

    def from_left(self, step):
        slot = step + 1 - self.chip
        pltpu.make_async_remote_copy(
            src_ref=self.keep(self.chips - 1 - step),
            dst_ref=self.got.at[slot],
            send_sem=self.sems[0].at[step],
            recv_sem=self.sems[1].at[step],
            device_id=(self.ctx - 2, self.me),
            device_id_type=MESH,
        ).wait_recv()
        return self.got.at[slot]

    def from_right(self, step):
        slot = step + 2
        self.left(step).wait_recv()
        return self.got.at[slot]

    def left(self, step):
        return remote(
            self.keep(step + 1),
            self.got.at[step + 2],
            self.sems[2].at[step],
            self.sems[3].at[step],
            (self.ctx - 2, self.me),
        )

    def step(self, step):
        chip, chips = self.chip, self.chips
        far_right, far_left = chips - 1 - step, step + 1

        @pl.when(chip <= step)
        def _():
            parts = self.held(far_right)
            if step == 0:
                add_into(self.keep(far_right), parts())
            else:

                @pl.when(chip == 0)
                def _():
                    add_into(self.keep(far_right), parts())

                @pl.when(chip >= 1)
                def _():
                    add_into(self.keep(far_right), [self.from_left(step - 1)] + parts())

            self.right(step).start()

        @pl.when(chip >= chips - 1 - step)
        def _():
            parts = self.held(far_left)
            if step == 0:
                add_into(self.keep(far_left), parts())
            else:

                @pl.when(chip == chips - 1)
                def _():
                    add_into(self.keep(far_left), parts())

                @pl.when(chip < chips - 1)
                def _():
                    add_into(self.keep(far_left), [self.from_right(step - 1)] + parts())

            self.left(step).start()

    def total(self, target):
        chip, chips, last = self.chip, self.chips, self.chips - 2
        parts = self.held(0)

        @pl.when(chip == 0)
        def _():
            add_into(target, [self.from_right(last)] + parts())

        @pl.when(chip == chips - 1)
        def _():
            add_into(target, [self.from_left(last)] + parts())

        @pl.when((chip >= 1) & (chip < chips - 1))
        def _():
            add_into(target, [self.from_right(last), self.from_left(last)] + parts())

    def finish(self, steps=None):
        for step in range(self.chips - 1 if steps is None else steps):

            @pl.when(self.chip <= step)
            def _():
                self.right(step).wait_send()

            @pl.when(self.chip >= self.chips - 1 - step)
            def _():
                self.left(step).wait_send()


DENSE_BUFFERS = 5
DENSE_SEMS = 14


class DenseSum:
    def __init__(self, local, held, out, buffers, sems, fsdp, chips):
        self.local, self.held, self.out = local, held, out
        self.pair, self.cross, self.sums, got, self.spread = buffers
        self.sems = sems
        self.chips = chips
        self.ctx, self.me, self.chip, self.core, self.sibling = place()
        self.owners = peers_of(self.me, fsdp) + [self.me]
        self.cut = out.shape[2] // chips
        self.line = LineSum(
            chips,
            lambda r: lambda: [self.keep_ref(r)],
            lambda r: self.keep_ref(r),
            got,
            sems[4:8],
        )

    def keep_ref(self, r):
        return self.sums.at[:, self.columns(r)]

    def columns(self, r):
        owner = lax.rem(self.chip + r, self.chips)
        return pl.ds(pl.multiple_of(owner * self.cut, LANES), self.cut)

    def swap(self, j):
        return remote(
            self.local.at[self.owners[j], 1 - self.core],
            self.pair.at[j],
            self.sems[0].at[j],
            self.sems[1].at[j],
            (self.sibling, self.me),
        )

    def crossing(self, j):
        return remote(
            self.pair.at[j],
            self.cross.at[j],
            self.sems[2].at[j],
            self.sems[3].at[j],
            (self.ctx, self.owners[j]),
        )

    def to_right(self, step):
        return remote(
            self.spread.at[0, (self.chips - step) % self.chips],
            self.spread.at[0, self.chips - 1 - step],
            self.sems[8].at[step],
            self.sems[9].at[step],
            (self.ctx + 2, self.me),
        )

    def to_left(self, step):
        return remote(
            self.spread.at[0, step],
            self.spread.at[0, step + 1],
            self.sems[10].at[step],
            self.sems[11].at[step],
            (self.ctx - 2, self.me),
        )

    def across(self, slot):
        return remote(
            self.spread.at[0, slot],
            self.spread.at[1, slot],
            self.sems[12].at[slot],
            self.sems[13].at[slot],
            (self.sibling, self.me),
        )

    def start(self):
        for j in range(len(self.owners)):
            self.swap(j).start()

    def cross_over(self):
        for j, owner in enumerate(self.owners):
            self.swap(j).wait_recv()
            add_into(self.pair.at[j], [self.held(j, owner), self.pair.at[j]])
            if j < len(self.owners) - 1:
                self.crossing(j).start()

    def stages(self):
        chip, chips = self.chip, self.chips

        def open_up():
            for j in range(len(self.owners) - 1):
                self.crossing(j).wait_recv()
            add_into(
                self.sums,
                [self.cross.at[j] for j in range(len(self.owners) - 1)]
                + [self.pair.at[len(self.owners) - 1]],
            )
            self.line.step(0)

        def summed():
            self.line.total(self.spread.at[0, 0])
            hand_on(0)

        def hand_on(step):
            @pl.when((chip + 1 < chips) & (chip >= step))
            def _():
                self.to_right(step).start()

            @pl.when((chip >= 1) & (chip + step < chips))
            def _():
                self.to_left(step).start()

            if step == 0:
                self.across(0).start()

        def take(step):
            @pl.when(chip >= step + 1)
            def _():
                self.to_right(step).wait_recv()
                self.across(chips - 1 - step).start()

            @pl.when(chip + step + 1 < chips)
            def _():
                self.to_left(step).wait_recv()
                self.across(step + 1).start()

        def pass_on(step):
            def run():
                take(step - 1)
                hand_on(step)

            return run

        def line_step(step):
            return lambda: self.line.step(step)

        return (
            [open_up]
            + [line_step(step) for step in range(1, chips - 1)]
            + [summed]
            + [pass_on(step) for step in range(1, chips - 1)]
            + [lambda: take(chips - 2)]
        )

    def finish(self):
        chip, chips = self.chip, self.chips
        for r in range(chips):
            self.out[self.core, :, self.columns(r)] = self.spread[0, r]
        for r in range(chips):
            self.across(r).wait()
            self.out[1 - self.core, :, self.columns(r)] = self.spread[1, r]
        for step in range(chips - 1):

            @pl.when((chip + 1 < chips) & (chip >= step))
            def _():
                self.to_right(step).wait_send()

            @pl.when((chip >= 1) & (chip + step < chips))
            def _():
                self.to_left(step).wait_send()

        self.line.finish()
        for j in range(len(self.owners) - 1):
            self.crossing(j).wait_send()
        for j in range(len(self.owners)):
            self.swap(j).wait_send()


def dense_reduce_kernel(fsdp, chips, cuts, *refs):
    count = len(cuts)
    arrays = max(cut[0] for cut in cuts) + 1
    ins, refs = [None] + list(refs[: arrays - 1]), refs[arrays - 1 :]
    right_ref, left_ref, gain_ref = refs[:3]
    loaded, refs = refs[3:10], refs[10:]
    outs, total_ref, input_ref, refs = (
        refs[:arrays],
        refs[arrays],
        refs[arrays + 1],
        refs[arrays + 2 :],
    )
    from_left, from_right, r_send, r_recv, l_send, l_recv = refs[:6]
    small_v, local_v, load_sem = refs[6:9]
    held, rest = refs[9:16], refs[16:]
    normed_ref, dq_ref, dkv_ref, qkv_v, tokens_ref, middle_ref, own_ref = held
    loads = [
        pltpu.make_async_copy(src, dst, load_sem.at[k])
        for k, (src, dst) in enumerate(zip(loaded, held))
    ]
    for copy in loads:
        copy.start()
    ctx, me, chip, core, sibling = place()
    greet(chips, peers_of(me, fsdp), True)

    to_right = remote(right_ref, from_left, r_send, r_recv, (ctx + 2, me))
    to_left = remote(left_ref, from_right, l_send, l_recv, (ctx - 2, me))

    @pl.when(chip + 1 < chips)
    def _():
        to_right.start()

    @pl.when(chip >= 1)
    def _():
        to_left.start()

    sums = []
    for i, (which, start, size) in enumerate(cuts):
        buffers = rest[i * DENSE_BUFFERS : (i + 1) * DENSE_BUFFERS]
        sems = rest[count * DENSE_BUFFERS + i * DENSE_SEMS :][:DENSE_SEMS]
        local = (local_v, small_v, ins[-1])[which].at[:, :, :, pl.ds(start, size)]
        sums.append(
            DenseSum(
                local,
                lambda j, owner, local=local: local.at[owner, core],
                outs[which].at[:, :, pl.ds(start, size)],
                buffers,
                sems,
                fsdp,
                chips,
            )
        )
    large = [one for one, cut in zip(sums, cuts) if cut[0] != 1]
    small = [one for one, cut in zip(sums, cuts) if cut[0] == 1]
    rows, width = tokens_ref.shape
    shard = width // fsdp
    per = 1 if shard % LANES == 0 else 2
    for copy in loads[:3]:
        copy.wait()
    for one, (which, start, size) in zip(sums, cuts):
        if which == 0:
            for f in range(0, fsdp, per):
                left = normed_ref[:, f * shard : (f + per) * shard]
                for begin in range(start, start + size, KEY_TILE):
                    right = (
                        dq_ref[:, begin : begin + KEY_TILE]
                        if begin < width
                        else dkv_ref[:, begin - width : begin - width + KEY_TILE]
                    )
                    value = dot(left, right, TN).astype(BF16)
                    for k in range(2 * per):
                        local_v[f + k // 2, k % 2, :, begin : begin + KEY_TILE] = value[
                            k * shard // 2 : (k + 1) * shard // 2, :
                        ]
        if which != 1:
            one.start()
    for one in large:
        one.cross_over()

    for copy in loads[3:]:
        copy.wait()
    gain_grad = jnp.zeros((1, width), F32)
    for part in (pl.ds(0, rows // 2), pl.ds(rows // 2, rows // 2)):
        grad = dot(dq_ref[part, :], qkv_v[:, :width], NT)
        grad = grad + dot(dkv_ref[part, :], qkv_v[:, width:], NT)
        value = tokens_ref[part, :].astype(F32)
        scale = lax.rsqrt(jnp.mean(value * value, axis=-1, keepdims=True) + EPSILON)
        unit = value * scale
        scaled = grad * gain_ref[...]
        slope = jnp.mean(scaled * unit, axis=-1, keepdims=True)
        input_ref[part, :] = (middle_ref[part, :] + scale * (scaled - unit * slope)).astype(BF16)
        gain_grad = gain_grad + jnp.sum(grad * unit, axis=0, keepdims=True)
    small_v[...] = ins[1][...]
    first_row = lax.broadcasted_iota(jnp.int32, (small_v.shape[2], shard), 0) == 0
    for f in range(fsdp):
        held = small_v[f, 1, :, :shard].astype(F32)
        mine = jnp.broadcast_to(gain_grad[:, f * shard : (f + 1) * shard], held.shape)
        small_v[f, 1, :, :shard] = jnp.where(first_row, mine, held).astype(BF16)
    for one in small:
        one.start()
    for one in small:
        one.cross_over()

    stages = [one.stages() for one in sums]
    lag = chips - 1
    offsets = []
    for which, start, size in cuts:
        turn = sum(1 for other in cuts[: len(offsets)] if other[0] != 1)
        offsets.append(lag * (max(0, turn - 1) if which == 1 else turn))
    for tick in range(len(stages[0]) + max(offsets)):
        for i in range(count):
            if 0 <= tick - offsets[i] < len(stages[i]):
                stages[i][tick - offsets[i]]()
    @pl.when(chip >= 1)
    def _():
        to_right.wait_recv()

    @pl.when(chip + 1 < chips)
    def _():
        to_left.wait_recv()

    @pl.when(chip == 0)
    def _():
        add_into(total_ref, [from_right, own_ref])

    @pl.when(chip == chips - 1)
    def _():
        add_into(total_ref, [from_left, own_ref])

    @pl.when((chip >= 1) & (chip + 1 < chips))
    def _():
        add_into(total_ref, [from_left, from_right, own_ref])

    for one in sums:
        one.finish()

    @pl.when(chip + 1 < chips)
    def _():
        to_right.wait_send()

    @pl.when(chip >= 1)
    def _():
        to_left.wait_send()


def dense_buffers(rows, size, fsdp, chips):
    cut = size // chips
    return [
        pltpu.VMEM((fsdp, rows, size), BF16),
        pltpu.VMEM((fsdp - 1, rows, size), BF16),
        pltpu.VMEM((rows, size), BF16),
        pltpu.VMEM((chips + 1, rows, cut), BF16),
        pltpu.VMEM((2, chips, rows, cut), BF16),
    ]


def dense_sems(fsdp, chips):
    return (
        [pltpu.SemaphoreType.DMA((fsdp,)) for unused in range(2)]
        + [pltpu.SemaphoreType.DMA((fsdp - 1,)) for unused in range(2)]
        + [pltpu.SemaphoreType.DMA((chips - 1,)) for unused in range(8)]
        + [pltpu.SemaphoreType.DMA((chips,)) for unused in range(2)]
    )


def dense_reduce(
    arrays,
    own,
    right,
    left,
    query_grad,
    kv_grad,
    normed,
    tokens,
    middle_grad,
    gain,
    qkv,
    piece,
    fsdp,
    chips,
    collective_id,
):
    vmem = pl.BlockSpec(memory_space=pltpu.VMEM)
    cuts, buffers = [], []
    for i, a in enumerate(arrays):
        rows, width = a.shape[2:]
        for start in range(0, width, piece):
            size = min(piece, width - start)
            cuts.append((i, start, size))
            buffers += dense_buffers(rows, size, fsdp, chips)
    sems = dense_sems(fsdp, chips)
    loaded = [normed, query_grad, kv_grad, qkv, tokens, middle_grad, own]
    anywhere = pl.BlockSpec(memory_space=pl.ANY)
    return pl.pallas_call(
        functools.partial(dense_reduce_kernel, fsdp, chips, tuple(cuts)),
        out_shape=[jax.ShapeDtypeStruct(a.shape[1:], BF16) for a in arrays]
        + [jax.ShapeDtypeStruct(own.shape, F32), jax.ShapeDtypeStruct(tokens.shape, BF16)],
        in_specs=[vmem] * (len(arrays) - 1)
        + [anywhere, anywhere, vmem]
        + [anywhere] * 7,
        out_specs=[vmem] * (len(arrays) + 2),
        scratch_shapes=[pltpu.VMEM(own.shape, BF16)] * 2
        + [pltpu.SemaphoreType.DMA] * 4
        + [
            pltpu.VMEM(arrays[1].shape, BF16),
            pltpu.VMEM(arrays[0].shape, BF16),
            pltpu.SemaphoreType.DMA((len(loaded),)),
        ]
        + [pltpu.VMEM(a.shape, a.dtype) for a in loaded]
        + buffers
        + sems * len(cuts),
        compiler_params=pltpu.CompilerParams(
            collective_id=collective_id, has_side_effects=True, vmem_limit_bytes=DENSE_VMEM_BYTES
        ),
        name="dense_reduce",
    )(
        *arrays[1:],
        right,
        left,
        gain[None, :],
        *loaded,
    )


def after(value, *others):
    return lax.optimization_barrier((value,) + others)[0]


def chunk_order(chip, i, chips):
    right_half = lax.div(2 * chip, chips)
    near = chip + right_half * (chips - 1 - 2 * chip)
    alone = chips - 1 - 2 * near
    paired = lax.div(i - alone + chips, chips)
    turn = (i - alone) * paired
    odd = lax.rem(turn, 2)
    pair = lax.div(turn, 2)
    distance = (1 - paired) * (chips - 1 - near - i) + paired * (
        (1 - odd) * (near - pair) + odd * (chips - near + pair)
    )
    return lax.rem(distance + right_half * (chips - 2 * distance), chips)


def front_kernel(
    scale,
    chips,
    fsdp,
    expert_count,
    tokens_ref,
    gain_a_ref,
    gain_b_ref,
    small_ref,
    cos_ref,
    sin_ref,
    oq_ref,
    pq_ref,
    ok_ref,
    routed_ref,
    table_ref,
    qkv_ref,
    wo_ref,
    gate_w_ref,
    passed_ref,
    table_all_ref,
    lse_ref,
    gate_ref,
    weights_ref,
    q_hbm,
    normed_hbm,
    kv_hbm,
    attended_hbm,
    middle_hbm,
    hidden_hbm,
    hidden_all_ref,
    gate_full_ref,
    grad_ref,
    q_ref,
    normed_ref,
    kv_ref,
    attended_ref,
    middle_ref,
    qkv_v,
    wo_v,
    gate_v,
    hidden_v,
    bias,
    top,
    total,
    acc,
    load_sem,
    own_sem,
    gate_own,
    gate_s0,
    gate_s1,
    gate_s2,
    gate_s3,
    keep_sem,
    *line_sems,
):
    ctx, me, chip, core, sibling = place()
    rows = tokens_ref.shape[0]
    width = tokens_ref.shape[1]
    half = rows // 2
    kv_width = KVH * HEAD_SIZE
    per_group = QUERY_HEADS // KVH
    parts = [pl.ds(0, half), pl.ds(half, half)]
    loads = [
        pltpu.make_async_copy(src, dst, load_sem.at[k])
        for k, (src, dst) in enumerate(((qkv_ref, qkv_v), (wo_ref, wo_v)))
    ]
    for copy in loads:
        copy.start()
    greet(chips, peers_of(me, fsdp), True)
    gate_gather = ShardGather(
        gate_w_ref,
        gate_full_ref,
        gate_v,
        (gate_own, gate_s0, gate_s1, gate_s2, gate_s3),
        fsdp,
    )
    gate_gather.start()
    kv_line = LineGather(
        [kv_ref.at[0, 0], table_all_ref.at[0, 0]], [kv_ref, table_all_ref], line_sems[:7], chips
    )
    grad_line = LineGather([None], [grad_ref], line_sems[7:14], chips)
    hidden_lines = [
        LineGather(
            [hidden_v.at[parts[0]]], [hidden_all_ref.at[:, :, parts[0]]], line_sems[14:21], chips
        ),
        LineGather(
            [hidden_v.at[parts[1]], weights_ref.at[0, 0]],
            [hidden_all_ref.at[:, :, parts[1]], weights_ref],
            line_sems[21:28],
            chips,
        ),
    ]

    def normed(value, gain):
        return value * lax.rsqrt(jnp.mean(value * value, axis=-1, keepdims=True) + EPSILON) * gain

    table_all_ref[0, 0] = table_ref[...]
    for part in parts:
        normed_ref[part, :] = normed(
            tokens_ref[part, :].astype(F32), gain_a_ref[...]
        ).astype(BF16)
    loads[0].wait()
    for part in parts:
        rows_one = normed_ref[part, :]
        cosine, sine = cos_ref[part, :], sin_ref[part, :]
        for h in range(KVH):
            columns = slice(width + h * HEAD_SIZE, width + (h + 1) * HEAD_SIZE)
            value = dot(rows_one, qkv_v[:, columns], NN)
            value = value * cosine + pltpu.roll(value, HEAD_SIZE // 2, 1) * sine
            kv_ref[0, 0, part, h * HEAD_SIZE : (h + 1) * HEAD_SIZE] = value.astype(BF16)
        kv_ref[0, 0, part, kv_width:] = dot(
            rows_one, qkv_v[:, width + kv_width :], NN
        ).astype(BF16)
    kv_line.send(0)
    for i in range(2):
        kv_line.across(i, 0).start()
    for part in parts:
        rows_one = normed_ref[part, :]
        cosine, sine = cos_ref[part, :], sin_ref[part, :]
        for h in range(0, QUERY_HEADS, 2):
            pre = dot(rows_one, qkv_v[:, h * HEAD_SIZE : (h + 2) * HEAD_SIZE], NN)
            for k in range(2):
                value = pre[:, k * HEAD_SIZE : (k + 1) * HEAD_SIZE]
                value = value * cosine + pltpu.roll(value, HEAD_SIZE // 2, 1) * sine
                q_ref[part, (h + k) * HEAD_SIZE : (h + k + 1) * HEAD_SIZE] = value.astype(BF16)

    def turn(index, r):
        part = parts[index]
        for q in range(2):
            gap = oq_ref[part, :] - ok_ref[q * chips + r]
            bias[:, q * rows : (q + 1) * rows] = jnp.where(
                (gap >= 0) & (gap <= pq_ref[part, :]), 0.0, MASKED
            )

        def one(h, carry):
            group = lax.div(h, per_group)
            columns = pl.ds(pl.multiple_of(h * HEAD_SIZE, HEAD_SIZE), HEAD_SIZE)
            key_columns = pl.ds(pl.multiple_of(group * HEAD_SIZE, HEAD_SIZE), HEAD_SIZE)
            value_columns = pl.ds(
                pl.multiple_of(kv_width + group * HEAD_SIZE, HEAD_SIZE), HEAD_SIZE
            )
            query = q_ref[part, columns]
            scores = []
            peak = top[h, part, :]
            for q in range(2):
                raw = dot(query, kv_ref[q, r, :, key_columns], NT) * (scale * LOG2E)
                raw = raw + bias[:, q * rows : (q + 1) * rows]
                scores.append(raw)
            best = scores[0][:, :LANES]
            for q in range(2):
                for k in range(rows // LANES):
                    best = jnp.maximum(best, scores[q][:, k * LANES : (k + 1) * LANES])
            new = jnp.maximum(peak, jnp.max(best, axis=1, keepdims=True))
            fade = jnp.exp2(peak - new)
            wide = jnp.concatenate([new] * (rows // LANES), axis=1)
            mass = total[h] * fade
            out = acc[:, columns] * fade
            for q in range(2):
                probs = jnp.exp2(scores[q] - wide)
                for k in range(rows // LANES):
                    mass = mass + probs[:, k * LANES : (k + 1) * LANES]
                out = out + dot(probs.astype(BF16), kv_ref[q, r, :, value_columns], NN)
            top[h, part, :] = new
            total[h] = mass
            acc[:, columns] = out
            return carry

        lax.fori_loop(0, QUERY_HEADS, one, 0)

    def begin(index):
        top[:, parts[index], :] = jnp.full((QUERY_HEADS, half, LANES), MASKED, F32)
        total[...] = jnp.zeros_like(total)
        acc[...] = jnp.zeros_like(acc)

    def end(index):
        part = parts[index]
        for h in range(QUERY_HEADS):
            columns = slice(h * HEAD_SIZE, (h + 1) * HEAD_SIZE)
            mass = jnp.sum(total[h], axis=1, keepdims=True)
            attended_ref[part, columns] = (acc[:, columns] / mass).astype(BF16)
            top[h, part, :] = top[h, part, :] + jnp.log2(mass)
        if index == 0:
            loads[1].wait()
        middle = tokens_ref[part, :].astype(F32) + dot(attended_ref[part, :], wo_v[...], NN)
        middle_ref[part, :] = middle
        rows_two = normed(middle, gain_b_ref[...]).astype(BF16)
        hidden_v[part, :] = rows_two
        routed = routed_ref[part, :] > 0.0
        logits = jnp.where(routed, dot(rows_two, small_ref[...], NN), MASKED)
        power = jnp.exp(logits - jnp.max(logits, axis=1, keepdims=True))
        power = jnp.where(routed, power, 0.0)
        gate_ref[part, :] = power / jnp.sum(power, axis=1, keepdims=True)
        if index == 1:
            weights_ref[0, 0] = gate_ref[...].T[:expert_count, :]
        line = hidden_lines[index]
        line.send(0)
        for i in range(line.count):
            line.across(i, 0).start()
        own(index).start()

    def keep(k, src, dst):
        return pltpu.make_async_copy(src, dst, keep_sem.at[k])

    def own(index):
        return pltpu.make_async_copy(
            hidden_v.at[parts[index]],
            hidden_all_ref.at[0, 0, parts[index]],
            own_sem.at[index],
        )

    begin(0)
    keep(0, q_ref, q_hbm).start()
    keep(1, normed_ref, normed_hbm).start()

    def first_turn(t, carry):
        for k in range(1, chips):

            @pl.when(t == k)
            def _():
                kv_line.receive(k - 1)
                if k < chips - 1:
                    kv_line.send(k)
                else:
                    grad_line.send(chips - 2)

        r = chunk_order(chip, chips - 1 - t, chips)
        kv_line.arrived(r)
        turn(0, r)
        return carry

    lax.fori_loop(0, chips, first_turn, 0)
    end(0)
    begin(1)
    gate_gather.hand_on()
    keep(2, kv_ref, kv_hbm).start()
    early = [step for step in range(chips - 1) if 2 * step + 2 < chips]

    def second_turn(t, carry):
        for step in early:

            @pl.when(t == 2 * step + 2)
            def _():
                hidden_lines[0].receive(step)
                if step + 1 < chips - 1:
                    hidden_lines[0].send(step + 1)

        turn(1, t)
        return carry

    lax.fori_loop(0, chips, second_turn, 0)
    grad_line.receive(chips - 2)
    late = [step for step in range(chips - 1) if step not in early]
    for step in late[:1]:
        hidden_lines[0].receive(step)
        if step + 1 < chips - 1:
            hidden_lines[0].send(step + 1)
    end(1)
    keep(3, attended_ref, attended_hbm).start()
    keep(4, middle_ref, middle_hbm).start()
    keep(5, hidden_v, hidden_hbm).start()
    for h in range(QUERY_HEADS):
        lse_ref[h] = top[h].T[:1, :]
    for step in late[1:]:
        hidden_lines[0].receive(step)
        if step + 1 < chips - 1:
            hidden_lines[0].send(step + 1)
    for step in range(chips - 1):
        hidden_lines[1].receive(step)
        if step + 1 < chips - 1:
            hidden_lines[1].send(step + 1)
    for line in hidden_lines:
        for slot in range(chips):
            line.arrived(slot)
        line.sent()
    kv_line.sent()
    gate_gather.finish()
    grad_line.finish(chips - 2)
    for index in range(2):
        own(index).wait()
    for k, (src, dst) in enumerate(
        (
            (q_ref, q_hbm),
            (normed_ref, normed_hbm),
            (kv_ref, kv_hbm),
            (attended_ref, attended_hbm),
            (middle_ref, middle_hbm),
            (hidden_v, hidden_hbm),
        )
    ):
        keep(k, src, dst).wait()


def front(
    tokens,
    gain_a,
    gain_b,
    small,
    cosine,
    sine,
    order_mine,
    pos_mine,
    order_keys,
    routed,
    table,
    qkv,
    w_out,
    w_gate,
    grad_all,
    chips,
    fsdp,
    collective_id,
):
    rows, width = tokens.shape
    expert_count = table.shape[0]
    kv_width = KVH * HEAD_SIZE
    vmem = pl.BlockSpec(memory_space=pltpu.VMEM)
    anywhere = pl.BlockSpec(memory_space=pl.ANY)
    shapes = [
        ((2, chips, expert_count, rows), F32),
        ((QUERY_HEADS, 1, rows), F32),
        ((rows, LANES), F32),
        ((2, chips, expert_count, rows), F32),
    ]
    kept = [
        ((rows, width), BF16),
        ((rows, width), BF16),
        ((2, chips, rows, 2 * kv_width), BF16),
        ((rows, width), BF16),
        ((rows, width), F32),
    ]
    gathered = [
        ((rows, width), BF16),
        ((2, chips, rows, width), BF16),
        ((w_gate.shape[0], width, w_gate.shape[2]), BF16),
        (grad_all.shape, BF16),
    ]
    flops = 4 * rows * (2 * chips * rows) * width + 2 * rows * width * (2 * width + 2 * kv_width)
    return pl.pallas_call(
        functools.partial(front_kernel, HEAD_SIZE ** (-0.5), chips, fsdp, expert_count),
        out_shape=[
            jax.ShapeDtypeStruct(shape, kind) for shape, kind in shapes + kept + gathered
        ],
        in_specs=[vmem] * 11 + [anywhere] * 4,
        out_specs=[vmem] * 4 + [anywhere] * 9,
        scratch_shapes=[pltpu.VMEM(shape, kind) for shape, kind in kept]
        + [
            pltpu.VMEM(qkv.shape, BF16),
            pltpu.VMEM(w_out.shape, BF16),
            pltpu.VMEM(w_gate.shape, BF16),
            pltpu.VMEM((rows, width), BF16),
            pltpu.VMEM((rows // 2, 2 * rows), F32),
            pltpu.VMEM((QUERY_HEADS, rows, LANES), F32),
            pltpu.VMEM((QUERY_HEADS, rows // 2, LANES), F32),
            pltpu.VMEM((rows // 2, width), F32),
            pltpu.SemaphoreType.DMA((2,)),
            pltpu.SemaphoreType.DMA((2,)),
            pltpu.SemaphoreType.DMA,
        ]
        + spread_sems(fsdp)
        + [pltpu.SemaphoreType.DMA((6,))]
        + line_scratch([None] * 2, chips)
        + line_scratch([None], chips)
        + line_scratch([None], chips)
        + line_scratch([None] * 2, chips),
        input_output_aliases={14: 12},
        compiler_params=pltpu.CompilerParams(
            collective_id=collective_id, has_side_effects=True, vmem_limit_bytes=FRONT_VMEM_BYTES
        ),
        cost_estimate=pl.CostEstimate(
            flops=flops, bytes_accessed=40_000_000, transcendentals=rows * rows * chips * 24
        ),
        name="front",
    )(
        tokens,
        gain_a[None, :],
        gain_b[None, :],
        small,
        cosine,
        sine,
        order_mine[:, None],
        pos_mine[:, None],
        order_keys.reshape(2 * chips, 1, rows),
        routed,
        table,
        qkv,
        w_out,
        w_gate,
        grad_all,
    )


def attention_back_kernel(
    scale,
    chips,
    fsdp,
    early_dense,
    q_ref,
    k_ref,
    v_ref,
    o_ref,
    do_ref,
    lse_ref,
    oq_ref,
    pq_ref,
    ok_ref,
    cos_ref,
    sin_ref,
    rows_ref,
    dense_ref,
    dq_ref,
    kv_ref,
    own_ref,
    right_ref,
    left_ref,
    dense_out_ref,
    bias,
    dk_acc,
    dv_acc,
    kv_total,
    mine_v,
    pair,
    got,
    kv_v,
    kv_pair,
    kv_got,
    load_sem,
    store_sem,
    swap_send,
    swap_recv,
    r_send,
    r_recv,
    l_send,
    l_recv,
    kv_swap_send,
    kv_swap_recv,
    kr_send,
    kr_recv,
    kl_send,
    kl_recv,
    *dense_refs,
):
    ctx, me, chip, core, sibling = place()
    keys = k_ref.shape[0]
    tiles = keys // KEY_TILE
    rows = q_ref.shape[0]
    per_group = QUERY_HEADS // KVH
    head = pl.program_id(0)

    order = []
    for step in range(chips - 1):
        for r in (chips - 1 - step, step + 1):
            if r not in order:
                order.append(r)
    order.append(0)
    swaps = [
        remote(rows_ref.at[1, r], pair.at[r], swap_send.at[r], swap_recv.at[r], (sibling, me))
        for r in range(chips)
    ]
    slots = mine_v.shape[0]
    loads = [
        pltpu.make_async_copy(rows_ref.at[0, r], mine_v.at[j % slots], load_sem.at[j % slots])
        for j, r in enumerate(order)
    ]
    line = LineSum(
        chips,
        lambda r: lambda: [pair.at[r]],
        lambda r: pair.at[r],
        got,
        (r_send, r_recv, l_send, l_recv),
    )

    def join(j):
        loads[j].wait()
        swaps[order[j]].wait_recv()
        add_into(pair.at[order[j]], [pair.at[order[j]], mine_v.at[j % slots]])
        if j + slots < chips:
            loads[j + slots].start()

    if early_dense:
        dense_v, dense_load = dense_refs[:2]
        buffers = dense_refs[2 : 2 + DENSE_BUFFERS]
        dense = DenseSum(
            dense_ref,
            lambda j, owner: dense_v.at[j],
            dense_out_ref,
            buffers,
            dense_refs[2 + DENSE_BUFFERS :],
            fsdp,
            chips,
        )
        dense_loads = [
            pltpu.make_async_copy(dense_ref.at[owner, core], dense_v.at[j], dense_load.at[j])
            for j, owner in enumerate(dense.owners)
        ]
        stages = dense.stages()
        at_head = {QUERY_HEADS - 1 - len(stages) // 2 + k: k for k in range(len(stages) // 2)}

    def kv_swap(group, r):
        return remote(
            kv_v.at[group, 1, r],
            kv_pair.at[group, r],
            kv_swap_send.at[group, r],
            kv_swap_recv.at[group, r],
            (sibling, me),
        )

    def kv_line(group):
        def held(r):
            kv_swap(group, r).wait_recv()
            return lambda: [kv_v.at[group, 0, r], kv_pair.at[group, r]]

        return LineSum(
            chips,
            held,
            lambda r: kv_pair.at[group, r],
            kv_got.at[group],
            tuple(sem.at[group] for sem in (kr_send, kr_recv, kl_send, kl_recv)),
        )

    def kv_start(group):
        for q in range(2):
            for r in range(chips):
                part = pl.ds((q * chips + r) * rows, rows)
                kv_v[group, q, r, :, :HEAD_SIZE] = (dk_acc[part, :] * scale).astype(BF16)
                kv_v[group, q, r, :, HEAD_SIZE:] = dv_acc[part, :].astype(BF16)
        for r in order:
            kv_swap(group, r).start()

    @pl.when(head == 0)
    def _():
        greet(chips, peers_of(me, fsdp) if early_dense else [], True)
        if early_dense:
            for copy in dense_loads:
                copy.start()
            dense.start()
        for r in order:
            swaps[r].start()
        for copy in loads[:slots]:
            copy.start()

        def fill(t, carry):
            tile = pl.ds(pl.multiple_of(t * KEY_TILE, KEY_TILE), KEY_TILE)
            key_order = jnp.broadcast_to(ok_ref[:, tile], (8, KEY_TILE)).T[:, :1]
            gap = oq_ref[...] - key_order
            bias[tile, :] = jnp.where((gap >= 0) & (gap <= pq_ref[...]), 0.0, MASKED)
            return carry

        lax.fori_loop(0, tiles, fill, 0)

    @pl.when(lax.rem(head, per_group) == 0)
    def _():
        dk_acc[...] = jnp.zeros_like(dk_acc)
        dv_acc[...] = jnp.zeros_like(dv_acc)

    query = q_ref[...]
    grad = do_ref[...]
    lse = lse_ref[0]
    product = grad.astype(F32) * o_ref[...].astype(F32)
    delta = jnp.sum(product.T, axis=0, keepdims=True)

    def step(t, acc):
        tile = pl.ds(pl.multiple_of(t * KEY_TILE, KEY_TILE), KEY_TILE)
        key = k_ref[tile, :]
        raw = dot(key, query, NT) * (scale * LOG2E) + bias[tile, :]
        probs = jnp.exp2(raw - lse)
        prob_grad = dot(v_ref[tile, :], grad, NT)
        score_grad = (probs * (prob_grad - delta)).astype(BF16)
        dv_acc[tile, :] += dot(probs.astype(BF16), grad, NN)
        dk_acc[tile, :] += dot(score_grad, query, NN)
        return acc + dot(score_grad, key, TN)

    acc = lax.fori_loop(0, tiles, step, jnp.zeros((rows, HEAD_SIZE), F32))
    def turn_back(value):
        back = value * cos_ref[...] - pltpu.roll(value, HEAD_SIZE // 2, 1) * sin_ref[...]
        return back.astype(BF16)

    dq_ref[...] = turn_back(acc * scale)

    last = QUERY_HEADS - 1
    stride = max(1, last // (chips - 2))
    early = {per_group + 2 * s: s for s in range(chips - 1) if per_group + 2 * s < last}
    for h in range(QUERY_HEADS):

        @pl.when(head == h)
        def _():
            if h == 0:
                for j in range(min(2, chips)):
                    join(j)
            if h == 1:
                for j in range(2, chips):
                    join(j)
            if early_dense and h == 1:
                for copy in dense_loads:
                    copy.wait()
                dense.cross_over()
            if early_dense and h in at_head:
                stages[at_head[h]]()
            for s in range(chips - 2):
                if h == (s * stride if s == 0 else max(1, s * stride)):
                    line.step(s)
            if h % per_group == per_group - 1:
                kv_start(h // per_group)
            if h in early:
                kv_line(0).step(early[h])

    @pl.when(head == last)
    def _():
        def store(k, r, target):
            return pltpu.make_async_copy(pair.at[r], target, store_sem.at[k])

        @pl.when((chip >= 1) & (chip + 1 < chips))
        def _():
            add_into(pair.at[1], [pair.at[1], line.from_left(chips - 3)])
            add_into(pair.at[chips - 1], [pair.at[chips - 1], line.from_right(chips - 3)])

        for copy in (
            store(0, 0, own_ref),
            store(1, 1, right_ref),
            store(2, chips - 1, left_ref),
        ):
            copy.start()
        rest = stages[len(stages) // 2 :] if early_dense else []
        for group in range(KVH):
            one = kv_line(group)
            for s in range(chips - 1):
                if group > 0 or s not in early.values():
                    one.step(s)
                    if rest:
                        rest.pop(0)()
            one.total(kv_total)
            kv_ref[:, group * HEAD_SIZE : (group + 1) * HEAD_SIZE] = turn_back(
                kv_total[:, :HEAD_SIZE]
            )
            kv_ref[:, (KVH + group) * HEAD_SIZE : (KVH + group + 1) * HEAD_SIZE] = kv_total[
                :, HEAD_SIZE:
            ].astype(BF16)
        for stage in rest:
            stage()
        if early_dense:
            dense.finish()
        for group in range(KVH):
            kv_line(group).finish()
            for r in range(chips):
                kv_swap(group, r).wait_send()
        line.finish(chips - 2)
        for swap in swaps:
            swap.wait_send()
        for copy in (
            store(0, 0, own_ref),
            store(1, 1, right_ref),
            store(2, chips - 1, left_ref),
        ):
            copy.wait()


def attention_back(
    queries,
    kv,
    attended,
    attended_grad,
    lse,
    order_mine,
    pos_mine,
    order_keys,
    cosine,
    sine,
    out_rows,
    dense,
    fsdp,
    early_dense,
    collective_id,
):
    rows = queries.shape[0]
    keys = kv.shape[0]
    unused, chips, unused, width = out_rows.shape
    per_group = QUERY_HEADS // KVH
    head_rows = pl.BlockSpec((rows, HEAD_SIZE), lambda h: (0, h))
    anywhere = pl.BlockSpec(memory_space=pl.ANY)
    return pl.pallas_call(
        functools.partial(
            attention_back_kernel, HEAD_SIZE ** (-0.5), chips, fsdp, early_dense
        ),
        grid=(QUERY_HEADS,),
        out_shape=[
            jax.ShapeDtypeStruct(queries.shape, BF16),
            jax.ShapeDtypeStruct((rows, 2 * KVH * HEAD_SIZE), BF16),
        ]
        + [jax.ShapeDtypeStruct((rows, width), BF16)] * 3
        + [jax.ShapeDtypeStruct(dense.shape[1:] if early_dense else (16, LANES), BF16)],
        in_specs=[
            head_rows,
            pl.BlockSpec((keys, HEAD_SIZE), lambda h: (0, h // per_group)),
            pl.BlockSpec((keys, HEAD_SIZE), lambda h: (0, KVH + h // per_group)),
            head_rows,
            head_rows,
            pl.BlockSpec((1, 1, rows), lambda h: (h, 0, 0)),
            pl.BlockSpec((1, rows), lambda h: (0, 0)),
            pl.BlockSpec((1, rows), lambda h: (0, 0)),
            pl.BlockSpec((1, keys), lambda h: (0, 0)),
            pl.BlockSpec((rows, HEAD_SIZE), lambda h: (0, 0)),
            pl.BlockSpec((rows, HEAD_SIZE), lambda h: (0, 0)),
            anywhere,
            anywhere,
        ],
        out_specs=[
            head_rows,
            pl.BlockSpec((rows, 2 * KVH * HEAD_SIZE), lambda h: (0, 0)),
            anywhere,
            anywhere,
            anywhere,
            pl.BlockSpec(dense.shape[1:], lambda h: (0, 0, 0)) if early_dense else anywhere,
        ],
        scratch_shapes=[
            pltpu.VMEM((keys, rows), F32),
            pltpu.VMEM((keys, HEAD_SIZE), F32),
            pltpu.VMEM((keys, HEAD_SIZE), F32),
            pltpu.VMEM((rows, 2 * HEAD_SIZE), F32),
            pltpu.VMEM((2 if chips <= 4 else 1, rows, width), BF16),
            pltpu.VMEM((chips, rows, width), BF16),
            pltpu.VMEM((chips + 1, rows, width), BF16),
            pltpu.VMEM((KVH, 2, chips, rows, 2 * HEAD_SIZE), BF16),
            pltpu.VMEM((KVH, chips, rows, 2 * HEAD_SIZE), BF16),
            pltpu.VMEM((KVH, chips + 1, rows, 2 * HEAD_SIZE), BF16),
            pltpu.SemaphoreType.DMA((2,)),
            pltpu.SemaphoreType.DMA((3,)),
            pltpu.SemaphoreType.DMA((chips,)),
            pltpu.SemaphoreType.DMA((chips,)),
        ]
        + [pltpu.SemaphoreType.DMA((chips - 1,)) for unused in range(4)]
        + [pltpu.SemaphoreType.DMA((KVH, chips)) for unused in range(2)]
        + [pltpu.SemaphoreType.DMA((KVH, chips - 1)) for unused in range(4)]
        + (
            [
                pltpu.VMEM((fsdp,) + dense.shape[2:], BF16),
                pltpu.SemaphoreType.DMA((fsdp,)),
            ]
            + dense_buffers(dense.shape[2], dense.shape[3], fsdp, chips)
            + dense_sems(fsdp, chips)
            if early_dense
            else []
        ),
        compiler_params=pltpu.CompilerParams(
            collective_id=collective_id, has_side_effects=True, vmem_limit_bytes=BACK_VMEM_BYTES
        ),
        cost_estimate=pl.CostEstimate(
            flops=10 * rows * keys * HEAD_SIZE * QUERY_HEADS,
            bytes_accessed=10 * rows * QUERY_HEADS * HEAD_SIZE + 8 * keys * KVH * HEAD_SIZE,
            transcendentals=rows * keys * QUERY_HEADS,
        ),
        name="attention_back",
    )(
        queries,
        kv,
        kv,
        attended,
        attended_grad,
        lse,
        order_mine[None, :],
        pos_mine[None, :],
        order_keys[None, :],
        cosine,
        sine,
        out_rows,
        dense,
    )


def experts_kernel(
    capacity,
    local_experts,
    expert_count,
    chips,
    fsdp,
    per,
    hidden_ref,
    grad_ref,
    table_ref,
    weight_ref,
    gate_ref,
    up_ref,
    down_ref,
    returned_ref,
    out_ref,
    gate_grad_ref,
    gate_got_ref,
    up_grad_ref,
    down_grad_ref,
    x_ref,
    pg_ref,
    inner_ref,
    da_ref,
    db_ref,
    gate_v,
    up_v,
    down_v,
    hidden_v,
    grad_v,
    out_v,
    x_v,
    pg_v,
    g_v,
    inner_v,
    da_v,
    db_v,
    mine_v,
    other_v,
    pair,
    got,
    stage_tall,
    weight_sem,
    load_sem,
    out_sem,
    save_sem,
    swap_send,
    swap_recv,
    right_send,
    right_recv,
    left_send,
    left_recv,
    stage_sem,
    tile_own,
    tile_send,
    tile_recv,
):
    ctx, me, chip, core, sibling = place()
    peers = peers_of(me, fsdp)
    tokens = hidden_v.shape[1]
    width = hidden_v.shape[2]
    slots = x_v.shape[1]
    slot_rows = slots // 2
    units = inner_v.shape[2]
    total_rows = x_ref.shape[1]
    first = ctx * local_experts

    weights_in = [
        pltpu.make_async_copy(src, dst, weight_sem.at[k])
        for k, (src, dst) in enumerate(
            ((gate_ref, gate_v), (up_ref, up_v), (down_ref, down_v))
        )
    ]

    def load(i):
        r = chunk_order(chip, i, chips)
        return [
            pltpu.make_async_copy(hidden_ref.at[:, r], hidden_v, load_sem.at[0]),
            pltpu.make_async_copy(grad_ref.at[:, r], grad_v, load_sem.at[1]),
        ]

    def saves(i):
        rows = pl.ds(i * slots, slots)
        return [
            pltpu.make_async_copy(src, dst.at[:, rows], save_sem.at[k])
            for k, (src, dst) in enumerate(
                ((x_v, x_ref), (pg_v, pg_ref), (inner_v, inner_ref), (da_v, da_ref), (db_v, db_ref))
            )
        ]

    def out_copies(i):
        r = chunk_order(chip, i, chips)
        return [
            pltpu.make_async_copy(out_v.at[q], out_ref.at[q, r], out_sem.at[q]) for q in range(2)
        ]

    def swap(i):
        r = chunk_order(chip, i, chips)
        return remote(
            other_v.at[lax.rem(i, 2)],
            pair.at[r],
            swap_send.at[r],
            swap_recv.at[r],
            (sibling, me),
        )

    def join(i):
        r = chunk_order(chip, i, chips)
        swap(i).wait_recv()
        add_into(pair.at[r], [pair.at[r], mine_v.at[lax.rem(i, 2)]])

    line = LineSum(
        chips,
        lambda r: lambda: [pair.at[r]],
        lambda r: pair.at[r],
        got,
        (right_send, right_recv, left_send, left_recv),
    )

    for copy in load(0) + weights_in:
        copy.start()
    greet(chips, peers if per == 1 else [], True)

    slot = lax.broadcasted_iota(jnp.int32, (slot_rows, tokens), 0).astype(F32) + 1.0
    slot = jnp.where(slot <= capacity, slot, -1.0)
    lane = lax.broadcasted_iota(jnp.int32, (slots, LANES), 1)

    def chunk(i, carry):
        r = chunk_order(chip, i, chips)
        for copy in load(i):
            copy.wait()

        @pl.when(i >= 1)
        def _():
            for copy in saves(i - 1):
                copy.wait()

        picks = [[], []]
        weight_rows = []
        for e in range(local_experts):
            rows_w = []
            for q in range(2):
                hit = slot == table_ref[q, r, pl.ds(first + e, 1), :]
                pick = jnp.where(hit, 1.0, 0.0).astype(BF16)
                weight = weight_ref[q, r, pl.ds(first + e, 1), :]
                w = jnp.sum(jnp.where(hit, weight, 0.0), axis=1, keepdims=True)
                rows = pl.ds(q * slot_rows, slot_rows)
                x_v[e, rows, :] = dot(pick, hidden_v[q], NN).astype(BF16)
                g = dot(pick, grad_v[q], NN)
                g_v[e, rows, :] = g.astype(BF16)
                pg_v[e, rows, :] = (w * g).astype(BF16)
                picks[q].append(pick)
                rows_w.append(w)
            weight_rows.append(jnp.concatenate(rows_w, axis=0))

        @pl.when(i + 1 < chips)
        def _():
            for copy in load(i + 1):
                copy.start()

        @pl.when(i == 0)
        def _():
            for copy in weights_in:
                copy.wait()

        outs = [[], []]
        backs = [[], []]
        for e in range(local_experts):
            x = x_v[e]
            pair_grad = pg_v[e]
            w = weight_rows[e]
            gate = gate_v[e * width : (e + 1) * width, :]
            up = up_v[e * width : (e + 1) * width, :]
            down = down_v[e * units : (e + 1) * units, :]
            gate_pre = dot(x, gate, NN)
            up_pre = dot(x, up, NN)
            sig = jax.nn.sigmoid(gate_pre)
            silu = gate_pre * sig
            inner = (silu * up_pre).astype(BF16)
            inner_v[e] = inner
            expert_out = dot(inner, down, NN).astype(BF16).astype(F32)
            gate_grad = jnp.sum(expert_out * g_v[e].astype(F32), axis=1, keepdims=True)
            inner_grad = dot(pair_grad, down, NT)
            da = (inner_grad * up_pre * sig * (1.0 + gate_pre * (1.0 - sig))).astype(BF16)
            db = (inner_grad * silu).astype(BF16)
            da_v[e] = da
            db_v[e] = db
            row_grad = (dot(da, gate, NT) + dot(db, up, NT)).astype(BF16)
            high = gate_grad.astype(BF16).astype(F32)
            extra = jnp.where(lane == first + e, high, 0.0) + jnp.where(
                lane == expert_count + first + e, gate_grad - high, 0.0
            )
            back = jnp.concatenate([row_grad, extra.astype(BF16)], axis=1)
            out_rows = (w * expert_out).astype(BF16)
            for q in range(2):
                part = slice(q * slot_rows, (q + 1) * slot_rows)
                outs[q].append(out_rows[part])
                backs[q].append(back[part])

        for copy in saves(i):
            copy.start()

        @pl.when(i >= 1)
        def _():
            for copy in out_copies(i - 1):
                copy.wait()

        @pl.when(i >= 2)
        def _():
            swap(i - 2).wait_send()

        for q in range(2):
            pick = jnp.concatenate(picks[q], axis=0)
            held = other_v if q else mine_v
            held[lax.rem(i, 2)] = dot(pick, jnp.concatenate(backs[q], axis=0), TN).astype(BF16)
            if q:
                swap(i).start()
        for q in range(2):
            pick = jnp.concatenate(picks[q], axis=0)
            out_v[q] = dot(pick, jnp.concatenate(outs[q], axis=0), TN).astype(BF16)
        for copy in out_copies(i):
            copy.start()

        @pl.when(i == 0)
        def _():
            join(0)
            line.step(0)

        @pl.when(i >= 2)
        def _():
            join(i - 1)

        for step in range(1, chips - 1):
            if 2 * step < chips:

                @pl.when(i == 2 * step)
                def _():
                    line.step(step)

        return carry

    lax.fori_loop(0, chips, chunk, 0)
    join(chips - 1)
    for copy in saves(chips - 1):
        copy.wait()
    for copy in out_copies(chips - 1):
        copy.wait()
    for i in range(max(0, chips - 2), chips):
        swap(i).wait_send()

    shard = width // fsdp
    blocks = fsdp // per
    block = per * shard

    def fetch(copies):
        copies = [
            pltpu.make_async_copy(src, dst, save_sem.at[k])
            for k, (src, dst) in enumerate(copies)
        ]
        for copy in copies:
            copy.start()
        for copy in copies:
            copy.wait()

    def products(e, staged, target, product):
        def write(f):
            return [
                pltpu.make_async_copy(
                    staged(lax.rem(f, 2), p),
                    target.at[f * per + p, e],
                    stage_sem.at[lax.rem(f, 2), p],
                )
                for p in range(per)
            ]

        def one(f, carry):
            @pl.when(f >= 2)
            def _():
                for copy in write(f - 2):
                    copy.wait()

            product(f)
            for copy in write(f):
                copy.start()
            return carry

        lax.fori_loop(0, blocks, one, 0)
        for f in range(max(0, blocks - 2), blocks):
            for copy in write(f):
                copy.wait()

    def stage_wide(slot, p):
        return hidden_v.at[slot, pl.ds(p * shard, shard), pl.ds(0, units)]

    def wide(e, held, staged, target):
        def product(f):
            columns = pl.ds(pl.multiple_of(f * block, LANES), block)
            value = dot(
                down_v[:total_rows, columns],
                held[e * total_rows : (e + 1) * total_rows, :],
                TN,
            ).astype(BF16)
            for p in range(per):
                staged(lax.rem(f, 2), p)[...] = value[p * shard : (p + 1) * shard, :]

        products(e, staged, target, product)

    def tall(e, target):
        def product(f):
            columns = pl.ds(pl.multiple_of(f * block, LANES), block)
            value = dot(
                gate_v[e * total_rows : (e + 1) * total_rows, :],
                down_v[:total_rows, columns],
                TN,
            ).astype(BF16)
            for p in range(per):
                stage_tall[lax.rem(f, 2), p] = value[:, p * shard : (p + 1) * shard]

        products(e, lambda slot, p: stage_tall.at[slot, p], target, product)

    def tile(e, j):
        held = (hidden_v, grad_v)[e]
        return held.at[j // 2, pl.ds(0, shard), pl.ds((j % 2) * units, units)]

    def tile_copy(e, j):
        if j == len(peers):
            return pltpu.make_async_copy(tile(e, j), gate_grad_ref.at[e], tile_own.at[e])
        return remote(
            tile(e, j),
            gate_got_ref.at[j, e],
            tile_send.at[e, j],
            tile_recv.at[e, j],
            (ctx, peers[j]),
        )

    def gate_tiles(e):
        for j, owner in enumerate(peers + [me]):
            columns = pl.ds(pl.multiple_of(owner * shard, LANES), shard)
            tile(e, j)[...] = dot(
                down_v[:total_rows, columns],
                gate_v[e * total_rows : (e + 1) * total_rows, :],
                TN,
            ).astype(BF16)
            tile_copy(e, j).start()

    def fetch_x(e):
        copies = [(x_ref.at[e], down_v.at[:total_rows])]
        if e == 0:
            for k in range(local_experts):
                held = pl.ds(k * total_rows, total_rows)
                copies += [(da_ref.at[k], gate_v.at[held]), (db_ref.at[k], up_v.at[held])]
        return lambda: fetch(copies)

    def stage_up(slot, p):
        return out_v.at[slot, pl.ds(p * shard, shard), pl.ds(0, units)]

    work = []
    for e in range(local_experts):
        work.append(fetch_x(e))
        if per == 1:
            work.append(lambda e=e: gate_tiles(e))
        else:
            work.append(lambda e=e: wide(e, gate_v, stage_wide, gate_grad_ref))
        if e > 0:
            work.append(lambda e=e: wide(e, up_v, stage_up, up_grad_ref))
    work.append(lambda: fetch([(x_ref.at[0], down_v.at[:total_rows])]))
    work.append(lambda: wide(0, up_v, stage_up, up_grad_ref))
    for e in range(local_experts):
        copies = [(pg_ref.at[e], down_v.at[:total_rows])]
        if e == 0:
            for k in range(local_experts):
                copies.append((inner_ref.at[k], gate_v.at[pl.ds(k * total_rows, total_rows)]))
        work.append(lambda copies=copies: fetch(copies))
        work.append(lambda e=e: tall(e, down_grad_ref))
    late = [step for step in range(1, chips - 1) if 2 * step >= chips]
    for n, task in enumerate(work):
        task()
        if n == LINE_TASK or (n > LINE_TASK and late):
            if late:
                line.step(late.pop(0))
    for step in late:
        line.step(step)

    line.total(returned_ref)
    line.finish()
    if per == 1:
        for e in range(local_experts):
            for j in range(fsdp):
                tile_copy(e, j).wait()


def experts_pass(
    hidden, grad, table, weights, gate, up, down, capacity, expert_count, fsdp, collective_id
):
    unused, chips, tokens, width = grad.shape
    local_experts, unused, units = gate.shape
    slots = 2 * SLOT_STEP * -(-capacity // SLOT_STEP)
    total = chips * slots
    shard = width // fsdp
    per = 1 if shard % LANES == 0 else 2
    wide = width + LANES
    anywhere = pl.BlockSpec(memory_space=pl.ANY)
    vmem = pl.BlockSpec(memory_space=pltpu.VMEM)
    flops = 2 * total * width * units * local_experts * 9 + 8 * total * tokens * width
    saved = [(local_experts, total, width)] * 2 + [(local_experts, total, units)] * 3
    held = [(local_experts, slots, width)] * 3 + [(local_experts, slots, units)] * 3
    outs = pl.pallas_call(
        functools.partial(
            experts_kernel, capacity, local_experts, expert_count, chips, fsdp, per
        ),
        out_shape=[
            jax.ShapeDtypeStruct((tokens, wide), BF16),
            jax.ShapeDtypeStruct(hidden.shape, BF16),
            jax.ShapeDtypeStruct(
                ((fsdp,) if per > 1 else ()) + (local_experts, shard, units), BF16
            ),
            jax.ShapeDtypeStruct(
                (fsdp - 1, local_experts, shard, units) if per == 1 else (1, 1, 16, LANES), BF16
            ),
            jax.ShapeDtypeStruct((fsdp, local_experts, shard, units), BF16),
            jax.ShapeDtypeStruct((fsdp, local_experts, units, shard), BF16),
        ]
        + [jax.ShapeDtypeStruct(shape, BF16) for shape in saved],
        in_specs=[anywhere, anywhere, vmem, vmem, anywhere, anywhere, anywhere],
        out_specs=[vmem] + [anywhere] * 10,
        input_output_aliases={0: 1},
        scratch_shapes=[
            pltpu.VMEM((local_experts * width, units), BF16),
            pltpu.VMEM((local_experts * width, units), BF16),
            pltpu.VMEM((local_experts * units, width), BF16),
            pltpu.VMEM((2, tokens, width), BF16),
            pltpu.VMEM((2, tokens, width), BF16),
            pltpu.VMEM((2, tokens, width), BF16),
        ]
        + [pltpu.VMEM(shape, BF16) for shape in held]
        + [
            pltpu.VMEM((2, tokens, wide), BF16),
            pltpu.VMEM((2, tokens, wide), BF16),
            pltpu.VMEM((chips, tokens, wide), BF16),
            pltpu.VMEM((chips + 1, tokens, wide), BF16),
            pltpu.VMEM((2, per, units, shard), BF16),
            pltpu.SemaphoreType.DMA((3,)),
            pltpu.SemaphoreType.DMA((2,)),
            pltpu.SemaphoreType.DMA((2,)),
            pltpu.SemaphoreType.DMA((5,)),
            pltpu.SemaphoreType.DMA((chips,)),
            pltpu.SemaphoreType.DMA((chips,)),
        ]
        + [pltpu.SemaphoreType.DMA((chips - 1,)) for unused in range(4)]
        + [pltpu.SemaphoreType.DMA((2, per)), pltpu.SemaphoreType.DMA((local_experts,))]
        + [pltpu.SemaphoreType.DMA((local_experts, fsdp - 1)) for unused in range(2)],
        compiler_params=pltpu.CompilerParams(
            collective_id=collective_id, has_side_effects=True, vmem_limit_bytes=EXPERT_VMEM_BYTES
        ),
        cost_estimate=pl.CostEstimate(
            flops=flops, bytes_accessed=100_000_000, transcendentals=total * units * 2
        ),
        name="experts",
    )(
        hidden,
        grad,
        table,
        weights,
        gate.reshape(local_experts * width, units),
        up.reshape(local_experts * width, units),
        down.reshape(local_experts * units, width),
    )
    return outs[:6]


def body(
    tokens,
    grad_out,
    order,
    lengths,
    routes,
    gain_one,
    gain_two,
    w_query,
    w_key,
    w_value,
    w_out,
    w_router,
    w_gate,
    w_up,
    w_down,
):
    fsdp = lax.axis_size("fsdp")
    chips = lax.axis_size("ctx") // 2
    ctx_index = lax.axis_index("ctx")
    chip = ctx_index // 2
    core = lax.rem(ctx_index, 2)
    tok_rows = tokens.shape[1]
    width = tokens.shape[2]
    top_count = routes.shape[2]
    local_experts = w_gate.shape[0]
    expert_count = local_experts * chips * 2
    capacity = 5 * tok_rows * top_count // (4 * expert_count)
    kv_width = KVH * HEAD_SIZE
    shard = gain_one.shape[0]

    small = jnp.concatenate(
        [
            w_router,
            gain_one[:, None],
            gain_two[:, None],
            jnp.zeros((shard, LANES - expert_count - 2), BF16),
        ],
        axis=1,
    )
    qkv_full, small_full, out_full, grad_all = gather(
        [w_query, w_key, w_value, small, w_out], 3, [grad_out[0]], chips - 2, fsdp, chips, 0
    )

    qkv_full, w_up, w_down = lax.optimization_barrier((qkv_full, w_up, w_down))
    up_full, down_full = (
        lax.all_gather(w_up, "fsdp", axis=1, tiled=True),
        lax.all_gather(w_down, "fsdp", axis=2, tiled=True),
    )
    router_full = small_full[:, :expert_count]
    gain_a = small_full[:, expert_count].astype(F32)
    gain_b = small_full[:, expert_count + 1].astype(F32)

    order_row = order[0]
    start_row = ctx_index * tok_rows
    order_mine = lax.dynamic_slice_in_dim(order_row, start_row, tok_rows)
    ends = jnp.cumsum(lengths[0])
    starts = ends - lengths[0]
    past = order_mine[:, None] >= ends[None, :]
    doc_start = jnp.max(jnp.where(past, ends[None, :], starts[:1]), axis=1)
    pos_mine = order_mine - doc_start
    by_chip = jnp.roll(order_row.reshape(chips, 2, tok_rows), -chip, axis=0)
    by_chip = jnp.where(core == 0, by_chip, by_chip[:, ::-1])
    order_keys = jnp.swapaxes(by_chip, 0, 1).reshape(-1)

    route_rows = routes[0]
    route_onehot = (route_rows[:, :, None] == jnp.arange(expert_count)[None, None, :]).astype(F32)
    routed = jnp.sum(route_onehot, axis=1)
    earlier = (order_mine[None, :] < order_mine[:, None]).astype(BF16)
    ranks = jnp.dot(earlier, routed.astype(BF16), preferred_element_type=F32)
    table = jnp.where(routed > 0, jnp.minimum(ranks, capacity) + 1.0, 0.0)

    half_dim = HEAD_SIZE // 2
    freqs = ROPE_BASE ** (-2.0 * jnp.arange(half_dim).astype(F32) / HEAD_SIZE)
    angles = pos_mine.astype(F32)[:, None] * freqs[None, :]
    cosine = jnp.concatenate([jnp.cos(angles), jnp.cos(angles)], axis=1)
    sine = jnp.concatenate([-jnp.sin(angles), jnp.sin(angles)], axis=1)

    inputs = tokens[0].astype(F32)
    (
        table_all,
        lse,
        gate_weights,
        weights_all,
        queries,
        hidden_one,
        kv_all,
        attended,
        middle,
        hidden_two,
        hidden_all,
        gate_full,
        grad_all,
    ) = front(
        tokens[0],
        gain_a,
        gain_b,
        small_full,
        cosine,
        sine,
        order_mine,
        pos_mine,
        order_keys,
        jnp.pad(routed, ((0, 0), (0, LANES - expert_count))),
        table.T,
        qkv_full,
        out_full,
        w_gate,
        grad_all,
        chips,
        fsdp,
        1,
    )
    kv_all = kv_all.reshape(-1, 2 * kv_width)
    gate_weights = gate_weights[:, :expert_count]

    returned, out_rows, gate_local, gate_got, up_local, down_local = experts_pass(
        hidden_all,
        grad_all,
        table_all,
        weights_all,
        gate_full,
        up_full,
        down_full,
        capacity,
        expert_count,
        fsdp,
        5,
    )
    direct = gate_local.ndim == 3
    if not direct:
        gate_local = lax.psum_scatter(gate_local, "fsdp", scatter_dimension=0, tiled=True)[0]
    up_sum, down_sum = (
        lax.psum_scatter(part, "fsdp", scatter_dimension=0, tiled=True)
        for part in (up_local, down_local)
    )

    out_grad = grad_out[0].astype(F32)
    returned = returned.astype(F32)
    extra = returned[:, width:]
    gate_grad = extra[:, :expert_count] + extra[:, expert_count : 2 * expert_count]
    logit_grad = (
        gate_weights * (gate_grad - jnp.sum(gate_weights * gate_grad, axis=-1, keepdims=True))
    ).astype(BF16)
    router_local = jnp.einsum("td,te->de", hidden_two, logit_grad, preferred_element_type=F32)
    hidden_two_grad = returned[:, :width] + jnp.einsum(
        "te,de->td", logit_grad, router_full, preferred_element_type=F32
    )
    unused_two, norm_two_back = jax.vjp(rms_scale, middle, gain_b)
    middle_part, gain_two_local = norm_two_back(hidden_two_grad)
    middle_grad = out_grad + middle_part
    branch_grad = middle_grad.astype(BF16)
    out_local = jnp.einsum("tc,td->cd", attended, branch_grad, preferred_element_type=F32)
    attended_grad = jnp.einsum(
        "td,cd->tc", branch_grad, out_full, preferred_element_type=F32
    ).astype(BF16)

    def halves(local):
        local = local.astype(BF16).reshape(fsdp, 2, shard // 2, local.shape[1])
        pad = -local.shape[3] % (LANES * chips)
        return jnp.pad(local, ((0, 0), (0, 0), (0, 0), (0, pad))) if pad else local

    early_dense = chips <= 4
    query_grad, kv_grad, out_own, out_right, out_left, out_proj_sum = attention_back(
        queries,
        kv_all,
        attended,
        attended_grad,
        lse,
        order_mine,
        pos_mine,
        order_keys,
        cosine,
        sine,
        out_rows,
        halves(out_local) if early_dense else out_local[:16, :LANES].astype(BF16),
        fsdp,
        early_dense,
        3,
    )
    span = shard * expert_count // 16
    wide = LANES * chips * -(-max(span, shard) // (LANES * chips))
    small_local = jnp.stack(
        [
            jnp.pad(
                router_local.astype(BF16).reshape(fsdp, 16, span),
                ((0, 0), (0, 0), (0, wide - span)),
            ),
            jnp.pad(
                gain_two_local.reshape(fsdp, 1, shard).astype(BF16),
                ((0, 0), (1, 14), (0, wide - shard)),
            ),
        ],
        axis=1,
    )
    *sums, out_sum, input_grad = dense_reduce(
        [
            jax.ShapeDtypeStruct((fsdp, 2, shard // 2, width + 2 * kv_width), BF16),
            small_local,
        ]
        + ([] if early_dense else [halves(out_local)]),
        out_own,
        out_right,
        out_left,
        query_grad,
        kv_grad,
        hidden_one,
        tokens[0],
        middle_grad,
        gain_a,
        qkv_full,
        DENSE_PIECE,
        fsdp,
        chips,
        4,
    )
    qkv_sum, small_sum = sums[:2]
    if not early_dense:
        out_proj_sum = sums[2]
    edge = width + 2 * kv_width
    qkv_grads = qkv_sum.reshape(shard, -1)
    out_proj_grad = out_proj_sum.reshape(shard, -1)[:, :width]
    up_grad_out, down_grad_out = (
        after(part, kv_grad)[0].astype(F32) for part in (up_sum, down_sum)
    )
    if direct:
        gate_local, gate_got = lax.optimization_barrier((gate_local, gate_got, kv_grad))[:2]
        gate_grad_out = add(gate_local, *[gate_got[j] for j in range(fsdp - 1)])
    else:
        gate_grad_out = after(gate_local, kv_grad).astype(F32)
    result = middle + out_sum
    return (
        result.astype(BF16)[None],
        input_grad[None],
        small_sum[1, 0, :shard].astype(F32),
        small_sum[1, 1, :shard].astype(F32),
        qkv_grads[:, :width].astype(F32),
        qkv_grads[:, width : width + kv_width].astype(F32),
        qkv_grads[:, width + kv_width : edge].astype(F32),
        out_proj_grad.astype(F32),
        small_sum[0, :, :span].reshape(shard, expert_count).astype(F32),
        gate_grad_out,
        up_grad_out,
        down_grad_out,
    )


def solution(mesh):
    placed = (
        P("fsdp", "ctx", None),
        P("fsdp", "ctx", None),
        P("fsdp", None),
        P("fsdp", None),
        P("fsdp", "ctx", None),
        P("fsdp"),
        P("fsdp"),
        P("fsdp", None),
        P("fsdp", None),
        P("fsdp", None),
        P("fsdp", None),
        P("fsdp", None),
        P("ctx", "fsdp", None),
        P("ctx", "fsdp", None),
        P("ctx", None, "fsdp"),
    )
    return jax.shard_map(
        body,
        mesh=mesh,
        in_specs=placed,
        out_specs=(
            P("fsdp", "ctx", None),
            P("fsdp", "ctx", None),
            P("fsdp"),
            P("fsdp"),
            P("fsdp", None),
            P("fsdp", None),
            P("fsdp", None),
            P("fsdp", None),
            P("fsdp", None),
            P("ctx", "fsdp", None),
            P("ctx", "fsdp", None),
            P("ctx", None, "fsdp"),
        ),
        check_vma=False,
    )
```

```python
import functools

import jax
import jax.numpy as jnp
from jax import lax
from jax.experimental import pallas as pl
from jax.experimental.pallas import tpu as pltpu
from jax.sharding import PartitionSpec as P

QUERY_HEADS = 12
KVH = 2
HEAD_SIZE = 128

EPSILON = 1e-06
ROPE_BASE = 10000.0
MASKED = -1e30
LOG2E = 1.4426950408889634
LANES = 128
SLOT_STEP = 64
DENSE_PIECE = 1024
LINE_TASK = 4
KEY_TILE = 512
VMEM_BYTES = 56 * 1024 * 1024
EXPERT_VMEM_BYTES = 119 * 512 * 1024
BACK_VMEM_BYTES = 61 * 1024 * 1024
FRONT_VMEM_BYTES = 50 * 1024 * 1024
DENSE_VMEM_BYTES = 50 * 1024 * 1024
MESH = pl.DeviceIdType.MESH
F32 = jnp.float32
BF16 = jnp.bfloat16


def dot(left, right, contract):
    return lax.dot_general(left, right, (contract, ((), ())), preferred_element_type=F32)


NN = ((1,), (0,))
NT = ((1,), (1,))
TN = ((0,), (0,))


def rms_scale(value_rows, gain):
    return (
        value_rows
        * lax.rsqrt(jnp.mean(value_rows * value_rows, axis=-1, keepdims=True) + EPSILON)
        * gain
    )


def place():
    ctx = lax.axis_index("ctx")
    core = lax.rem(ctx, 2)
    return ctx, lax.axis_index("fsdp"), ctx // 2, core, ctx + 1 - 2 * core


def peers_of(me, fsdp):
    peers = []
    for shift in range(1, fsdp):
        peer = me
        for bit in range(fsdp.bit_length() - 1):
            if (shift >> bit) & 1:
                digit = lax.rem(me // (1 << bit), 2)
                peer = peer + (1 << bit) - (2 << bit) * digit
        peers.append(peer)
    return peers


def greet(chips, peers, line):
    ctx, me, chip, core, sibling = place()
    barrier = pltpu.get_barrier_semaphore()
    for peer in peers:
        pl.semaphore_signal(barrier, inc=1, device_id=(ctx, peer), device_id_type=MESH)
    pl.semaphore_signal(barrier, inc=1, device_id=(sibling, me), device_id_type=MESH)
    known = len(peers) + 1
    if not line:
        pl.semaphore_wait(barrier, known)
        return
    has_right = chip + 1 < chips
    has_left = chip >= 1

    @pl.when(has_right)
    def _():
        pl.semaphore_signal(barrier, inc=1, device_id=(ctx + 2, me), device_id_type=MESH)

    @pl.when(has_left)
    def _():
        pl.semaphore_signal(barrier, inc=1, device_id=(ctx - 2, me), device_id_type=MESH)

    @pl.when(has_right & has_left)
    def _():
        pl.semaphore_wait(barrier, known + 2)

    @pl.when(jnp.logical_not(has_right & has_left))
    def _():
        pl.semaphore_wait(barrier, known + 1)


class Bounce:
    def __init__(self, src, dst, buffer, sem):
        self.inward = pltpu.make_async_copy(src, buffer, sem)
        self.outward = pltpu.make_async_copy(buffer, dst, sem)

    def start(self):
        self.inward.start()

    def turn(self):
        self.inward.wait()
        self.outward.start()

    def wait(self):
        self.outward.wait()


def remote(src, dst, send_sem, recv_sem, device):
    return pltpu.make_async_remote_copy(
        src_ref=src,
        dst_ref=dst,
        send_sem=send_sem,
        recv_sem=recv_sem,
        device_id=device,
        device_id_type=MESH,
    )


class Spread:
    def __init__(self, block, place_of, size, sems, fsdp):
        send_sem, recv_sem, on_send, on_recv = sems
        ctx, me, chip, core, sibling = place()
        self.peers = peers_of(me, fsdp)
        self.square = fsdp == 4
        near = self.peers[:2] if self.square else self.peers
        self.sends = [
            remote(block, place_of(me, 0, size), send_sem.at[j], recv_sem.at[j], (ctx, peer))
            for j, peer in enumerate(near)
        ]
        self.on, self.last = [], []
        if self.square:
            half = size // 2
            across_x, across_y, far = self.peers
            for k, (owner, target) in enumerate(((across_x, across_y), (across_y, across_x))):
                part = place_of(owner, k * half, half)
                self.on.append(remote(part, part, on_send.at[k], on_recv.at[k], (ctx, target)))
                part = place_of(far, k * half, half)
                self.last.append(remote(part, part, on_send.at[k], on_recv.at[k], (ctx, target)))

    def start(self):
        for copy in self.sends:
            copy.start()

    def hand_on(self, also=lambda j: None):
        for j, copy in enumerate(self.sends):
            copy.wait_recv()
            if self.square:
                self.on[j].start()
            also(j)

    def finish(self, also=lambda j: None):
        for copy in self.last:
            copy.wait_recv()
        if self.square:
            also(2)
        for copy in self.sends + self.on:
            copy.wait_send()


def spread_sems(fsdp):
    return [pltpu.SemaphoreType.DMA((fsdp - 1,)) for unused in range(4)]


class DenseGather:
    def __init__(self, ins, outs, sems, fsdp):
        buffers, local_sem, pass_sem, took_sem, spread_refs = sems
        ctx, me, chip, core, sibling = place()
        peers = peers_of(me, fsdp)
        self.spreads, self.passes, self.locals = [], [], []
        for i in range(len(ins)):
            rows = ins[i].shape[0]
            half = rows // 2

            def place_of(owner, begin, size, i=i, rows=rows, half=half):
                return outs[i].at[pl.ds(owner * rows + core * half + begin, size)]

            self.spreads.append(
                Spread(
                    ins[i].at[pl.ds(core * half, half)],
                    place_of,
                    half,
                    spread_refs[4 * i : 4 * i + 4],
                    fsdp,
                )
            )
            self.passes.append([])
            for j, peer in enumerate(peers):
                got = place_of(peer, 0, half)
                self.passes[i].append(
                    remote(got, got, pass_sem.at[i, j], took_sem.at[i, j], (sibling, me))
                )
            self.locals.append(
                Bounce(ins[i], outs[i].at[pl.ds(me * rows, rows)], buffers[i], local_sem.at[i])
            )

    def start(self):
        for spread in self.spreads:
            spread.start()
        for copy in self.locals:
            copy.start()

    def hand_on(self):
        for copy in self.locals:
            copy.turn()
        for i, spread in enumerate(self.spreads):
            spread.hand_on(lambda j, i=i: self.passes[i][j].start())

    def finish(self):
        for i, spread in enumerate(self.spreads):
            spread.finish(lambda j, i=i: self.passes[i][j].start())
        for passes in self.passes:
            for copy in passes:
                copy.wait()
        for copy in self.locals:
            copy.wait()


def dense_scratch(arrays, fsdp):
    count = len(arrays)
    return (
        [pltpu.VMEM(a.shape, a.dtype) for a in arrays]
        + [pltpu.SemaphoreType.DMA((count,))]
        + [pltpu.SemaphoreType.DMA((count, fsdp - 1)) for unused in range(2)]
        + spread_sems(fsdp) * count
    )


class ShardGather:
    def __init__(self, ref, out, buffer, sems, fsdp):
        ctx, me, chip, core, sibling = place()
        rows = ref.shape[1]

        def place_of(owner, begin, size):
            return out.at[:, pl.ds(owner * rows + begin, size)]

        self.spread = Spread(ref, place_of, rows, sems[1:], fsdp)
        self.own = Bounce(ref, place_of(me, 0, rows), buffer, sems[0])

    def start(self):
        self.spread.start()
        self.own.start()

    def hand_on(self):
        self.spread.hand_on()
        self.own.turn()

    def finish(self):
        self.spread.finish()
        self.own.wait()


class LineGather:
    def __init__(self, ins, outs, sems, chips):
        self.ins, self.outs, self.chips = ins, outs, chips
        self.buffers, self.sems = sems[:-7], sems[-7:]
        self.ctx, self.me, self.chip, core, self.sibling = place()
        self.count = len(ins)

    def to_right(self, i, step):
        outs, chips = self.outs, self.chips
        return remote(
            self.ins[i] if step == 0 else outs[i].at[0, chips - step],
            outs[i].at[0, chips - 1 - step],
            self.sems[1].at[i, step],
            self.sems[2].at[i, step],
            (self.ctx + 2, self.me),
        )

    def to_left(self, i, step):
        outs = self.outs
        return remote(
            self.ins[i] if step == 0 else outs[i].at[0, step],
            outs[i].at[0, step + 1],
            self.sems[3].at[i, step],
            self.sems[4].at[i, step],
            (self.ctx - 2, self.me),
        )

    def across(self, i, slot):
        return remote(
            self.ins[i] if slot == 0 else self.outs[i].at[0, slot],
            self.outs[i].at[1, slot],
            self.sems[5].at[i, slot],
            self.sems[6].at[i, slot],
            (self.sibling, self.me),
        )

    def local(self, i):
        return Bounce(self.ins[i], self.outs[i].at[0, 0], self.buffers[i], self.sems[0].at[i])

    def send(self, step):
        chip, chips, count = self.chip, self.chips, self.count

        @pl.when((chip + 1 < chips) & (chip >= step))
        def _():
            for i in range(count):
                self.to_right(i, step).start()

        @pl.when((chip >= 1) & (chip + step < chips))
        def _():
            for i in range(count):
                self.to_left(i, step).start()

    def receive(self, step):
        chip, chips, count = self.chip, self.chips, self.count

        @pl.when(chip >= step + 1)
        def _():
            for i in range(count):
                self.to_right(i, step).wait_recv()
                self.across(i, chips - 1 - step).start()

        @pl.when(chip + step + 1 < chips)
        def _():
            for i in range(count):
                self.to_left(i, step).wait_recv()
                self.across(i, step + 1).start()

    def own(self):
        for i in range(self.count):
            self.across(i, 0).start()
            self.local(i).start()

    def turn_own(self):
        for i in range(self.count):
            self.local(i).turn()

    def finish_own(self):
        for i in range(self.count):
            self.across(i, 0).wait()
            self.local(i).wait()

    def arrived(self, slot):
        for i in range(self.count):
            remote(
                self.outs[i].at[0, slot],
                self.outs[i].at[1, slot],
                self.sems[5].at[i, slot],
                self.sems[6].at[i, slot],
                (self.sibling, self.me),
            ).wait_recv()

    def sent(self):
        chip, chips, count = self.chip, self.chips, self.count
        for step in range(chips - 1):

            @pl.when((chip + 1 < chips) & (chip >= step))
            def _():
                for i in range(count):
                    self.to_right(i, step).wait_send()

            @pl.when((chip >= 1) & (chip + step < chips))
            def _():
                for i in range(count):
                    self.to_left(i, step).wait_send()

        for slot in range(chips):
            for i in range(count):
                self.across(i, slot).wait_send()

    def finish(self, step):
        chip, chips, count = self.chip, self.chips, self.count

        @pl.when((chip + 1 < chips) & (chip >= step))
        def _():
            for i in range(count):
                self.to_right(i, step).wait_send()

        @pl.when((chip >= 1) & (chip + step < chips))
        def _():
            for i in range(count):
                self.to_left(i, step).wait_send()

        @pl.when(chip >= step + 1)
        def _():
            for i in range(count):
                self.across(i, chips - 1 - step).wait()

        @pl.when(chip + step + 1 < chips)
        def _():
            for i in range(count):
                self.across(i, step + 1).wait()


def line_scratch(arrays, chips):
    count = len(arrays)
    return (
        [pltpu.VMEM(a.shape, a.dtype) for a in arrays if a is not None]
        + [pltpu.SemaphoreType.DMA((count,))]
        + [pltpu.SemaphoreType.DMA((count, chips - 1)) for unused in range(4)]
        + [pltpu.SemaphoreType.DMA((count, chips)) for unused in range(2)]
    )


def gather_kernel(dense, line, merged, steps, fsdp, chips, *refs):
    count = dense + line
    ins, refs = refs[:count], refs[count:]
    outs, scratch = list(refs[: count - merged + 1]), refs[count - merged + 1 :]
    columns, start = [], 0
    for ref in ins[:merged]:
        columns.append(outs[0].at[:, pl.ds(start, ref.shape[1])])
        start += ref.shape[1]
    outs = columns + outs[1:]
    ctx, me, chip, core, sibling = place()
    greet(chips, peers_of(me, fsdp) if dense else [], line > 0)
    if dense:
        own, scratch = scratch[: 5 * dense + 3], scratch[5 * dense + 3 :]
        first = DenseGather(
            ins[:dense],
            outs[:dense],
            (own[:dense],) + tuple(own[dense : dense + 3]) + (own[dense + 3 :],),
            fsdp,
        )
        first.start()
    if line:
        own, scratch = scratch[: line + 7], scratch[line + 7 :]
        second = LineGather(ins[dense:], outs[dense:], own, chips)
        for step in range(steps):
            second.send(step)
            if step == 0:
                second.own()
            if step == steps - 1 and dense:
                first.hand_on()
            second.receive(step)
            if step == 0:
                second.turn_own()
    if dense:
        first.finish()
    if line:
        second.finish_own()
        for step in range(steps):
            second.finish(step)


def gather(dense, merged, line, steps, fsdp, chips, collective_id):
    arrays = list(dense) + list(line)
    joined = sum(a.shape[1] for a in dense[:merged])
    shapes = [(fsdp * dense[0].shape[0], joined)]
    shapes += [(fsdp * a.shape[0],) + a.shape[1:] for a in dense[merged:]]
    shapes += [(2, chips) + a.shape for a in line]
    return pl.pallas_call(
        functools.partial(gather_kernel, len(dense), len(line), merged, steps, fsdp, chips),
        out_shape=[jax.ShapeDtypeStruct(shape, BF16) for shape in shapes],
        in_specs=[pl.BlockSpec(memory_space=pl.ANY)] * len(arrays),
        out_specs=[pl.BlockSpec(memory_space=pl.ANY)] * len(shapes),
        scratch_shapes=dense_scratch(dense, fsdp) + line_scratch(line, chips),
        compiler_params=pltpu.CompilerParams(
            collective_id=collective_id, has_side_effects=True, vmem_limit_bytes=VMEM_BYTES
        ),
        name="gather",
    )(*arrays)


def add(*parts):
    total = parts[0].astype(F32)
    for part in parts[1:]:
        total = total + part.astype(F32)
    return total


def add_into(target, parts):
    rows = target.shape[0]
    tile = 32 if rows % 32 == 0 else 16

    def some(t, carry):
        part = pl.ds(pl.multiple_of(t * tile, tile), tile)
        target[part, :] = add(*[ref[part, :] for ref in parts]).astype(target.dtype)
        return carry

    lax.fori_loop(0, rows // tile, some, 0)


class LineSum:
    def __init__(self, chips, held, keep, got, sems):
        self.chips, self.held, self.keep, self.got = chips, held, keep, got
        self.sems = sems
        self.ctx, self.me, self.chip, core, sibling = place()

    def right(self, step):
        return remote(
            self.keep(self.chips - 1 - step),
            self.got.at[step - self.chip],
            self.sems[0].at[step],
            self.sems[1].at[step],
            (self.ctx + 2, self.me),
        )

    def from_left(self, step):
        slot = step + 1 - self.chip
        pltpu.make_async_remote_copy(
            src_ref=self.keep(self.chips - 1 - step),
            dst_ref=self.got.at[slot],
            send_sem=self.sems[0].at[step],
            recv_sem=self.sems[1].at[step],
            device_id=(self.ctx - 2, self.me),
            device_id_type=MESH,
        ).wait_recv()
        return self.got.at[slot]

    def from_right(self, step):
        slot = step + 2
        self.left(step).wait_recv()
        return self.got.at[slot]

    def left(self, step):
        return remote(
            self.keep(step + 1),
            self.got.at[step + 2],
            self.sems[2].at[step],
            self.sems[3].at[step],
            (self.ctx - 2, self.me),
        )

    def step(self, step):
        chip, chips = self.chip, self.chips
        far_right, far_left = chips - 1 - step, step + 1

        @pl.when(chip <= step)
        def _():
            parts = self.held(far_right)
            if step == 0:
                add_into(self.keep(far_right), parts())
            else:

                @pl.when(chip == 0)
                def _():
                    add_into(self.keep(far_right), parts())

                @pl.when(chip >= 1)
                def _():
                    add_into(self.keep(far_right), [self.from_left(step - 1)] + parts())

            self.right(step).start()

        @pl.when(chip >= chips - 1 - step)
        def _():
            parts = self.held(far_left)
            if step == 0:
                add_into(self.keep(far_left), parts())
            else:

                @pl.when(chip == chips - 1)
                def _():
                    add_into(self.keep(far_left), parts())

                @pl.when(chip < chips - 1)
                def _():
                    add_into(self.keep(far_left), [self.from_right(step - 1)] + parts())

            self.left(step).start()

    def total(self, target):
        chip, chips, last = self.chip, self.chips, self.chips - 2
        parts = self.held(0)

        @pl.when(chip == 0)
        def _():
            add_into(target, [self.from_right(last)] + parts())

        @pl.when(chip == chips - 1)
        def _():
            add_into(target, [self.from_left(last)] + parts())

        @pl.when((chip >= 1) & (chip < chips - 1))
        def _():
            add_into(target, [self.from_right(last), self.from_left(last)] + parts())

    def finish(self, steps=None):
        for step in range(self.chips - 1 if steps is None else steps):

            @pl.when(self.chip <= step)
            def _():
                self.right(step).wait_send()

            @pl.when(self.chip >= self.chips - 1 - step)
            def _():
                self.left(step).wait_send()


DENSE_BUFFERS = 5
DENSE_SEMS = 14


class DenseSum:
    def __init__(self, local, held, out, buffers, sems, fsdp, chips):
        self.local, self.held, self.out = local, held, out
        self.pair, self.cross, self.sums, got, self.spread = buffers
        self.sems = sems
        self.chips = chips
        self.ctx, self.me, self.chip, self.core, self.sibling = place()
        self.owners = peers_of(self.me, fsdp) + [self.me]
        self.cut = out.shape[2] // chips
        self.line = LineSum(
            chips,
            lambda r: lambda: [self.keep_ref(r)],
            lambda r: self.keep_ref(r),
            got,
            sems[4:8],
        )

    def keep_ref(self, r):
        return self.sums.at[:, self.columns(r)]

    def columns(self, r):
        owner = lax.rem(self.chip + r, self.chips)
        return pl.ds(pl.multiple_of(owner * self.cut, LANES), self.cut)

    def swap(self, j):
        return remote(
            self.local.at[self.owners[j], 1 - self.core],
            self.pair.at[j],
            self.sems[0].at[j],
            self.sems[1].at[j],
            (self.sibling, self.me),
        )

    def crossing(self, j):
        return remote(
            self.pair.at[j],
            self.cross.at[j],
            self.sems[2].at[j],
            self.sems[3].at[j],
            (self.ctx, self.owners[j]),
        )

    def to_right(self, step):
        return remote(
            self.spread.at[0, (self.chips - step) % self.chips],
            self.spread.at[0, self.chips - 1 - step],
            self.sems[8].at[step],
            self.sems[9].at[step],
            (self.ctx + 2, self.me),
        )

    def to_left(self, step):
        return remote(
            self.spread.at[0, step],
            self.spread.at[0, step + 1],
            self.sems[10].at[step],
            self.sems[11].at[step],
            (self.ctx - 2, self.me),
        )

    def across(self, slot):
        return remote(
            self.spread.at[0, slot],
            self.spread.at[1, slot],
            self.sems[12].at[slot],
            self.sems[13].at[slot],
            (self.sibling, self.me),
        )

    def start(self):
        for j in range(len(self.owners)):
            self.swap(j).start()

    def cross_over(self):
        for j, owner in enumerate(self.owners):
            self.swap(j).wait_recv()
            add_into(self.pair.at[j], [self.held(j, owner), self.pair.at[j]])
            if j < len(self.owners) - 1:
                self.crossing(j).start()

    def stages(self):
        chip, chips = self.chip, self.chips

        def open_up():
            for j in range(len(self.owners) - 1):
                self.crossing(j).wait_recv()
            add_into(
                self.sums,
                [self.cross.at[j] for j in range(len(self.owners) - 1)]
                + [self.pair.at[len(self.owners) - 1]],
            )
            self.line.step(0)

        def summed():
            self.line.total(self.spread.at[0, 0])
            hand_on(0)

        def hand_on(step):
            @pl.when((chip + 1 < chips) & (chip >= step))
            def _():
                self.to_right(step).start()

            @pl.when((chip >= 1) & (chip + step < chips))
            def _():
                self.to_left(step).start()

            if step == 0:
                self.across(0).start()

        def take(step):
            @pl.when(chip >= step + 1)
            def _():
                self.to_right(step).wait_recv()
                self.across(chips - 1 - step).start()

            @pl.when(chip + step + 1 < chips)
            def _():
                self.to_left(step).wait_recv()
                self.across(step + 1).start()

        def pass_on(step):
            def run():
                take(step - 1)
                hand_on(step)

            return run

        def line_step(step):
            return lambda: self.line.step(step)

        return (
            [open_up]
            + [line_step(step) for step in range(1, chips - 1)]
            + [summed]
            + [pass_on(step) for step in range(1, chips - 1)]
            + [lambda: take(chips - 2)]
        )

    def finish(self):
        chip, chips = self.chip, self.chips
        for r in range(chips):
            self.out[self.core, :, self.columns(r)] = self.spread[0, r]
        for r in range(chips):
            self.across(r).wait()
            self.out[1 - self.core, :, self.columns(r)] = self.spread[1, r]
        for step in range(chips - 1):

            @pl.when((chip + 1 < chips) & (chip >= step))
            def _():
                self.to_right(step).wait_send()

            @pl.when((chip >= 1) & (chip + step < chips))
            def _():
                self.to_left(step).wait_send()

        self.line.finish()
        for j in range(len(self.owners) - 1):
            self.crossing(j).wait_send()
        for j in range(len(self.owners)):
            self.swap(j).wait_send()


def dense_reduce_kernel(fsdp, chips, cuts, *refs):
    count = len(cuts)
    arrays = max(cut[0] for cut in cuts) + 1
    ins, refs = [None] + list(refs[: arrays - 1]), refs[arrays - 1 :]
    right_ref, left_ref, gain_ref = refs[:3]
    loaded, refs = refs[3:10], refs[10:]
    outs, total_ref, input_ref, refs = (
        refs[:arrays],
        refs[arrays],
        refs[arrays + 1],
        refs[arrays + 2 :],
    )
    from_left, from_right, r_send, r_recv, l_send, l_recv = refs[:6]
    small_v, local_v, load_sem = refs[6:9]
    held, rest = refs[9:16], refs[16:]
    normed_ref, dq_ref, dkv_ref, qkv_v, tokens_ref, middle_ref, own_ref = held
    loads = [
        pltpu.make_async_copy(src, dst, load_sem.at[k])
        for k, (src, dst) in enumerate(zip(loaded, held))
    ]
    for copy in loads:
        copy.start()
    ctx, me, chip, core, sibling = place()
    greet(chips, peers_of(me, fsdp), True)

    to_right = remote(right_ref, from_left, r_send, r_recv, (ctx + 2, me))
    to_left = remote(left_ref, from_right, l_send, l_recv, (ctx - 2, me))

    @pl.when(chip + 1 < chips)
    def _():
        to_right.start()

    @pl.when(chip >= 1)
    def _():
        to_left.start()

    sums = []
    for i, (which, start, size) in enumerate(cuts):
        buffers = rest[i * DENSE_BUFFERS : (i + 1) * DENSE_BUFFERS]
        sems = rest[count * DENSE_BUFFERS + i * DENSE_SEMS :][:DENSE_SEMS]
        local = (local_v, small_v, ins[-1])[which].at[:, :, :, pl.ds(start, size)]
        sums.append(
            DenseSum(
                local,
                lambda j, owner, local=local: local.at[owner, core],
                outs[which].at[:, :, pl.ds(start, size)],
                buffers,
                sems,
                fsdp,
                chips,
            )
        )
    large = [one for one, cut in zip(sums, cuts) if cut[0] != 1]
    small = [one for one, cut in zip(sums, cuts) if cut[0] == 1]
    rows, width = tokens_ref.shape
    shard = width // fsdp
    per = 1 if shard % LANES == 0 else 2
    for copy in loads[:3]:
        copy.wait()
    for one, (which, start, size) in zip(sums, cuts):
        if which == 0:
            for f in range(0, fsdp, per):
                left = normed_ref[:, f * shard : (f + per) * shard]
                for begin in range(start, start + size, KEY_TILE):
                    right = (
                        dq_ref[:, begin : begin + KEY_TILE]
                        if begin < width
                        else dkv_ref[:, begin - width : begin - width + KEY_TILE]
                    )
                    value = dot(left, right, TN).astype(BF16)
                    for k in range(2 * per):
                        local_v[f + k // 2, k % 2, :, begin : begin + KEY_TILE] = value[
                            k * shard // 2 : (k + 1) * shard // 2, :
                        ]
        if which != 1:
            one.start()
    for one in large:
        one.cross_over()

    for copy in loads[3:]:
        copy.wait()
    gain_grad = jnp.zeros((1, width), F32)
    for part in (pl.ds(0, rows // 2), pl.ds(rows // 2, rows // 2)):
        grad = dot(dq_ref[part, :], qkv_v[:, :width], NT)
        grad = grad + dot(dkv_ref[part, :], qkv_v[:, width:], NT)
        value = tokens_ref[part, :].astype(F32)
        scale = lax.rsqrt(jnp.mean(value * value, axis=-1, keepdims=True) + EPSILON)
        unit = value * scale
        scaled = grad * gain_ref[...]
        slope = jnp.mean(scaled * unit, axis=-1, keepdims=True)
        input_ref[part, :] = (middle_ref[part, :] + scale * (scaled - unit * slope)).astype(BF16)
        gain_grad = gain_grad + jnp.sum(grad * unit, axis=0, keepdims=True)
    small_v[...] = ins[1][...]
    first_row = lax.broadcasted_iota(jnp.int32, (small_v.shape[2], shard), 0) == 0
    for f in range(fsdp):
        held = small_v[f, 1, :, :shard].astype(F32)
        mine = jnp.broadcast_to(gain_grad[:, f * shard : (f + 1) * shard], held.shape)
        small_v[f, 1, :, :shard] = jnp.where(first_row, mine, held).astype(BF16)
    for one in small:
        one.start()
    for one in small:
        one.cross_over()

    stages = [one.stages() for one in sums]
    lag = chips - 1
    offsets = []
    for which, start, size in cuts:
        turn = sum(1 for other in cuts[: len(offsets)] if other[0] != 1)
        offsets.append(lag * (max(0, turn - 1) if which == 1 else turn))
    for tick in range(len(stages[0]) + max(offsets)):
        for i in range(count):
            if 0 <= tick - offsets[i] < len(stages[i]):
                stages[i][tick - offsets[i]]()
    @pl.when(chip >= 1)
    def _():
        to_right.wait_recv()

    @pl.when(chip + 1 < chips)
    def _():
        to_left.wait_recv()

    @pl.when(chip == 0)
    def _():
        add_into(total_ref, [from_right, own_ref])

    @pl.when(chip == chips - 1)
    def _():
        add_into(total_ref, [from_left, own_ref])

    @pl.when((chip >= 1) & (chip + 1 < chips))
    def _():
        add_into(total_ref, [from_left, from_right, own_ref])

    for one in sums:
        one.finish()

    @pl.when(chip + 1 < chips)
    def _():
        to_right.wait_send()

    @pl.when(chip >= 1)
    def _():
        to_left.wait_send()


def dense_buffers(rows, size, fsdp, chips):
    cut = size // chips
    return [
        pltpu.VMEM((fsdp, rows, size), BF16),
        pltpu.VMEM((fsdp - 1, rows, size), BF16),
        pltpu.VMEM((rows, size), BF16),
        pltpu.VMEM((chips + 1, rows, cut), BF16),
        pltpu.VMEM((2, chips, rows, cut), BF16),
    ]


def dense_sems(fsdp, chips):
    return (
        [pltpu.SemaphoreType.DMA((fsdp,)) for unused in range(2)]
        + [pltpu.SemaphoreType.DMA((fsdp - 1,)) for unused in range(2)]
        + [pltpu.SemaphoreType.DMA((chips - 1,)) for unused in range(8)]
        + [pltpu.SemaphoreType.DMA((chips,)) for unused in range(2)]
    )


def dense_reduce(
    arrays,
    own,
    right,
    left,
    query_grad,
    kv_grad,
    normed,
    tokens,
    middle_grad,
    gain,
    qkv,
    piece,
    fsdp,
    chips,
    collective_id,
):
    vmem = pl.BlockSpec(memory_space=pltpu.VMEM)
    cuts, buffers = [], []
    for i, a in enumerate(arrays):
        rows, width = a.shape[2:]
        for start in range(0, width, piece):
            size = min(piece, width - start)
            cuts.append((i, start, size))
            buffers += dense_buffers(rows, size, fsdp, chips)
    sems = dense_sems(fsdp, chips)
    loaded = [normed, query_grad, kv_grad, qkv, tokens, middle_grad, own]
    anywhere = pl.BlockSpec(memory_space=pl.ANY)
    return pl.pallas_call(
        functools.partial(dense_reduce_kernel, fsdp, chips, tuple(cuts)),
        out_shape=[jax.ShapeDtypeStruct(a.shape[1:], BF16) for a in arrays]
        + [jax.ShapeDtypeStruct(own.shape, F32), jax.ShapeDtypeStruct(tokens.shape, BF16)],
        in_specs=[vmem] * (len(arrays) - 1)
        + [anywhere, anywhere, vmem]
        + [anywhere] * 7,
        out_specs=[vmem] * (len(arrays) + 2),
        scratch_shapes=[pltpu.VMEM(own.shape, BF16)] * 2
        + [pltpu.SemaphoreType.DMA] * 4
        + [
            pltpu.VMEM(arrays[1].shape, BF16),
            pltpu.VMEM(arrays[0].shape, BF16),
            pltpu.SemaphoreType.DMA((len(loaded),)),
        ]
        + [pltpu.VMEM(a.shape, a.dtype) for a in loaded]
        + buffers
        + sems * len(cuts),
        compiler_params=pltpu.CompilerParams(
            collective_id=collective_id, has_side_effects=True, vmem_limit_bytes=DENSE_VMEM_BYTES
        ),
        name="dense_reduce",
    )(
        *arrays[1:],
        right,
        left,
        gain[None, :],
        *loaded,
    )


def after(value, *others):
    return lax.optimization_barrier((value,) + others)[0]


def chunk_order(chip, i, chips):
    right_half = lax.div(2 * chip, chips)
    near = chip + right_half * (chips - 1 - 2 * chip)
    alone = chips - 1 - 2 * near
    paired = lax.div(i - alone + chips, chips)
    turn = (i - alone) * paired
    odd = lax.rem(turn, 2)
    pair = lax.div(turn, 2)
    distance = (1 - paired) * (chips - 1 - near - i) + paired * (
        (1 - odd) * (near - pair) + odd * (chips - near + pair)
    )
    return lax.rem(distance + right_half * (chips - 2 * distance), chips)


def front_kernel(
    scale,
    chips,
    fsdp,
    expert_count,
    tokens_ref,
    gain_a_ref,
    gain_b_ref,
    small_ref,
    cos_ref,
    sin_ref,
    oq_ref,
    pq_ref,
    ok_ref,
    routed_ref,
    table_ref,
    qkv_ref,
    wo_ref,
    gate_w_ref,
    passed_ref,
    table_all_ref,
    lse_ref,
    gate_ref,
    weights_ref,
    q_hbm,
    normed_hbm,
    kv_hbm,
    attended_hbm,
    middle_hbm,
    hidden_hbm,
    hidden_all_ref,
    gate_full_ref,
    grad_ref,
    q_ref,
    normed_ref,
    kv_ref,
    attended_ref,
    middle_ref,
    qkv_v,
    wo_v,
    gate_v,
    hidden_v,
    bias,
    top,
    total,
    acc,
    load_sem,
    own_sem,
    gate_own,
    gate_s0,
    gate_s1,
    gate_s2,
    gate_s3,
    keep_sem,
    *line_sems,
):
    ctx, me, chip, core, sibling = place()
    rows = tokens_ref.shape[0]
    width = tokens_ref.shape[1]
    half = rows // 2
    kv_width = KVH * HEAD_SIZE
    per_group = QUERY_HEADS // KVH
    parts = [pl.ds(0, half), pl.ds(half, half)]
    loads = [
        pltpu.make_async_copy(src, dst, load_sem.at[k])
        for k, (src, dst) in enumerate(((qkv_ref, qkv_v), (wo_ref, wo_v)))
    ]
    for copy in loads:
        copy.start()
    greet(chips, peers_of(me, fsdp), True)
    gate_gather = ShardGather(
        gate_w_ref,
        gate_full_ref,
        gate_v,
        (gate_own, gate_s0, gate_s1, gate_s2, gate_s3),
        fsdp,
    )
    gate_gather.start()
    kv_line = LineGather(
        [kv_ref.at[0, 0], table_all_ref.at[0, 0]], [kv_ref, table_all_ref], line_sems[:7], chips
    )
    grad_line = LineGather([None], [grad_ref], line_sems[7:14], chips)
    hidden_lines = [
        LineGather(
            [hidden_v.at[parts[0]]], [hidden_all_ref.at[:, :, parts[0]]], line_sems[14:21], chips
        ),
        LineGather(
            [hidden_v.at[parts[1]], weights_ref.at[0, 0]],
            [hidden_all_ref.at[:, :, parts[1]], weights_ref],
            line_sems[21:28],
            chips,
        ),
    ]

    def normed(value, gain):
        return value * lax.rsqrt(jnp.mean(value * value, axis=-1, keepdims=True) + EPSILON) * gain

    table_all_ref[0, 0] = table_ref[...]
    for part in parts:
        normed_ref[part, :] = normed(
            tokens_ref[part, :].astype(F32), gain_a_ref[...]
        ).astype(BF16)
    loads[0].wait()
    for part in parts:
        rows_one = normed_ref[part, :]
        cosine, sine = cos_ref[part, :], sin_ref[part, :]
        for h in range(KVH):
            columns = slice(width + h * HEAD_SIZE, width + (h + 1) * HEAD_SIZE)
            value = dot(rows_one, qkv_v[:, columns], NN)
            value = value * cosine + pltpu.roll(value, HEAD_SIZE // 2, 1) * sine
            kv_ref[0, 0, part, h * HEAD_SIZE : (h + 1) * HEAD_SIZE] = value.astype(BF16)
        kv_ref[0, 0, part, kv_width:] = dot(
            rows_one, qkv_v[:, width + kv_width :], NN
        ).astype(BF16)
    kv_line.send(0)
    for i in range(2):
        kv_line.across(i, 0).start()
    for part in parts:
        rows_one = normed_ref[part, :]
        cosine, sine = cos_ref[part, :], sin_ref[part, :]
        for h in range(0, QUERY_HEADS, 2):
            pre = dot(rows_one, qkv_v[:, h * HEAD_SIZE : (h + 2) * HEAD_SIZE], NN)
            for k in range(2):
                value = pre[:, k * HEAD_SIZE : (k + 1) * HEAD_SIZE]
                value = value * cosine + pltpu.roll(value, HEAD_SIZE // 2, 1) * sine
                q_ref[part, (h + k) * HEAD_SIZE : (h + k + 1) * HEAD_SIZE] = value.astype(BF16)

    def turn(index, r):
        part = parts[index]
        for q in range(2):
            gap = oq_ref[part, :] - ok_ref[q * chips + r]
            bias[:, q * rows : (q + 1) * rows] = jnp.where(
                (gap >= 0) & (gap <= pq_ref[part, :]), 0.0, MASKED
            )

        def one(h, carry):
            group = lax.div(h, per_group)
            columns = pl.ds(pl.multiple_of(h * HEAD_SIZE, HEAD_SIZE), HEAD_SIZE)
            key_columns = pl.ds(pl.multiple_of(group * HEAD_SIZE, HEAD_SIZE), HEAD_SIZE)
            value_columns = pl.ds(
                pl.multiple_of(kv_width + group * HEAD_SIZE, HEAD_SIZE), HEAD_SIZE
            )
            query = q_ref[part, columns]
            scores = []
            peak = top[h, part, :]
            for q in range(2):
                raw = dot(query, kv_ref[q, r, :, key_columns], NT) * (scale * LOG2E)
                raw = raw + bias[:, q * rows : (q + 1) * rows]
                scores.append(raw)
            best = scores[0][:, :LANES]
            for q in range(2):
                for k in range(rows // LANES):
                    best = jnp.maximum(best, scores[q][:, k * LANES : (k + 1) * LANES])
            new = jnp.maximum(peak, jnp.max(best, axis=1, keepdims=True))
            fade = jnp.exp2(peak - new)
            wide = jnp.concatenate([new] * (rows // LANES), axis=1)
            mass = total[h] * fade
            out = acc[:, columns] * fade
            for q in range(2):
                probs = jnp.exp2(scores[q] - wide)
                for k in range(rows // LANES):
                    mass = mass + probs[:, k * LANES : (k + 1) * LANES]
                out = out + dot(probs.astype(BF16), kv_ref[q, r, :, value_columns], NN)
            top[h, part, :] = new
            total[h] = mass
            acc[:, columns] = out
            return carry

        lax.fori_loop(0, QUERY_HEADS, one, 0)

    def begin(index):
        top[:, parts[index], :] = jnp.full((QUERY_HEADS, half, LANES), MASKED, F32)
        total[...] = jnp.zeros_like(total)
        acc[...] = jnp.zeros_like(acc)

    def end(index):
        part = parts[index]
        for h in range(QUERY_HEADS):
            columns = slice(h * HEAD_SIZE, (h + 1) * HEAD_SIZE)
            mass = jnp.sum(total[h], axis=1, keepdims=True)
            attended_ref[part, columns] = (acc[:, columns] / mass).astype(BF16)
            top[h, part, :] = top[h, part, :] + jnp.log2(mass)
        if index == 0:
            loads[1].wait()
        middle = tokens_ref[part, :].astype(F32) + dot(attended_ref[part, :], wo_v[...], NN)
        middle_ref[part, :] = middle
        rows_two = normed(middle, gain_b_ref[...]).astype(BF16)
        hidden_v[part, :] = rows_two
        routed = routed_ref[part, :] > 0.0
        logits = jnp.where(routed, dot(rows_two, small_ref[...], NN), MASKED)
        power = jnp.exp(logits - jnp.max(logits, axis=1, keepdims=True))
        power = jnp.where(routed, power, 0.0)
        gate_ref[part, :] = power / jnp.sum(power, axis=1, keepdims=True)
        if index == 1:
            weights_ref[0, 0] = gate_ref[...].T[:expert_count, :]
        line = hidden_lines[index]
        line.send(0)
        for i in range(line.count):
            line.across(i, 0).start()
        own(index).start()

    def keep(k, src, dst):
        return pltpu.make_async_copy(src, dst, keep_sem.at[k])

    def own(index):
        return pltpu.make_async_copy(
            hidden_v.at[parts[index]],
            hidden_all_ref.at[0, 0, parts[index]],
            own_sem.at[index],
        )

    begin(0)
    keep(0, q_ref, q_hbm).start()
    keep(1, normed_ref, normed_hbm).start()

    def first_turn(t, carry):
        for k in range(1, chips):

            @pl.when(t == k)
            def _():
                kv_line.receive(k - 1)
                if k < chips - 1:
                    kv_line.send(k)
                if k == chips - 2:
                    grad_line.send(chips - 2)

        r = chunk_order(chip, chips - 1 - t, chips)
        kv_line.arrived(r)
        turn(0, r)
        return carry

    lax.fori_loop(0, chips, first_turn, 0)
    end(0)
    begin(1)
    gate_gather.hand_on()
    keep(2, kv_ref, kv_hbm).start()
    early = [step for step in range(chips - 1) if 2 * step + 2 < chips]

    def second_turn(t, carry):
        for step in early:

            @pl.when(t == 2 * step + 2)
            def _():
                hidden_lines[0].receive(step)
                if step + 1 < chips - 1:
                    hidden_lines[0].send(step + 1)

        turn(1, t)
        return carry

    lax.fori_loop(0, chips, second_turn, 0)
    grad_line.receive(chips - 2)
    late = [step for step in range(chips - 1) if step not in early]
    for step in late[:1]:
        hidden_lines[0].receive(step)
        if step + 1 < chips - 1:
            hidden_lines[0].send(step + 1)
    end(1)
    keep(3, attended_ref, attended_hbm).start()
    keep(4, middle_ref, middle_hbm).start()
    keep(5, hidden_v, hidden_hbm).start()
    for h in range(QUERY_HEADS):
        lse_ref[h] = top[h].T[:1, :]
    for step in late[1:]:
        hidden_lines[0].receive(step)
        if step + 1 < chips - 1:
            hidden_lines[0].send(step + 1)
    for step in range(chips - 1):
        hidden_lines[1].receive(step)
        if step + 1 < chips - 1:
            hidden_lines[1].send(step + 1)
    for line in hidden_lines:
        for slot in range(chips):
            line.arrived(slot)
        line.sent()
    kv_line.sent()
    gate_gather.finish()
    grad_line.finish(chips - 2)
    for index in range(2):
        own(index).wait()
    for k, (src, dst) in enumerate(
        (
            (q_ref, q_hbm),
            (normed_ref, normed_hbm),
            (kv_ref, kv_hbm),
            (attended_ref, attended_hbm),
            (middle_ref, middle_hbm),
            (hidden_v, hidden_hbm),
        )
    ):
        keep(k, src, dst).wait()


def front(
    tokens,
    gain_a,
    gain_b,
    small,
    cosine,
    sine,
    order_mine,
    pos_mine,
    order_keys,
    routed,
    table,
    qkv,
    w_out,
    w_gate,
    grad_all,
    chips,
    fsdp,
    collective_id,
):
    rows, width = tokens.shape
    expert_count = table.shape[0]
    kv_width = KVH * HEAD_SIZE
    vmem = pl.BlockSpec(memory_space=pltpu.VMEM)
    anywhere = pl.BlockSpec(memory_space=pl.ANY)
    shapes = [
        ((2, chips, expert_count, rows), F32),
        ((QUERY_HEADS, 1, rows), F32),
        ((rows, LANES), F32),
        ((2, chips, expert_count, rows), F32),
    ]
    kept = [
        ((rows, width), BF16),
        ((rows, width), BF16),
        ((2, chips, rows, 2 * kv_width), BF16),
        ((rows, width), BF16),
        ((rows, width), F32),
    ]
    gathered = [
        ((rows, width), BF16),
        ((2, chips, rows, width), BF16),
        ((w_gate.shape[0], width, w_gate.shape[2]), BF16),
        (grad_all.shape, BF16),
    ]
    flops = 4 * rows * (2 * chips * rows) * width + 2 * rows * width * (2 * width + 2 * kv_width)
    return pl.pallas_call(
        functools.partial(front_kernel, HEAD_SIZE ** (-0.5), chips, fsdp, expert_count),
        out_shape=[
            jax.ShapeDtypeStruct(shape, kind) for shape, kind in shapes + kept + gathered
        ],
        in_specs=[vmem] * 11 + [anywhere] * 4,
        out_specs=[vmem] * 4 + [anywhere] * 9,
        scratch_shapes=[pltpu.VMEM(shape, kind) for shape, kind in kept]
        + [
            pltpu.VMEM(qkv.shape, BF16),
            pltpu.VMEM(w_out.shape, BF16),
            pltpu.VMEM(w_gate.shape, BF16),
            pltpu.VMEM((rows, width), BF16),
            pltpu.VMEM((rows // 2, 2 * rows), F32),
            pltpu.VMEM((QUERY_HEADS, rows, LANES), F32),
            pltpu.VMEM((QUERY_HEADS, rows // 2, LANES), F32),
            pltpu.VMEM((rows // 2, width), F32),
            pltpu.SemaphoreType.DMA((2,)),
            pltpu.SemaphoreType.DMA((2,)),
            pltpu.SemaphoreType.DMA,
        ]
        + spread_sems(fsdp)
        + [pltpu.SemaphoreType.DMA((6,))]
        + line_scratch([None] * 2, chips)
        + line_scratch([None], chips)
        + line_scratch([None], chips)
        + line_scratch([None] * 2, chips),
        input_output_aliases={14: 12},
        compiler_params=pltpu.CompilerParams(
            collective_id=collective_id, has_side_effects=True, vmem_limit_bytes=FRONT_VMEM_BYTES
        ),
        cost_estimate=pl.CostEstimate(
            flops=flops, bytes_accessed=40_000_000, transcendentals=rows * rows * chips * 24
        ),
        name="front",
    )(
        tokens,
        gain_a[None, :],
        gain_b[None, :],
        small,
        cosine,
        sine,
        order_mine[:, None],
        pos_mine[:, None],
        order_keys.reshape(2 * chips, 1, rows),
        routed,
        table,
        qkv,
        w_out,
        w_gate,
        grad_all,
    )


def attention_back_kernel(
    scale,
    chips,
    fsdp,
    early_dense,
    q_ref,
    k_ref,
    v_ref,
    o_ref,
    do_ref,
    lse_ref,
    oq_ref,
    pq_ref,
    ok_ref,
    cos_ref,
    sin_ref,
    rows_ref,
    dense_ref,
    dq_ref,
    kv_ref,
    own_ref,
    right_ref,
    left_ref,
    dense_out_ref,
    bias,
    dk_acc,
    dv_acc,
    kv_total,
    mine_v,
    pair,
    got,
    kv_v,
    kv_pair,
    kv_got,
    load_sem,
    store_sem,
    swap_send,
    swap_recv,
    r_send,
    r_recv,
    l_send,
    l_recv,
    kv_swap_send,
    kv_swap_recv,
    kr_send,
    kr_recv,
    kl_send,
    kl_recv,
    *dense_refs,
):
    ctx, me, chip, core, sibling = place()
    keys = k_ref.shape[0]
    tiles = keys // KEY_TILE
    rows = q_ref.shape[0]
    per_group = QUERY_HEADS // KVH
    head = pl.program_id(0)

    order = []
    for step in range(chips - 1):
        for r in (chips - 1 - step, step + 1):
            if r not in order:
                order.append(r)
    order.append(0)
    swaps = [
        remote(rows_ref.at[1, r], pair.at[r], swap_send.at[r], swap_recv.at[r], (sibling, me))
        for r in range(chips)
    ]
    slots = mine_v.shape[0]
    loads = [
        pltpu.make_async_copy(rows_ref.at[0, r], mine_v.at[j % slots], load_sem.at[j % slots])
        for j, r in enumerate(order)
    ]
    line = LineSum(
        chips,
        lambda r: lambda: [pair.at[r]],
        lambda r: pair.at[r],
        got,
        (r_send, r_recv, l_send, l_recv),
    )

    def join(j):
        loads[j].wait()
        swaps[order[j]].wait_recv()
        add_into(pair.at[order[j]], [pair.at[order[j]], mine_v.at[j % slots]])
        if j + slots < chips:
            loads[j + slots].start()

    if early_dense:
        dense_v, dense_load = dense_refs[:2]
        buffers = dense_refs[2 : 2 + DENSE_BUFFERS]
        dense = DenseSum(
            dense_ref,
            lambda j, owner: dense_v.at[j],
            dense_out_ref,
            buffers,
            dense_refs[2 + DENSE_BUFFERS :],
            fsdp,
            chips,
        )
        dense_loads = [
            pltpu.make_async_copy(dense_ref.at[owner, core], dense_v.at[j], dense_load.at[j])
            for j, owner in enumerate(dense.owners)
        ]
        stages = dense.stages()
        ahead = len(stages) // 2 + 1
        at_head = {QUERY_HEADS - 1 - ahead + k: k for k in range(ahead)}

    def kv_swap(group, r):
        return remote(
            kv_v.at[group, 1, r],
            kv_pair.at[group, r],
            kv_swap_send.at[group, r],
            kv_swap_recv.at[group, r],
            (sibling, me),
        )

    def kv_line(group):
        def held(r):
            kv_swap(group, r).wait_recv()
            return lambda: [kv_v.at[group, 0, r], kv_pair.at[group, r]]

        return LineSum(
            chips,
            held,
            lambda r: kv_pair.at[group, r],
            kv_got.at[group],
            tuple(sem.at[group] for sem in (kr_send, kr_recv, kl_send, kl_recv)),
        )

    def kv_start(group):
        for q in range(2):
            for r in range(chips):
                part = pl.ds((q * chips + r) * rows, rows)
                kv_v[group, q, r, :, :HEAD_SIZE] = (dk_acc[part, :] * scale).astype(BF16)
                kv_v[group, q, r, :, HEAD_SIZE:] = dv_acc[part, :].astype(BF16)
        for r in order:
            kv_swap(group, r).start()

    @pl.when(head == 0)
    def _():
        greet(chips, peers_of(me, fsdp) if early_dense else [], True)
        if early_dense:
            for copy in dense_loads:
                copy.start()
            dense.start()
        for r in order:
            swaps[r].start()
        for copy in loads[:slots]:
            copy.start()

        def fill(t, carry):
            tile = pl.ds(pl.multiple_of(t * KEY_TILE, KEY_TILE), KEY_TILE)
            key_order = jnp.broadcast_to(ok_ref[:, tile], (8, KEY_TILE)).T[:, :1]
            gap = oq_ref[...] - key_order
            bias[tile, :] = jnp.where((gap >= 0) & (gap <= pq_ref[...]), 0.0, MASKED)
            return carry

        lax.fori_loop(0, tiles, fill, 0)

    @pl.when(lax.rem(head, per_group) == 0)
    def _():
        dk_acc[...] = jnp.zeros_like(dk_acc)
        dv_acc[...] = jnp.zeros_like(dv_acc)

    query = q_ref[...]
    grad = do_ref[...]
    lse = lse_ref[0]
    product = grad.astype(F32) * o_ref[...].astype(F32)
    delta = jnp.sum(product.T, axis=0, keepdims=True)

    def step(t, acc):
        tile = pl.ds(pl.multiple_of(t * KEY_TILE, KEY_TILE), KEY_TILE)
        key = k_ref[tile, :]
        raw = dot(key, query, NT) * (scale * LOG2E) + bias[tile, :]
        probs = jnp.exp2(raw - lse)
        prob_grad = dot(v_ref[tile, :], grad, NT)
        score_grad = (probs * (prob_grad - delta)).astype(BF16)
        dv_acc[tile, :] += dot(probs.astype(BF16), grad, NN)
        dk_acc[tile, :] += dot(score_grad, query, NN)
        return acc + dot(score_grad, key, TN)

    acc = lax.fori_loop(0, tiles, step, jnp.zeros((rows, HEAD_SIZE), F32))
    def turn_back(value):
        back = value * cos_ref[...] - pltpu.roll(value, HEAD_SIZE // 2, 1) * sin_ref[...]
        return back.astype(BF16)

    dq_ref[...] = turn_back(acc * scale)

    last = QUERY_HEADS - 1
    stride = max(1, last // (chips - 2))
    early = {per_group + 2 * s: s for s in range(chips - 1) if per_group + 2 * s < last}
    for h in range(QUERY_HEADS):

        @pl.when(head == h)
        def _():
            if h == 0:
                for j in range(min(2, chips)):
                    join(j)
            if h == 1:
                for j in range(2, chips):
                    join(j)
            if early_dense and h == 1:
                for copy in dense_loads:
                    copy.wait()
                dense.cross_over()
            if early_dense and h in at_head:
                stages[at_head[h]]()
            for s in range(chips - 2):
                if h == (s * stride if s == 0 else max(1, s * stride)):
                    line.step(s)
            if h % per_group == per_group - 1:
                kv_start(h // per_group)
            if h in early:
                kv_line(0).step(early[h])

    @pl.when(head == last)
    def _():
        def store(k, r, target):
            return pltpu.make_async_copy(pair.at[r], target, store_sem.at[k])

        @pl.when((chip >= 1) & (chip + 1 < chips))
        def _():
            add_into(pair.at[1], [pair.at[1], line.from_left(chips - 3)])
            add_into(pair.at[chips - 1], [pair.at[chips - 1], line.from_right(chips - 3)])

        for copy in (
            store(0, 0, own_ref),
            store(1, 1, right_ref),
            store(2, chips - 1, left_ref),
        ):
            copy.start()
        rest = stages[ahead:] if early_dense else []
        for group in range(KVH):
            one = kv_line(group)
            for s in range(chips - 1):
                if group > 0 or s not in early.values():
                    one.step(s)
                    if rest:
                        rest.pop(0)()
            one.total(kv_total)
            kv_ref[:, group * HEAD_SIZE : (group + 1) * HEAD_SIZE] = turn_back(
                kv_total[:, :HEAD_SIZE]
            )
            kv_ref[:, (KVH + group) * HEAD_SIZE : (KVH + group + 1) * HEAD_SIZE] = kv_total[
                :, HEAD_SIZE:
            ].astype(BF16)
        for stage in rest:
            stage()
        if early_dense:
            dense.finish()
        for group in range(KVH):
            kv_line(group).finish()
            for r in range(chips):
                kv_swap(group, r).wait_send()
        line.finish(chips - 2)
        for swap in swaps:
            swap.wait_send()
        for copy in (
            store(0, 0, own_ref),
            store(1, 1, right_ref),
            store(2, chips - 1, left_ref),
        ):
            copy.wait()


def attention_back(
    queries,
    kv,
    attended,
    attended_grad,
    lse,
    order_mine,
    pos_mine,
    order_keys,
    cosine,
    sine,
    out_rows,
    dense,
    fsdp,
    early_dense,
    collective_id,
):
    rows = queries.shape[0]
    keys = kv.shape[0]
    unused, chips, unused, width = out_rows.shape
    per_group = QUERY_HEADS // KVH
    head_rows = pl.BlockSpec((rows, HEAD_SIZE), lambda h: (0, h))
    anywhere = pl.BlockSpec(memory_space=pl.ANY)
    return pl.pallas_call(
        functools.partial(
            attention_back_kernel, HEAD_SIZE ** (-0.5), chips, fsdp, early_dense
        ),
        grid=(QUERY_HEADS,),
        out_shape=[
            jax.ShapeDtypeStruct(queries.shape, BF16),
            jax.ShapeDtypeStruct((rows, 2 * KVH * HEAD_SIZE), BF16),
        ]
        + [jax.ShapeDtypeStruct((rows, width), BF16)] * 3
        + [jax.ShapeDtypeStruct(dense.shape[1:] if early_dense else (16, LANES), BF16)],
        in_specs=[
            head_rows,
            pl.BlockSpec((keys, HEAD_SIZE), lambda h: (0, h // per_group)),
            pl.BlockSpec((keys, HEAD_SIZE), lambda h: (0, KVH + h // per_group)),
            head_rows,
            head_rows,
            pl.BlockSpec((1, 1, rows), lambda h: (h, 0, 0)),
            pl.BlockSpec((1, rows), lambda h: (0, 0)),
            pl.BlockSpec((1, rows), lambda h: (0, 0)),
            pl.BlockSpec((1, keys), lambda h: (0, 0)),
            pl.BlockSpec((rows, HEAD_SIZE), lambda h: (0, 0)),
            pl.BlockSpec((rows, HEAD_SIZE), lambda h: (0, 0)),
            anywhere,
            anywhere,
        ],
        out_specs=[
            head_rows,
            pl.BlockSpec((rows, 2 * KVH * HEAD_SIZE), lambda h: (0, 0)),
            anywhere,
            anywhere,
            anywhere,
            pl.BlockSpec(dense.shape[1:], lambda h: (0, 0, 0)) if early_dense else anywhere,
        ],
        scratch_shapes=[
            pltpu.VMEM((keys, rows), F32),
            pltpu.VMEM((keys, HEAD_SIZE), F32),
            pltpu.VMEM((keys, HEAD_SIZE), F32),
            pltpu.VMEM((rows, 2 * HEAD_SIZE), F32),
            pltpu.VMEM((2 if chips <= 4 else 1, rows, width), BF16),
            pltpu.VMEM((chips, rows, width), BF16),
            pltpu.VMEM((chips + 1, rows, width), BF16),
            pltpu.VMEM((KVH, 2, chips, rows, 2 * HEAD_SIZE), BF16),
            pltpu.VMEM((KVH, chips, rows, 2 * HEAD_SIZE), BF16),
            pltpu.VMEM((KVH, chips + 1, rows, 2 * HEAD_SIZE), BF16),
            pltpu.SemaphoreType.DMA((2,)),
            pltpu.SemaphoreType.DMA((3,)),
            pltpu.SemaphoreType.DMA((chips,)),
            pltpu.SemaphoreType.DMA((chips,)),
        ]
        + [pltpu.SemaphoreType.DMA((chips - 1,)) for unused in range(4)]
        + [pltpu.SemaphoreType.DMA((KVH, chips)) for unused in range(2)]
        + [pltpu.SemaphoreType.DMA((KVH, chips - 1)) for unused in range(4)]
        + (
            [
                pltpu.VMEM((fsdp,) + dense.shape[2:], BF16),
                pltpu.SemaphoreType.DMA((fsdp,)),
            ]
            + dense_buffers(dense.shape[2], dense.shape[3], fsdp, chips)
            + dense_sems(fsdp, chips)
            if early_dense
            else []
        ),
        compiler_params=pltpu.CompilerParams(
            collective_id=collective_id, has_side_effects=True, vmem_limit_bytes=BACK_VMEM_BYTES
        ),
        cost_estimate=pl.CostEstimate(
            flops=10 * rows * keys * HEAD_SIZE * QUERY_HEADS,
            bytes_accessed=10 * rows * QUERY_HEADS * HEAD_SIZE + 8 * keys * KVH * HEAD_SIZE,
            transcendentals=rows * keys * QUERY_HEADS,
        ),
        name="attention_back",
    )(
        queries,
        kv,
        kv,
        attended,
        attended_grad,
        lse,
        order_mine[None, :],
        pos_mine[None, :],
        order_keys[None, :],
        cosine,
        sine,
        out_rows,
        dense,
    )


def experts_kernel(
    capacity,
    local_experts,
    expert_count,
    chips,
    fsdp,
    per,
    hidden_ref,
    grad_ref,
    table_ref,
    weight_ref,
    gate_ref,
    up_ref,
    down_ref,
    returned_ref,
    out_ref,
    gate_grad_ref,
    gate_got_ref,
    up_grad_ref,
    down_grad_ref,
    x_ref,
    pg_ref,
    inner_ref,
    da_ref,
    db_ref,
    gate_v,
    up_v,
    down_v,
    hidden_v,
    grad_v,
    out_v,
    x_v,
    pg_v,
    g_v,
    inner_v,
    da_v,
    db_v,
    mine_v,
    other_v,
    pair,
    got,
    stage_tall,
    weight_sem,
    load_sem,
    out_sem,
    save_sem,
    swap_send,
    swap_recv,
    right_send,
    right_recv,
    left_send,
    left_recv,
    stage_sem,
    tile_own,
    tile_send,
    tile_recv,
):
    ctx, me, chip, core, sibling = place()
    peers = peers_of(me, fsdp)
    tokens = hidden_v.shape[1]
    width = hidden_v.shape[2]
    slots = x_v.shape[1]
    slot_rows = slots // 2
    units = inner_v.shape[2]
    total_rows = x_ref.shape[1]
    first = ctx * local_experts

    weights_in = [
        pltpu.make_async_copy(src, dst, weight_sem.at[k])
        for k, (src, dst) in enumerate(
            ((gate_ref, gate_v), (up_ref, up_v), (down_ref, down_v))
        )
    ]

    def load(i):
        r = chunk_order(chip, i, chips)
        return [
            pltpu.make_async_copy(hidden_ref.at[:, r], hidden_v, load_sem.at[0]),
            pltpu.make_async_copy(grad_ref.at[:, r], grad_v, load_sem.at[1]),
        ]

    def saves(i):
        rows = pl.ds(i * slots, slots)
        return [
            pltpu.make_async_copy(src, dst.at[:, rows], save_sem.at[k])
            for k, (src, dst) in enumerate(
                ((x_v, x_ref), (pg_v, pg_ref), (inner_v, inner_ref), (da_v, da_ref), (db_v, db_ref))
            )
        ]

    def out_copies(i):
        r = chunk_order(chip, i, chips)
        return [
            pltpu.make_async_copy(out_v.at[q], out_ref.at[q, r], out_sem.at[q]) for q in range(2)
        ]

    def swap(i):
        r = chunk_order(chip, i, chips)
        return remote(
            other_v.at[lax.rem(i, 2)],
            pair.at[r],
            swap_send.at[r],
            swap_recv.at[r],
            (sibling, me),
        )

    def join(i):
        r = chunk_order(chip, i, chips)
        swap(i).wait_recv()
        add_into(pair.at[r], [pair.at[r], mine_v.at[lax.rem(i, 2)]])

    line = LineSum(
        chips,
        lambda r: lambda: [pair.at[r]],
        lambda r: pair.at[r],
        got,
        (right_send, right_recv, left_send, left_recv),
    )

    for copy in load(0) + weights_in:
        copy.start()
    greet(chips, peers if per == 1 else [], True)

    slot = lax.broadcasted_iota(jnp.int32, (slot_rows, tokens), 0).astype(F32) + 1.0
    slot = jnp.where(slot <= capacity, slot, -1.0)
    lane = lax.broadcasted_iota(jnp.int32, (slots, LANES), 1)

    def chunk(i, carry):
        r = chunk_order(chip, i, chips)
        for copy in load(i):
            copy.wait()

        @pl.when(i >= 1)
        def _():
            for copy in saves(i - 1):
                copy.wait()

        picks = [[], []]
        weight_rows = []
        for e in range(local_experts):
            rows_w = []
            for q in range(2):
                hit = slot == table_ref[q, r, pl.ds(first + e, 1), :]
                pick = jnp.where(hit, 1.0, 0.0).astype(BF16)
                weight = weight_ref[q, r, pl.ds(first + e, 1), :]
                w = jnp.sum(jnp.where(hit, weight, 0.0), axis=1, keepdims=True)
                rows = pl.ds(q * slot_rows, slot_rows)
                x_v[e, rows, :] = dot(pick, hidden_v[q], NN).astype(BF16)
                g = dot(pick, grad_v[q], NN)
                g_v[e, rows, :] = g.astype(BF16)
                pg_v[e, rows, :] = (w * g).astype(BF16)
                picks[q].append(pick)
                rows_w.append(w)
            weight_rows.append(jnp.concatenate(rows_w, axis=0))

        @pl.when(i + 1 < chips)
        def _():
            for copy in load(i + 1):
                copy.start()

        @pl.when(i == 0)
        def _():
            for copy in weights_in:
                copy.wait()

        outs = [[], []]
        backs = [[], []]
        for e in range(local_experts):
            x = x_v[e]
            pair_grad = pg_v[e]
            w = weight_rows[e]
            gate = gate_v[e * width : (e + 1) * width, :]
            up = up_v[e * width : (e + 1) * width, :]
            down = down_v[e * units : (e + 1) * units, :]
            gate_pre = dot(x, gate, NN)
            up_pre = dot(x, up, NN)
            sig = jax.nn.sigmoid(gate_pre)
            silu = gate_pre * sig
            inner = (silu * up_pre).astype(BF16)
            inner_v[e] = inner
            expert_out = dot(inner, down, NN).astype(BF16).astype(F32)
            gate_grad = jnp.sum(expert_out * g_v[e].astype(F32), axis=1, keepdims=True)
            inner_grad = dot(pair_grad, down, NT)
            da = (inner_grad * up_pre * sig * (1.0 + gate_pre * (1.0 - sig))).astype(BF16)
            db = (inner_grad * silu).astype(BF16)
            da_v[e] = da
            db_v[e] = db
            row_grad = (dot(da, gate, NT) + dot(db, up, NT)).astype(BF16)
            high = gate_grad.astype(BF16).astype(F32)
            extra = jnp.where(lane == first + e, high, 0.0) + jnp.where(
                lane == expert_count + first + e, gate_grad - high, 0.0
            )
            back = jnp.concatenate([row_grad, extra.astype(BF16)], axis=1)
            out_rows = (w * expert_out).astype(BF16)
            for q in range(2):
                part = slice(q * slot_rows, (q + 1) * slot_rows)
                outs[q].append(out_rows[part])
                backs[q].append(back[part])

        for copy in saves(i):
            copy.start()

        @pl.when(i >= 1)
        def _():
            for copy in out_copies(i - 1):
                copy.wait()

        @pl.when(i >= 2)
        def _():
            swap(i - 2).wait_send()

        for q in range(2):
            pick = jnp.concatenate(picks[q], axis=0)
            held = other_v if q else mine_v
            held[lax.rem(i, 2)] = dot(pick, jnp.concatenate(backs[q], axis=0), TN).astype(BF16)
            if q:
                swap(i).start()
        for q in range(2):
            pick = jnp.concatenate(picks[q], axis=0)
            out_v[q] = dot(pick, jnp.concatenate(outs[q], axis=0), TN).astype(BF16)
        for copy in out_copies(i):
            copy.start()

        @pl.when(i == 0)
        def _():
            join(0)
            line.step(0)

        @pl.when(i >= 2)
        def _():
            join(i - 1)

        for step in range(1, chips - 1):
            if 2 * step < chips:

                @pl.when(i == 2 * step)
                def _():
                    line.step(step)

        return carry

    lax.fori_loop(0, chips, chunk, 0)
    join(chips - 1)
    for copy in saves(chips - 1):
        copy.wait()
    for copy in out_copies(chips - 1):
        copy.wait()
    for i in range(max(0, chips - 2), chips):
        swap(i).wait_send()

    shard = width // fsdp
    blocks = fsdp // per
    block = per * shard

    def fetch(copies):
        copies = [
            pltpu.make_async_copy(src, dst, save_sem.at[k])
            for k, (src, dst) in enumerate(copies)
        ]
        for copy in copies:
            copy.start()
        for copy in copies:
            copy.wait()

    def products(e, staged, target, product):
        def write(f):
            return [
                pltpu.make_async_copy(
                    staged(lax.rem(f, 2), p),
                    target.at[f * per + p, e],
                    stage_sem.at[lax.rem(f, 2), p],
                )
                for p in range(per)
            ]

        def one(f, carry):
            @pl.when(f >= 2)
            def _():
                for copy in write(f - 2):
                    copy.wait()

            product(f)
            for copy in write(f):
                copy.start()
            return carry

        lax.fori_loop(0, blocks, one, 0)
        for f in range(max(0, blocks - 2), blocks):
            for copy in write(f):
                copy.wait()

    def stage_wide(slot, p):
        return hidden_v.at[slot, pl.ds(p * shard, shard), pl.ds(0, units)]

    def wide(e, held, staged, target):
        def product(f):
            columns = pl.ds(pl.multiple_of(f * block, LANES), block)
            value = dot(
                down_v[:total_rows, columns],
                held[e * total_rows : (e + 1) * total_rows, :],
                TN,
            ).astype(BF16)
            for p in range(per):
                staged(lax.rem(f, 2), p)[...] = value[p * shard : (p + 1) * shard, :]

        products(e, staged, target, product)

    def tall(e, target):
        def product(f):
            columns = pl.ds(pl.multiple_of(f * block, LANES), block)
            value = dot(
                gate_v[e * total_rows : (e + 1) * total_rows, :],
                down_v[:total_rows, columns],
                TN,
            ).astype(BF16)
            for p in range(per):
                stage_tall[lax.rem(f, 2), p] = value[:, p * shard : (p + 1) * shard]

        products(e, lambda slot, p: stage_tall.at[slot, p], target, product)

    def tile(e, j):
        held = (hidden_v, grad_v)[e]
        return held.at[j // 2, pl.ds(0, shard), pl.ds((j % 2) * units, units)]

    def tile_copy(e, j):
        if j == len(peers):
            return pltpu.make_async_copy(tile(e, j), gate_grad_ref.at[e], tile_own.at[e])
        return remote(
            tile(e, j),
            gate_got_ref.at[j, e],
            tile_send.at[e, j],
            tile_recv.at[e, j],
            (ctx, peers[j]),
        )

    def gate_tiles(e):
        for j, owner in enumerate(peers + [me]):
            columns = pl.ds(pl.multiple_of(owner * shard, LANES), shard)
            tile(e, j)[...] = dot(
                down_v[:total_rows, columns],
                gate_v[e * total_rows : (e + 1) * total_rows, :],
                TN,
            ).astype(BF16)
            tile_copy(e, j).start()

    def held_rows(k):
        return pl.ds(k * total_rows, total_rows)

    later = [
        pltpu.make_async_copy(db_ref.at[k], up_v.at[held_rows(k)], save_sem.at[1 + local_experts + k])
        for k in range(local_experts)
    ]

    def fetch_x(e):
        copies = [(x_ref.at[e], down_v.at[:total_rows])]
        if e == 0:
            copies += [(da_ref.at[k], gate_v.at[held_rows(k)]) for k in range(local_experts)]

        def run():
            if e == 0:
                for copy in later:
                    copy.start()
            fetch(copies)
            if e == 1:
                for copy in later:
                    copy.wait()

        return run

    def stage_up(slot, p):
        return out_v.at[slot, pl.ds(p * shard, shard), pl.ds(0, units)]

    work = []
    for e in range(local_experts):
        work.append(fetch_x(e))
        if per == 1:
            work.append(lambda e=e: gate_tiles(e))
        else:
            work.append(lambda e=e: wide(e, gate_v, stage_wide, gate_grad_ref))
        if e > 0:
            work.append(lambda e=e: wide(e, up_v, stage_up, up_grad_ref))
    work.append(lambda: fetch([(x_ref.at[0], down_v.at[:total_rows])]))
    work.append(lambda: wide(0, up_v, stage_up, up_grad_ref))
    for e in range(local_experts):
        copies = [(pg_ref.at[e], down_v.at[:total_rows])]
        if e == 0:
            for k in range(local_experts):
                copies.append((inner_ref.at[k], gate_v.at[pl.ds(k * total_rows, total_rows)]))
        work.append(lambda copies=copies: fetch(copies))
        work.append(lambda e=e: tall(e, down_grad_ref))
    late = [step for step in range(1, chips - 1) if 2 * step >= chips]
    for n, task in enumerate(work):
        task()
        if n == LINE_TASK or (n > LINE_TASK and late):
            if late:
                line.step(late.pop(0))
    for step in late:
        line.step(step)

    line.total(returned_ref)
    line.finish()
    if per == 1:
        for e in range(local_experts):
            for j in range(fsdp):
                tile_copy(e, j).wait()


def experts_pass(
    hidden, grad, table, weights, gate, up, down, capacity, expert_count, fsdp, collective_id
):
    unused, chips, tokens, width = grad.shape
    local_experts, unused, units = gate.shape
    slots = 2 * SLOT_STEP * -(-capacity // SLOT_STEP)
    total = chips * slots
    shard = width // fsdp
    per = 1 if shard % LANES == 0 else 2
    wide = width + LANES
    anywhere = pl.BlockSpec(memory_space=pl.ANY)
    vmem = pl.BlockSpec(memory_space=pltpu.VMEM)
    flops = 2 * total * width * units * local_experts * 9 + 8 * total * tokens * width
    saved = [(local_experts, total, width)] * 2 + [(local_experts, total, units)] * 3
    held = [(local_experts, slots, width)] * 3 + [(local_experts, slots, units)] * 3
    outs = pl.pallas_call(
        functools.partial(
            experts_kernel, capacity, local_experts, expert_count, chips, fsdp, per
        ),
        out_shape=[
            jax.ShapeDtypeStruct((tokens, wide), BF16),
            jax.ShapeDtypeStruct(hidden.shape, BF16),
            jax.ShapeDtypeStruct(
                ((fsdp,) if per > 1 else ()) + (local_experts, shard, units), BF16
            ),
            jax.ShapeDtypeStruct(
                (fsdp - 1, local_experts, shard, units) if per == 1 else (1, 1, 16, LANES), BF16
            ),
            jax.ShapeDtypeStruct((fsdp, local_experts, shard, units), BF16),
            jax.ShapeDtypeStruct((fsdp, local_experts, units, shard), BF16),
        ]
        + [jax.ShapeDtypeStruct(shape, BF16) for shape in saved],
        in_specs=[anywhere, anywhere, vmem, vmem, anywhere, anywhere, anywhere],
        out_specs=[vmem] + [anywhere] * 10,
        input_output_aliases={0: 1},
        scratch_shapes=[
            pltpu.VMEM((local_experts * width, units), BF16),
            pltpu.VMEM((local_experts * width, units), BF16),
            pltpu.VMEM((local_experts * units, width), BF16),
            pltpu.VMEM((2, tokens, width), BF16),
            pltpu.VMEM((2, tokens, width), BF16),
            pltpu.VMEM((2, tokens, width), BF16),
        ]
        + [pltpu.VMEM(shape, BF16) for shape in held]
        + [
            pltpu.VMEM((2, tokens, wide), BF16),
            pltpu.VMEM((2, tokens, wide), BF16),
            pltpu.VMEM((chips, tokens, wide), BF16),
            pltpu.VMEM((chips + 1, tokens, wide), BF16),
            pltpu.VMEM((2, per, units, shard), BF16),
            pltpu.SemaphoreType.DMA((3,)),
            pltpu.SemaphoreType.DMA((2,)),
            pltpu.SemaphoreType.DMA((2,)),
            pltpu.SemaphoreType.DMA((5,)),
            pltpu.SemaphoreType.DMA((chips,)),
            pltpu.SemaphoreType.DMA((chips,)),
        ]
        + [pltpu.SemaphoreType.DMA((chips - 1,)) for unused in range(4)]
        + [pltpu.SemaphoreType.DMA((2, per)), pltpu.SemaphoreType.DMA((local_experts,))]
        + [pltpu.SemaphoreType.DMA((local_experts, fsdp - 1)) for unused in range(2)],
        compiler_params=pltpu.CompilerParams(
            collective_id=collective_id, has_side_effects=True, vmem_limit_bytes=EXPERT_VMEM_BYTES
        ),
        cost_estimate=pl.CostEstimate(
            flops=flops, bytes_accessed=100_000_000, transcendentals=total * units * 2
        ),
        name="experts",
    )(
        hidden,
        grad,
        table,
        weights,
        gate.reshape(local_experts * width, units),
        up.reshape(local_experts * width, units),
        down.reshape(local_experts * units, width),
    )
    return outs[:6]


def body(
    tokens,
    grad_out,
    order,
    lengths,
    routes,
    gain_one,
    gain_two,
    w_query,
    w_key,
    w_value,
    w_out,
    w_router,
    w_gate,
    w_up,
    w_down,
):
    fsdp = lax.axis_size("fsdp")
    chips = lax.axis_size("ctx") // 2
    ctx_index = lax.axis_index("ctx")
    chip = ctx_index // 2
    core = lax.rem(ctx_index, 2)
    tok_rows = tokens.shape[1]
    width = tokens.shape[2]
    top_count = routes.shape[2]
    local_experts = w_gate.shape[0]
    expert_count = local_experts * chips * 2
    capacity = 5 * tok_rows * top_count // (4 * expert_count)
    kv_width = KVH * HEAD_SIZE
    shard = gain_one.shape[0]

    small = jnp.concatenate(
        [
            w_router,
            gain_one[:, None],
            gain_two[:, None],
            jnp.zeros((shard, LANES - expert_count - 2), BF16),
        ],
        axis=1,
    )
    qkv_full, small_full, out_full, grad_all = gather(
        [w_query, w_key, w_value, small, w_out], 3, [grad_out[0]], chips - 2, fsdp, chips, 0
    )

    qkv_full, w_up, w_down = lax.optimization_barrier((qkv_full, w_up, w_down))
    up_full, down_full = (
        lax.all_gather(w_up, "fsdp", axis=1, tiled=True),
        lax.all_gather(w_down, "fsdp", axis=2, tiled=True),
    )
    router_full = small_full[:, :expert_count]
    gain_a = small_full[:, expert_count].astype(F32)
    gain_b = small_full[:, expert_count + 1].astype(F32)

    order_row = order[0]
    start_row = ctx_index * tok_rows
    order_mine = lax.dynamic_slice_in_dim(order_row, start_row, tok_rows)
    ends = jnp.cumsum(lengths[0])
    starts = ends - lengths[0]
    past = order_mine[:, None] >= ends[None, :]
    doc_start = jnp.max(jnp.where(past, ends[None, :], starts[:1]), axis=1)
    pos_mine = order_mine - doc_start
    by_chip = jnp.roll(order_row.reshape(chips, 2, tok_rows), -chip, axis=0)
    by_chip = jnp.where(core == 0, by_chip, by_chip[:, ::-1])
    order_keys = jnp.swapaxes(by_chip, 0, 1).reshape(-1)

    route_rows = routes[0]
    route_onehot = (route_rows[:, :, None] == jnp.arange(expert_count)[None, None, :]).astype(F32)
    routed = jnp.sum(route_onehot, axis=1)
    earlier = (order_mine[None, :] < order_mine[:, None]).astype(BF16)
    ranks = jnp.dot(earlier, routed.astype(BF16), preferred_element_type=F32)
    table = jnp.where(routed > 0, jnp.minimum(ranks, capacity) + 1.0, 0.0)

    half_dim = HEAD_SIZE // 2
    freqs = ROPE_BASE ** (-2.0 * jnp.arange(half_dim).astype(F32) / HEAD_SIZE)
    angles = pos_mine.astype(F32)[:, None] * freqs[None, :]
    cosine = jnp.concatenate([jnp.cos(angles), jnp.cos(angles)], axis=1)
    sine = jnp.concatenate([-jnp.sin(angles), jnp.sin(angles)], axis=1)

    inputs = tokens[0].astype(F32)
    (
        table_all,
        lse,
        gate_weights,
        weights_all,
        queries,
        hidden_one,
        kv_all,
        attended,
        middle,
        hidden_two,
        hidden_all,
        gate_full,
        grad_all,
    ) = front(
        tokens[0],
        gain_a,
        gain_b,
        small_full,
        cosine,
        sine,
        order_mine,
        pos_mine,
        order_keys,
        jnp.pad(routed, ((0, 0), (0, LANES - expert_count))),
        table.T,
        qkv_full,
        out_full,
        w_gate,
        grad_all,
        chips,
        fsdp,
        1,
    )
    kv_all = kv_all.reshape(-1, 2 * kv_width)
    gate_weights = gate_weights[:, :expert_count]

    returned, out_rows, gate_local, gate_got, up_local, down_local = experts_pass(
        hidden_all,
        grad_all,
        table_all,
        weights_all,
        gate_full,
        up_full,
        down_full,
        capacity,
        expert_count,
        fsdp,
        5,
    )
    direct = gate_local.ndim == 3
    if not direct:
        gate_local = lax.psum_scatter(gate_local, "fsdp", scatter_dimension=0, tiled=True)[0]
    up_sum, down_sum = (
        lax.psum_scatter(part, "fsdp", scatter_dimension=0, tiled=True)
        for part in (up_local, down_local)
    )

    out_grad = grad_out[0].astype(F32)
    returned = returned.astype(F32)
    extra = returned[:, width:]
    gate_grad = extra[:, :expert_count] + extra[:, expert_count : 2 * expert_count]
    logit_grad = (
        gate_weights * (gate_grad - jnp.sum(gate_weights * gate_grad, axis=-1, keepdims=True))
    ).astype(BF16)
    router_local = jnp.einsum("td,te->de", hidden_two, logit_grad, preferred_element_type=F32)
    hidden_two_grad = returned[:, :width] + jnp.einsum(
        "te,de->td", logit_grad, router_full, preferred_element_type=F32
    )
    unused_two, norm_two_back = jax.vjp(rms_scale, middle, gain_b)
    middle_part, gain_two_local = norm_two_back(hidden_two_grad)
    middle_grad = out_grad + middle_part
    branch_grad = middle_grad.astype(BF16)
    out_local = jnp.einsum("tc,td->cd", attended, branch_grad, preferred_element_type=F32)
    attended_grad = jnp.einsum(
        "td,cd->tc", branch_grad, out_full, preferred_element_type=F32
    ).astype(BF16)

    def halves(local):
        local = local.astype(BF16).reshape(fsdp, 2, shard // 2, local.shape[1])
        pad = -local.shape[3] % (LANES * chips)
        return jnp.pad(local, ((0, 0), (0, 0), (0, 0), (0, pad))) if pad else local

    early_dense = chips <= 4
    query_grad, kv_grad, out_own, out_right, out_left, out_proj_sum = attention_back(
        queries,
        kv_all,
        attended,
        attended_grad,
        lse,
        order_mine,
        pos_mine,
        order_keys,
        cosine,
        sine,
        out_rows,
        halves(out_local) if early_dense else out_local[:16, :LANES].astype(BF16),
        fsdp,
        early_dense,
        3,
    )
    span = shard * expert_count // 16
    wide = LANES * chips * -(-max(span, shard) // (LANES * chips))
    small_local = jnp.stack(
        [
            jnp.pad(
                router_local.astype(BF16).reshape(fsdp, 16, span),
                ((0, 0), (0, 0), (0, wide - span)),
            ),
            jnp.pad(
                gain_two_local.reshape(fsdp, 1, shard).astype(BF16),
                ((0, 0), (1, 14), (0, wide - shard)),
            ),
        ],
        axis=1,
    )
    *sums, out_sum, input_grad = dense_reduce(
        [
            jax.ShapeDtypeStruct((fsdp, 2, shard // 2, width + 2 * kv_width), BF16),
            small_local,
        ]
        + ([] if early_dense else [halves(out_local)]),
        out_own,
        out_right,
        out_left,
        query_grad,
        kv_grad,
        hidden_one,
        tokens[0],
        middle_grad,
        gain_a,
        qkv_full,
        DENSE_PIECE,
        fsdp,
        chips,
        4,
    )
    qkv_sum, small_sum = sums[:2]
    if not early_dense:
        out_proj_sum = sums[2]
    edge = width + 2 * kv_width
    qkv_grads = qkv_sum.reshape(shard, -1)
    out_proj_grad = out_proj_sum.reshape(shard, -1)[:, :width]
    up_grad_out, down_grad_out = (
        after(part, kv_grad)[0].astype(F32) for part in (up_sum, down_sum)
    )
    if direct:
        gate_local, gate_got = lax.optimization_barrier((gate_local, gate_got, kv_grad))[:2]
        gate_grad_out = add(gate_local, *[gate_got[j] for j in range(fsdp - 1)])
    else:
        gate_grad_out = after(gate_local, kv_grad).astype(F32)
    result = middle + out_sum
    return (
        result.astype(BF16)[None],
        input_grad[None],
        small_sum[1, 0, :shard].astype(F32),
        small_sum[1, 1, :shard].astype(F32),
        qkv_grads[:, :width].astype(F32),
        qkv_grads[:, width : width + kv_width].astype(F32),
        qkv_grads[:, width + kv_width : edge].astype(F32),
        out_proj_grad.astype(F32),
        small_sum[0, :, :span].reshape(shard, expert_count).astype(F32),
        gate_grad_out,
        up_grad_out,
        down_grad_out,
    )


def solution(mesh):
    placed = (
        P("fsdp", "ctx", None),
        P("fsdp", "ctx", None),
        P("fsdp", None),
        P("fsdp", None),
        P("fsdp", "ctx", None),
        P("fsdp"),
        P("fsdp"),
        P("fsdp", None),
        P("fsdp", None),
        P("fsdp", None),
        P("fsdp", None),
        P("fsdp", None),
        P("ctx", "fsdp", None),
        P("ctx", "fsdp", None),
        P("ctx", None, "fsdp"),
    )
    return jax.shard_map(
        body,
        mesh=mesh,
        in_specs=placed,
        out_specs=(
            P("fsdp", "ctx", None),
            P("fsdp", "ctx", None),
            P("fsdp"),
            P("fsdp"),
            P("fsdp", None),
            P("fsdp", None),
            P("fsdp", None),
            P("fsdp", None),
            P("fsdp", None),
            P("ctx", "fsdp", None),
            P("ctx", "fsdp", None),
            P("ctx", None, "fsdp"),
        ),
        check_vma=False,
    )
```
